32 devices in a mesh: gy: 8 (over y, x, core), gz: 4 (over z).
Axes of the slice: x: 2, y: 2, z: 4, core: 2. Of those that a mesh axis runs over, the one named last changes fastest.
Arguments:
- reference_image: bfloat16 [64, 512, 2048], P(None, 'gy', 'gz'), may hold values from -6 to 6
- deformed: bfloat16 [64, 512, 2048], P(None, 'gy', 'gz'), may hold values from -12 to 12
- displacement: bfloat16 [3, 64, 512, 2048], P(None, None, 'gy', 'gz'), may hold values from -1 to 1
- plane_factors: float32 [2, 32, 8, 64], P(None, None, None, 'gy'), may hold values from -2.5 to 2.5
- depth_factors: float32 [2, 32, 2048], P(None, None, 'gz'), may hold values from -6 to 6
Outputs:
- residual: bfloat16 [64, 512, 2048], P(None, 'gy', 'gz')
- step_plane: float32 [2, 32, 8, 64], P(None, None, None, 'gy')
- step_depth: float32 [2, 32, 2048], P(None, None, 'gz')
The draws below stay inside these ranges and needn't reach their ends.
All inputs are finite; a program needn't handle non-finite values.
Results may differ from the reference program's by a relative error of at most 0.0004.
Values may be sent and summed in bfloat16 or wider, within the bound.
No kernel may reach another device: no remote copies, remote signals or barrier semaphores. Data moves between devices by JAX's collectives and lax.ppermute only.
A program may use at most 256 MiB of HBM per device.

```python
import jax
import jax.numpy as jnp
from jax import lax

SLAB = 64
STRIP_Y = 64
RANK = 32
KNOT = 8
NODES_X = 8
FULL_Y = 512
FULL_Z = 2048
NODES_Y = 64
N_GY = 8


def draw_deformed(key, part):
    along_y = (jnp.arange(FULL_Y, dtype=jnp.float32) / FULL_Y)[None, :, None]
    along_z = (jnp.arange(FULL_Z, dtype=jnp.float32) / FULL_Z)[None, None, :]
    scale = 0.4 + 1.2 * along_y + 1.2 * along_z
    noise = jax.random.truncated_normal(key, -4.0, 4.0, (SLAB, FULL_Y, FULL_Z), jnp.float32)
    values = scale * noise
    return values.astype(jnp.bfloat16)


def block_levels(stream_key, shape, pieces, least, largest):
    gain, own = 1.0, jax.random.fold_in(stream_key, 6)
    for position, parts in pieces:
        steps = jnp.exp(jax.random.uniform(jax.random.fold_in(own, position), (parts,), jnp.float32, least / len(pieces), largest / len(pieces)))
        gain = gain * jnp.repeat(steps, shape[position] // parts).reshape([-1 if axis == position else 1 for axis in range(len(shape))])
    return gain


def bell_draw(key, shape, width, most, cuts=(), held_as=jnp.bfloat16):
    values = jax.random.normal(key, shape, jnp.float32) * width
    if len(cuts) > 0:
        values = block_levels(key, shape, cuts, -0.22, 0.18) * values
    return jnp.clip(values, min=-most, max=most).astype(held_as)


def setup_inputs(seed: int = 0) -> dict:
    splits = jax.random.split(jax.random.key(seed), 6)
    return {
        "reference_image": bell_draw(splits[0], (SLAB, FULL_Y, FULL_Z), 1.0, 6.0, ((1, 8), (2, 4))),
        "deformed": draw_deformed(jax.random.fold_in(splits[5], 71), 0),
        "displacement": jnp.clip(jax.random.uniform(splits[2], (3, SLAB, FULL_Y, FULL_Z), jnp.float32, -1.0, 1.0) * block_levels(splits[2], (3, SLAB, FULL_Y, FULL_Z), ((2, 8), (3, 4)), -0.4, 0.0), -1.0, 1.0).astype(jnp.bfloat16),
        "plane_factors": bell_draw(splits[3], (2, RANK, NODES_X, NODES_Y), 0.18, 2.5, ((3, 8),), jnp.float32),
        "depth_factors": bell_draw(splits[4], (2, RANK, FULL_Z), 1.0, 6.0, ((2, 4),), jnp.float32),
    }


epsilon = 1e-6
damping = 0.01
highest = lax.Precision.HIGHEST


def tent_weights(shift):
    moved = shift.astype(jnp.float32)
    return [jnp.maximum(0.0, 1.0 - jnp.abs(moved - offset)) for offset in (-1.0, 0.0, 1.0)]


def warp_image(padded, displacement):
    depth_x, width_y, width_z = displacement.shape[1:]
    weight_x = tent_weights(displacement[0])
    weight_y = tent_weights(displacement[1])
    weight_z = tent_weights(displacement[2])
    summed = jnp.zeros((depth_x, width_y, width_z), jnp.float32)
    for along_x in range(3):
        for along_y in range(3):
            partial_z = jnp.zeros((depth_x, width_y, width_z), jnp.float32)
            for along_z in range(3):
                window = padded[along_x:along_x + depth_x, along_y:along_y + width_y, along_z:along_z + width_z]
                partial_z = partial_z + weight_z[along_z] * window.astype(jnp.float32)
            summed = summed + weight_x[along_x] * weight_y[along_y] * partial_z
    return summed


def expand_nodes(nodes):
    return jnp.repeat(jnp.repeat(nodes, KNOT, axis=2), KNOT, axis=3)


def reduce_nodes(field):
    leading = field.shape[:-2]
    depth_x, width_y = field.shape[-2:]
    shaped = field.reshape(leading + (depth_x // KNOT, KNOT, width_y // KNOT, KNOT))
    return jnp.sum(shaped, axis=(-3, -1))


def contract_rank(left, right):
    return lax.dot_general(left, right, (((0,), (0,)), ((), ())), precision=highest)


def contract_cells(left, right):
    return jnp.dot(left, right, precision=highest)


def contract_depth(left, right):
    return lax.dot_general(left, right, (((1,), (1,)), ((), ())), precision=highest)


def strip_terms(image, padded, displacement, plane_voxels, depth_factors):
    depth_x, width_y, width_z = image.shape
    cells = depth_x * width_y
    warped = warp_image(padded, displacement).reshape(cells, width_z)
    values = image.astype(jnp.float32).reshape(cells, width_z)
    flat_plane = plane_voxels.reshape(2, plane_voxels.shape[1], cells)
    contrast = contract_rank(flat_plane[0], depth_factors[0])
    brightness = contract_rank(flat_plane[1], depth_factors[1])
    misfit = warped - contrast * values - brightness
    product = misfit * values
    squares = values * values
    grad_depth = -jnp.stack([contract_cells(flat_plane[0], product), contract_cells(flat_plane[1], misfit)])
    level_sum = jnp.sum(flat_plane[1] * flat_plane[1], axis=1)
    diag_depth = jnp.stack([contract_cells(flat_plane[0] * flat_plane[0], squares),
                            jnp.broadcast_to(level_sum[:, None], (level_sum.shape[0], width_z))])
    grad_voxels = -jnp.stack([contract_depth(depth_factors[0], product), contract_depth(depth_factors[1], misfit)])
    diag_voxels = contract_depth(depth_factors[0] * depth_factors[0], squares)
    grad_plane = reduce_nodes(grad_voxels.reshape(2, -1, depth_x, width_y))
    first_diag = reduce_nodes(diag_voxels.reshape(-1, depth_x, width_y))
    depth_level = KNOT * KNOT * jnp.sum(depth_factors[1] * depth_factors[1], axis=1)
    diag_plane = jnp.stack([first_diag, jnp.broadcast_to(depth_level[:, None, None], first_diag.shape)])
    squared_sum = jnp.sum(misfit * misfit)
    residual = misfit.reshape(depth_x, width_y, width_z).astype(jnp.bfloat16)
    return residual, squared_sum, grad_plane, diag_plane, grad_depth, diag_depth


def reference(reference_image, deformed, displacement, plane_factors, depth_factors):
    padded = jnp.pad(deformed, 1)
    plane_voxels = expand_nodes(plane_factors)

    def one_strip(strip):
        start = (strip * STRIP_Y).astype(jnp.int32)
        image_part = lax.dynamic_slice_in_dim(reference_image, start, STRIP_Y, 1)
        padded_part = lax.dynamic_slice_in_dim(padded, start, STRIP_Y + 2, 1)
        shift_part = lax.dynamic_slice_in_dim(displacement, start, STRIP_Y, 2)
        plane_part = lax.dynamic_slice_in_dim(plane_voxels, start, STRIP_Y, 3)
        return strip_terms(image_part, padded_part, shift_part, plane_part, depth_factors)

    strips = jnp.arange(N_GY, dtype=jnp.int32)
    residual, squared_sums, grad_plane, diag_plane, grad_depth, diag_depth = lax.map(one_strip, strips)
    residual = jnp.transpose(residual, (1, 0, 2, 3)).reshape(SLAB, FULL_Y, FULL_Z)
    energy = jnp.sum(squared_sums)
    grad_plane = jnp.transpose(grad_plane, (1, 2, 3, 0, 4)).reshape(2, RANK, NODES_X, NODES_Y)
    diag_plane = jnp.transpose(diag_plane, (1, 2, 3, 0, 4)).reshape(2, RANK, NODES_X, NODES_Y)
    grad_depth = jnp.sum(grad_depth, axis=0)
    diag_depth = jnp.sum(diag_depth, axis=0)
    lam_plane = damping * RANK * energy / (NODES_X * NODES_Y)
    lam_depth = damping * energy / FULL_Z
    step_plane = -grad_plane / (diag_plane + lam_plane + epsilon)
    step_depth = -grad_depth / (diag_depth + lam_depth + epsilon)
    return residual, step_plane, step_depth
```

```python
import functools

import jax
import jax.numpy as jnp
from jax import lax
from jax.experimental import pallas as pl
from jax.experimental.pallas import tpu as pltpu
from jax.sharding import PartitionSpec as P

RANK = 32
KNOT = 8
LANES = 128
TOP = 8

epsilon = 1e-06
damping = 0.01
highest = lax.Precision.HIGHEST
f32 = jnp.float32
bf16 = jnp.bfloat16


def dot(left, right, dims):
    return lax.dot_general(left, right, ((dims[0], dims[1]), ((), ())), precision=highest, preferred_element_type=f32)


def joined(ref):
    return jnp.concatenate([ref[tile] for tile in range(ref.shape[0])], axis=1)


def grid_params():
    return pltpu.CompilerParams(dimension_semantics=("arbitrary",), vmem_limit_bytes=60000000)


def plain_params():
    return pltpu.CompilerParams(vmem_limit_bytes=32000000)


def edges_kernel(cells_ref, first_ref, last_ref, low_ref, high_ref, cols):
    step = pl.program_id(0)
    planes, rows, width = cells_ref.shape
    lane = lax.broadcasted_iota(jnp.int32, (rows, LANES), 1)

    @pl.when(step == 0)
    def _():
        cols[...] = jnp.zeros_like(cols)

    first, last = cols[0], cols[1]
    for k in range(planes):
        x = step * planes + k
        left = cells_ref[k, :, 0:LANES].astype(f32)
        right = cells_ref[k, :, width - LANES : width].astype(f32)
        first = jnp.where(lane == x, pltpu.roll(left, x, 1), first)
        last = jnp.where(lane == x, pltpu.roll(right, x + 1, 1), last)
    cols[0] = first
    cols[1] = last
    low = [cells_ref[k, 0:16, :].astype(f32)[0:1] for k in range(planes)]
    high = [cells_ref[k, rows - 16 : rows, :].astype(f32)[15:16] for k in range(planes)]
    low_ref[...] = jnp.concatenate(low, axis=0)
    high_ref[...] = jnp.concatenate(high, axis=0)

    @pl.when(step == pl.num_programs(0) - 1)
    def _():
        first_ref[...] = first.astype(bf16)
        last_ref[...] = last.astype(bf16)


def edges(cells):
    depth, rows, width = cells.shape
    whole = lambda i: (0, 0)
    return pl.pallas_call(
        edges_kernel,
        grid=(depth // KNOT,),
        in_specs=[pl.BlockSpec((KNOT, rows, width), lambda i: (i, 0, 0))],
        out_specs=[
            pl.BlockSpec((rows, LANES), whole),
            pl.BlockSpec((rows, LANES), whole),
            pl.BlockSpec((KNOT, width), lambda i: (i, 0)),
            pl.BlockSpec((KNOT, width), lambda i: (i, 0)),
        ],
        out_shape=[
            jax.ShapeDtypeStruct((rows, LANES), bf16),
            jax.ShapeDtypeStruct((rows, LANES), bf16),
            jax.ShapeDtypeStruct((depth, width), f32),
            jax.ShapeDtypeStruct((depth, width), f32),
        ],
        scratch_shapes=[pltpu.VMEM((2, rows, LANES), f32)],
        compiler_params=grid_params(),
        name="edges",
    )(cells)


def rows_kernel(left_ref, right_ref, low_ref, high_ref, low_out, high_out):
    depth, width = low_ref.shape
    rows = left_ref.shape[0]
    lane = lax.broadcasted_iota(jnp.int32, (depth, LANES), 1)
    pad = jnp.zeros((LANES - rows, LANES), f32)
    left = jnp.transpose(jnp.concatenate([left_ref[...].astype(f32), pad], axis=0))[0:depth]
    right = jnp.transpose(jnp.concatenate([right_ref[...].astype(f32), pad], axis=0))[0:depth]
    for row, body, out in ((0, low_ref, low_out), (rows - 1, high_ref, high_out)):
        after = pltpu.roll(right, (LANES - row) % LANES, 1)
        before = pltpu.roll(left, LANES - 1 - row, 1)
        out[:, 0:width] = body[...].astype(bf16)
        out[:, width : width + LANES] = jnp.where(lane == 0, after, before).astype(bf16)


def packed_rows(left, right, low, high):
    depth, width = low.shape
    return pl.pallas_call(
        rows_kernel,
        out_shape=[jax.ShapeDtypeStruct((depth, width + LANES), bf16)] * 2,
        compiler_params=plain_params(),
        name="rows",
    )(left, right, low, high)


def shifted(part, axis, back):
    count = lax.axis_size(axis)
    if back:
        return lax.ppermute(part, axis, [(i + 1, i) for i in range(count - 1)])
    return lax.ppermute(part, axis, [(i, i + 1) for i in range(count - 1)])


def squares_kernel(image_ref, plane_ref, depth_ref, field_ref, diag_depth_ref, diag_plane_ref, sums):
    step = pl.program_id(0)
    planes, rows, width = image_ref.shape
    nodes = rows // KNOT
    tiles = width // LANES

    def one(t, carry):
        at = pl.multiple_of((t % tiles) * LANES, LANES)
        top = pl.multiple_of((t // tiles) * 16, 16)
        total = jnp.zeros((16, LANES), f32)
        for k in range(planes):
            values = image_ref[k, pl.ds(top, 16), pl.ds(at, LANES)].astype(f32)
            total = total + values * values
        for half in range(2):
            row = step * nodes + (t // tiles) * 2 + half
            sums[t % tiles, pl.ds(row, 1), :] = jnp.sum(total[8 * half : 8 * half + 8], axis=0, keepdims=True)
        return carry

    lax.fori_loop(0, (rows // 16) * tiles, one, 0)

    @pl.when(step == pl.num_programs(0) - 1)
    def _():
        for k in range(2):
            field = dot(plane_ref[k], depth_ref[k], ((1,), (0,)))
            for tile in range(tiles):
                field_ref[k, tile] = field[:, tile * LANES : (tile + 1) * LANES]
        squared = joined(sums)
        cells = jnp.full(squared.shape, float(KNOT * KNOT), f32)
        first, second = plane_ref[0], plane_ref[1]
        diag_depth_ref[0] = dot(first * first, squared, ((0,), (0,)))
        diag_depth_ref[1] = dot(second * second, cells, ((0,), (0,)))
        first, second = depth_ref[0], depth_ref[1]
        diag_plane_ref[0] = dot(squared, first * first, ((1,), (1,)))
        diag_plane_ref[1] = dot(cells, second * second, ((1,), (1,)))


def squares(image, plane, depth_factors):
    depth, rows, width = image.shape
    nodes = plane.shape[1]
    whole = lambda i: (0, 0, 0)
    return pl.pallas_call(
        squares_kernel,
        grid=(depth // KNOT,),
        in_specs=[
            pl.BlockSpec((KNOT, rows, width), lambda i: (i, 0, 0)),
            pl.BlockSpec(plane.shape, whole),
            pl.BlockSpec(depth_factors.shape, whole),
        ],
        out_specs=[
            pl.BlockSpec((2, width // LANES, nodes, LANES), lambda i: (0, 0, 0, 0)),
            pl.BlockSpec((2, RANK, width), whole),
            pl.BlockSpec((2, nodes, RANK), whole),
        ],
        out_shape=[
            jax.ShapeDtypeStruct((2, width // LANES, nodes, LANES), f32),
            jax.ShapeDtypeStruct((2, RANK, width), f32),
            jax.ShapeDtypeStruct((2, nodes, RANK), f32),
        ],
        scratch_shapes=[pltpu.VMEM((width // LANES, nodes, LANES), f32)],
        compiler_params=grid_params(),
        cost_estimate=pl.CostEstimate(flops=3 * image.size, bytes_accessed=2 * image.size, transcendentals=0),
        name="squares",
    )(image, plane, depth_factors)


def warp_kernel(
    cells_ref, image_ref, shift_ref, left_ref, right_ref, low_ref, high_ref, field_ref, plane_ref, depth_ref,
    diag_depth_ref, diag_plane_ref,
    residual_ref, depth_out, plane_out,
    window, columns, blocks, energy,
):
    step = pl.program_id(0)
    last = pl.num_programs(0) - 1
    planes, rows, width = cells_ref.shape
    nodes = rows // KNOT
    tiles = width // LANES
    depth = planes * last

    @pl.when(step == 0)
    def _():
        columns[0] = left_ref[...].astype(f32)
        columns[1] = right_ref[...].astype(f32)
        energy[...] = jnp.zeros_like(energy)
        nothing = jnp.zeros((rows + 2 * TOP, LANES), f32)
        for c in range(3):
            for tile in range(tiles):
                window[c, 0, tile] = nothing
                window[c, depth + 1, tile] = nothing

    @pl.when(step < last)
    def _():
        lane = lax.broadcasted_iota(jnp.int32, (rows, LANES), 1)

        def one(k, carry):
            x = step * planes + k
            middle = cells_ref[k].astype(f32)
            after = pltpu.roll(columns[1], (LANES - x) % LANES, 1)
            before = pltpu.roll(columns[0], LANES - 1 - x, 1)
            wide = jnp.concatenate([middle, jnp.where(lane == 0, after, before)], axis=1)
            moved = (pltpu.roll(wide, 1, 1), wide, pltpu.roll(wide, width + LANES - 1, 1))
            for c in range(3):
                for tile in range(tiles):
                    window[c, x + 1, tile, TOP : TOP + rows, :] = moved[c][:, tile * LANES : (tile + 1) * LANES]
            return carry

        lax.fori_loop(0, planes, one, 0)
        start = pl.multiple_of(step * planes, planes)
        for source, row in ((low_ref, TOP - 1), (high_ref, TOP + rows)):
            wide = source[...].astype(f32)
            moved = (pltpu.roll(wide, 1, 1), wide, pltpu.roll(wide, width + LANES - 1, 1))
            for c in range(3):
                for tile in range(tiles):
                    for k in range(planes):
                        window[c, start + k + 1, tile, row : row + 1, :] = moved[c][
                            k : k + 1, tile * LANES : (tile + 1) * LANES
                        ]

    @pl.when(step > 0)
    def _():
        base = (step - 1) * planes

        def one(t, total):
            tile = t % tiles
            pair = t // tiles
            at = pl.multiple_of(tile * LANES, LANES)
            top = pl.multiple_of(pair * 16, 16)

            def taps(x):
                return [[window[c, base + x, tile, pl.ds(TOP + top + b, 16), :] for c in range(3)] for b in (-1, 0, 1)]

            def node_rows(k):
                start = (step - 1) * nodes + pair * 2
                parts = [
                    jnp.broadcast_to(field_ref[k, tile, pl.ds(start + half, 1), :], (8, LANES))
                    for half in range(2)
                ]
                return jnp.concatenate(parts, axis=0)

            contrast, brightness = node_rows(0), node_rows(1)
            by_image = jnp.zeros((16, LANES), f32)
            plain = jnp.zeros((16, LANES), f32)
            before, here = taps(0), taps(1)
            for k in range(planes):
                after = taps(k + 2)
                place = (k, pl.ds(top, 16), pl.ds(at, LANES))
                sx, sy, sz = (shift_ref[(axis,) + place].astype(f32) for axis in range(3))
                image = image_ref[place].astype(f32)
                px, py, pz = sx > 0, sy > 0, sz > 0
                ax, ay, az = jnp.abs(sx), jnp.abs(sy), jnp.abs(sz)
                side = [[jnp.where(px, after[b][c], before[b][c]) for c in range(3)] for b in range(3)]

                def corners(values):
                    line = [jnp.where(py, values[2][c], values[0][c]) for c in range(3)]
                    return [[row[1], jnp.where(pz, row[2], row[0])] for row in (values[1], line)]

                near, far = corners(here), corners(side)
                flat = [[near[b][c] + ax * (far[b][c] - near[b][c]) for c in range(2)] for b in range(2)]
                line = [flat[0][c] + ay * (flat[1][c] - flat[0][c]) for c in range(2)]
                warped = line[0] + az * (line[1] - line[0])
                misfit = warped - contrast * image - brightness
                residual_ref[place] = misfit.astype(bf16)
                by_image = by_image + misfit * image
                plain = plain + misfit
                total = total + misfit * misfit
                before, here = here, after
            for k, value in ((0, by_image), (1, plain)):
                for half in range(2):
                    row = (step - 1) * nodes + pair * 2 + half
                    blocks[k, tile, pl.ds(row, 1), :] = jnp.sum(value[8 * half : 8 * half + 8], axis=0, keepdims=True)
            return total

        energy[...] = lax.fori_loop(0, (rows // 16) * tiles, one, energy[...])

    @pl.when(step == last)
    def _():
        parts = depth_out.shape[0]
        share = RANK // parts
        sums = [joined(blocks.at[k]) for k in range(2)]
        kinds = [dot(plane_ref[k], sums[k], ((0,), (0,))) for k in range(2)]
        kinds = kinds + [diag_depth_ref[0], diag_depth_ref[1]]
        for p in range(parts):
            for k in range(4):
                depth_out[p, k * share : (k + 1) * share, :] = kinds[k][p * share : (p + 1) * share]
        local = jnp.sum(energy[...])
        kinds = [dot(sums[k], depth_ref[k], ((1,), (1,))) for k in range(2)]
        kinds = kinds + [diag_plane_ref[0], diag_plane_ref[1]]
        for k in range(4):
            plane_out[:, k * RANK : (k + 1) * RANK] = kinds[k]
        cells = plane_out.shape[0]
        plane_out[cells // 2 :, 3 * RANK :] = jnp.full((cells // 2, RANK), local, f32)


def warp(cells, image, shift, left, right, low, high, field, plane, depth_factors, diag_depth, diag_plane, parts):
    depth, rows, width = cells.shape
    nodes = plane.shape[1]
    count = depth // KNOT
    behind = lambda i: (jnp.maximum(i - 1, 0), 0, 0)
    ahead = lambda i: (jnp.minimum(i, count - 1), 0, 0)
    flat = lambda i: (0, 0)
    whole = lambda i: (0, 0, 0)
    return pl.pallas_call(
        warp_kernel,
        grid=(count + 1,),
        in_specs=[
            pl.BlockSpec((KNOT, rows, width), ahead),
            pl.BlockSpec((KNOT, rows, width), behind),
            pl.BlockSpec((3, KNOT, rows, width), lambda i: (0, jnp.maximum(i - 1, 0), 0, 0)),
            pl.BlockSpec(left.shape, flat),
            pl.BlockSpec(right.shape, flat),
            pl.BlockSpec((KNOT, low.shape[1]), lambda i: (jnp.minimum(i, count - 1), 0)),
            pl.BlockSpec((KNOT, high.shape[1]), lambda i: (jnp.minimum(i, count - 1), 0)),
            pl.BlockSpec(field.shape, lambda i: (0, 0, 0, 0)),
            pl.BlockSpec(plane.shape, whole),
            pl.BlockSpec(depth_factors.shape, whole),
            pl.BlockSpec(diag_depth.shape, whole),
            pl.BlockSpec(diag_plane.shape, whole),
        ],
        out_specs=[
            pl.BlockSpec((KNOT, rows, width), behind),
            pl.BlockSpec((parts, 4 * RANK // parts, width), whole),
            pl.BlockSpec((nodes, 4 * RANK), flat),
        ],
        out_shape=[
            jax.ShapeDtypeStruct(cells.shape, bf16),
            jax.ShapeDtypeStruct((parts, 4 * RANK // parts, width), f32),
            jax.ShapeDtypeStruct((nodes, 4 * RANK), f32),
        ],
        scratch_shapes=[
            pltpu.VMEM((3, depth + 2, width // LANES, rows + 2 * TOP, LANES), f32),
            pltpu.VMEM((2, rows, LANES), f32),
            pltpu.VMEM((2, width // LANES, nodes, LANES), f32),
            pltpu.VMEM((16, LANES), f32),
        ],
        compiler_params=grid_params(),
        cost_estimate=pl.CostEstimate(flops=60 * cells.size, bytes_accessed=12 * cells.size, transcendentals=0),
        name="warp",
    )(cells, image, shift, left, right, low, high, field, plane, depth_factors, diag_depth, diag_plane)


def gather_kernel(depth_ref, plane_ref, depth_out, plane_out):
    total = jnp.sum(depth_ref[...], axis=0)
    planes = jnp.sum(plane_ref[...], axis=0)
    plane_out[...] = planes
    cells = planes.shape[0]
    share, width = total.shape[0] // 4, total.shape[1]
    row = lax.broadcasted_iota(jnp.int32, total.shape, 0)
    lane = lax.broadcasted_iota(jnp.int32, total.shape, 1)
    partial = planes[cells - 1, 4 * RANK - 1]
    total = jnp.where((row >= 3 * share) & (lane >= width // 2), partial, total)
    for p in range(depth_out.shape[0]):
        depth_out[p] = total


def step_kernel(full_z, node_count, depth_ref, plane_ref, depth_out, plane_out):
    parts, share, width = depth_ref.shape[0], depth_ref.shape[1] // 4, depth_ref.shape[2]
    energy = depth_ref[0, 3 * share, width - 1]
    for p in range(1, parts):
        energy = energy + depth_ref[p, 3 * share, width - 1]
    lam_depth = damping * energy / full_z
    lam_plane = damping * RANK * energy / node_count
    for p in range(parts):
        got = depth_ref[p]
        levels = got[3 * share :, 0 : width // 2]
        levels = jnp.concatenate([levels, levels], axis=1)
        rows = slice(p * share, (p + 1) * share)
        depth_out[0, rows, :] = got[0:share] / (got[2 * share : 3 * share] + lam_depth + epsilon)
        depth_out[1, rows, :] = got[share : 2 * share] / (levels + lam_depth + epsilon)
    planes = plane_ref[...]
    plane_out[0] = planes[:, 0:RANK] / (planes[:, 2 * RANK : 3 * RANK] + lam_plane + epsilon)
    plane_out[1] = planes[:, RANK : 2 * RANK] / (planes[0:1, 3 * RANK :] + lam_plane + epsilon)


def local(image, deformed, displacement, plane_factors, depth_factors):
    n_gy, n_gz = lax.axis_size("gy"), lax.axis_size("gz")
    nodes_x, nodes_y = plane_factors.shape[2:]
    plane = jnp.transpose(plane_factors, (0, 2, 3, 1)).reshape(2, nodes_x * nodes_y, RANK)
    first, last, low, high = edges(deformed)
    right = shifted(first, "gz", True)
    left = shifted(last, "gz", False)
    field, diag_depth, diag_plane = squares(image, plane, depth_factors)
    low, high = packed_rows(left, right, low, high)
    above = shifted(low, "gy", True)
    below = shifted(high, "gy", False)
    residual, depth_terms, plane_terms = warp(
        deformed, image, displacement, left, right, below, above, field, plane, depth_factors, diag_depth, diag_plane,
        n_gy,
    )
    depth_terms = lax.all_to_all(depth_terms, "gy", 0, 0)
    plane_terms = lax.all_to_all(jnp.broadcast_to(plane_terms[None], (n_gz,) + plane_terms.shape), "gz", 0, 0)
    depth_terms, plane_terms = pl.pallas_call(
        gather_kernel,
        out_shape=[
            jax.ShapeDtypeStruct(depth_terms.shape, f32),
            jax.ShapeDtypeStruct(plane_terms.shape[1:], f32),
        ],
        compiler_params=plain_params(),
        name="gather",
    )(depth_terms, plane_terms)
    depth_terms = lax.all_to_all(depth_terms, "gy", 0, 0)
    width = depth_factors.shape[2]
    step_depth, step_plane = pl.pallas_call(
        functools.partial(step_kernel, width * n_gz, nodes_x * nodes_y * n_gy),
        out_shape=[
            jax.ShapeDtypeStruct(depth_factors.shape, f32),
            jax.ShapeDtypeStruct(plane.shape, f32),
        ],
        compiler_params=plain_params(),
        name="steps",
    )(depth_terms, plane_terms)
    step_plane = jnp.transpose(step_plane.reshape(2, nodes_x, nodes_y, RANK), (0, 3, 1, 2))
    return residual, step_plane, step_depth


def solution(mesh):
    placed = (
        P(None, "gy", "gz"),
        P(None, "gy", "gz"),
        P(None, None, "gy", "gz"),
        P(None, None, None, "gy"),
        P(None, None, "gz"),
    )
    return jax.shard_map(
        local,
        mesh=mesh,
        in_specs=placed,
        out_specs=(P(None, "gy", "gz"), P(None, None, None, "gy"), P(None, None, "gz")),
        check_vma=False,
    )
```

```python
import functools

import jax
import jax.numpy as jnp
from jax import lax
from jax.experimental import pallas as pl
from jax.experimental.pallas import tpu as pltpu
from jax.sharding import PartitionSpec as P

RANK = 32
KNOT = 8
LANES = 128
TOP = 8

epsilon = 1e-06
damping = 0.01
highest = lax.Precision.HIGHEST
f32 = jnp.float32
bf16 = jnp.bfloat16


def dot(left, right, dims):
    return lax.dot_general(left, right, ((dims[0], dims[1]), ((), ())), precision=highest, preferred_element_type=f32)


def split_dot(left, right, dim):
    left_high, right_high = left.astype(bf16), right.astype(bf16)
    left_low = (left - left_high.astype(f32)).astype(bf16)
    right_low = (right - right_high.astype(f32)).astype(bf16)
    left = jnp.concatenate([left_high, left_high, left_low], axis=dim)
    right = jnp.concatenate([right_high, right_low, right_high], axis=dim)
    return lax.dot_general(left, right, (((dim,), (dim,)), ((), ())), preferred_element_type=f32)


def joined(ref):
    return jnp.concatenate([ref[tile] for tile in range(ref.shape[0])], axis=1)


def grid_params():
    return pltpu.CompilerParams(dimension_semantics=("arbitrary",), vmem_limit_bytes=60000000)


def plain_params():
    return pltpu.CompilerParams(vmem_limit_bytes=32000000)


def columns_kernel(near_ref, far_ref, first_ref, last_ref):
    depth, rows = near_ref.shape[0:2]
    lane = lax.broadcasted_iota(jnp.int32, (rows, LANES), 1)
    first = jnp.zeros((rows, LANES), f32)
    last = jnp.zeros((rows, LANES), f32)
    for x in range(depth):
        first = jnp.where(lane == x, pltpu.roll(near_ref[x].astype(f32), x, 1), first)
        last = jnp.where(lane == x, pltpu.roll(far_ref[x].astype(f32), (x + 1) % LANES, 1), last)
    first_ref[...] = first.astype(bf16)
    last_ref[...] = last.astype(bf16)


def end_columns(cells):
    depth, rows, width = cells.shape
    tiles = width // LANES
    return pl.pallas_call(
        columns_kernel,
        grid=(1,),
        in_specs=[
            pl.BlockSpec((depth, rows, LANES), lambda i: (0, 0, 0)),
            pl.BlockSpec((depth, rows, LANES), lambda i: (0, 0, tiles - 1)),
        ],
        out_specs=[pl.BlockSpec((rows, LANES), lambda i: (0, 0))] * 2,
        out_shape=[jax.ShapeDtypeStruct((rows, LANES), bf16)] * 2,
        compiler_params=grid_params(),
        name="columns",
    )(cells, cells)


def rows_kernel(left_ref, right_ref, low_ref, high_ref, low_out, high_out):
    depth, width = low_ref.shape
    rows = left_ref.shape[0]
    lane = lax.broadcasted_iota(jnp.int32, (depth, LANES), 1)
    pad = jnp.zeros((LANES - rows, LANES), f32)
    left = jnp.transpose(jnp.concatenate([left_ref[...].astype(f32), pad], axis=0))[0:depth]
    right = jnp.transpose(jnp.concatenate([right_ref[...].astype(f32), pad], axis=0))[0:depth]
    for row, body, out in ((0, low_ref, low_out), (rows - 1, high_ref, high_out)):
        after = pltpu.roll(right, (LANES - row) % LANES, 1)
        before = pltpu.roll(left, LANES - 1 - row, 1)
        out[:, 0:width] = body[...].astype(bf16)
        out[:, width : width + LANES] = jnp.where(lane == 0, after, before).astype(bf16)


def packed_rows(left, right, low, high):
    depth, width = low.shape
    return pl.pallas_call(
        rows_kernel,
        out_shape=[jax.ShapeDtypeStruct((depth, width + LANES), bf16)] * 2,
        compiler_params=plain_params(),
        name="rows",
    )(left, right, low, high)


def shifted(part, axis, back):
    count = lax.axis_size(axis)
    if back:
        return lax.ppermute(part, axis, [(i + 1, i) for i in range(count - 1)])
    return lax.ppermute(part, axis, [(i, i + 1) for i in range(count - 1)])


def squares_kernel(image_ref, top_ref, bottom_ref, sums, low_ref, high_ref):
    step = pl.program_id(0)
    planes, rows, width = image_ref.shape
    nodes = rows // KNOT
    tiles = width // LANES

    def one(t, carry):
        at = pl.multiple_of((t % tiles) * LANES, LANES)
        top = pl.multiple_of((t // tiles) * 16, 16)
        total = jnp.zeros((16, LANES), f32)
        for k in range(planes):
            values = image_ref[k, pl.ds(top, 16), pl.ds(at, LANES)].astype(f32)
            total = total + values * values
        for half in range(2):
            row = step * nodes + (t // tiles) * 2 + half
            sums[t % tiles, pl.ds(row, 1), :] = jnp.sum(total[8 * half : 8 * half + 8], axis=0, keepdims=True)
        return carry

    lax.fori_loop(0, (rows // 16) * tiles, one, 0)
    low_ref[...] = jnp.concatenate([top_ref[k].astype(f32)[0:1] for k in range(planes)], axis=0)
    high_ref[...] = jnp.concatenate([bottom_ref[k].astype(f32)[15:16] for k in range(planes)], axis=0)


def squares(image, cells, nodes):
    depth, rows, width = image.shape
    return pl.pallas_call(
        squares_kernel,
        grid=(depth // KNOT,),
        in_specs=[
            pl.BlockSpec((KNOT, rows, width), lambda i: (i, 0, 0)),
            pl.BlockSpec((KNOT, 16, width), lambda i: (i, 0, 0)),
            pl.BlockSpec((KNOT, 16, width), lambda i: (i, rows // 16 - 1, 0)),
        ],
        out_specs=[
            pl.BlockSpec((width // LANES, nodes, LANES), lambda i: (0, 0, 0)),
            pl.BlockSpec((KNOT, width), lambda i: (i, 0)),
            pl.BlockSpec((KNOT, width), lambda i: (i, 0)),
        ],
        out_shape=[
            jax.ShapeDtypeStruct((width // LANES, nodes, LANES), f32),
            jax.ShapeDtypeStruct((depth, width), f32),
            jax.ShapeDtypeStruct((depth, width), f32),
        ],
        compiler_params=grid_params(),
        cost_estimate=pl.CostEstimate(flops=3 * image.size, bytes_accessed=2 * image.size, transcendentals=0),
        name="squares",
    )(image, cells, cells)


def terms_kernel(sums, plane_ref, depth_ref, field_ref, diag_depth_ref, diag_plane_ref):
    tiles = sums.shape[0]
    for k in range(2):
        field = dot(plane_ref[k], depth_ref[k], ((1,), (0,)))
        for tile in range(tiles):
            field_ref[k, tile] = field[:, tile * LANES : (tile + 1) * LANES]
    squared = joined(sums)
    cells = jnp.full(squared.shape, float(KNOT * KNOT), f32)
    first, second = plane_ref[0], plane_ref[1]
    diag_depth_ref[0] = dot(first * first, squared, ((0,), (0,)))
    diag_depth_ref[1] = dot(second * second, cells, ((0,), (0,)))
    first, second = depth_ref[0], depth_ref[1]
    diag_plane_ref[0] = dot(squared, first * first, ((1,), (1,)))
    diag_plane_ref[1] = dot(cells, second * second, ((1,), (1,)))


def terms(sums, plane, depth_factors):
    nodes, width = plane.shape[1], depth_factors.shape[2]
    return pl.pallas_call(
        terms_kernel,
        out_shape=[
            jax.ShapeDtypeStruct((2, width // LANES, nodes, LANES), f32),
            jax.ShapeDtypeStruct((2, RANK, width), f32),
            jax.ShapeDtypeStruct((2, nodes, RANK), f32),
        ],
        compiler_params=plain_params(),
        cost_estimate=pl.CostEstimate(flops=40 * nodes * RANK * width, bytes_accessed=1 << 20, transcendentals=0),
        name="terms",
    )(sums, plane, depth_factors)


def warp_kernel(
    cells_ref, image_ref, shift_ref, left_ref, right_ref, low_ref, high_ref, field_ref, plane_ref, depth_ref,
    diag_depth_ref, diag_plane_ref,
    residual_ref, depth_out, plane_out,
    window, columns, blocks, energy, held,
):
    step = pl.program_id(0)
    last = pl.num_programs(0) - 1
    planes, rows, width = cells_ref.shape
    nodes = rows // KNOT
    tiles = width // LANES
    depth = planes * last

    @pl.when(step == 0)
    def _():
        columns[0] = left_ref[...].astype(f32)
        columns[1] = right_ref[...].astype(f32)
        energy[...] = jnp.zeros_like(energy)
        nothing = jnp.zeros((rows + 2 * TOP, LANES), f32)
        for c in range(3):
            for tile in range(tiles):
                window[c, 0, tile] = nothing
                window[c, depth + 1, tile] = nothing

    @pl.when(step < last)
    def _():
        lane = lax.broadcasted_iota(jnp.int32, (rows, LANES), 1)

        def one(k, carry):
            x = step * planes + k
            middle = cells_ref[k].astype(f32)
            after = pltpu.roll(columns[1], (LANES - x) % LANES, 1)
            before = pltpu.roll(columns[0], LANES - 1 - x, 1)
            wide = jnp.concatenate([middle, jnp.where(lane == 0, after, before)], axis=1)
            moved = (pltpu.roll(wide, 1, 1), wide, pltpu.roll(wide, width + LANES - 1, 1))
            for c in range(3):
                for tile in range(tiles):
                    window[c, x + 1, tile, TOP : TOP + rows, :] = moved[c][:, tile * LANES : (tile + 1) * LANES]
            return carry

        lax.fori_loop(0, planes, one, 0)
        start = pl.multiple_of(step * planes, planes)
        for source, row in ((low_ref, TOP - 1), (high_ref, TOP + rows)):
            wide = source[...].astype(f32)
            moved = (pltpu.roll(wide, 1, 1), wide, pltpu.roll(wide, width + LANES - 1, 1))
            for c in range(3):
                for tile in range(tiles):
                    for k in range(planes):
                        window[c, start + k + 1, tile, row : row + 1, :] = moved[c][
                            k : k + 1, tile * LANES : (tile + 1) * LANES
                        ]

    @pl.when(step > 0)
    def _():
        base = (step - 1) * planes

        def one(t, total):
            tile = t % tiles
            pair = t // tiles
            at = pl.multiple_of(tile * LANES, LANES)
            top = pl.multiple_of(pair * 16, 16)
            for half in range(2):
                start = TOP + top + 8 * half
                node = (step - 1) * nodes + pair * 2 + half
                mine = slice(8 * half, 8 * half + 8)

                def taps(x):
                    return [[window[c, base + x, tile, pl.ds(start + b, 8), :] for c in range(3)] for b in (-1, 0, 1)]

                contrast = jnp.broadcast_to(field_ref[0, tile, pl.ds(node, 1), :], (8, LANES))
                brightness = jnp.broadcast_to(field_ref[1, tile, pl.ds(node, 1), :], (8, LANES))
                by_image = jnp.zeros((8, LANES), f32)
                plain = jnp.zeros((8, LANES), f32)
                before, here = taps(0), taps(1)
                for k in range(planes):
                    after = taps(k + 2)
                    place = (k, pl.ds(top, 16), pl.ds(at, LANES))
                    sx, sy, sz = (shift_ref[(axis,) + place].astype(f32)[mine] for axis in range(3))
                    image = image_ref[place].astype(f32)[mine]
                    px, py, pz = sx > 0, sy > 0, sz > 0
                    ax, ay, az = jnp.abs(sx), jnp.abs(sy), jnp.abs(sz)

                    def sides(c):
                        far = [jnp.where(px, after[b][c], before[b][c]) for b in range(3)]
                        near = [here[b][c] for b in range(3)]
                        return [(v[1], jnp.where(py, v[2], v[0])) for v in (near, far)]

                    below, middle, above = sides(0), sides(1), sides(2)
                    lines = []
                    for b in range(2):
                        ends = []
                        for v in range(2):
                            ends.append((middle[v][b], jnp.where(pz, above[v][b], below[v][b])))
                        near, far = ends
                        lines.append([near[c] + ax * (far[c] - near[c]) for c in range(2)])
                    flat = [lines[0][c] + ay * (lines[1][c] - lines[0][c]) for c in range(2)]
                    warped = flat[0] + az * (flat[1] - flat[0])
                    misfit = warped - contrast * image - brightness
                    if half == 0:
                        held[k] = misfit
                    else:
                        residual_ref[place] = jnp.concatenate([held[k], misfit], axis=0).astype(bf16)
                    by_image = by_image + misfit * image
                    plain = plain + misfit
                    total = total + misfit * misfit
                    before, here = here, after
                for k, value in ((0, by_image), (1, plain)):
                    blocks[k, tile, pl.ds(node, 1), :] = jnp.sum(value, axis=0, keepdims=True)
            return total

        energy[...] = lax.fori_loop(0, (rows // 16) * tiles, one, energy[...])

    @pl.when(step == last)
    def _():
        parts = depth_out.shape[0]
        share = RANK // parts
        sums = [joined(blocks.at[k]) for k in range(2)]
        kinds = [split_dot(plane_ref[k], sums[k], 0) for k in range(2)]
        kinds = kinds + [diag_depth_ref[0], diag_depth_ref[1]]
        for p in range(parts):
            for k in range(4):
                depth_out[p, k * share : (k + 1) * share, :] = kinds[k][p * share : (p + 1) * share]
        local = jnp.sum(energy[...])
        kinds = [split_dot(sums[k], depth_ref[k], 1) for k in range(2)]
        kinds = kinds + [diag_plane_ref[0], diag_plane_ref[1]]
        for k in range(4):
            plane_out[:, k * RANK : (k + 1) * RANK] = kinds[k]
        cells = plane_out.shape[0]
        plane_out[cells // 2 :, 3 * RANK :] = jnp.full((cells // 2, RANK), local, f32)


def warp(cells, image, shift, left, right, low, high, field, plane, depth_factors, diag_depth, diag_plane, parts):
    depth, rows, width = cells.shape
    nodes = plane.shape[1]
    count = depth // KNOT
    behind = lambda i: (jnp.maximum(i - 1, 0), 0, 0)
    ahead = lambda i: (jnp.minimum(i, count - 1), 0, 0)
    flat = lambda i: (0, 0)
    whole = lambda i: (0, 0, 0)
    return pl.pallas_call(
        warp_kernel,
        grid=(count + 1,),
        in_specs=[
            pl.BlockSpec((KNOT, rows, width), ahead),
            pl.BlockSpec((KNOT, rows, width), behind),
            pl.BlockSpec((3, KNOT, rows, width), lambda i: (0, jnp.maximum(i - 1, 0), 0, 0)),
            pl.BlockSpec(left.shape, flat),
            pl.BlockSpec(right.shape, flat),
            pl.BlockSpec((KNOT, low.shape[1]), lambda i: (jnp.minimum(i, count - 1), 0)),
            pl.BlockSpec((KNOT, high.shape[1]), lambda i: (jnp.minimum(i, count - 1), 0)),
            pl.BlockSpec(field.shape, lambda i: (0, 0, 0, 0)),
            pl.BlockSpec(plane.shape, whole),
            pl.BlockSpec(depth_factors.shape, whole),
            pl.BlockSpec(diag_depth.shape, whole),
            pl.BlockSpec(diag_plane.shape, whole),
        ],
        out_specs=[
            pl.BlockSpec((KNOT, rows, width), behind),
            pl.BlockSpec((parts, 4 * RANK // parts, width), whole),
            pl.BlockSpec((nodes, 4 * RANK), flat),
        ],
        out_shape=[
            jax.ShapeDtypeStruct(cells.shape, bf16),
            jax.ShapeDtypeStruct((parts, 4 * RANK // parts, width), f32),
            jax.ShapeDtypeStruct((nodes, 4 * RANK), f32),
        ],
        scratch_shapes=[
            pltpu.VMEM((3, depth + 2, width // LANES, rows + 2 * TOP, LANES), f32),
            pltpu.VMEM((2, rows, LANES), f32),
            pltpu.VMEM((2, width // LANES, nodes, LANES), f32),
            pltpu.VMEM((8, LANES), f32),
            pltpu.VMEM((KNOT, 8, LANES), f32),
        ],
        compiler_params=grid_params(),
        cost_estimate=pl.CostEstimate(flops=60 * cells.size, bytes_accessed=12 * cells.size, transcendentals=0),
        name="warp",
    )(cells, image, shift, left, right, low, high, field, plane, depth_factors, diag_depth, diag_plane)


def gather_kernel(depth_ref, *refs):
    depth_out, plane_out = refs[-2:]
    total = jnp.sum(depth_ref[...], axis=0)
    found = [ref[...] for ref in refs[:-2]]
    while len(found) > 1:
        half = len(found) // 2
        found = [found[k] + found[k + half] for k in range(half)]
    planes = found[0]
    plane_out[...] = planes
    cells = planes.shape[0]
    share, width = total.shape[0] // 4, total.shape[1]
    row = lax.broadcasted_iota(jnp.int32, total.shape, 0)
    lane = lax.broadcasted_iota(jnp.int32, total.shape, 1)
    partial = planes[cells - 1, 4 * RANK - 1]
    total = jnp.where((row >= 3 * share) & (lane >= width // 2), partial, total)
    for p in range(depth_out.shape[0]):
        depth_out[p] = total


def step_kernel(full_z, node_count, depth_ref, plane_ref, depth_out, plane_out):
    parts, share, width = depth_ref.shape[0], depth_ref.shape[1] // 4, depth_ref.shape[2]
    energy = depth_ref[0, 3 * share, width - 1]
    for p in range(1, parts):
        energy = energy + depth_ref[p, 3 * share, width - 1]
    lam_depth = damping * energy / full_z
    lam_plane = damping * RANK * energy / node_count
    for p in range(parts):
        got = depth_ref[p]
        levels = got[3 * share :, 0 : width // 2]
        levels = jnp.concatenate([levels, levels], axis=1)
        rows = slice(p * share, (p + 1) * share)
        depth_out[0, rows, :] = got[0:share] / (got[2 * share : 3 * share] + lam_depth + epsilon)
        depth_out[1, rows, :] = got[share : 2 * share] / (levels + lam_depth + epsilon)
    planes = plane_ref[...]
    plane_out[0] = planes[:, 0:RANK] / (planes[:, 2 * RANK : 3 * RANK] + lam_plane + epsilon)
    plane_out[1] = planes[:, RANK : 2 * RANK] / (planes[0:1, 3 * RANK :] + lam_plane + epsilon)


def local(image, deformed, displacement, plane_factors, depth_factors):
    n_gy, n_gz = lax.axis_size("gy"), lax.axis_size("gz")
    nodes_x, nodes_y = plane_factors.shape[2:]
    plane = jnp.transpose(plane_factors, (0, 2, 3, 1)).reshape(2, nodes_x * nodes_y, RANK)
    first, last = end_columns(deformed)
    right = shifted(first, "gz", True)
    left = shifted(last, "gz", False)
    sums, low, high = squares(image, deformed, nodes_x * nodes_y)
    low, high = packed_rows(left, right, low, high)
    above = shifted(low, "gy", True)
    below = shifted(high, "gy", False)
    field, diag_depth, diag_plane = terms(sums, plane, depth_factors)
    residual, depth_terms, plane_terms = warp(
        deformed, image, displacement, left, right, below, above, field, plane, depth_factors, diag_depth, diag_plane,
        n_gy,
    )
    others = [
        lax.ppermute(plane_terms, "gz", [(i, (i + hop) % n_gz) for i in range(n_gz)]) for hop in range(1, n_gz)
    ]
    depth_terms = lax.all_to_all(depth_terms, "gy", 0, 0)
    depth_terms, plane_terms = pl.pallas_call(
        gather_kernel,
        out_shape=[
            jax.ShapeDtypeStruct(depth_terms.shape, f32),
            jax.ShapeDtypeStruct(plane_terms.shape, f32),
        ],
        compiler_params=plain_params(),
        name="gather",
    )(depth_terms, plane_terms, *others)
    depth_terms = lax.all_to_all(depth_terms, "gy", 0, 0)
    width = depth_factors.shape[2]
    step_depth, step_plane = pl.pallas_call(
        functools.partial(step_kernel, width * n_gz, nodes_x * nodes_y * n_gy),
        out_shape=[
            jax.ShapeDtypeStruct(depth_factors.shape, f32),
            jax.ShapeDtypeStruct(plane.shape, f32),
        ],
        compiler_params=plain_params(),
        name="steps",
    )(depth_terms, plane_terms)
    step_plane = jnp.transpose(step_plane.reshape(2, nodes_x, nodes_y, RANK), (0, 3, 1, 2))
    return residual, step_plane, step_depth


def solution(mesh):
    placed = (
        P(None, "gy", "gz"),
        P(None, "gy", "gz"),
        P(None, None, "gy", "gz"),
        P(None, None, None, "gy"),
        P(None, None, "gz"),
    )
    return jax.shard_map(
        local,
        mesh=mesh,
        in_specs=placed,
        out_specs=(P(None, "gy", "gz"), P(None, None, None, "gy"), P(None, None, "gz")),
        check_vma=False,
    )
```

```python
import functools

import jax
import jax.numpy as jnp
from jax import lax
from jax.experimental import pallas as pl
from jax.experimental.pallas import tpu as pltpu
from jax.sharding import PartitionSpec as P

RANK = 32
KNOT = 8
LANES = 128
TOP = 8

epsilon = 1e-06
damping = 0.01
highest = lax.Precision.HIGHEST
f32 = jnp.float32
bf16 = jnp.bfloat16


def dot(left, right, dims):
    return lax.dot_general(left, right, ((dims[0], dims[1]), ((), ())), precision=highest, preferred_element_type=f32)


def split_dot(left, right, dim):
    left_high, right_high = left.astype(bf16), right.astype(bf16)
    left_low = (left - left_high.astype(f32)).astype(bf16)
    right_low = (right - right_high.astype(f32)).astype(bf16)
    left = jnp.concatenate([left_high, left_high, left_low], axis=dim)
    right = jnp.concatenate([right_high, right_low, right_high], axis=dim)
    return lax.dot_general(left, right, (((dim,), (dim,)), ((), ())), preferred_element_type=f32)


def joined(ref):
    tiles, rows = ref.shape[0:2]
    return jnp.concatenate([jnp.sum(ref[t].reshape(rows // 8, 8, LANES), axis=1) for t in range(tiles)], axis=1)


def grid_params():
    return pltpu.CompilerParams(dimension_semantics=("arbitrary",), vmem_limit_bytes=40000000)


def plain_params():
    return pltpu.CompilerParams(vmem_limit_bytes=32000000)


def columns_kernel(near_ref, far_ref, first_ref, last_ref):
    depth, rows = near_ref.shape[0:2]
    lane = lax.broadcasted_iota(jnp.int32, (rows, LANES), 1)
    first = jnp.zeros((rows, LANES), f32)
    last = jnp.zeros((rows, LANES), f32)
    for x in range(depth):
        first = jnp.where(lane == x, pltpu.roll(near_ref[x].astype(f32), x, 1), first)
        last = jnp.where(lane == x, pltpu.roll(far_ref[x].astype(f32), (x + 1) % LANES, 1), last)
    first_ref[...] = first.astype(bf16)
    last_ref[...] = last.astype(bf16)


def end_columns(cells):
    depth, rows, width = cells.shape
    tiles = width // LANES
    return pl.pallas_call(
        columns_kernel,
        grid=(1,),
        in_specs=[
            pl.BlockSpec((depth, rows, LANES), lambda i: (0, 0, 0)),
            pl.BlockSpec((depth, rows, LANES), lambda i: (0, 0, tiles - 1)),
        ],
        out_specs=[pl.BlockSpec((rows, LANES), lambda i: (0, 0))] * 2,
        out_shape=[jax.ShapeDtypeStruct((rows, LANES), bf16)] * 2,
        compiler_params=grid_params(),
        name="columns",
    )(cells, cells)


def rows_kernel(left_ref, right_ref, low_ref, high_ref, low_out, high_out):
    depth, width = low_ref.shape
    rows = left_ref.shape[0]
    lane = lax.broadcasted_iota(jnp.int32, (depth, LANES), 1)
    pad = jnp.zeros((LANES - rows, LANES), f32)
    left = jnp.transpose(jnp.concatenate([left_ref[...].astype(f32), pad], axis=0))[0:depth]
    right = jnp.transpose(jnp.concatenate([right_ref[...].astype(f32), pad], axis=0))[0:depth]
    for row, body, out in ((0, low_ref, low_out), (rows - 1, high_ref, high_out)):
        after = pltpu.roll(right, (LANES - row) % LANES, 1)
        before = pltpu.roll(left, LANES - 1 - row, 1)
        out[:, 0:width] = body[...].astype(bf16)
        out[:, width : width + LANES] = jnp.where(lane == 0, after, before).astype(bf16)


def packed_rows(left, right, low, high):
    depth, width = low.shape
    return pl.pallas_call(
        rows_kernel,
        out_shape=[jax.ShapeDtypeStruct((depth, width + LANES), bf16)] * 2,
        compiler_params=plain_params(),
        name="rows",
    )(left, right, low, high)


def shifted(part, axis, back):
    count = lax.axis_size(axis)
    if back:
        return lax.ppermute(part, axis, [(i + 1, i) for i in range(count - 1)])
    return lax.ppermute(part, axis, [(i, i + 1) for i in range(count - 1)])


def squares_kernel(image_ref, top_ref, bottom_ref, sums, low_ref, high_ref):
    step = pl.program_id(0)
    planes, rows, width = image_ref.shape
    tiles = width // LANES

    def one(tile, carry):
        at = pl.multiple_of(tile * LANES, LANES)
        for pair in range(rows // 16):
            total = jnp.zeros((16, LANES), f32)
            for k in range(planes):
                values = image_ref[k, 16 * pair : 16 * pair + 16, pl.ds(at, LANES)].astype(f32)
                total = total + values * values
            sums[tile, pl.ds(step * rows + 16 * pair, 16), :] = total
        return carry

    lax.fori_loop(0, tiles, one, 0)
    low_ref[...] = jnp.concatenate([top_ref[k].astype(f32)[0:1] for k in range(planes)], axis=0)
    high_ref[...] = jnp.concatenate([bottom_ref[k].astype(f32)[15:16] for k in range(planes)], axis=0)


def squares(image, cells):
    depth, rows, width = image.shape
    return pl.pallas_call(
        squares_kernel,
        grid=(depth // KNOT,),
        in_specs=[
            pl.BlockSpec((KNOT, rows, width), lambda i: (i, 0, 0)),
            pl.BlockSpec((KNOT, 16, width), lambda i: (i, 0, 0)),
            pl.BlockSpec((KNOT, 16, width), lambda i: (i, rows // 16 - 1, 0)),
        ],
        out_specs=[
            pl.BlockSpec((width // LANES, depth * rows // KNOT, LANES), lambda i: (0, 0, 0)),
            pl.BlockSpec((KNOT, width), lambda i: (i, 0)),
            pl.BlockSpec((KNOT, width), lambda i: (i, 0)),
        ],
        out_shape=[
            jax.ShapeDtypeStruct((width // LANES, depth * rows // KNOT, LANES), f32),
            jax.ShapeDtypeStruct((depth, width), f32),
            jax.ShapeDtypeStruct((depth, width), f32),
        ],
        compiler_params=grid_params(),
        cost_estimate=pl.CostEstimate(flops=3 * image.size, bytes_accessed=2 * image.size, transcendentals=0),
        name="squares",
    )(image, cells, cells)


def warp_kernel(
    cells_ref, image_ref, shift_ref, left_ref, right_ref, low_ref, high_ref, squares_ref, plane_ref, depth_ref,
    residual_ref, depth_out, plane_out,
    window, columns, field, blocks, energy, held,
):
    step = pl.program_id(0)
    last = pl.num_programs(0) - 1
    planes, rows, width = cells_ref.shape
    nodes = rows // KNOT
    tiles = width // LANES
    slots = window.shape[1]

    def store_row(plane, moved, k, row):
        for c in range(3):
            for tile in range(tiles):
                window[c, plane, tile, row : row + 1, :] = moved[c][k : k + 1, tile * LANES : (tile + 1) * LANES]

    def differences(wide):
        ahead = pltpu.roll(wide, wide.shape[1] - 1, 1) - wide
        return ahead, wide, pltpu.roll(ahead, 1, 1)

    @pl.when(step == 0)
    def _():
        columns[0] = left_ref[...].astype(f32)
        columns[1] = right_ref[...].astype(f32)
        energy[...] = jnp.zeros_like(energy)
        nothing = jnp.zeros((rows + 2 * TOP, LANES), f32)
        for c in range(3):
            for tile in range(tiles):
                window[c, slots - 1, tile] = nothing
        for k in range(2):
            values = dot(plane_ref[k], depth_ref[k], ((1,), (0,)))
            for tile in range(tiles):
                field[k, tile] = values[:, tile * LANES : (tile + 1) * LANES]

    @pl.when(step < last)
    def _():
        lane = lax.broadcasted_iota(jnp.int32, (rows, LANES), 1)
        slot = (step % 3) * planes

        def one(k, carry):
            x = step * planes + k
            middle = cells_ref[k].astype(f32)
            after = pltpu.roll(columns[1], (LANES - x) % LANES, 1)
            before = pltpu.roll(columns[0], LANES - 1 - x, 1)
            moved = differences(jnp.concatenate([middle, jnp.where(lane == 0, after, before)], axis=1))
            for c in range(3):
                for tile in range(tiles):
                    window[c, slot + k, tile, TOP : TOP + rows, :] = moved[c][:, tile * LANES : (tile + 1) * LANES]
            return carry

        lax.fori_loop(0, planes, one, 0)
        for source, row in ((low_ref, TOP - 1), (high_ref, TOP + rows)):
            moved = differences(source[...].astype(f32))
            for k in range(planes):
                store_row(slot + k, moved, k, row)

    @pl.when(step == last)
    def _():
        nothing = jnp.zeros((rows + 2 * TOP, LANES), f32)
        for c in range(3):
            for tile in range(tiles):
                window[c, (step % 3) * planes, tile] = nothing

    @pl.when(step > 0)
    def _():
        base = ((step + 2) % 3) * planes
        places = [(base + slots - 1) % slots] + [base + k for k in range(planes)] + [(base + planes) % slots]

        def one(t, total):
            tile = t % tiles
            pair = t // tiles
            at = pl.multiple_of(tile * LANES, LANES)
            top = pl.multiple_of(pair * 16, 16)
            for half in range(2):
                start = TOP + top + 8 * half
                node = (step - 1) * nodes + pair * 2 + half
                mine = slice(8 * half, 8 * half + 8)

                def taps(x):
                    return [
                        [window[c, places[x], tile, pl.ds(start + b, 8), :] for c in range(3)] for b in (-1, 0, 1)
                    ]

                contrast = jnp.broadcast_to(field[0, tile, pl.ds(node, 1), :], (8, LANES))
                brightness = jnp.broadcast_to(field[1, tile, pl.ds(node, 1), :], (8, LANES))
                by_image = jnp.zeros((8, LANES), f32)
                plain = jnp.zeros((8, LANES), f32)
                before, here = taps(0), taps(1)
                results = []
                for k in range(planes):
                    after = taps(k + 2)
                    place = (k, pl.ds(top, 16), pl.ds(at, LANES))
                    sx, sy, sz = (shift_ref[(axis,) + place].astype(f32)[mine] for axis in range(3))
                    image = image_ref[place].astype(f32)[mine]
                    px, py, pz = sx > 0, sy > 0, sz > 0
                    ax, ay = jnp.abs(sx), jnp.abs(sy)

                    def sides(c):
                        far = [jnp.where(px, after[b][c], before[b][c]) for b in range(3)]
                        near = [here[b][c] for b in range(3)]
                        return [(v[1], jnp.where(py, v[2], v[0])) for v in (near, far)]

                    ahead, middle, behind = sides(0), sides(1), sides(2)
                    lines = []
                    for b in range(2):
                        near, far = (middle[v][b] + sz * jnp.where(pz, ahead[v][b], behind[v][b]) for v in range(2))
                        lines.append(near + ax * (far - near))
                    warped = lines[0] + ay * (lines[1] - lines[0])
                    misfit = warped - contrast * image - brightness
                    results.append(misfit)
                    by_image = by_image + misfit * image
                    plain = plain + misfit
                    total = total + misfit * misfit
                    before, here = here, after
                for k in range(planes):
                    if half == 0:
                        held[k] = results[k]
                    else:
                        place = (k, pl.ds(top, 16), pl.ds(at, LANES))
                        residual_ref[place] = jnp.concatenate([held[k], results[k]], axis=0).astype(bf16)
                for k, value in ((0, by_image), (1, plain)):
                    blocks[k, tile, pl.ds(pl.multiple_of(node * 8, 8), 8), :] = value
            return total

        energy[...] = lax.fori_loop(0, (rows // 16) * tiles, one, energy[...])

    @pl.when(step == last)
    def _():
        parts = depth_out.shape[0]
        share = RANK // parts
        sums = [joined(blocks.at[k]) for k in range(2)]
        kinds = [split_dot(plane_ref[k], sums[k], 0) for k in range(2)]
        squared = joined(squares_ref)
        cells = jnp.full(squared.shape, float(KNOT * KNOT), f32)
        second = plane_ref[1]
        kinds = kinds + [split_dot(plane_ref[0] * plane_ref[0], squared, 0), split_dot(second * second, cells, 0)]
        for p in range(parts):
            for k in range(4):
                depth_out[p, k * share : (k + 1) * share, :] = kinds[k][p * share : (p + 1) * share]
        local = jnp.sum(energy[...])
        kinds = [split_dot(sums[k], depth_ref[k], 1) for k in range(2)]
        second = depth_ref[1]
        kinds = kinds + [split_dot(squared, depth_ref[0] * depth_ref[0], 1), split_dot(cells, second * second, 1)]
        for k in range(4):
            plane_out[:, k * RANK : (k + 1) * RANK] = kinds[k]
        count = plane_out.shape[0]
        plane_out[count // 2 :, 3 * RANK :] = jnp.full((count // 2, RANK), local, f32)


def warp(cells, image, shift, left, right, low, high, squared, plane, depth_factors, parts):
    depth, rows, width = cells.shape
    nodes = plane.shape[1]
    tiles = width // LANES
    count = depth // KNOT
    behind = lambda i: (jnp.maximum(i - 1, 0), 0, 0)
    ahead = lambda i: (jnp.minimum(i, count - 1), 0, 0)
    flat = lambda i: (0, 0)
    whole = lambda i: (0, 0, 0)
    return pl.pallas_call(
        warp_kernel,
        grid=(count + 1,),
        in_specs=[
            pl.BlockSpec((KNOT, rows, width), ahead),
            pl.BlockSpec((KNOT, rows, width), behind),
            pl.BlockSpec((3, KNOT, rows, width), lambda i: (0, jnp.maximum(i - 1, 0), 0, 0)),
            pl.BlockSpec(left.shape, flat),
            pl.BlockSpec(right.shape, flat),
            pl.BlockSpec((KNOT, low.shape[1]), lambda i: (jnp.minimum(i, count - 1), 0)),
            pl.BlockSpec((KNOT, high.shape[1]), lambda i: (jnp.minimum(i, count - 1), 0)),
            pl.BlockSpec(squared.shape, whole),
            pl.BlockSpec(plane.shape, whole),
            pl.BlockSpec(depth_factors.shape, whole),
        ],
        out_specs=[
            pl.BlockSpec((KNOT, rows, width), behind),
            pl.BlockSpec((parts, 4 * RANK // parts, width), whole),
            pl.BlockSpec((nodes, 4 * RANK), flat),
        ],
        out_shape=[
            jax.ShapeDtypeStruct(cells.shape, bf16),
            jax.ShapeDtypeStruct((parts, 4 * RANK // parts, width), f32),
            jax.ShapeDtypeStruct((nodes, 4 * RANK), f32),
        ],
        scratch_shapes=[
            pltpu.VMEM((3, 3 * KNOT, tiles, rows + 2 * TOP, LANES), f32),
            pltpu.VMEM((2, rows, LANES), f32),
            pltpu.VMEM((2, tiles, nodes, LANES), f32),
            pltpu.VMEM((2, tiles, 8 * nodes, LANES), f32),
            pltpu.VMEM((8, LANES), f32),
            pltpu.VMEM((KNOT, 8, LANES), f32),
        ],
        compiler_params=grid_params(),
        cost_estimate=pl.CostEstimate(flops=60 * cells.size, bytes_accessed=12 * cells.size, transcendentals=0),
        name="warp",
    )(cells, image, shift, left, right, low, high, squared, plane, depth_factors)


def gather_kernel(depth_ref, *refs):
    depth_out, plane_out = refs[-2:]
    total = jnp.sum(depth_ref[...], axis=0)
    found = [ref[...] for ref in refs[:-2]]
    while len(found) > 1:
        half = len(found) // 2
        found = [found[k] + found[k + half] for k in range(half)]
    planes = found[0]
    plane_out[...] = planes
    cells = planes.shape[0]
    share, width = total.shape[0] // 4, total.shape[1]
    row = lax.broadcasted_iota(jnp.int32, total.shape, 0)
    lane = lax.broadcasted_iota(jnp.int32, total.shape, 1)
    partial = planes[cells - 1, 4 * RANK - 1]
    total = jnp.where((row >= 3 * share) & (lane >= width // 2), partial, total)
    for p in range(depth_out.shape[0]):
        depth_out[p] = total


def step_kernel(full_z, node_count, depth_ref, plane_ref, depth_out, plane_out):
    parts, share, width = depth_ref.shape[0], depth_ref.shape[1] // 4, depth_ref.shape[2]
    energy = depth_ref[0, 3 * share, width - 1]
    for p in range(1, parts):
        energy = energy + depth_ref[p, 3 * share, width - 1]
    lam_depth = damping * energy / full_z
    lam_plane = damping * RANK * energy / node_count
    for p in range(parts):
        got = depth_ref[p]
        levels = got[3 * share :, 0 : width // 2]
        levels = jnp.concatenate([levels, levels], axis=1)
        rows = slice(p * share, (p + 1) * share)
        depth_out[0, rows, :] = got[0:share] / (got[2 * share : 3 * share] + lam_depth + epsilon)
        depth_out[1, rows, :] = got[share : 2 * share] / (levels + lam_depth + epsilon)
    planes = plane_ref[...]
    plane_out[0] = planes[:, 0:RANK] / (planes[:, 2 * RANK : 3 * RANK] + lam_plane + epsilon)
    plane_out[1] = planes[:, RANK : 2 * RANK] / (planes[0:1, 3 * RANK :] + lam_plane + epsilon)


def local(image, deformed, displacement, plane_factors, depth_factors):
    n_gy, n_gz = lax.axis_size("gy"), lax.axis_size("gz")
    nodes_x, nodes_y = plane_factors.shape[2:]
    plane = jnp.transpose(plane_factors, (0, 2, 3, 1)).reshape(2, nodes_x * nodes_y, RANK)
    first, last = end_columns(deformed)
    right = shifted(first, "gz", True)
    left = shifted(last, "gz", False)
    sums, low, high = squares(image, deformed)
    low, high = packed_rows(left, right, low, high)
    above = shifted(low, "gy", True)
    below = shifted(high, "gy", False)
    residual, depth_terms, plane_terms = warp(
        deformed, image, displacement, left, right, below, above, sums, plane, depth_factors, n_gy
    )
    others = [
        lax.ppermute(plane_terms, "gz", [(i, (i + hop) % n_gz) for i in range(n_gz)]) for hop in range(1, n_gz)
    ]
    depth_terms = lax.all_to_all(depth_terms, "gy", 0, 0)
    depth_terms, plane_terms = pl.pallas_call(
        gather_kernel,
        out_shape=[
            jax.ShapeDtypeStruct(depth_terms.shape, f32),
            jax.ShapeDtypeStruct(plane_terms.shape, f32),
        ],
        compiler_params=plain_params(),
        name="gather",
    )(depth_terms, plane_terms, *others)
    depth_terms = lax.all_to_all(depth_terms, "gy", 0, 0)
    width = depth_factors.shape[2]
    step_depth, step_plane = pl.pallas_call(
        functools.partial(step_kernel, width * n_gz, nodes_x * nodes_y * n_gy),
        out_shape=[
            jax.ShapeDtypeStruct(depth_factors.shape, f32),
            jax.ShapeDtypeStruct(plane.shape, f32),
        ],
        compiler_params=plain_params(),
        name="steps",
    )(depth_terms, plane_terms)
    step_plane = jnp.transpose(step_plane.reshape(2, nodes_x, nodes_y, RANK), (0, 3, 1, 2))
    return residual, step_plane, step_depth


def solution(mesh):
    placed = (
        P(None, "gy", "gz"),
        P(None, "gy", "gz"),
        P(None, None, "gy", "gz"),
        P(None, None, None, "gy"),
        P(None, None, "gz"),
    )
    return jax.shard_map(
        local,
        mesh=mesh,
        in_specs=placed,
        out_specs=(P(None, "gy", "gz"), P(None, None, None, "gy"), P(None, None, "gz")),
        check_vma=False,
    )
```

```python
import functools

import jax
import jax.numpy as jnp
from jax import lax
from jax.experimental import pallas as pl
from jax.experimental.pallas import tpu as pltpu
from jax.sharding import PartitionSpec as P

RANK = 32
KNOT = 8
LANES = 128
TOP = 8

epsilon = 1e-06
damping = 0.01
highest = lax.Precision.HIGHEST
f32 = jnp.float32
bf16 = jnp.bfloat16


def dot(left, right, dims):
    return lax.dot_general(left, right, ((dims[0], dims[1]), ((), ())), precision=highest, preferred_element_type=f32)


def split_dot(left, right, dim):
    left_high, right_high = left.astype(bf16), right.astype(bf16)
    left_low = (left - left_high.astype(f32)).astype(bf16)
    right_low = (right - right_high.astype(f32)).astype(bf16)
    left = jnp.concatenate([left_high, left_high, left_low], axis=dim)
    right = jnp.concatenate([right_high, right_low, right_high], axis=dim)
    return lax.dot_general(left, right, (((dim,), (dim,)), ((), ())), preferred_element_type=f32)


def joined(ref):
    tiles, rows = ref.shape[0:2]
    return jnp.concatenate([jnp.sum(ref[t].reshape(rows // 8, 8, LANES), axis=1) for t in range(tiles)], axis=1)


def grid_params():
    return pltpu.CompilerParams(dimension_semantics=("arbitrary",), vmem_limit_bytes=40000000)


def plain_params():
    return pltpu.CompilerParams(vmem_limit_bytes=32000000)


def columns_kernel(near_ref, far_ref, first_ref, last_ref):
    depth, rows = near_ref.shape[0:2]
    lane = lax.broadcasted_iota(jnp.int32, (rows, LANES), 1)
    first = jnp.zeros((rows, LANES), f32)
    last = jnp.zeros((rows, LANES), f32)
    for x in range(depth):
        first = jnp.where(lane == x, pltpu.roll(near_ref[x].astype(f32), x, 1), first)
        last = jnp.where(lane == x, pltpu.roll(far_ref[x].astype(f32), (x + 1) % LANES, 1), last)
    first_ref[...] = first.astype(bf16)
    last_ref[...] = last.astype(bf16)


def end_columns(cells):
    depth, rows, width = cells.shape
    tiles = width // LANES
    return pl.pallas_call(
        columns_kernel,
        grid=(1,),
        in_specs=[
            pl.BlockSpec((depth, rows, LANES), lambda i: (0, 0, 0)),
            pl.BlockSpec((depth, rows, LANES), lambda i: (0, 0, tiles - 1)),
        ],
        out_specs=[pl.BlockSpec((rows, LANES), lambda i: (0, 0))] * 2,
        out_shape=[jax.ShapeDtypeStruct((rows, LANES), bf16)] * 2,
        compiler_params=grid_params(),
        name="columns",
    )(cells, cells)


def rows_kernel(left_ref, right_ref, low_ref, high_ref, low_out, high_out):
    depth, width = low_ref.shape
    rows = left_ref.shape[0]
    lane = lax.broadcasted_iota(jnp.int32, (depth, LANES), 1)
    pad = jnp.zeros((LANES - rows, LANES), f32)
    left = jnp.transpose(jnp.concatenate([left_ref[...].astype(f32), pad], axis=0))[0:depth]
    right = jnp.transpose(jnp.concatenate([right_ref[...].astype(f32), pad], axis=0))[0:depth]
    for row, body, out in ((0, low_ref, low_out), (rows - 1, high_ref, high_out)):
        after = pltpu.roll(right, (LANES - row) % LANES, 1)
        before = pltpu.roll(left, LANES - 1 - row, 1)
        out[:, 0:width] = body[...].astype(bf16)
        out[:, width : width + LANES] = jnp.where(lane == 0, after, before).astype(bf16)


def packed_rows(left, right, low, high):
    depth, width = low.shape
    return pl.pallas_call(
        rows_kernel,
        out_shape=[jax.ShapeDtypeStruct((depth, width + LANES), bf16)] * 2,
        compiler_params=plain_params(),
        name="rows",
    )(left, right, low, high)


def shifted(part, axis, back):
    count = lax.axis_size(axis)
    if back:
        return lax.ppermute(part, axis, [(i + 1, i) for i in range(count - 1)])
    return lax.ppermute(part, axis, [(i, i + 1) for i in range(count - 1)])


def squares_kernel(image_ref, top_ref, bottom_ref, sums, low_ref, high_ref):
    step = pl.program_id(0)
    planes, rows, width = image_ref.shape
    tiles = width // LANES

    def one(tile, carry):
        at = pl.multiple_of(tile * LANES, LANES)
        for pair in range(rows // 16):
            total = jnp.zeros((16, LANES), f32)
            for k in range(planes):
                values = image_ref[k, 16 * pair : 16 * pair + 16, pl.ds(at, LANES)].astype(f32)
                total = total + values * values
            sums[tile, pl.ds(step * rows + 16 * pair, 16), :] = total
        return carry

    lax.fori_loop(0, tiles, one, 0)
    low_ref[...] = jnp.concatenate([top_ref[k].astype(f32)[0:1] for k in range(planes)], axis=0)
    high_ref[...] = jnp.concatenate([bottom_ref[k].astype(f32)[15:16] for k in range(planes)], axis=0)


def squares(image, cells):
    depth, rows, width = image.shape
    return pl.pallas_call(
        squares_kernel,
        grid=(depth // KNOT,),
        in_specs=[
            pl.BlockSpec((KNOT, rows, width), lambda i: (i, 0, 0)),
            pl.BlockSpec((KNOT, 16, width), lambda i: (i, 0, 0)),
            pl.BlockSpec((KNOT, 16, width), lambda i: (i, rows // 16 - 1, 0)),
        ],
        out_specs=[
            pl.BlockSpec((width // LANES, depth * rows // KNOT, LANES), lambda i: (0, 0, 0)),
            pl.BlockSpec((KNOT, width), lambda i: (i, 0)),
            pl.BlockSpec((KNOT, width), lambda i: (i, 0)),
        ],
        out_shape=[
            jax.ShapeDtypeStruct((width // LANES, depth * rows // KNOT, LANES), f32),
            jax.ShapeDtypeStruct((depth, width), f32),
            jax.ShapeDtypeStruct((depth, width), f32),
        ],
        compiler_params=grid_params(),
        cost_estimate=pl.CostEstimate(flops=3 * image.size, bytes_accessed=2 * image.size, transcendentals=0),
        name="squares",
    )(image, cells, cells)


def warp_kernel(
    cells_ref, image_ref, shift_ref, left_ref, right_ref, low_ref, high_ref, squares_ref, plane_ref, depth_ref,
    residual_ref, depth_out, plane_out,
    window, columns, field, blocks, energy,
):
    step = pl.program_id(0)
    last = pl.num_programs(0) - 1
    planes, rows, width = cells_ref.shape
    nodes = rows // KNOT
    tiles = width // LANES
    slots = window.shape[1]

    def store_row(plane, moved, k, row):
        for c in range(3):
            for tile in range(tiles):
                window[c, plane, tile, row : row + 1, :] = moved[c][k : k + 1, tile * LANES : (tile + 1) * LANES]

    def differences(wide):
        ahead = pltpu.roll(wide, wide.shape[1] - 1, 1) - wide
        return ahead, wide, pltpu.roll(ahead, 1, 1)

    @pl.when(step == 0)
    def _():
        columns[0] = left_ref[...].astype(f32)
        columns[1] = right_ref[...].astype(f32)
        energy[...] = jnp.zeros_like(energy)
        nothing = jnp.zeros((rows + 2 * TOP, LANES), f32)
        for c in range(3):
            for tile in range(tiles):
                window[c, slots - 1, tile] = nothing
        for k in range(2):
            values = dot(plane_ref[k], depth_ref[k], ((1,), (0,)))
            for tile in range(tiles):
                field[k, tile] = values[:, tile * LANES : (tile + 1) * LANES]

    @pl.when(step < last)
    def _():
        lane = lax.broadcasted_iota(jnp.int32, (16, LANES), 1)
        slot = (step % 3) * planes

        def one(k, carry):
            x = step * planes + k
            raw = cells_ref[k]
            right, left = columns[1], columns[0]
            for group in range(rows // 16):
                mine = slice(16 * group, 16 * group + 16)
                after = pltpu.roll(right[mine], (LANES - x) % LANES, 1)
                before = pltpu.roll(left[mine], LANES - 1 - x, 1)
                beyond = jnp.where(lane == 0, after, before)
                moved = differences(jnp.concatenate([raw[mine].astype(f32), beyond], axis=1))
                for c in range(3):
                    for tile in range(tiles):
                        window[c, slot + k, tile, TOP + 16 * group : TOP + 16 * group + 16, :] = moved[c][
                            :, tile * LANES : (tile + 1) * LANES
                        ]
            return carry

        lax.fori_loop(0, planes, one, 0)
        for source, row in ((low_ref, TOP - 1), (high_ref, TOP + rows)):
            moved = differences(source[...].astype(f32))
            for k in range(planes):
                store_row(slot + k, moved, k, row)

    @pl.when(step == last)
    def _():
        nothing = jnp.zeros((rows + 2 * TOP, LANES), f32)
        for c in range(3):
            for tile in range(tiles):
                window[c, (step % 3) * planes, tile] = nothing

    @pl.when(step > 0)
    def _():
        base = ((step + 2) % 3) * planes

        def row_pair(pair, total):
            top = pl.multiple_of(pair * 16, 16)
            outputs = [(tile, half) for tile in range(tiles) for half in range(2)]

            def plane(k, carry):
                total, by_image, plain = carry[0], list(carry[1]), list(carry[2])
                here = base + k
                before = jnp.where(here == 0, slots - 1, here - 1)
                after = jnp.where(here == slots - 1, 0, here + 1)
                inputs, results = [], []
                for tile in range(tiles):
                    place = (k, pl.ds(top, 16), slice(tile * LANES, (tile + 1) * LANES))
                    loaded = [shift_ref[(axis,) + place].astype(f32) for axis in range(3)]
                    inputs.append(loaded + [image_ref[place].astype(f32)])
                for n, (tile, half) in enumerate(outputs):
                    sx, sy, sz, image = (v[8 * half : 8 * half + 8] for v in inputs[tile])
                    px, py, pz = sx > 0, sy > 0, sz > 0
                    start = TOP + top + 8 * half
                    node = (step - 1) * nodes + pair * 2 + half

                    def tap(x, b, c):
                        return window[c, x, tile, pl.ds(start + b, 8), :]

                    def sides(c):
                        near = [tap(here, b, c) for b in (-1, 0, 1)]
                        far = [jnp.where(px, tap(after, b, c), tap(before, b, c)) for b in (-1, 0, 1)]
                        return [(v[1], jnp.where(py, v[2], v[0])) for v in (near, far)]

                    ahead, middle, behind = sides(0), sides(1), sides(2)
                    lines = []
                    for b in range(2):
                        near, far = (middle[v][b] + sz * jnp.where(pz, ahead[v][b], behind[v][b]) for v in range(2))
                        lines.append(near + jnp.abs(sx) * (far - near))
                    warped = lines[0] + jnp.abs(sy) * (lines[1] - lines[0])
                    contrast = jnp.broadcast_to(field[0, tile, pl.ds(node, 1), :], (8, LANES))
                    brightness = jnp.broadcast_to(field[1, tile, pl.ds(node, 1), :], (8, LANES))
                    misfit = warped - contrast * image - brightness
                    results.append(misfit)
                    by_image[n] = by_image[n] + misfit * image
                    plain[n] = plain[n] + misfit
                    total = total + misfit * misfit
                for tile in range(tiles):
                    place = (k, pl.ds(top, 16), slice(tile * LANES, (tile + 1) * LANES))
                    residual_ref[place] = jnp.concatenate(results[2 * tile : 2 * tile + 2], axis=0).astype(bf16)
                return total, tuple(by_image), tuple(plain)

            none = tuple(jnp.zeros((8, LANES), f32) for _ in outputs)
            total, by_image, plain = lax.fori_loop(0, planes, plane, (total, none, none))
            for n, (tile, half) in enumerate(outputs):
                node = (step - 1) * nodes + pair * 2 + half
                place = pl.ds(pl.multiple_of(node * 8, 8), 8)
                blocks[0, tile, place, :] = by_image[n]
                blocks[1, tile, place, :] = plain[n]
            return total

        energy[...] = lax.fori_loop(0, rows // 16, row_pair, energy[...])

    @pl.when(step == last)
    def _():
        parts = depth_out.shape[0]
        share = RANK // parts
        sums = [joined(blocks.at[k]) for k in range(2)]
        kinds = [split_dot(plane_ref[k], sums[k], 0) for k in range(2)]
        squared = joined(squares_ref)
        cells = jnp.full(squared.shape, float(KNOT * KNOT), f32)
        second = plane_ref[1]
        kinds = kinds + [split_dot(plane_ref[0] * plane_ref[0], squared, 0), split_dot(second * second, cells, 0)]
        for p in range(parts):
            for k in range(4):
                depth_out[p, k * share : (k + 1) * share, :] = kinds[k][p * share : (p + 1) * share]
        local = jnp.sum(energy[...])
        kinds = [split_dot(sums[k], depth_ref[k], 1) for k in range(2)]
        second = depth_ref[1]
        kinds = kinds + [split_dot(squared, depth_ref[0] * depth_ref[0], 1), split_dot(cells, second * second, 1)]
        for k in range(4):
            plane_out[:, k * RANK : (k + 1) * RANK] = kinds[k]
        count = plane_out.shape[0]
        plane_out[count // 2 :, 3 * RANK :] = jnp.full((count // 2, RANK), local, f32)


def warp(cells, image, shift, left, right, low, high, squared, plane, depth_factors, parts):
    depth, rows, width = cells.shape
    nodes = plane.shape[1]
    tiles = width // LANES
    count = depth // KNOT
    behind = lambda i: (jnp.maximum(i - 1, 0), 0, 0)
    ahead = lambda i: (jnp.minimum(i, count - 1), 0, 0)
    flat = lambda i: (0, 0)
    whole = lambda i: (0, 0, 0)
    return pl.pallas_call(
        warp_kernel,
        grid=(count + 1,),
        in_specs=[
            pl.BlockSpec((KNOT, rows, width), ahead),
            pl.BlockSpec((KNOT, rows, width), behind),
            pl.BlockSpec((3, KNOT, rows, width), lambda i: (0, jnp.maximum(i - 1, 0), 0, 0)),
            pl.BlockSpec(left.shape, flat),
            pl.BlockSpec(right.shape, flat),
            pl.BlockSpec((KNOT, low.shape[1]), lambda i: (jnp.minimum(i, count - 1), 0)),
            pl.BlockSpec((KNOT, high.shape[1]), lambda i: (jnp.minimum(i, count - 1), 0)),
            pl.BlockSpec(squared.shape, whole),
            pl.BlockSpec(plane.shape, whole),
            pl.BlockSpec(depth_factors.shape, whole),
        ],
        out_specs=[
            pl.BlockSpec((KNOT, rows, width), behind),
            pl.BlockSpec((parts, 4 * RANK // parts, width), whole),
            pl.BlockSpec((nodes, 4 * RANK), flat),
        ],
        out_shape=[
            jax.ShapeDtypeStruct(cells.shape, bf16),
            jax.ShapeDtypeStruct((parts, 4 * RANK // parts, width), f32),
            jax.ShapeDtypeStruct((nodes, 4 * RANK), f32),
        ],
        scratch_shapes=[
            pltpu.VMEM((3, 3 * KNOT, tiles, rows + 2 * TOP, LANES), f32),
            pltpu.VMEM((2, rows, LANES), f32),
            pltpu.VMEM((2, tiles, nodes, LANES), f32),
            pltpu.VMEM((2, tiles, 8 * nodes, LANES), f32),
            pltpu.VMEM((8, LANES), f32),
        ],
        compiler_params=grid_params(),
        cost_estimate=pl.CostEstimate(flops=60 * cells.size, bytes_accessed=12 * cells.size, transcendentals=0),
        name="warp",
    )(cells, image, shift, left, right, low, high, squared, plane, depth_factors)


def gather_kernel(depth_ref, *refs):
    depth_out, plane_out = refs[-2:]
    total = jnp.sum(depth_ref[...], axis=0)
    found = [ref[...] for ref in refs[:-2]]
    while len(found) > 1:
        half = len(found) // 2
        found = [found[k] + found[k + half] for k in range(half)]
    planes = found[0]
    plane_out[...] = planes
    cells = planes.shape[0]
    share, width = total.shape[0] // 4, total.shape[1]
    row = lax.broadcasted_iota(jnp.int32, total.shape, 0)
    lane = lax.broadcasted_iota(jnp.int32, total.shape, 1)
    partial = planes[cells - 1, 4 * RANK - 1]
    total = jnp.where((row >= 3 * share) & (lane >= width // 2), partial, total)
    for p in range(depth_out.shape[0]):
        depth_out[p] = total


def step_kernel(full_z, node_count, depth_ref, plane_ref, depth_out, plane_out):
    parts, share, width = depth_ref.shape[0], depth_ref.shape[1] // 4, depth_ref.shape[2]
    energy = depth_ref[0, 3 * share, width - 1]
    for p in range(1, parts):
        energy = energy + depth_ref[p, 3 * share, width - 1]
    lam_depth = damping * energy / full_z
    lam_plane = damping * RANK * energy / node_count
    for p in range(parts):
        got = depth_ref[p]
        levels = got[3 * share :, 0 : width // 2]
        levels = jnp.concatenate([levels, levels], axis=1)
        rows = slice(p * share, (p + 1) * share)
        depth_out[0, rows, :] = got[0:share] / (got[2 * share : 3 * share] + lam_depth + epsilon)
        depth_out[1, rows, :] = got[share : 2 * share] / (levels + lam_depth + epsilon)
    planes = plane_ref[...]
    plane_out[0] = planes[:, 0:RANK] / (planes[:, 2 * RANK : 3 * RANK] + lam_plane + epsilon)
    plane_out[1] = planes[:, RANK : 2 * RANK] / (planes[0:1, 3 * RANK :] + lam_plane + epsilon)


def local(image, deformed, displacement, plane_factors, depth_factors):
    n_gy, n_gz = lax.axis_size("gy"), lax.axis_size("gz")
    nodes_x, nodes_y = plane_factors.shape[2:]
    plane = jnp.transpose(plane_factors, (0, 2, 3, 1)).reshape(2, nodes_x * nodes_y, RANK)
    first, last = end_columns(deformed)
    right = shifted(first, "gz", True)
    left = shifted(last, "gz", False)
    sums, low, high = squares(image, deformed)
    low, high = packed_rows(left, right, low, high)
    above = shifted(low, "gy", True)
    below = shifted(high, "gy", False)
    residual, depth_terms, plane_terms = warp(
        deformed, image, displacement, left, right, below, above, sums, plane, depth_factors, n_gy
    )
    others = [
        lax.ppermute(plane_terms, "gz", [(i, (i + hop) % n_gz) for i in range(n_gz)]) for hop in range(1, n_gz)
    ]
    depth_terms = lax.all_to_all(depth_terms, "gy", 0, 0)
    depth_terms, plane_terms = pl.pallas_call(
        gather_kernel,
        out_shape=[
            jax.ShapeDtypeStruct(depth_terms.shape, f32),
            jax.ShapeDtypeStruct(plane_terms.shape, f32),
        ],
        compiler_params=plain_params(),
        name="gather",
    )(depth_terms, plane_terms, *others)
    depth_terms = lax.all_to_all(depth_terms, "gy", 0, 0)
    width = depth_factors.shape[2]
    step_depth, step_plane = pl.pallas_call(
        functools.partial(step_kernel, width * n_gz, nodes_x * nodes_y * n_gy),
        out_shape=[
            jax.ShapeDtypeStruct(depth_factors.shape, f32),
            jax.ShapeDtypeStruct(plane.shape, f32),
        ],
        compiler_params=plain_params(),
        name="steps",
    )(depth_terms, plane_terms)
    step_plane = jnp.transpose(step_plane.reshape(2, nodes_x, nodes_y, RANK), (0, 3, 1, 2))
    return residual, step_plane, step_depth


def solution(mesh):
    placed = (
        P(None, "gy", "gz"),
        P(None, "gy", "gz"),
        P(None, None, "gy", "gz"),
        P(None, None, None, "gy"),
        P(None, None, "gz"),
    )
    return jax.shard_map(
        local,
        mesh=mesh,
        in_specs=placed,
        out_specs=(P(None, "gy", "gz"), P(None, None, None, "gy"), P(None, None, "gz")),
        check_vma=False,
    )
```

```python
import functools

import jax
import jax.numpy as jnp
from jax import lax
from jax.experimental import pallas as pl
from jax.experimental.pallas import tpu as pltpu
from jax.sharding import PartitionSpec as P

RANK = 32
KNOT = 8
LANES = 128
TOP = 8

epsilon = 1e-06
damping = 0.01
highest = lax.Precision.HIGHEST
f32 = jnp.float32
bf16 = jnp.bfloat16


def dot(left, right, dims):
    return lax.dot_general(left, right, ((dims[0], dims[1]), ((), ())), precision=highest, preferred_element_type=f32)


def split_dot(left, right, dim):
    left_high, right_high = left.astype(bf16), right.astype(bf16)
    left_low = (left - left_high.astype(f32)).astype(bf16)
    right_low = (right - right_high.astype(f32)).astype(bf16)
    left = jnp.concatenate([left_high, left_high, left_low], axis=dim)
    right = jnp.concatenate([right_high, right_low, right_high], axis=dim)
    return lax.dot_general(left, right, (((dim,), (dim,)), ((), ())), preferred_element_type=f32)


def joined(ref):
    tiles, rows = ref.shape[0:2]
    return jnp.concatenate([jnp.sum(ref[t].reshape(rows // 8, 8, LANES), axis=1) for t in range(tiles)], axis=1)


def grid_params():
    return pltpu.CompilerParams(dimension_semantics=("arbitrary",), vmem_limit_bytes=40000000)


def plain_params():
    return pltpu.CompilerParams(vmem_limit_bytes=32000000)


def columns_kernel(near_ref, far_ref, first_ref, last_ref):
    depth, rows = near_ref.shape[0:2]
    lane = lax.broadcasted_iota(jnp.int32, (rows, LANES), 1)
    first = jnp.zeros((rows, LANES), f32)
    last = jnp.zeros((rows, LANES), f32)
    for x in range(depth):
        first = jnp.where(lane == x, pltpu.roll(near_ref[x].astype(f32), x, 1), first)
        last = jnp.where(lane == x, pltpu.roll(far_ref[x].astype(f32), (x + 1) % LANES, 1), last)
    first_ref[...] = first.astype(bf16)
    last_ref[...] = last.astype(bf16)


def end_columns(cells):
    depth, rows, width = cells.shape
    tiles = width // LANES
    return pl.pallas_call(
        columns_kernel,
        grid=(1,),
        in_specs=[
            pl.BlockSpec((depth, rows, LANES), lambda i: (0, 0, 0)),
            pl.BlockSpec((depth, rows, LANES), lambda i: (0, 0, tiles - 1)),
        ],
        out_specs=[pl.BlockSpec((rows, LANES), lambda i: (0, 0))] * 2,
        out_shape=[jax.ShapeDtypeStruct((rows, LANES), bf16)] * 2,
        compiler_params=grid_params(),
        name="columns",
    )(cells, cells)


def rows_kernel(left_ref, right_ref, low_ref, high_ref, low_out, high_out):
    depth, width = low_ref.shape
    rows = left_ref.shape[0]
    lane = lax.broadcasted_iota(jnp.int32, (depth, LANES), 1)
    pad = jnp.zeros((LANES - rows, LANES), f32)
    left = jnp.transpose(jnp.concatenate([left_ref[...].astype(f32), pad], axis=0))[0:depth]
    right = jnp.transpose(jnp.concatenate([right_ref[...].astype(f32), pad], axis=0))[0:depth]
    for row, body, out in ((0, low_ref, low_out), (rows - 1, high_ref, high_out)):
        after = pltpu.roll(right, (LANES - row) % LANES, 1)
        before = pltpu.roll(left, LANES - 1 - row, 1)
        out[:, 0:width] = body[...].astype(bf16)
        out[:, width : width + LANES] = jnp.where(lane == 0, after, before).astype(bf16)


def packed_rows(left, right, low, high):
    depth, width = low.shape
    return pl.pallas_call(
        rows_kernel,
        out_shape=[jax.ShapeDtypeStruct((depth, width + LANES), bf16)] * 2,
        compiler_params=plain_params(),
        name="rows",
    )(left, right, low, high)


def shifted(part, axis, back):
    count = lax.axis_size(axis)
    if back:
        return lax.ppermute(part, axis, [(i + 1, i) for i in range(count - 1)])
    return lax.ppermute(part, axis, [(i, i + 1) for i in range(count - 1)])


def squares_kernel(image_ref, top_ref, bottom_ref, sums, low_ref, high_ref):
    step = pl.program_id(0)
    planes, rows, width = image_ref.shape
    tiles = width // LANES

    def one(tile, carry):
        at = pl.multiple_of(tile * LANES, LANES)
        for pair in range(rows // 16):
            total = jnp.zeros((16, LANES), f32)
            for k in range(planes):
                values = image_ref[k, 16 * pair : 16 * pair + 16, pl.ds(at, LANES)].astype(f32)
                total = total + values * values
            sums[tile, pl.ds(step * rows + 16 * pair, 16), :] = total
        return carry

    lax.fori_loop(0, tiles, one, 0)
    low_ref[...] = jnp.concatenate([top_ref[k].astype(f32)[0:1] for k in range(planes)], axis=0)
    high_ref[...] = jnp.concatenate([bottom_ref[k].astype(f32)[15:16] for k in range(planes)], axis=0)


def squares(image, cells):
    depth, rows, width = image.shape
    return pl.pallas_call(
        squares_kernel,
        grid=(depth // KNOT,),
        in_specs=[
            pl.BlockSpec((KNOT, rows, width), lambda i: (i, 0, 0)),
            pl.BlockSpec((KNOT, 16, width), lambda i: (i, 0, 0)),
            pl.BlockSpec((KNOT, 16, width), lambda i: (i, rows // 16 - 1, 0)),
        ],
        out_specs=[
            pl.BlockSpec((width // LANES, depth * rows // KNOT, LANES), lambda i: (0, 0, 0)),
            pl.BlockSpec((KNOT, width), lambda i: (i, 0)),
            pl.BlockSpec((KNOT, width), lambda i: (i, 0)),
        ],
        out_shape=[
            jax.ShapeDtypeStruct((width // LANES, depth * rows // KNOT, LANES), f32),
            jax.ShapeDtypeStruct((depth, width), f32),
            jax.ShapeDtypeStruct((depth, width), f32),
        ],
        compiler_params=grid_params(),
        cost_estimate=pl.CostEstimate(flops=3 * image.size, bytes_accessed=2 * image.size, transcendentals=0),
        name="squares",
    )(image, cells, cells)


def warp_kernel(
    cells_ref, image_ref, shift_ref, left_ref, right_ref, low_ref, high_ref, squares_ref, plane_ref, depth_ref,
    residual_ref, depth_out, plane_out,
    ahead_ref, here_ref, behind_ref, columns, field, blocks, energy, held,
):
    step = pl.program_id(0)
    last = pl.num_programs(0) - 1
    planes, rows, width = cells_ref.shape
    nodes = rows // KNOT
    tiles = width // LANES
    window = (ahead_ref, here_ref, behind_ref)
    pitch = rows + 2 * TOP
    plane_rows = tiles * pitch
    block_rows = planes * plane_rows

    def store_row(plane, moved, k, row):
        for c in range(3):
            for tile in range(tiles):
                piece = moved[c][k : k + 1, tile * LANES : (tile + 1) * LANES]
                window[c][pl.ds(plane + tile * pitch + row, 1), :] = piece

    def differences(wide):
        ahead = pltpu.roll(wide, wide.shape[1] - 1, 1) - wide
        return ahead, wide, pltpu.roll(ahead, 1, 1)

    @pl.when(step == 0)
    def _():
        columns[0] = left_ref[...].astype(f32)
        columns[1] = right_ref[...].astype(f32)
        energy[...] = jnp.zeros_like(energy)
        for c in range(3):
            window[c][3 * block_rows - plane_rows : 3 * block_rows, :] = jnp.zeros((plane_rows, LANES), f32)
        for k in range(2):
            values = dot(plane_ref[k], depth_ref[k], ((1,), (0,)))
            for tile in range(tiles):
                field[k, tile] = values[:, tile * LANES : (tile + 1) * LANES]

    @pl.when(step < last)
    def _():
        lane = lax.broadcasted_iota(jnp.int32, (16, LANES), 1)
        slot = (step % 3) * block_rows

        def one(k, carry):
            x = step * planes + k
            first = pl.multiple_of(slot + k * plane_rows, 8)
            raw = cells_ref[k]
            right, left = columns[1], columns[0]
            for group in range(rows // 16):
                mine = slice(16 * group, 16 * group + 16)
                after = pltpu.roll(right[mine], (LANES - x) % LANES, 1)
                before = pltpu.roll(left[mine], LANES - 1 - x, 1)
                beyond = jnp.where(lane == 0, after, before)
                moved = differences(jnp.concatenate([raw[mine].astype(f32), beyond], axis=1))
                for c in range(3):
                    for tile in range(tiles):
                        window[c][pl.ds(first + tile * pitch + TOP + 16 * group, 16), :] = moved[c][
                            :, tile * LANES : (tile + 1) * LANES
                        ]
            return carry

        lax.fori_loop(0, planes, one, 0)
        for source, row in ((low_ref, TOP - 1), (high_ref, TOP + rows)):
            moved = differences(source[...].astype(f32))
            for k in range(planes):
                store_row(slot + k * plane_rows, moved, k, row)

    @pl.when(step == last)
    def _():
        first = pl.multiple_of((step % 3) * block_rows, 8)
        for c in range(3):
            window[c][pl.ds(first, plane_rows), :] = jnp.zeros((plane_rows, LANES), f32)

    @pl.when(step > 0)
    def _():
        mid = (step + 2) % 3
        first_rows = (
            jnp.where(mid == 0, 3, mid) * block_rows - plane_rows,
            mid * block_rows,
            jnp.where(mid == 2, 0, mid + 1) * block_rows,
        )

        def one(t, total):
            tile = t % tiles
            pair = t // tiles
            at = pl.multiple_of(tile * LANES, LANES)
            top = pl.multiple_of(pair * 16, 16)
            origins = [first + tile * pitch + top + TOP for first in first_rows]
            for half in range(2):
                node = (step - 1) * nodes + pair * 2 + half
                mine = slice(8 * half, 8 * half + 8)

                def taps(x):
                    part = 0 if x == 0 else 2 if x == planes + 1 else 1
                    plus = (x - 1) * plane_rows + 8 * half if part == 1 else 8 * half
                    return [
                        [window[c][pl.ds(origins[part] + (plus + b), 8), :] for c in range(3)] for b in (-1, 0, 1)
                    ]

                contrast = jnp.broadcast_to(field[0, tile, pl.ds(node, 1), :], (8, LANES))
                brightness = jnp.broadcast_to(field[1, tile, pl.ds(node, 1), :], (8, LANES))
                by_image = jnp.zeros((8, LANES), f32)
                plain = jnp.zeros((8, LANES), f32)
                before, here = taps(0), taps(1)
                results = []
                for k in range(planes):
                    after = taps(k + 2)
                    place = (k, pl.ds(top, 16), pl.ds(at, LANES))
                    sx, sy, sz = (shift_ref[(axis,) + place].astype(f32)[mine] for axis in range(3))
                    image = image_ref[place].astype(f32)[mine]
                    px, py, pz = sx > 0, sy > 0, sz > 0
                    ax, ay = jnp.abs(sx), jnp.abs(sy)

                    def sides(c):
                        far = [jnp.where(px, after[b][c], before[b][c]) for b in range(3)]
                        near = [here[b][c] for b in range(3)]
                        return [(v[1], jnp.where(py, v[2], v[0])) for v in (near, far)]

                    ahead, middle, behind = sides(0), sides(1), sides(2)
                    lines = []
                    for b in range(2):
                        near, far = (middle[v][b] + sz * jnp.where(pz, ahead[v][b], behind[v][b]) for v in range(2))
                        lines.append(near + ax * (far - near))
                    warped = lines[0] + ay * (lines[1] - lines[0])
                    misfit = warped - contrast * image - brightness
                    results.append(misfit)
                    by_image = by_image + misfit * image
                    plain = plain + misfit
                    total = total + misfit * misfit
                    before, here = here, after
                for k in range(planes):
                    if half == 0:
                        held[k] = results[k]
                    else:
                        place = (k, pl.ds(top, 16), pl.ds(at, LANES))
                        residual_ref[place] = jnp.concatenate([held[k], results[k]], axis=0).astype(bf16)
                for k, value in ((0, by_image), (1, plain)):
                    blocks[k, tile, pl.ds(pl.multiple_of(node * 8, 8), 8), :] = value
            return total

        energy[...] = lax.fori_loop(0, (rows // 16) * tiles, one, energy[...])

    @pl.when(step == last)
    def _():
        parts = depth_out.shape[0]
        share = RANK // parts
        sums = [joined(blocks.at[k]) for k in range(2)]
        kinds = [split_dot(plane_ref[k], sums[k], 0) for k in range(2)]
        squared = joined(squares_ref)
        cells = jnp.full(squared.shape, float(KNOT * KNOT), f32)
        second = plane_ref[1]
        kinds = kinds + [split_dot(plane_ref[0] * plane_ref[0], squared, 0), split_dot(second * second, cells, 0)]
        for p in range(parts):
            for k in range(4):
                depth_out[p, k * share : (k + 1) * share, :] = kinds[k][p * share : (p + 1) * share]
        local = jnp.sum(energy[...])
        kinds = [split_dot(sums[k], depth_ref[k], 1) for k in range(2)]
        second = depth_ref[1]
        kinds = kinds + [split_dot(squared, depth_ref[0] * depth_ref[0], 1), split_dot(cells, second * second, 1)]
        for k in range(4):
            plane_out[:, k * RANK : (k + 1) * RANK] = kinds[k]
        count = plane_out.shape[0]
        plane_out[count // 2 :, 3 * RANK :] = jnp.full((count // 2, RANK), local, f32)


def warp(cells, image, shift, left, right, low, high, squared, plane, depth_factors, parts):
    depth, rows, width = cells.shape
    nodes = plane.shape[1]
    tiles = width // LANES
    count = depth // KNOT
    behind = lambda i: (jnp.maximum(i - 1, 0), 0, 0)
    ahead = lambda i: (jnp.minimum(i, count - 1), 0, 0)
    flat = lambda i: (0, 0)
    whole = lambda i: (0, 0, 0)
    return pl.pallas_call(
        warp_kernel,
        grid=(count + 1,),
        in_specs=[
            pl.BlockSpec((KNOT, rows, width), ahead),
            pl.BlockSpec((KNOT, rows, width), behind),
            pl.BlockSpec((3, KNOT, rows, width), lambda i: (0, jnp.maximum(i - 1, 0), 0, 0)),
            pl.BlockSpec(left.shape, flat),
            pl.BlockSpec(right.shape, flat),
            pl.BlockSpec((KNOT, low.shape[1]), lambda i: (jnp.minimum(i, count - 1), 0)),
            pl.BlockSpec((KNOT, high.shape[1]), lambda i: (jnp.minimum(i, count - 1), 0)),
            pl.BlockSpec(squared.shape, whole),
            pl.BlockSpec(plane.shape, whole),
            pl.BlockSpec(depth_factors.shape, whole),
        ],
        out_specs=[
            pl.BlockSpec((KNOT, rows, width), behind),
            pl.BlockSpec((parts, 4 * RANK // parts, width), whole),
            pl.BlockSpec((nodes, 4 * RANK), flat),
        ],
        out_shape=[
            jax.ShapeDtypeStruct(cells.shape, bf16),
            jax.ShapeDtypeStruct((parts, 4 * RANK // parts, width), f32),
            jax.ShapeDtypeStruct((nodes, 4 * RANK), f32),
        ],
        scratch_shapes=[
            *[pltpu.VMEM((3 * KNOT * tiles * (rows + 2 * TOP), LANES), f32)] * 3,
            pltpu.VMEM((2, rows, LANES), f32),
            pltpu.VMEM((2, tiles, nodes, LANES), f32),
            pltpu.VMEM((2, tiles, 8 * nodes, LANES), f32),
            pltpu.VMEM((8, LANES), f32),
            pltpu.VMEM((KNOT, 8, LANES), f32),
        ],
        compiler_params=grid_params(),
        cost_estimate=pl.CostEstimate(flops=60 * cells.size, bytes_accessed=12 * cells.size, transcendentals=0),
        name="warp",
    )(cells, image, shift, left, right, low, high, squared, plane, depth_factors)


def gather_kernel(depth_ref, *refs):
    depth_out, plane_out = refs[-2:]
    total = jnp.sum(depth_ref[...], axis=0)
    found = [ref[...] for ref in refs[:-2]]
    while len(found) > 1:
        half = len(found) // 2
        found = [found[k] + found[k + half] for k in range(half)]
    planes = found[0]
    plane_out[...] = planes
    cells = planes.shape[0]
    share, width = total.shape[0] // 4, total.shape[1]
    row = lax.broadcasted_iota(jnp.int32, total.shape, 0)
    lane = lax.broadcasted_iota(jnp.int32, total.shape, 1)
    partial = planes[cells - 1, 4 * RANK - 1]
    total = jnp.where((row >= 3 * share) & (lane >= width // 2), partial, total)
    for p in range(depth_out.shape[0]):
        depth_out[p] = total


def step_kernel(full_z, node_count, depth_ref, plane_ref, depth_out, plane_out):
    parts, share, width = depth_ref.shape[0], depth_ref.shape[1] // 4, depth_ref.shape[2]
    energy = depth_ref[0, 3 * share, width - 1]
    for p in range(1, parts):
        energy = energy + depth_ref[p, 3 * share, width - 1]
    lam_depth = damping * energy / full_z
    lam_plane = damping * RANK * energy / node_count
    for p in range(parts):
        got = depth_ref[p]
        levels = got[3 * share :, 0 : width // 2]
        levels = jnp.concatenate([levels, levels], axis=1)
        rows = slice(p * share, (p + 1) * share)
        depth_out[0, rows, :] = got[0:share] / (got[2 * share : 3 * share] + lam_depth + epsilon)
        depth_out[1, rows, :] = got[share : 2 * share] / (levels + lam_depth + epsilon)
    planes = plane_ref[...]
    plane_out[0] = planes[:, 0:RANK] / (planes[:, 2 * RANK : 3 * RANK] + lam_plane + epsilon)
    plane_out[1] = planes[:, RANK : 2 * RANK] / (planes[0:1, 3 * RANK :] + lam_plane + epsilon)


def local(image, deformed, displacement, plane_factors, depth_factors):
    n_gy, n_gz = lax.axis_size("gy"), lax.axis_size("gz")
    nodes_x, nodes_y = plane_factors.shape[2:]
    plane = jnp.transpose(plane_factors, (0, 2, 3, 1)).reshape(2, nodes_x * nodes_y, RANK)
    first, last = end_columns(deformed)
    right = shifted(first, "gz", True)
    left = shifted(last, "gz", False)
    sums, low, high = squares(image, deformed)
    low, high = packed_rows(left, right, low, high)
    above = shifted(low, "gy", True)
    below = shifted(high, "gy", False)
    residual, depth_terms, plane_terms = warp(
        deformed, image, displacement, left, right, below, above, sums, plane, depth_factors, n_gy
    )
    others = [
        lax.ppermute(plane_terms, "gz", [(i, (i + hop) % n_gz) for i in range(n_gz)]) for hop in range(1, n_gz)
    ]
    depth_terms = lax.all_to_all(depth_terms, "gy", 0, 0)
    depth_terms, plane_terms = pl.pallas_call(
        gather_kernel,
        out_shape=[
            jax.ShapeDtypeStruct(depth_terms.shape, f32),
            jax.ShapeDtypeStruct(plane_terms.shape, f32),
        ],
        compiler_params=plain_params(),
        name="gather",
    )(depth_terms, plane_terms, *others)
    depth_terms = lax.all_to_all(depth_terms, "gy", 0, 0)
    width = depth_factors.shape[2]
    step_depth, step_plane = pl.pallas_call(
        functools.partial(step_kernel, width * n_gz, nodes_x * nodes_y * n_gy),
        out_shape=[
            jax.ShapeDtypeStruct(depth_factors.shape, f32),
            jax.ShapeDtypeStruct(plane.shape, f32),
        ],
        compiler_params=plain_params(),
        name="steps",
    )(depth_terms, plane_terms)
    step_plane = jnp.transpose(step_plane.reshape(2, nodes_x, nodes_y, RANK), (0, 3, 1, 2))
    return residual, step_plane, step_depth


def solution(mesh):
    placed = (
        P(None, "gy", "gz"),
        P(None, "gy", "gz"),
        P(None, None, "gy", "gz"),
        P(None, None, None, "gy"),
        P(None, None, "gz"),
    )
    return jax.shard_map(
        local,
        mesh=mesh,
        in_specs=placed,
        out_specs=(P(None, "gy", "gz"), P(None, None, None, "gy"), P(None, None, "gz")),
        check_vma=False,
    )
```

```python
import functools

import jax
import jax.numpy as jnp
from jax import lax
from jax.experimental import pallas as pl
from jax.experimental.pallas import tpu as pltpu
from jax.sharding import PartitionSpec as P

RANK = 32
KNOT = 8
LANES = 128
TOP = 8

epsilon = 1e-06
damping = 0.01
highest = lax.Precision.HIGHEST
f32 = jnp.float32
bf16 = jnp.bfloat16


def dot(left, right, dims):
    return lax.dot_general(left, right, ((dims[0], dims[1]), ((), ())), precision=highest, preferred_element_type=f32)


def split_dot(left, right, dim):
    left_high, right_high = left.astype(bf16), right.astype(bf16)
    left_low = (left - left_high.astype(f32)).astype(bf16)
    right_low = (right - right_high.astype(f32)).astype(bf16)
    left = jnp.concatenate([left_high, left_high, left_low], axis=dim)
    right = jnp.concatenate([right_high, right_low, right_high], axis=dim)
    return lax.dot_general(left, right, (((dim,), (dim,)), ((), ())), preferred_element_type=f32)


def joined(ref):
    tiles, rows = ref.shape[0:2]
    return jnp.concatenate([jnp.sum(ref[t].reshape(rows // 8, 8, LANES), axis=1) for t in range(tiles)], axis=1)


def grid_params():
    return pltpu.CompilerParams(dimension_semantics=("arbitrary",), vmem_limit_bytes=40000000)


def plain_params():
    return pltpu.CompilerParams(vmem_limit_bytes=32000000)


def columns_kernel(near_ref, far_ref, first_ref, last_ref):
    depth, rows = near_ref.shape[0:2]
    lane = lax.broadcasted_iota(jnp.int32, (rows, LANES), 1)
    first = jnp.zeros((rows, LANES), f32)
    last = jnp.zeros((rows, LANES), f32)
    for x in range(depth):
        first = jnp.where(lane == x, pltpu.roll(near_ref[x].astype(f32), x, 1), first)
        last = jnp.where(lane == x, pltpu.roll(far_ref[x].astype(f32), (x + 1) % LANES, 1), last)
    first_ref[...] = first.astype(bf16)
    last_ref[...] = last.astype(bf16)


def end_columns(cells):
    depth, rows, width = cells.shape
    tiles = width // LANES
    return pl.pallas_call(
        columns_kernel,
        grid=(1,),
        in_specs=[
            pl.BlockSpec((depth, rows, LANES), lambda i: (0, 0, 0)),
            pl.BlockSpec((depth, rows, LANES), lambda i: (0, 0, tiles - 1)),
        ],
        out_specs=[pl.BlockSpec((rows, LANES), lambda i: (0, 0))] * 2,
        out_shape=[jax.ShapeDtypeStruct((rows, LANES), bf16)] * 2,
        compiler_params=grid_params(),
        name="columns",
    )(cells, cells)


def rows_kernel(left_ref, right_ref, low_ref, high_ref, low_out, high_out):
    depth, width = low_ref.shape
    rows = left_ref.shape[0]
    lane = lax.broadcasted_iota(jnp.int32, (depth, LANES), 1)
    pad = jnp.zeros((LANES - rows, LANES), f32)
    left = jnp.transpose(jnp.concatenate([left_ref[...].astype(f32), pad], axis=0))[0:depth]
    right = jnp.transpose(jnp.concatenate([right_ref[...].astype(f32), pad], axis=0))[0:depth]
    for row, body, out in ((0, low_ref, low_out), (rows - 1, high_ref, high_out)):
        after = pltpu.roll(right, (LANES - row) % LANES, 1)
        before = pltpu.roll(left, LANES - 1 - row, 1)
        out[:, 0:width] = body[...].astype(bf16)
        out[:, width : width + LANES] = jnp.where(lane == 0, after, before).astype(bf16)


def packed_rows(left, right, low, high):
    depth, width = low.shape
    return pl.pallas_call(
        rows_kernel,
        out_shape=[jax.ShapeDtypeStruct((depth, width + LANES), bf16)] * 2,
        compiler_params=plain_params(),
        name="rows",
    )(left, right, low, high)


def shifted(part, axis, back):
    count = lax.axis_size(axis)
    if back:
        return lax.ppermute(part, axis, [(i + 1, i) for i in range(count - 1)])
    return lax.ppermute(part, axis, [(i, i + 1) for i in range(count - 1)])


def squares_kernel(image_ref, top_ref, bottom_ref, sums, low_ref, high_ref):
    step = pl.program_id(0)
    planes, rows, width = image_ref.shape
    tiles = width // LANES

    def one(tile, carry):
        at = pl.multiple_of(tile * LANES, LANES)
        for pair in range(rows // 16):
            total = jnp.zeros((16, LANES), f32)
            for k in range(planes):
                values = image_ref[k, 16 * pair : 16 * pair + 16, pl.ds(at, LANES)].astype(f32)
                total = total + values * values
            sums[tile, pl.ds(step * rows + 16 * pair, 16), :] = total
        return carry

    lax.fori_loop(0, tiles, one, 0)
    low_ref[...] = jnp.concatenate([top_ref[k].astype(f32)[0:1] for k in range(planes)], axis=0)
    high_ref[...] = jnp.concatenate([bottom_ref[k].astype(f32)[15:16] for k in range(planes)], axis=0)


def squares(image, cells):
    depth, rows, width = image.shape
    return pl.pallas_call(
        squares_kernel,
        grid=(depth // KNOT,),
        in_specs=[
            pl.BlockSpec((KNOT, rows, width), lambda i: (i, 0, 0)),
            pl.BlockSpec((KNOT, 16, width), lambda i: (i, 0, 0)),
            pl.BlockSpec((KNOT, 16, width), lambda i: (i, rows // 16 - 1, 0)),
        ],
        out_specs=[
            pl.BlockSpec((width // LANES, depth * rows // KNOT, LANES), lambda i: (0, 0, 0)),
            pl.BlockSpec((KNOT, width), lambda i: (i, 0)),
            pl.BlockSpec((KNOT, width), lambda i: (i, 0)),
        ],
        out_shape=[
            jax.ShapeDtypeStruct((width // LANES, depth * rows // KNOT, LANES), f32),
            jax.ShapeDtypeStruct((depth, width), f32),
            jax.ShapeDtypeStruct((depth, width), f32),
        ],
        compiler_params=grid_params(),
        cost_estimate=pl.CostEstimate(flops=3 * image.size, bytes_accessed=2 * image.size, transcendentals=0),
        name="squares",
    )(image, cells, cells)


def warp_kernel(
    cells_ref, image_ref, shift_ref, left_ref, right_ref, low_ref, high_ref, squares_ref, plane_ref, depth_ref,
    residual_ref, depth_out, plane_out,
    ahead_ref, here_ref, behind_ref, columns, field, blocks, energy, held,
):
    step = pl.program_id(0)
    last = pl.num_programs(0) - 1
    planes, rows, width = cells_ref.shape
    nodes = rows // KNOT
    tiles = width // LANES
    window = (ahead_ref, here_ref, behind_ref)
    pitch = rows + 2 * TOP
    plane_rows = tiles * pitch
    block_rows = planes * plane_rows

    def store_row(plane, moved, k, row):
        for c in range(3):
            for tile in range(tiles):
                piece = moved[c][k : k + 1, tile * LANES : (tile + 1) * LANES]
                window[c][pl.ds(plane + tile * pitch + row, 1), :] = piece

    def differences(wide):
        ahead = pltpu.roll(wide, wide.shape[1] - 1, 1) - wide
        return ahead, wide, pltpu.roll(ahead, 1, 1)

    @pl.when(step == 0)
    def _():
        columns[0] = left_ref[...].astype(f32)
        columns[1] = right_ref[...].astype(f32)
        energy[...] = jnp.zeros_like(energy)
        for c in range(3):
            window[c][3 * block_rows - plane_rows : 3 * block_rows, :] = jnp.zeros((plane_rows, LANES), f32)
        for k in range(2):
            values = dot(plane_ref[k], depth_ref[k], ((1,), (0,)))
            for tile in range(tiles):
                field[k, tile] = values[:, tile * LANES : (tile + 1) * LANES]

    @pl.when(step < last)
    def _():
        lane = lax.broadcasted_iota(jnp.int32, (16, LANES), 1)
        slot = (step % 3) * block_rows

        def one(k, carry):
            x = step * planes + k
            first = pl.multiple_of(slot + k * plane_rows, 8)
            raw = cells_ref[k]
            right, left = columns[1], columns[0]
            for group in range(rows // 16):
                mine = slice(16 * group, 16 * group + 16)
                after = pltpu.roll(right[mine], (LANES - x) % LANES, 1)
                before = pltpu.roll(left[mine], LANES - 1 - x, 1)
                beyond = jnp.where(lane == 0, after, before)
                moved = differences(jnp.concatenate([raw[mine].astype(f32), beyond], axis=1))
                for c in range(3):
                    for tile in range(tiles):
                        window[c][pl.ds(first + tile * pitch + TOP + 16 * group, 16), :] = moved[c][
                            :, tile * LANES : (tile + 1) * LANES
                        ]
            return carry

        lax.fori_loop(0, planes, one, 0)
        for source, row in ((low_ref, TOP - 1), (high_ref, TOP + rows)):
            moved = differences(source[...].astype(f32))
            for k in range(planes):
                store_row(slot + k * plane_rows, moved, k, row)

    @pl.when(step == last)
    def _():
        first = pl.multiple_of((step % 3) * block_rows, 8)
        for c in range(3):
            window[c][pl.ds(first, plane_rows), :] = jnp.zeros((plane_rows, LANES), f32)

    @pl.when(step > 0)
    def _():
        mid = (step + 2) % 3
        first_rows = (
            jnp.where(mid == 0, 3, mid) * block_rows - plane_rows,
            mid * block_rows,
            jnp.where(mid == 2, 0, mid + 1) * block_rows,
        )

        def one(t, total):
            tile = t % tiles
            pair = t // tiles
            at = pl.multiple_of(tile * LANES, LANES)
            top = pl.multiple_of(pair * 16, 16)
            origins = [first + tile * pitch + top + TOP for first in first_rows]
            for half in range(2):
                node = (step - 1) * nodes + pair * 2 + half
                mine = slice(8 * half, 8 * half + 8)

                def taps(x):
                    part = 0 if x == 0 else 2 if x == planes + 1 else 1
                    plus = (x - 1) * plane_rows + 8 * half if part == 1 else 8 * half
                    return [
                        [window[c][pl.ds(origins[part] + (plus + b), 8), :] for c in range(3)] for b in (-1, 0, 1)
                    ]

                contrast = jnp.broadcast_to(field[0, tile, pl.ds(node, 1), :], (8, LANES))
                brightness = jnp.broadcast_to(field[1, tile, pl.ds(node, 1), :], (8, LANES))
                by_image = jnp.zeros((8, LANES), f32)
                plain = jnp.zeros((8, LANES), f32)
                before, here = taps(0), taps(1)
                for k in range(planes):
                    after = taps(k + 2)
                    place = (k, pl.ds(top, 16), pl.ds(at, LANES))
                    sx, sy, sz = (shift_ref[(axis,) + place].astype(f32)[mine] for axis in range(3))
                    image = image_ref[place].astype(f32)[mine]
                    px, py, pz = sx > 0, sy > 0, sz > 0
                    ax, ay = jnp.abs(sx), jnp.abs(sy)

                    def sides(c):
                        far = [jnp.where(px, after[b][c], before[b][c]) for b in range(3)]
                        near = [here[b][c] for b in range(3)]
                        return [(v[1], jnp.where(py, v[2], v[0])) for v in (near, far)]

                    ahead, middle, behind = sides(0), sides(1), sides(2)
                    lines = []
                    for b in range(2):
                        near, far = (middle[v][b] + sz * jnp.where(pz, ahead[v][b], behind[v][b]) for v in range(2))
                        lines.append(near + ax * (far - near))
                    warped = lines[0] + ay * (lines[1] - lines[0])
                    misfit = warped - contrast * image - brightness
                    if half == 0:
                        held[k] = misfit
                    else:
                        residual_ref[place] = jnp.concatenate([held[k], misfit], axis=0).astype(bf16)
                    by_image = by_image + misfit * image
                    plain = plain + misfit
                    total = total + misfit * misfit
                    before, here = here, after
                for k, value in ((0, by_image), (1, plain)):
                    blocks[k, tile, pl.ds(pl.multiple_of(node * 8, 8), 8), :] = value
            return total

        energy[...] = lax.fori_loop(0, (rows // 16) * tiles, one, energy[...])

    @pl.when(step == last)
    def _():
        parts = depth_out.shape[0]
        share = RANK // parts
        sums = [joined(blocks.at[k]) for k in range(2)]
        kinds = [split_dot(plane_ref[k], sums[k], 0) for k in range(2)]
        squared = joined(squares_ref)
        cells = jnp.full(squared.shape, float(KNOT * KNOT), f32)
        second = plane_ref[1]
        kinds = kinds + [split_dot(plane_ref[0] * plane_ref[0], squared, 0), split_dot(second * second, cells, 0)]
        for p in range(parts):
            for k in range(4):
                depth_out[p, k * share : (k + 1) * share, :] = kinds[k][p * share : (p + 1) * share]
        local = jnp.sum(energy[...])
        kinds = [split_dot(sums[k], depth_ref[k], 1) for k in range(2)]
        second = depth_ref[1]
        kinds = kinds + [split_dot(squared, depth_ref[0] * depth_ref[0], 1), split_dot(cells, second * second, 1)]
        for k in range(4):
            plane_out[:, k * RANK : (k + 1) * RANK] = kinds[k]
        count = plane_out.shape[0]
        plane_out[count // 2 :, 3 * RANK :] = jnp.full((count // 2, RANK), local, f32)


def warp(cells, image, shift, left, right, low, high, squared, plane, depth_factors, parts):
    depth, rows, width = cells.shape
    nodes = plane.shape[1]
    tiles = width // LANES
    count = depth // KNOT
    behind = lambda i: (jnp.maximum(i - 1, 0), 0, 0)
    ahead = lambda i: (jnp.minimum(i, count - 1), 0, 0)
    flat = lambda i: (0, 0)
    whole = lambda i: (0, 0, 0)
    return pl.pallas_call(
        warp_kernel,
        grid=(count + 1,),
        in_specs=[
            pl.BlockSpec((KNOT, rows, width), ahead),
            pl.BlockSpec((KNOT, rows, width), behind),
            pl.BlockSpec((3, KNOT, rows, width), lambda i: (0, jnp.maximum(i - 1, 0), 0, 0)),
            pl.BlockSpec(left.shape, flat),
            pl.BlockSpec(right.shape, flat),
            pl.BlockSpec((KNOT, low.shape[1]), lambda i: (jnp.minimum(i, count - 1), 0)),
            pl.BlockSpec((KNOT, high.shape[1]), lambda i: (jnp.minimum(i, count - 1), 0)),
            pl.BlockSpec(squared.shape, whole),
            pl.BlockSpec(plane.shape, whole),
            pl.BlockSpec(depth_factors.shape, whole),
        ],
        out_specs=[
            pl.BlockSpec((KNOT, rows, width), behind),
            pl.BlockSpec((parts, 4 * RANK // parts, width), whole),
            pl.BlockSpec((nodes, 4 * RANK), flat),
        ],
        out_shape=[
            jax.ShapeDtypeStruct(cells.shape, bf16),
            jax.ShapeDtypeStruct((parts, 4 * RANK // parts, width), f32),
            jax.ShapeDtypeStruct((nodes, 4 * RANK), f32),
        ],
        scratch_shapes=[
            *[pltpu.VMEM((3 * KNOT * tiles * (rows + 2 * TOP), LANES), f32)] * 3,
            pltpu.VMEM((2, rows, LANES), f32),
            pltpu.VMEM((2, tiles, nodes, LANES), f32),
            pltpu.VMEM((2, tiles, 8 * nodes, LANES), f32),
            pltpu.VMEM((8, LANES), f32),
            pltpu.VMEM((KNOT, 8, LANES), f32),
        ],
        compiler_params=grid_params(),
        cost_estimate=pl.CostEstimate(flops=60 * cells.size, bytes_accessed=12 * cells.size, transcendentals=0),
        name="warp",
    )(cells, image, shift, left, right, low, high, squared, plane, depth_factors)


def gather_kernel(depth_ref, *refs):
    depth_out, plane_out = refs[-2:]
    total = jnp.sum(depth_ref[...], axis=0)
    found = [ref[...] for ref in refs[:-2]]
    while len(found) > 1:
        half = len(found) // 2
        found = [found[k] + found[k + half] for k in range(half)]
    planes = found[0]
    plane_out[...] = planes
    cells = planes.shape[0]
    share, width = total.shape[0] // 4, total.shape[1]
    row = lax.broadcasted_iota(jnp.int32, total.shape, 0)
    lane = lax.broadcasted_iota(jnp.int32, total.shape, 1)
    partial = planes[cells - 1, 4 * RANK - 1]
    total = jnp.where((row >= 3 * share) & (lane >= width // 2), partial, total)
    for p in range(depth_out.shape[0]):
        depth_out[p] = total


def step_kernel(full_z, node_count, depth_ref, plane_ref, depth_out, plane_out):
    parts, share, width = depth_ref.shape[0], depth_ref.shape[1] // 4, depth_ref.shape[2]
    energy = depth_ref[0, 3 * share, width - 1]
    for p in range(1, parts):
        energy = energy + depth_ref[p, 3 * share, width - 1]
    lam_depth = damping * energy / full_z
    lam_plane = damping * RANK * energy / node_count
    for p in range(parts):
        got = depth_ref[p]
        levels = got[3 * share :, 0 : width // 2]
        levels = jnp.concatenate([levels, levels], axis=1)
        rows = slice(p * share, (p + 1) * share)
        depth_out[0, rows, :] = got[0:share] / (got[2 * share : 3 * share] + lam_depth + epsilon)
        depth_out[1, rows, :] = got[share : 2 * share] / (levels + lam_depth + epsilon)
    planes = plane_ref[...]
    plane_out[0] = planes[:, 0:RANK] / (planes[:, 2 * RANK : 3 * RANK] + lam_plane + epsilon)
    plane_out[1] = planes[:, RANK : 2 * RANK] / (planes[0:1, 3 * RANK :] + lam_plane + epsilon)


def local(image, deformed, displacement, plane_factors, depth_factors):
    n_gy, n_gz = lax.axis_size("gy"), lax.axis_size("gz")
    nodes_x, nodes_y = plane_factors.shape[2:]
    plane = jnp.transpose(plane_factors, (0, 2, 3, 1)).reshape(2, nodes_x * nodes_y, RANK)
    first, last = end_columns(deformed)
    right = shifted(first, "gz", True)
    left = shifted(last, "gz", False)
    sums, low, high = squares(image, deformed)
    low, high = packed_rows(left, right, low, high)
    above = shifted(low, "gy", True)
    below = shifted(high, "gy", False)
    residual, depth_terms, plane_terms = warp(
        deformed, image, displacement, left, right, below, above, sums, plane, depth_factors, n_gy
    )
    others = [
        lax.ppermute(plane_terms, "gz", [(i, (i + hop) % n_gz) for i in range(n_gz)]) for hop in range(1, n_gz)
    ]
    depth_terms = lax.all_to_all(depth_terms, "gy", 0, 0)
    depth_terms, plane_terms = pl.pallas_call(
        gather_kernel,
        out_shape=[
            jax.ShapeDtypeStruct(depth_terms.shape, f32),
            jax.ShapeDtypeStruct(plane_terms.shape, f32),
        ],
        compiler_params=plain_params(),
        name="gather",
    )(depth_terms, plane_terms, *others)
    depth_terms = lax.all_to_all(depth_terms, "gy", 0, 0)
    width = depth_factors.shape[2]
    step_depth, step_plane = pl.pallas_call(
        functools.partial(step_kernel, width * n_gz, nodes_x * nodes_y * n_gy),
        out_shape=[
            jax.ShapeDtypeStruct(depth_factors.shape, f32),
            jax.ShapeDtypeStruct(plane.shape, f32),
        ],
        compiler_params=plain_params(),
        name="steps",
    )(depth_terms, plane_terms)
    step_plane = jnp.transpose(step_plane.reshape(2, nodes_x, nodes_y, RANK), (0, 3, 1, 2))
    return residual, step_plane, step_depth


def solution(mesh):
    placed = (
        P(None, "gy", "gz"),
        P(None, "gy", "gz"),
        P(None, None, "gy", "gz"),
        P(None, None, None, "gy"),
        P(None, None, "gz"),
    )
    return jax.shard_map(
        local,
        mesh=mesh,
        in_specs=placed,
        out_specs=(P(None, "gy", "gz"), P(None, None, None, "gy"), P(None, None, "gz")),
        check_vma=False,
    )
```

```python
import functools

import jax
import jax.numpy as jnp
from jax import lax
from jax.experimental import pallas as pl
from jax.experimental.pallas import tpu as pltpu
from jax.sharding import PartitionSpec as P

RANK = 32
KNOT = 8
LANES = 128
TOP = 8

epsilon = 1e-06
damping = 0.01
highest = lax.Precision.HIGHEST
f32 = jnp.float32
bf16 = jnp.bfloat16


def dot(left, right, dims):
    return lax.dot_general(left, right, ((dims[0], dims[1]), ((), ())), precision=highest, preferred_element_type=f32)


def split_dot(left, right, dim):
    left_high, right_high = left.astype(bf16), right.astype(bf16)
    left_low = (left - left_high.astype(f32)).astype(bf16)
    right_low = (right - right_high.astype(f32)).astype(bf16)
    left = jnp.concatenate([left_high, left_high, left_low], axis=dim)
    right = jnp.concatenate([right_high, right_low, right_high], axis=dim)
    return lax.dot_general(left, right, (((dim,), (dim,)), ((), ())), preferred_element_type=f32)


def joined(ref):
    tiles, rows = ref.shape[0:2]
    return jnp.concatenate([jnp.sum(ref[t].reshape(rows // 8, 8, LANES), axis=1) for t in range(tiles)], axis=1)


def plain_params():
    return pltpu.CompilerParams(vmem_limit_bytes=32000000)


def columns_kernel(cells_ref, first_ref, last_ref):
    depth, rows, width = cells_ref.shape
    lane = lax.broadcasted_iota(jnp.int32, (rows, LANES), 1)
    first = jnp.zeros((rows, LANES), f32)
    last = jnp.zeros((rows, LANES), f32)
    for x in range(depth):
        near = cells_ref[x, :, 0:LANES].astype(f32)
        far = cells_ref[x, :, width - LANES : width].astype(f32)
        first = jnp.where(lane == x, pltpu.roll(near, x, 1), first)
        last = jnp.where(lane == x, pltpu.roll(far, (x + 1) % LANES, 1), last)
    first_ref[...] = first.astype(bf16)
    last_ref[...] = last.astype(bf16)


def end_columns(cells):
    rows = cells.shape[1]
    return pl.pallas_call(
        columns_kernel,
        out_shape=[jax.ShapeDtypeStruct((rows, LANES), bf16)] * 2,
        compiler_params=plain_params(),
        name="columns",
    )(cells)


def rows_kernel(left_ref, right_ref, low_ref, high_ref, low_out, high_out):
    depth, width = low_ref.shape
    rows = left_ref.shape[0]
    lane = lax.broadcasted_iota(jnp.int32, (depth, LANES), 1)
    pad = jnp.zeros((LANES - rows, LANES), f32)
    left = jnp.transpose(jnp.concatenate([left_ref[...].astype(f32), pad], axis=0))[0:depth]
    right = jnp.transpose(jnp.concatenate([right_ref[...].astype(f32), pad], axis=0))[0:depth]
    for row, body, out in ((0, low_ref, low_out), (rows - 1, high_ref, high_out)):
        after = pltpu.roll(right, (LANES - row) % LANES, 1)
        before = pltpu.roll(left, LANES - 1 - row, 1)
        out[:, 0:width] = body[...].astype(bf16)
        out[:, width : width + LANES] = jnp.where(lane == 0, after, before).astype(bf16)


def packed_rows(left, right, low, high):
    depth, width = low.shape
    return pl.pallas_call(
        rows_kernel,
        out_shape=[jax.ShapeDtypeStruct((depth, width + LANES), bf16)] * 2,
        compiler_params=plain_params(),
        name="rows",
    )(left, right, low, high)


def shifted(part, axis, back):
    count = lax.axis_size(axis)
    if back:
        return lax.ppermute(part, axis, [(i + 1, i) for i in range(count - 1)])
    return lax.ppermute(part, axis, [(i, i + 1) for i in range(count - 1)])


def squares_kernel(image_ref, cells_ref, sums, low_ref, high_ref):
    depth, rows, width = image_ref.shape
    tiles = width // LANES

    def one(t, carry):
        block, tile = t // tiles, t % tiles
        at = pl.multiple_of(tile * LANES, LANES)
        for pair in range(rows // 16):
            total = jnp.zeros((16, LANES), f32)
            for k in range(KNOT):
                values = image_ref[block * KNOT + k, 16 * pair : 16 * pair + 16, pl.ds(at, LANES)].astype(f32)
                total = total + values * values
            sums[tile, pl.ds(pl.multiple_of(block * rows + 16 * pair, 16), 16), :] = total
        return carry

    lax.fori_loop(0, depth // KNOT * tiles, one, 0)

    def ends(block, carry):
        x = pl.multiple_of(block * KNOT, KNOT)
        low = [cells_ref[x + k, 0:16, :].astype(f32)[0:1] for k in range(KNOT)]
        high = [cells_ref[x + k, rows - 16 : rows, :].astype(f32)[15:16] for k in range(KNOT)]
        low_ref[pl.ds(x, KNOT), :] = jnp.concatenate(low, axis=0)
        high_ref[pl.ds(x, KNOT), :] = jnp.concatenate(high, axis=0)
        return carry

    lax.fori_loop(0, depth // KNOT, ends, 0)


def squares(image, cells):
    depth, rows, width = image.shape
    return pl.pallas_call(
        squares_kernel,
        out_shape=[
            jax.ShapeDtypeStruct((width // LANES, depth * rows // KNOT, LANES), f32),
            jax.ShapeDtypeStruct((depth, width), f32),
            jax.ShapeDtypeStruct((depth, width), f32),
        ],
        compiler_params=plain_params(),
        cost_estimate=pl.CostEstimate(flops=3 * image.size, bytes_accessed=2 * image.size, transcendentals=0),
        name="squares",
    )(image, cells)


def warp_kernel(
    cells_ref, image_ref, shift_hbm, left_ref, right_ref, low_ref, high_ref, squares_ref, plane_ref, depth_ref,
    residual_hbm, depth_out, plane_out,
    ahead_ref, here_ref, behind_ref, shift_ref, residual_ref, columns, field, blocks, energy, held, got, sent,
):
    depth, rows, width = cells_ref.shape
    planes = KNOT
    count = depth // planes
    nodes = rows // KNOT
    tiles = width // LANES
    window = (ahead_ref, here_ref, behind_ref)
    pitch = rows + 2 * TOP
    plane_rows = tiles * pitch
    block_rows = planes * plane_rows

    def fetch(axis, n):
        part = (axis, pl.ds(n * planes, planes))
        return pltpu.make_async_copy(shift_hbm.at[part], shift_ref.at[part], got.at[axis, n])

    def send(n):
        part = pl.ds(n * planes, planes)
        return pltpu.make_async_copy(residual_ref.at[part], residual_hbm.at[part], sent.at[n])

    for n in range(count):
        for axis in range(3):
            fetch(axis, n).start()

    def store_row(plane, moved, k, row):
        for c in range(3):
            for tile in range(tiles):
                piece = moved[c][k : k + 1, tile * LANES : (tile + 1) * LANES]
                window[c][pl.ds(plane + tile * pitch + row, 1), :] = piece

    def differences(wide):
        ahead = pltpu.roll(wide, wide.shape[1] - 1, 1) - wide
        return ahead, wide, pltpu.roll(ahead, 1, 1)

    columns[0] = left_ref[...].astype(f32)
    columns[1] = right_ref[...].astype(f32)
    energy[...] = jnp.zeros_like(energy)
    for c in range(3):
        window[c][3 * block_rows - plane_rows : 3 * block_rows, :] = jnp.zeros((plane_rows, LANES), f32)
    for k in range(2):
        values = dot(plane_ref[k], depth_ref[k], ((1,), (0,)))
        for tile in range(tiles):
            field[k, tile] = values[:, tile * LANES : (tile + 1) * LANES]

    def build(step):
        lane = lax.broadcasted_iota(jnp.int32, (16, LANES), 1)
        slot = (step % 3) * block_rows

        def one(k, carry):
            x = step * planes + k
            first = pl.multiple_of(slot + k * plane_rows, 8)
            raw = cells_ref[x]
            right, left = columns[1], columns[0]
            for group in range(rows // 16):
                mine = slice(16 * group, 16 * group + 16)
                after = pltpu.roll(right[mine], (LANES - x) % LANES, 1)
                before = pltpu.roll(left[mine], LANES - 1 - x, 1)
                beyond = jnp.where(lane == 0, after, before)
                moved = differences(jnp.concatenate([raw[mine].astype(f32), beyond], axis=1))
                for c in range(3):
                    for tile in range(tiles):
                        window[c][pl.ds(first + tile * pitch + TOP + 16 * group, 16), :] = moved[c][
                            :, tile * LANES : (tile + 1) * LANES
                        ]
            return carry

        lax.fori_loop(0, planes, one, 0)
        for source, row in ((low_ref, TOP - 1), (high_ref, TOP + rows)):
            some = source[pl.ds(pl.multiple_of(step * planes // 16 * 16, 16), 16), :].astype(f32)
            moved = differences(jnp.where(step % 2 == 0, some[0:8], some[8:16]))
            for k in range(planes):
                store_row(slot + k * plane_rows, moved, k, row)

    build(0)

    def block(step, carry):
        @pl.when(step < count)
        def _():
            build(step)

        @pl.when(step == count)
        def _():
            first = pl.multiple_of((step % 3) * block_rows, 8)
            for c in range(3):
                window[c][pl.ds(first, plane_rows), :] = jnp.zeros((plane_rows, LANES), f32)

        for axis in range(3):
            fetch(axis, step - 1).wait()

        mid = (step + 2) % 3
        first_rows = (
            jnp.where(mid == 0, 3, mid) * block_rows - plane_rows,
            mid * block_rows,
            jnp.where(mid == 2, 0, mid + 1) * block_rows,
        )

        def one(t, total):
            tile = t % tiles
            pair = t // tiles
            at = pl.multiple_of(tile * LANES, LANES)
            top = pl.multiple_of(pair * 16, 16)
            origins = [first + tile * pitch + top + TOP for first in first_rows]
            for half in range(2):
                node = (step - 1) * nodes + pair * 2 + half
                mine = slice(8 * half, 8 * half + 8)

                def taps(x):
                    part = 0 if x == 0 else 2 if x == planes + 1 else 1
                    plus = (x - 1) * plane_rows + 8 * half if part == 1 else 8 * half
                    return [
                        [window[c][pl.ds(origins[part] + (plus + b), 8), :] for c in range(3)] for b in (-1, 0, 1)
                    ]

                contrast = jnp.broadcast_to(field[0, tile, pl.ds(node, 1), :], (8, LANES))
                brightness = jnp.broadcast_to(field[1, tile, pl.ds(node, 1), :], (8, LANES))
                by_image = jnp.zeros((8, LANES), f32)
                plain = jnp.zeros((8, LANES), f32)
                before, here = taps(0), taps(1)
                for k in range(planes):
                    after = taps(k + 2)
                    place = ((step - 1) * planes + k, pl.ds(top, 16), pl.ds(at, LANES))
                    sx, sy, sz = (shift_ref[(axis,) + place].astype(f32)[mine] for axis in range(3))
                    image = image_ref[place].astype(f32)[mine]
                    px, py, pz = sx > 0, sy > 0, sz > 0
                    ax, ay = jnp.abs(sx), jnp.abs(sy)

                    def sides(c):
                        far = [jnp.where(px, after[b][c], before[b][c]) for b in range(3)]
                        near = [here[b][c] for b in range(3)]
                        return [(v[1], jnp.where(py, v[2], v[0])) for v in (near, far)]

                    ahead, middle, behind = sides(0), sides(1), sides(2)
                    lines = []
                    for b in range(2):
                        near, far = (middle[v][b] + sz * jnp.where(pz, ahead[v][b], behind[v][b]) for v in range(2))
                        lines.append(near + ax * (far - near))
                    warped = lines[0] + ay * (lines[1] - lines[0])
                    misfit = warped - contrast * image - brightness
                    if half == 0:
                        held[k] = misfit
                    else:
                        residual_ref[place] = jnp.concatenate([held[k], misfit], axis=0).astype(bf16)
                    by_image = by_image + misfit * image
                    plain = plain + misfit
                    total = total + misfit * misfit
                    before, here = here, after
                for k, value in ((0, by_image), (1, plain)):
                    blocks[k, tile, pl.ds(pl.multiple_of(node * 8, 8), 8), :] = value
            return total

        energy[...] = lax.fori_loop(0, (rows // 16) * tiles, one, energy[...])

        send(step - 1).start()
        return carry

    lax.fori_loop(1, count + 1, block, 0)
    for n in range(count):
        send(n).wait()
    parts = depth_out.shape[0]
    share = RANK // parts
    sums = [joined(blocks.at[k]) for k in range(2)]
    kinds = [split_dot(plane_ref[k], sums[k], 0) for k in range(2)]
    squared = joined(squares_ref)
    cells = jnp.full(squared.shape, float(KNOT * KNOT), f32)
    second = plane_ref[1]
    kinds = kinds + [split_dot(plane_ref[0] * plane_ref[0], squared, 0), split_dot(second * second, cells, 0)]
    for p in range(parts):
        for k in range(4):
            depth_out[p, k * share : (k + 1) * share, :] = kinds[k][p * share : (p + 1) * share]
    local = jnp.sum(energy[...])
    kinds = [split_dot(sums[k], depth_ref[k], 1) for k in range(2)]
    second = depth_ref[1]
    kinds = kinds + [split_dot(squared, depth_ref[0] * depth_ref[0], 1), split_dot(cells, second * second, 1)]
    for k in range(4):
        plane_out[:, k * RANK : (k + 1) * RANK] = kinds[k]
    count = plane_out.shape[0]
    plane_out[count // 2 :, 3 * RANK :] = jnp.full((count // 2, RANK), local, f32)


def warp(cells, image, shift, left, right, low, high, squared, plane, depth_factors, parts):
    depth, rows, width = cells.shape
    nodes = plane.shape[1]
    tiles = width // LANES
    return pl.pallas_call(
        warp_kernel,
        in_specs=[pl.BlockSpec(memory_space=pltpu.HBM if n == 2 else pltpu.VMEM) for n in range(10)],
        out_specs=[pl.BlockSpec(memory_space=pltpu.HBM if n == 0 else pltpu.VMEM) for n in range(3)],
        out_shape=[
            jax.ShapeDtypeStruct(cells.shape, bf16),
            jax.ShapeDtypeStruct((parts, 4 * RANK // parts, width), f32),
            jax.ShapeDtypeStruct((nodes, 4 * RANK), f32),
        ],
        scratch_shapes=[
            *[pltpu.VMEM((3 * KNOT * tiles * (rows + 2 * TOP), LANES), f32)] * 3,
            pltpu.VMEM(shift.shape, bf16),
            pltpu.VMEM(cells.shape, bf16),
            pltpu.VMEM((2, rows, LANES), f32),
            pltpu.VMEM((2, tiles, nodes, LANES), f32),
            pltpu.VMEM((2, tiles, 8 * nodes, LANES), f32),
            pltpu.VMEM((8, LANES), f32),
            pltpu.VMEM((KNOT, 8, LANES), f32),
            pltpu.SemaphoreType.DMA((3, depth // KNOT)),
            pltpu.SemaphoreType.DMA((depth // KNOT,)),
        ],
        compiler_params=plain_params(),
        cost_estimate=pl.CostEstimate(flops=60 * cells.size, bytes_accessed=12 * cells.size, transcendentals=0),
        name="warp",
    )(cells, image, shift, left, right, low, high, squared, plane, depth_factors)


def gather_kernel(depth_ref, *refs):
    depth_out, plane_out = refs[-2:]
    total = jnp.sum(depth_ref[...], axis=0)
    found = [ref[...] for ref in refs[:-2]]
    while len(found) > 1:
        half = len(found) // 2
        found = [found[k] + found[k + half] for k in range(half)]
    planes = found[0]
    plane_out[...] = planes
    cells = planes.shape[0]
    share, width = total.shape[0] // 4, total.shape[1]
    row = lax.broadcasted_iota(jnp.int32, total.shape, 0)
    lane = lax.broadcasted_iota(jnp.int32, total.shape, 1)
    partial = planes[cells - 1, 4 * RANK - 1]
    total = jnp.where((row >= 3 * share) & (lane >= width // 2), partial, total)
    for p in range(depth_out.shape[0]):
        depth_out[p] = total


def step_kernel(full_z, node_count, depth_ref, plane_ref, depth_out, plane_out):
    parts, share, width = depth_ref.shape[0], depth_ref.shape[1] // 4, depth_ref.shape[2]
    energy = depth_ref[0, 3 * share, width - 1]
    for p in range(1, parts):
        energy = energy + depth_ref[p, 3 * share, width - 1]
    lam_depth = damping * energy / full_z
    lam_plane = damping * RANK * energy / node_count
    for p in range(parts):
        got = depth_ref[p]
        levels = got[3 * share :, 0 : width // 2]
        levels = jnp.concatenate([levels, levels], axis=1)
        rows = slice(p * share, (p + 1) * share)
        depth_out[0, rows, :] = got[0:share] / (got[2 * share : 3 * share] + lam_depth + epsilon)
        depth_out[1, rows, :] = got[share : 2 * share] / (levels + lam_depth + epsilon)
    planes = plane_ref[...]
    plane_out[0] = planes[:, 0:RANK] / (planes[:, 2 * RANK : 3 * RANK] + lam_plane + epsilon)
    plane_out[1] = planes[:, RANK : 2 * RANK] / (planes[0:1, 3 * RANK :] + lam_plane + epsilon)


def local(image, deformed, displacement, plane_factors, depth_factors):
    n_gy, n_gz = lax.axis_size("gy"), lax.axis_size("gz")
    nodes_x, nodes_y = plane_factors.shape[2:]
    plane = jnp.transpose(plane_factors, (0, 2, 3, 1)).reshape(2, nodes_x * nodes_y, RANK)
    first, last = end_columns(deformed)
    right = shifted(first, "gz", True)
    left = shifted(last, "gz", False)
    sums, low, high = squares(image, deformed)
    low, high = packed_rows(left, right, low, high)
    above = shifted(low, "gy", True)
    below = shifted(high, "gy", False)
    residual, depth_terms, plane_terms = warp(
        deformed, image, displacement, left, right, below, above, sums, plane, depth_factors, n_gy
    )
    others = [
        lax.ppermute(plane_terms, "gz", [(i, (i + hop) % n_gz) for i in range(n_gz)]) for hop in range(1, n_gz)
    ]
    depth_terms = lax.all_to_all(depth_terms, "gy", 0, 0)
    depth_terms, plane_terms = pl.pallas_call(
        gather_kernel,
        out_shape=[
            jax.ShapeDtypeStruct(depth_terms.shape, f32),
            jax.ShapeDtypeStruct(plane_terms.shape, f32),
        ],
        compiler_params=plain_params(),
        name="gather",
    )(depth_terms, plane_terms, *others)
    depth_terms = lax.all_to_all(depth_terms, "gy", 0, 0)
    width = depth_factors.shape[2]
    step_depth, step_plane = pl.pallas_call(
        functools.partial(step_kernel, width * n_gz, nodes_x * nodes_y * n_gy),
        out_shape=[
            jax.ShapeDtypeStruct(depth_factors.shape, f32),
            jax.ShapeDtypeStruct(plane.shape, f32),
        ],
        compiler_params=plain_params(),
        name="steps",
    )(depth_terms, plane_terms)
    step_plane = jnp.transpose(step_plane.reshape(2, nodes_x, nodes_y, RANK), (0, 3, 1, 2))
    return residual, step_plane, step_depth


def solution(mesh):
    placed = (
        P(None, "gy", "gz"),
        P(None, "gy", "gz"),
        P(None, None, "gy", "gz"),
        P(None, None, None, "gy"),
        P(None, None, "gz"),
    )
    return jax.shard_map(
        local,
        mesh=mesh,
        in_specs=placed,
        out_specs=(P(None, "gy", "gz"), P(None, None, None, "gy"), P(None, None, "gz")),
        check_vma=False,
    )
```

```python
import functools

import jax
import jax.numpy as jnp
from jax import lax
from jax.experimental import pallas as pl
from jax.experimental.pallas import tpu as pltpu
from jax.sharding import PartitionSpec as P

RANK = 32
KNOT = 8
LANES = 128
TOP = 8

epsilon = 1e-06
damping = 0.01
highest = lax.Precision.HIGHEST
f32 = jnp.float32
bf16 = jnp.bfloat16


def dot(left, right, dims):
    return lax.dot_general(left, right, ((dims[0], dims[1]), ((), ())), precision=highest, preferred_element_type=f32)


def split_dot(left, right, dim):
    left_high, right_high = left.astype(bf16), right.astype(bf16)
    left_low = (left - left_high.astype(f32)).astype(bf16)
    right_low = (right - right_high.astype(f32)).astype(bf16)
    left = jnp.concatenate([left_high, left_high, left_low], axis=dim)
    right = jnp.concatenate([right_high, right_low, right_high], axis=dim)
    return lax.dot_general(left, right, (((dim,), (dim,)), ((), ())), preferred_element_type=f32)


def joined(ref):
    return jnp.concatenate([ref[tile] for tile in range(ref.shape[0])], axis=1)


def grid_params():
    return pltpu.CompilerParams(dimension_semantics=("arbitrary",), vmem_limit_bytes=40000000)


def plain_params():
    return pltpu.CompilerParams(vmem_limit_bytes=32000000)


def columns_kernel(cells_ref, first_ref, last_ref):
    depth, rows, width = cells_ref.shape
    lane = lax.broadcasted_iota(jnp.int32, (rows, LANES), 1)
    first = jnp.zeros((rows, LANES), f32)
    last = jnp.zeros((rows, LANES), f32)
    for x in range(depth):
        near = cells_ref[x, :, 0:LANES].astype(f32)
        far = cells_ref[x, :, width - LANES : width].astype(f32)
        first = jnp.where(lane == x, pltpu.roll(near, x, 1), first)
        last = jnp.where(lane == x, pltpu.roll(far, (x + 1) % LANES, 1), last)
    first_ref[...] = first.astype(bf16)
    last_ref[...] = last.astype(bf16)


def end_columns(cells):
    rows = cells.shape[1]
    return pl.pallas_call(
        columns_kernel,
        out_shape=[jax.ShapeDtypeStruct((rows, LANES), bf16)] * 2,
        compiler_params=plain_params(),
        name="columns",
    )(cells)


def rows_kernel(left_ref, right_ref, low_ref, high_ref, low_out, high_out):
    depth, width = low_ref.shape
    rows = left_ref.shape[0]
    lane = lax.broadcasted_iota(jnp.int32, (depth, LANES), 1)
    pad = jnp.zeros((LANES - rows, LANES), f32)
    left = jnp.transpose(jnp.concatenate([left_ref[...].astype(f32), pad], axis=0))[0:depth]
    right = jnp.transpose(jnp.concatenate([right_ref[...].astype(f32), pad], axis=0))[0:depth]
    for row, body, out in ((0, low_ref, low_out), (rows - 1, high_ref, high_out)):
        after = pltpu.roll(right, (LANES - row) % LANES, 1)
        before = pltpu.roll(left, LANES - 1 - row, 1)
        out[:, 0:width] = body[...].astype(bf16)
        out[:, width : width + LANES] = jnp.where(lane == 0, after, before).astype(bf16)


def packed_rows(left, right, low, high):
    depth, width = low.shape
    return pl.pallas_call(
        rows_kernel,
        out_shape=[jax.ShapeDtypeStruct((depth, width + LANES), bf16)] * 2,
        compiler_params=plain_params(),
        name="rows",
    )(left, right, low, high)


def shifted(part, axis, back):
    count = lax.axis_size(axis)
    if back:
        return lax.ppermute(part, axis, [(i + 1, i) for i in range(count - 1)])
    return lax.ppermute(part, axis, [(i, i + 1) for i in range(count - 1)])


def squares_kernel(image_ref, cells_ref, sums, low_ref, high_ref):
    depth, rows, width = image_ref.shape
    tiles = width // LANES

    def one(t, carry):
        block, tile = t // tiles, t % tiles
        at = pl.multiple_of(tile * LANES, LANES)
        for pair in range(rows // 16):
            total = jnp.zeros((16, LANES), f32)
            for k in range(KNOT):
                values = image_ref[block * KNOT + k, 16 * pair : 16 * pair + 16, pl.ds(at, LANES)].astype(f32)
                total = total + values * values
            for half in range(2):
                row = block * (rows // KNOT) + 2 * pair + half
                sums[tile, pl.ds(row, 1), :] = jnp.sum(total[8 * half : 8 * half + 8], axis=0, keepdims=True)
        return carry

    lax.fori_loop(0, depth // KNOT * tiles, one, 0)

    def ends(block, carry):
        x = pl.multiple_of(block * KNOT, KNOT)
        low = [cells_ref[x + k, 0:16, :].astype(f32)[0:1] for k in range(KNOT)]
        high = [cells_ref[x + k, rows - 16 : rows, :].astype(f32)[15:16] for k in range(KNOT)]
        low_ref[pl.ds(x, KNOT), :] = jnp.concatenate(low, axis=0)
        high_ref[pl.ds(x, KNOT), :] = jnp.concatenate(high, axis=0)
        return carry

    lax.fori_loop(0, depth // KNOT, ends, 0)


def squares(image, cells):
    depth, rows, width = image.shape
    return pl.pallas_call(
        squares_kernel,
        out_shape=[
            jax.ShapeDtypeStruct((width // LANES, depth * rows // KNOT**2, LANES), f32),
            jax.ShapeDtypeStruct((depth, width), f32),
            jax.ShapeDtypeStruct((depth, width), f32),
        ],
        compiler_params=plain_params(),
        cost_estimate=pl.CostEstimate(flops=3 * image.size, bytes_accessed=2 * image.size, transcendentals=0),
        name="squares",
    )(image, cells)


def terms_kernel(sums, plane_ref, depth_ref, field_ref, diag_depth_ref, diag_plane_ref):
    tiles = sums.shape[0]
    for k in range(2):
        field = dot(plane_ref[k], depth_ref[k], ((1,), (0,)))
        for tile in range(tiles):
            field_ref[k, tile] = field[:, tile * LANES : (tile + 1) * LANES]
    squared = joined(sums)
    cells = jnp.full(squared.shape, float(KNOT * KNOT), f32)
    first, second = plane_ref[0], plane_ref[1]
    diag_depth_ref[0] = dot(first * first, squared, ((0,), (0,)))
    diag_depth_ref[1] = dot(second * second, cells, ((0,), (0,)))
    first, second = depth_ref[0], depth_ref[1]
    diag_plane_ref[0] = dot(squared, first * first, ((1,), (1,)))
    diag_plane_ref[1] = dot(cells, second * second, ((1,), (1,)))


def terms(sums, plane, depth_factors):
    nodes, width = plane.shape[1], depth_factors.shape[2]
    return pl.pallas_call(
        terms_kernel,
        out_shape=[
            jax.ShapeDtypeStruct((2, width // LANES, nodes, LANES), f32),
            jax.ShapeDtypeStruct((2, RANK, width), f32),
            jax.ShapeDtypeStruct((2, nodes, RANK), f32),
        ],
        compiler_params=plain_params(),
        cost_estimate=pl.CostEstimate(flops=40 * nodes * RANK * width, bytes_accessed=1 << 20, transcendentals=0),
        name="terms",
    )(sums, plane, depth_factors)


def warp_kernel(
    cells_ref, image_ref, shift_ref, left_ref, right_ref, low_ref, high_ref, field, plane_ref, depth_ref,
    diag_depth_ref, diag_plane_ref,
    residual_ref, depth_out, plane_out,
    ahead_ref, here_ref, behind_ref, columns, rims, blocks, energy, held,
):
    step = pl.program_id(0)
    last = pl.num_programs(0) - 1
    planes, rows, width = cells_ref.shape
    nodes = rows // KNOT
    tiles = width // LANES
    window = (ahead_ref, here_ref, behind_ref)
    pitch = rows + 2 * TOP
    plane_rows = tiles * pitch
    block_rows = planes * plane_rows

    def differences(wide):
        ahead = pltpu.roll(wide, wide.shape[1] - 1, 1) - wide
        return ahead, wide, pltpu.roll(ahead, 1, 1)

    @pl.when(step == 0)
    def _():
        columns[0] = left_ref[...].astype(f32)
        columns[1] = right_ref[...].astype(f32)
        energy[...] = jnp.zeros_like(energy)
        for c in range(3):
            window[c][3 * block_rows - plane_rows : 3 * block_rows, :] = jnp.zeros((plane_rows, LANES), f32)

    @pl.when(step < last)
    def _():
        lane = lax.broadcasted_iota(jnp.int32, (16, LANES), 1)
        slot = (step % 3) * block_rows
        for side, source in enumerate((low_ref, high_ref)):
            moved = differences(source[...].astype(f32))
            for c in range(3):
                for tile in range(tiles):
                    rims[(side * 3 + c) * tiles + tile] = moved[c][:, tile * LANES : (tile + 1) * LANES]

        def one(k, carry):
            x = step * planes + k
            first = pl.multiple_of(slot + k * plane_rows, 8)
            raw = cells_ref[k]
            right, left = columns[1], columns[0]
            for group in range(rows // 16):
                mine = slice(16 * group, 16 * group + 16)
                after = pltpu.roll(right[mine], (LANES - x) % LANES, 1)
                before = pltpu.roll(left[mine], LANES - 1 - x, 1)
                beyond = jnp.where(lane == 0, after, before)
                moved = differences(jnp.concatenate([raw[mine].astype(f32), beyond], axis=1))
                for c in range(3):
                    for tile in range(tiles):
                        window[c][pl.ds(first + tile * pitch + TOP + 16 * group, 16), :] = moved[c][
                            :, tile * LANES : (tile + 1) * LANES
                        ]
            for side, row in enumerate((0, TOP + rows)):
                for c in range(3):
                    for tile in range(tiles):
                        rim = rims[(side * 3 + c) * tiles + tile, pl.ds(k, 1), :]
                        window[c][pl.ds(first + tile * pitch + row, 8), :] = jnp.broadcast_to(rim, (8, LANES))
            return carry

        lax.fori_loop(0, planes, one, 0)
    @pl.when(step == last)
    def _():
        first = pl.multiple_of((step % 3) * block_rows, 8)
        for c in range(3):
            window[c][pl.ds(first, plane_rows), :] = jnp.zeros((plane_rows, LANES), f32)

    @pl.when(step > 0)
    def _():
        mid = (step + 2) % 3
        first_rows = (
            jnp.where(mid == 0, 3, mid) * block_rows - plane_rows,
            mid * block_rows,
            jnp.where(mid == 2, 0, mid + 1) * block_rows,
        )

        def one(t, total):
            tile = t % tiles
            pair = t // tiles
            at = pl.multiple_of(tile * LANES, LANES)
            top = pl.multiple_of(pair * 16, 16)
            origins = [first + tile * pitch + top + TOP for first in first_rows]
            for half in range(2):
                node = (step - 1) * nodes + pair * 2 + half
                mine = slice(8 * half, 8 * half + 8)

                def taps(x):
                    part = 0 if x == 0 else 2 if x == planes + 1 else 1
                    plus = (x - 1) * plane_rows + 8 * half if part == 1 else 8 * half
                    return [
                        [window[c][pl.ds(origins[part] + (plus + b), 8), :] for c in range(3)] for b in (-1, 0, 1)
                    ]

                contrast = jnp.broadcast_to(field[0, tile, pl.ds(node, 1), :], (8, LANES))
                brightness = jnp.broadcast_to(field[1, tile, pl.ds(node, 1), :], (8, LANES))
                by_image = jnp.zeros((8, LANES), f32)
                plain = jnp.zeros((8, LANES), f32)
                before, here = taps(0), taps(1)
                for k in range(planes):
                    after = taps(k + 2)
                    place = (k, pl.ds(top, 16), pl.ds(at, LANES))
                    sx, sy, sz = (shift_ref[(axis,) + place].astype(f32)[mine] for axis in range(3))
                    image = image_ref[place].astype(f32)[mine]
                    px, py, pz = sx > 0, sy > 0, sz > 0
                    ax, ay = jnp.abs(sx), jnp.abs(sy)

                    def sides(c):
                        far = [jnp.where(px, after[b][c], before[b][c]) for b in range(3)]
                        near = [here[b][c] for b in range(3)]
                        return [(v[1], jnp.where(py, v[2], v[0])) for v in (near, far)]

                    ahead, middle, behind = sides(0), sides(1), sides(2)
                    lines = []
                    for b in range(2):
                        near, far = (middle[v][b] + sz * jnp.where(pz, ahead[v][b], behind[v][b]) for v in range(2))
                        lines.append(near + ax * (far - near))
                    warped = lines[0] + ay * (lines[1] - lines[0])
                    misfit = warped - contrast * image - brightness
                    if half == 0:
                        held[k] = misfit
                    else:
                        residual_ref[place] = jnp.concatenate([held[k], misfit], axis=0).astype(bf16)
                    by_image = by_image + misfit * image
                    plain = plain + misfit
                    total = total + misfit * misfit
                    before, here = here, after
                for k, value in ((0, by_image), (1, plain)):
                    blocks[k, tile, pl.ds(node, 1), :] = jnp.sum(value, axis=0, keepdims=True)
            return total

        energy[...] = lax.fori_loop(0, (rows // 16) * tiles, one, energy[...])

    @pl.when(step == last)
    def _():
        parts = depth_out.shape[0]
        share = RANK // parts
        sums = [joined(blocks.at[k]) for k in range(2)]
        kinds = [split_dot(plane_ref[k], sums[k], 0) for k in range(2)]
        kinds = kinds + [diag_depth_ref[0], diag_depth_ref[1]]
        for p in range(parts):
            for k in range(4):
                depth_out[p, k * share : (k + 1) * share, :] = kinds[k][p * share : (p + 1) * share]
        local = jnp.sum(energy[...])
        kinds = [split_dot(sums[k], depth_ref[k], 1) for k in range(2)]
        kinds = kinds + [diag_plane_ref[0], diag_plane_ref[1]]
        for k in range(4):
            plane_out[:, k * RANK : (k + 1) * RANK] = kinds[k]
        count = plane_out.shape[0]
        plane_out[count // 2 :, 3 * RANK :] = jnp.full((count // 2, RANK), local, f32)


def warp(cells, image, shift, left, right, low, high, field, plane, depth_factors, diag_depth, diag_plane, parts):
    depth, rows, width = cells.shape
    nodes = plane.shape[1]
    tiles = width // LANES
    count = depth // KNOT
    behind = lambda i: (jnp.maximum(i - 1, 0), 0, 0)
    ahead = lambda i: (jnp.minimum(i, count - 1), 0, 0)
    flat = lambda i: (0, 0)
    whole = lambda i: (0, 0, 0)
    return pl.pallas_call(
        warp_kernel,
        grid=(count + 1,),
        in_specs=[
            pl.BlockSpec((KNOT, rows, width), ahead),
            pl.BlockSpec((KNOT, rows, width), behind),
            pl.BlockSpec((3, KNOT, rows, width), lambda i: (0, jnp.maximum(i - 1, 0), 0, 0)),
            pl.BlockSpec(left.shape, flat),
            pl.BlockSpec(right.shape, flat),
            pl.BlockSpec((KNOT, low.shape[1]), lambda i: (jnp.minimum(i, count - 1), 0)),
            pl.BlockSpec((KNOT, high.shape[1]), lambda i: (jnp.minimum(i, count - 1), 0)),
            pl.BlockSpec(field.shape, lambda i: (0, 0, 0, 0)),
            pl.BlockSpec(plane.shape, whole),
            pl.BlockSpec(depth_factors.shape, whole),
            pl.BlockSpec(diag_depth.shape, whole),
            pl.BlockSpec(diag_plane.shape, whole),
        ],
        out_specs=[
            pl.BlockSpec((KNOT, rows, width), behind),
            pl.BlockSpec((parts, 4 * RANK // parts, width), whole),
            pl.BlockSpec((nodes, 4 * RANK), flat),
        ],
        out_shape=[
            jax.ShapeDtypeStruct(cells.shape, bf16),
            jax.ShapeDtypeStruct((parts, 4 * RANK // parts, width), f32),
            jax.ShapeDtypeStruct((nodes, 4 * RANK), f32),
        ],
        scratch_shapes=[
            *[pltpu.VMEM((3 * KNOT * tiles * (rows + 2 * TOP), LANES), f32)] * 3,
            pltpu.VMEM((2, rows, LANES), f32),
            pltpu.VMEM((6 * tiles, KNOT, LANES), f32),
            pltpu.VMEM((2, tiles, nodes, LANES), f32),
            pltpu.VMEM((8, LANES), f32),
            pltpu.VMEM((KNOT, 8, LANES), f32),
        ],
        compiler_params=grid_params(),
        cost_estimate=pl.CostEstimate(flops=60 * cells.size, bytes_accessed=12 * cells.size, transcendentals=0),
        name="warp",
    )(cells, image, shift, left, right, low, high, field, plane, depth_factors, diag_depth, diag_plane)


def gather_kernel(depth_ref, *refs):
    depth_out, plane_out = refs[-2:]
    total = jnp.sum(depth_ref[...], axis=0)
    found = [ref[...] for ref in refs[:-2]]
    while len(found) > 1:
        half = len(found) // 2
        found = [found[k] + found[k + half] for k in range(half)]
    planes = found[0]
    plane_out[...] = planes
    cells = planes.shape[0]
    share, width = total.shape[0] // 4, total.shape[1]
    row = lax.broadcasted_iota(jnp.int32, total.shape, 0)
    lane = lax.broadcasted_iota(jnp.int32, total.shape, 1)
    partial = planes[cells - 1, 4 * RANK - 1]
    total = jnp.where((row >= 3 * share) & (lane >= width // 2), partial, total)
    for p in range(depth_out.shape[0]):
        depth_out[p] = total


def step_kernel(full_z, node_count, depth_ref, plane_ref, depth_out, plane_out):
    parts, share, width = depth_ref.shape[0], depth_ref.shape[1] // 4, depth_ref.shape[2]
    energy = depth_ref[0, 3 * share, width - 1]
    for p in range(1, parts):
        energy = energy + depth_ref[p, 3 * share, width - 1]
    lam_depth = damping * energy / full_z
    lam_plane = damping * RANK * energy / node_count
    for p in range(parts):
        got = depth_ref[p]
        levels = got[3 * share :, 0 : width // 2]
        levels = jnp.concatenate([levels, levels], axis=1)
        rows = slice(p * share, (p + 1) * share)
        depth_out[0, rows, :] = got[0:share] / (got[2 * share : 3 * share] + lam_depth + epsilon)
        depth_out[1, rows, :] = got[share : 2 * share] / (levels + lam_depth + epsilon)
    planes = plane_ref[...]
    plane_out[0] = planes[:, 0:RANK] / (planes[:, 2 * RANK : 3 * RANK] + lam_plane + epsilon)
    plane_out[1] = planes[:, RANK : 2 * RANK] / (planes[0:1, 3 * RANK :] + lam_plane + epsilon)


def local(image, deformed, displacement, plane_factors, depth_factors):
    n_gy, n_gz = lax.axis_size("gy"), lax.axis_size("gz")
    nodes_x, nodes_y = plane_factors.shape[2:]
    plane = jnp.transpose(plane_factors, (0, 2, 3, 1)).reshape(2, nodes_x * nodes_y, RANK)
    first, last = end_columns(deformed)
    right = shifted(first, "gz", True)
    left = shifted(last, "gz", False)
    sums, low, high = squares(image, deformed)
    low, high = packed_rows(left, right, low, high)
    above = shifted(low, "gy", True)
    below = shifted(high, "gy", False)
    field, diag_depth, diag_plane = terms(sums, plane, depth_factors)
    residual, depth_terms, plane_terms = warp(
        deformed, image, displacement, left, right, below, above, field, plane, depth_factors, diag_depth, diag_plane,
        n_gy,
    )
    others = [
        lax.ppermute(plane_terms, "gz", [(i, (i + hop) % n_gz) for i in range(n_gz)]) for hop in range(1, n_gz)
    ]
    depth_terms = lax.all_to_all(depth_terms, "gy", 0, 0)
    depth_terms, plane_terms = pl.pallas_call(
        gather_kernel,
        out_shape=[
            jax.ShapeDtypeStruct(depth_terms.shape, f32),
            jax.ShapeDtypeStruct(plane_terms.shape, f32),
        ],
        compiler_params=plain_params(),
        name="gather",
    )(depth_terms, plane_terms, *others)
    depth_terms = lax.all_to_all(depth_terms, "gy", 0, 0)
    width = depth_factors.shape[2]
    step_depth, step_plane = pl.pallas_call(
        functools.partial(step_kernel, width * n_gz, nodes_x * nodes_y * n_gy),
        out_shape=[
            jax.ShapeDtypeStruct(depth_factors.shape, f32),
            jax.ShapeDtypeStruct(plane.shape, f32),
        ],
        compiler_params=plain_params(),
        name="steps",
    )(depth_terms, plane_terms)
    step_plane = jnp.transpose(step_plane.reshape(2, nodes_x, nodes_y, RANK), (0, 3, 1, 2))
    return residual, step_plane, step_depth


def solution(mesh):
    placed = (
        P(None, "gy", "gz"),
        P(None, "gy", "gz"),
        P(None, None, "gy", "gz"),
        P(None, None, None, "gy"),
        P(None, None, "gz"),
    )
    return jax.shard_map(
        local,
        mesh=mesh,
        in_specs=placed,
        out_specs=(P(None, "gy", "gz"), P(None, None, None, "gy"), P(None, None, "gz")),
        check_vma=False,
    )
```

```python
import functools

import jax
import jax.numpy as jnp
from jax import lax
from jax.experimental import pallas as pl
from jax.experimental.pallas import tpu as pltpu
from jax.sharding import PartitionSpec as P

RANK = 32
KNOT = 8
LANES = 128
TOP = 8

epsilon = 1e-06
damping = 0.01
highest = lax.Precision.HIGHEST
f32 = jnp.float32
bf16 = jnp.bfloat16


def dot(left, right, dims):
    return lax.dot_general(left, right, ((dims[0], dims[1]), ((), ())), precision=highest, preferred_element_type=f32)


def split_dot(left, right, dim):
    left_high, right_high = left.astype(bf16), right.astype(bf16)
    left_low = (left - left_high.astype(f32)).astype(bf16)
    right_low = (right - right_high.astype(f32)).astype(bf16)
    left = jnp.concatenate([left_high, left_high, left_low], axis=dim)
    right = jnp.concatenate([right_high, right_low, right_high], axis=dim)
    return lax.dot_general(left, right, (((dim,), (dim,)), ((), ())), preferred_element_type=f32)


def joined(ref):
    return jnp.concatenate([ref[tile] for tile in range(ref.shape[0])], axis=1)


def grid_params():
    return pltpu.CompilerParams(dimension_semantics=("arbitrary",), vmem_limit_bytes=40000000)


def plain_params():
    return pltpu.CompilerParams(vmem_limit_bytes=32000000)


def columns_kernel(cells_ref, first_ref, last_ref):
    depth, rows, width = cells_ref.shape
    lane = lax.broadcasted_iota(jnp.int32, (rows, LANES), 1)
    first = jnp.zeros((rows, LANES), f32)
    last = jnp.zeros((rows, LANES), f32)
    for x in range(depth):
        near = cells_ref[x, :, 0:LANES].astype(f32)
        far = cells_ref[x, :, width - LANES : width].astype(f32)
        first = jnp.where(lane == x, pltpu.roll(near, x, 1), first)
        last = jnp.where(lane == x, pltpu.roll(far, (x + 1) % LANES, 1), last)
    first_ref[...] = first.astype(bf16)
    last_ref[...] = last.astype(bf16)


def end_columns(cells):
    rows = cells.shape[1]
    return pl.pallas_call(
        columns_kernel,
        out_shape=[jax.ShapeDtypeStruct((rows, LANES), bf16)] * 2,
        compiler_params=plain_params(),
        name="columns",
    )(cells)


def rows_kernel(left_ref, right_ref, low_ref, high_ref, low_out, high_out):
    depth, width = low_ref.shape
    rows = left_ref.shape[0]
    lane = lax.broadcasted_iota(jnp.int32, (depth, LANES), 1)
    pad = jnp.zeros((LANES - rows, LANES), f32)
    left = jnp.transpose(jnp.concatenate([left_ref[...].astype(f32), pad], axis=0))[0:depth]
    right = jnp.transpose(jnp.concatenate([right_ref[...].astype(f32), pad], axis=0))[0:depth]
    for row, body, out in ((0, low_ref, low_out), (rows - 1, high_ref, high_out)):
        after = pltpu.roll(right, (LANES - row) % LANES, 1)
        before = pltpu.roll(left, LANES - 1 - row, 1)
        out[:, 0:width] = body[...].astype(bf16)
        out[:, width : width + LANES] = jnp.where(lane == 0, after, before).astype(bf16)


def packed_rows(left, right, low, high):
    depth, width = low.shape
    return pl.pallas_call(
        rows_kernel,
        out_shape=[jax.ShapeDtypeStruct((depth, width + LANES), bf16)] * 2,
        compiler_params=plain_params(),
        name="rows",
    )(left, right, low, high)


def shifted(part, axis, back):
    count = lax.axis_size(axis)
    if back:
        return lax.ppermute(part, axis, [(i + 1, i) for i in range(count - 1)])
    return lax.ppermute(part, axis, [(i, i + 1) for i in range(count - 1)])


def squares_kernel(image_ref, cells_ref, sums, low_ref, high_ref):
    depth, rows, width = image_ref.shape
    tiles = width // LANES

    def one(t, carry):
        block, tile = t // tiles, t % tiles
        at = pl.multiple_of(tile * LANES, LANES)
        for pair in range(rows // 16):
            total = jnp.zeros((16, LANES), f32)
            for k in range(KNOT):
                values = image_ref[block * KNOT + k, 16 * pair : 16 * pair + 16, pl.ds(at, LANES)].astype(f32)
                total = total + values * values
            for half in range(2):
                row = block * (rows // KNOT) + 2 * pair + half
                sums[tile, pl.ds(row, 1), :] = jnp.sum(total[8 * half : 8 * half + 8], axis=0, keepdims=True)
        return carry

    lax.fori_loop(0, depth // KNOT * tiles, one, 0)

    def ends(block, carry):
        x = pl.multiple_of(block * KNOT, KNOT)
        low = [cells_ref[x + k, 0:16, :].astype(f32)[0:1] for k in range(KNOT)]
        high = [cells_ref[x + k, rows - 16 : rows, :].astype(f32)[15:16] for k in range(KNOT)]
        low_ref[pl.ds(x, KNOT), :] = jnp.concatenate(low, axis=0)
        high_ref[pl.ds(x, KNOT), :] = jnp.concatenate(high, axis=0)
        return carry

    lax.fori_loop(0, depth // KNOT, ends, 0)


def squares(image, cells):
    depth, rows, width = image.shape
    return pl.pallas_call(
        squares_kernel,
        out_shape=[
            jax.ShapeDtypeStruct((width // LANES, depth * rows // KNOT**2, LANES), f32),
            jax.ShapeDtypeStruct((depth, width), f32),
            jax.ShapeDtypeStruct((depth, width), f32),
        ],
        compiler_params=plain_params(),
        cost_estimate=pl.CostEstimate(flops=3 * image.size, bytes_accessed=2 * image.size, transcendentals=0),
        name="squares",
    )(image, cells)


def terms_kernel(sums, plane_ref, depth_ref, field_ref, diag_depth_ref, diag_plane_ref):
    tiles = sums.shape[0]
    for k in range(2):
        field = dot(plane_ref[k], depth_ref[k], ((1,), (0,)))
        for tile in range(tiles):
            field_ref[k, tile] = field[:, tile * LANES : (tile + 1) * LANES]
    squared = joined(sums)
    cells = jnp.full(squared.shape, float(KNOT * KNOT), f32)
    first, second = plane_ref[0], plane_ref[1]
    diag_depth_ref[0] = dot(first * first, squared, ((0,), (0,)))
    diag_depth_ref[1] = dot(second * second, cells, ((0,), (0,)))
    first, second = depth_ref[0], depth_ref[1]
    diag_plane_ref[0] = dot(squared, first * first, ((1,), (1,)))
    diag_plane_ref[1] = dot(cells, second * second, ((1,), (1,)))


def terms(sums, plane, depth_factors):
    nodes, width = plane.shape[1], depth_factors.shape[2]
    return pl.pallas_call(
        terms_kernel,
        out_shape=[
            jax.ShapeDtypeStruct((2, width // LANES, nodes, LANES), f32),
            jax.ShapeDtypeStruct((2, RANK, width), f32),
            jax.ShapeDtypeStruct((2, nodes, RANK), f32),
        ],
        compiler_params=plain_params(),
        cost_estimate=pl.CostEstimate(flops=40 * nodes * RANK * width, bytes_accessed=1 << 20, transcendentals=0),
        name="terms",
    )(sums, plane, depth_factors)


def warp_kernel(
    cells_ref, image_ref, shift_ref, left_ref, right_ref, low_ref, high_ref, field, plane_ref, depth_ref,
    diag_depth_ref, diag_plane_ref,
    residual_ref, depth_out, plane_out,
    ahead_ref, here_ref, behind_ref, columns, rims, blocks, energy, held,
):
    step = pl.program_id(0)
    last = pl.num_programs(0) - 1
    planes, rows, width = cells_ref.shape
    nodes = rows // KNOT
    tiles = width // LANES
    window = (ahead_ref, here_ref, behind_ref)
    pitch = rows + 2 * TOP
    plane_rows = tiles * pitch
    block_rows = planes * plane_rows

    def neighbours(wide):
        return pltpu.roll(wide, wide.shape[1] - 1, 1), wide, pltpu.roll(wide, 1, 1)

    @pl.when(step == 0)
    def _():
        columns[0] = left_ref[...].astype(f32)
        columns[1] = right_ref[...].astype(f32)
        energy[...] = jnp.zeros_like(energy)
        for c in range(3):
            window[c][3 * block_rows - plane_rows : 3 * block_rows, :] = jnp.zeros((plane_rows, LANES), f32)

    @pl.when(step < last)
    def _():
        lane = lax.broadcasted_iota(jnp.int32, (16, LANES), 1)
        slot = (step % 3) * block_rows
        for side, source in enumerate((low_ref, high_ref)):
            moved = neighbours(source[...].astype(f32))
            for c in range(3):
                for tile in range(tiles):
                    rims[(side * 3 + c) * tiles + tile] = moved[c][:, tile * LANES : (tile + 1) * LANES]

        def one(k, carry):
            x = step * planes + k
            first = pl.multiple_of(slot + k * plane_rows, 8)
            raw = cells_ref[k]
            right, left = columns[1], columns[0]
            for group in range(rows // 16):
                mine = slice(16 * group, 16 * group + 16)
                after = pltpu.roll(right[mine], (LANES - x) % LANES, 1)
                before = pltpu.roll(left[mine], LANES - 1 - x, 1)
                beyond = jnp.where(lane == 0, after, before)
                moved = neighbours(jnp.concatenate([raw[mine].astype(f32), beyond], axis=1))
                for c in range(3):
                    for tile in range(tiles):
                        window[c][pl.ds(first + tile * pitch + TOP + 16 * group, 16), :] = moved[c][
                            :, tile * LANES : (tile + 1) * LANES
                        ]
            for side, row in enumerate((0, TOP + rows)):
                for c in range(3):
                    for tile in range(tiles):
                        rim = rims[(side * 3 + c) * tiles + tile, pl.ds(k, 1), :]
                        window[c][pl.ds(first + tile * pitch + row, 8), :] = jnp.broadcast_to(rim, (8, LANES))
            return carry

        lax.fori_loop(0, planes, one, 0)
    @pl.when(step == last)
    def _():
        first = pl.multiple_of((step % 3) * block_rows, 8)
        for c in range(3):
            window[c][pl.ds(first, plane_rows), :] = jnp.zeros((plane_rows, LANES), f32)

    @pl.when(step > 0)
    def _():
        mid = (step + 2) % 3
        first_rows = (
            jnp.where(mid == 0, 3, mid) * block_rows - plane_rows,
            mid * block_rows,
            jnp.where(mid == 2, 0, mid + 1) * block_rows,
        )

        def one(t, total):
            tile = t % tiles
            pair = t // tiles
            at = pl.multiple_of(tile * LANES, LANES)
            top = pl.multiple_of(pair * 16, 16)
            origins = [first + tile * pitch + top + TOP for first in first_rows]
            for half in range(2):
                node = (step - 1) * nodes + pair * 2 + half
                mine = slice(8 * half, 8 * half + 8)

                def taps(x):
                    part = 0 if x == 0 else 2 if x == planes + 1 else 1
                    plus = (x - 1) * plane_rows + 8 * half if part == 1 else 8 * half
                    return [
                        [window[c][pl.ds(origins[part] + (plus + b), 8), :] for c in range(3)] for b in (-1, 0, 1)
                    ]

                contrast = jnp.broadcast_to(field[0, tile, pl.ds(node, 1), :], (8, LANES))
                brightness = jnp.broadcast_to(field[1, tile, pl.ds(node, 1), :], (8, LANES))
                by_image = jnp.zeros((8, LANES), f32)
                plain = jnp.zeros((8, LANES), f32)
                before, here = taps(0), taps(1)
                for k in range(planes):
                    after = taps(k + 2)
                    place = (k, pl.ds(top, 16), pl.ds(at, LANES))
                    sx, sy, sz = (shift_ref[(axis,) + place].astype(f32)[mine] for axis in range(3))
                    image = image_ref[place].astype(f32)[mine]
                    px, py, pz = sx > 0, sy > 0, sz > 0
                    ax, ay = jnp.abs(sx), jnp.abs(sy)

                    def sides(c):
                        far = [jnp.where(px, after[b][c], before[b][c]) for b in range(3)]
                        near = [here[b][c] for b in range(3)]
                        return [(v[1], jnp.where(py, v[2], v[0])) for v in (near, far)]

                    ahead, middle, behind = sides(0), sides(1), sides(2)
                    lines = []
                    for b in range(2):
                        ends = [(middle[v][b], jnp.where(pz, ahead[v][b], behind[v][b])) for v in range(2)]
                        near, far = ends
                        lines.append([near[c] + ax * (far[c] - near[c]) for c in range(2)])
                    flat = [lines[0][c] + ay * (lines[1][c] - lines[0][c]) for c in range(2)]
                    warped = flat[0] + jnp.abs(sz) * (flat[1] - flat[0])
                    misfit = warped - contrast * image - brightness
                    if half == 0:
                        held[k] = misfit
                    else:
                        residual_ref[place] = jnp.concatenate([held[k], misfit], axis=0).astype(bf16)
                    by_image = by_image + misfit * image
                    plain = plain + misfit
                    total = total + misfit * misfit
                    before, here = here, after
                for k, value in ((0, by_image), (1, plain)):
                    blocks[k, tile, pl.ds(node, 1), :] = jnp.sum(value, axis=0, keepdims=True)
            return total

        energy[...] = lax.fori_loop(0, (rows // 16) * tiles, one, energy[...])

    @pl.when(step == last)
    def _():
        parts = depth_out.shape[0]
        share = RANK // parts
        sums = [joined(blocks.at[k]) for k in range(2)]
        kinds = [split_dot(plane_ref[k], sums[k], 0) for k in range(2)]
        kinds = kinds + [diag_depth_ref[0], diag_depth_ref[1]]
        for p in range(parts):
            for k in range(4):
                depth_out[p, k * share : (k + 1) * share, :] = kinds[k][p * share : (p + 1) * share]
        local = jnp.sum(energy[...])
        kinds = [split_dot(sums[k], depth_ref[k], 1) for k in range(2)]
        kinds = kinds + [diag_plane_ref[0], diag_plane_ref[1]]
        for k in range(4):
            plane_out[:, k * RANK : (k + 1) * RANK] = kinds[k]
        count = plane_out.shape[0]
        plane_out[count // 2 :, 3 * RANK :] = jnp.full((count // 2, RANK), local, f32)


def warp(cells, image, shift, left, right, low, high, field, plane, depth_factors, diag_depth, diag_plane, parts):
    depth, rows, width = cells.shape
    nodes = plane.shape[1]
    tiles = width // LANES
    count = depth // KNOT
    behind = lambda i: (jnp.maximum(i - 1, 0), 0, 0)
    ahead = lambda i: (jnp.minimum(i, count - 1), 0, 0)
    flat = lambda i: (0, 0)
    whole = lambda i: (0, 0, 0)
    return pl.pallas_call(
        warp_kernel,
        grid=(count + 1,),
        in_specs=[
            pl.BlockSpec((KNOT, rows, width), ahead),
            pl.BlockSpec((KNOT, rows, width), behind),
            pl.BlockSpec((3, KNOT, rows, width), lambda i: (0, jnp.maximum(i - 1, 0), 0, 0)),
            pl.BlockSpec(left.shape, flat),
            pl.BlockSpec(right.shape, flat),
            pl.BlockSpec((KNOT, low.shape[1]), lambda i: (jnp.minimum(i, count - 1), 0)),
            pl.BlockSpec((KNOT, high.shape[1]), lambda i: (jnp.minimum(i, count - 1), 0)),
            pl.BlockSpec(field.shape, lambda i: (0, 0, 0, 0)),
            pl.BlockSpec(plane.shape, whole),
            pl.BlockSpec(depth_factors.shape, whole),
            pl.BlockSpec(diag_depth.shape, whole),
            pl.BlockSpec(diag_plane.shape, whole),
        ],
        out_specs=[
            pl.BlockSpec((KNOT, rows, width), behind),
            pl.BlockSpec((parts, 4 * RANK // parts, width), whole),
            pl.BlockSpec((nodes, 4 * RANK), flat),
        ],
        out_shape=[
            jax.ShapeDtypeStruct(cells.shape, bf16),
            jax.ShapeDtypeStruct((parts, 4 * RANK // parts, width), f32),
            jax.ShapeDtypeStruct((nodes, 4 * RANK), f32),
        ],
        scratch_shapes=[
            *[pltpu.VMEM((3 * KNOT * tiles * (rows + 2 * TOP), LANES), f32)] * 3,
            pltpu.VMEM((2, rows, LANES), f32),
            pltpu.VMEM((6 * tiles, KNOT, LANES), f32),
            pltpu.VMEM((2, tiles, nodes, LANES), f32),
            pltpu.VMEM((8, LANES), f32),
            pltpu.VMEM((KNOT, 8, LANES), f32),
        ],
        compiler_params=grid_params(),
        cost_estimate=pl.CostEstimate(flops=60 * cells.size, bytes_accessed=12 * cells.size, transcendentals=0),
        name="warp",
    )(cells, image, shift, left, right, low, high, field, plane, depth_factors, diag_depth, diag_plane)


def gather_kernel(depth_ref, *refs):
    depth_out, plane_out = refs[-2:]
    total = jnp.sum(depth_ref[...], axis=0)
    found = [ref[...] for ref in refs[:-2]]
    while len(found) > 1:
        half = len(found) // 2
        found = [found[k] + found[k + half] for k in range(half)]
    planes = found[0]
    plane_out[...] = planes
    cells = planes.shape[0]
    share, width = total.shape[0] // 4, total.shape[1]
    row = lax.broadcasted_iota(jnp.int32, total.shape, 0)
    lane = lax.broadcasted_iota(jnp.int32, total.shape, 1)
    partial = planes[cells - 1, 4 * RANK - 1]
    total = jnp.where((row >= 3 * share) & (lane >= width // 2), partial, total)
    for p in range(depth_out.shape[0]):
        depth_out[p] = total


def step_kernel(full_z, node_count, depth_ref, plane_ref, depth_out, plane_out):
    parts, share, width = depth_ref.shape[0], depth_ref.shape[1] // 4, depth_ref.shape[2]
    energy = depth_ref[0, 3 * share, width - 1]
    for p in range(1, parts):
        energy = energy + depth_ref[p, 3 * share, width - 1]
    lam_depth = damping * energy / full_z
    lam_plane = damping * RANK * energy / node_count
    for p in range(parts):
        got = depth_ref[p]
        levels = got[3 * share :, 0 : width // 2]
        levels = jnp.concatenate([levels, levels], axis=1)
        rows = slice(p * share, (p + 1) * share)
        depth_out[0, rows, :] = got[0:share] / (got[2 * share : 3 * share] + lam_depth + epsilon)
        depth_out[1, rows, :] = got[share : 2 * share] / (levels + lam_depth + epsilon)
    planes = plane_ref[...]
    plane_out[0] = planes[:, 0:RANK] / (planes[:, 2 * RANK : 3 * RANK] + lam_plane + epsilon)
    plane_out[1] = planes[:, RANK : 2 * RANK] / (planes[0:1, 3 * RANK :] + lam_plane + epsilon)


def local(image, deformed, displacement, plane_factors, depth_factors):
    n_gy, n_gz = lax.axis_size("gy"), lax.axis_size("gz")
    nodes_x, nodes_y = plane_factors.shape[2:]
    plane = jnp.transpose(plane_factors, (0, 2, 3, 1)).reshape(2, nodes_x * nodes_y, RANK)
    first, last = end_columns(deformed)
    right = shifted(first, "gz", True)
    left = shifted(last, "gz", False)
    sums, low, high = squares(image, deformed)
    low, high = packed_rows(left, right, low, high)
    above = shifted(low, "gy", True)
    below = shifted(high, "gy", False)
    field, diag_depth, diag_plane = terms(sums, plane, depth_factors)
    residual, depth_terms, plane_terms = warp(
        deformed, image, displacement, left, right, below, above, field, plane, depth_factors, diag_depth, diag_plane,
        n_gy,
    )
    others = [
        lax.ppermute(plane_terms, "gz", [(i, (i + hop) % n_gz) for i in range(n_gz)]) for hop in range(1, n_gz)
    ]
    depth_terms = lax.all_to_all(depth_terms, "gy", 0, 0)
    depth_terms, plane_terms = pl.pallas_call(
        gather_kernel,
        out_shape=[
            jax.ShapeDtypeStruct(depth_terms.shape, f32),
            jax.ShapeDtypeStruct(plane_terms.shape, f32),
        ],
        compiler_params=plain_params(),
        name="gather",
    )(depth_terms, plane_terms, *others)
    depth_terms = lax.all_to_all(depth_terms, "gy", 0, 0)
    width = depth_factors.shape[2]
    step_depth, step_plane = pl.pallas_call(
        functools.partial(step_kernel, width * n_gz, nodes_x * nodes_y * n_gy),
        out_shape=[
            jax.ShapeDtypeStruct(depth_factors.shape, f32),
            jax.ShapeDtypeStruct(plane.shape, f32),
        ],
        compiler_params=plain_params(),
        name="steps",
    )(depth_terms, plane_terms)
    step_plane = jnp.transpose(step_plane.reshape(2, nodes_x, nodes_y, RANK), (0, 3, 1, 2))
    return residual, step_plane, step_depth


def solution(mesh):
    placed = (
        P(None, "gy", "gz"),
        P(None, "gy", "gz"),
        P(None, None, "gy", "gz"),
        P(None, None, None, "gy"),
        P(None, None, "gz"),
    )
    return jax.shard_map(
        local,
        mesh=mesh,
        in_specs=placed,
        out_specs=(P(None, "gy", "gz"), P(None, None, None, "gy"), P(None, None, "gz")),
        check_vma=False,
    )
```

```python
import functools

import jax
import jax.numpy as jnp
from jax import lax
from jax.experimental import pallas as pl
from jax.experimental.pallas import tpu as pltpu
from jax.sharding import PartitionSpec as P

RANK = 32
KNOT = 8
LANES = 128
TOP = 8

epsilon = 1e-06
damping = 0.01
highest = lax.Precision.HIGHEST
f32 = jnp.float32
bf16 = jnp.bfloat16


def dot(left, right, dims):
    return lax.dot_general(left, right, ((dims[0], dims[1]), ((), ())), precision=highest, preferred_element_type=f32)


def split_dot(left, right, dim):
    left_high, right_high = left.astype(bf16), right.astype(bf16)
    left_low = (left - left_high.astype(f32)).astype(bf16)
    right_low = (right - right_high.astype(f32)).astype(bf16)
    left = jnp.concatenate([left_high, left_high, left_low], axis=dim)
    right = jnp.concatenate([right_high, right_low, right_high], axis=dim)
    return lax.dot_general(left, right, (((dim,), (dim,)), ((), ())), preferred_element_type=f32)


def joined(ref):
    return jnp.concatenate([ref[tile] for tile in range(ref.shape[0])], axis=1)


def grid_params():
    return pltpu.CompilerParams(dimension_semantics=("arbitrary",), vmem_limit_bytes=40000000)


def plain_params():
    return pltpu.CompilerParams(vmem_limit_bytes=32000000)


def columns_kernel(cells_ref, first_ref, last_ref):
    depth, rows, width = cells_ref.shape
    lane = lax.broadcasted_iota(jnp.int32, (rows, LANES), 1)
    first = jnp.zeros((rows, LANES), f32)
    last = jnp.zeros((rows, LANES), f32)
    for x in range(depth):
        near = cells_ref[x, :, 0:LANES].astype(f32)
        far = cells_ref[x, :, width - LANES : width].astype(f32)
        first = jnp.where(lane == x, pltpu.roll(near, x, 1), first)
        last = jnp.where(lane == x, pltpu.roll(far, (x + 1) % LANES, 1), last)
    first_ref[...] = first.astype(bf16)
    last_ref[...] = last.astype(bf16)


def end_columns(cells):
    rows = cells.shape[1]
    return pl.pallas_call(
        columns_kernel,
        out_shape=[jax.ShapeDtypeStruct((rows, LANES), bf16)] * 2,
        compiler_params=plain_params(),
        name="columns",
    )(cells)


def rows_kernel(left_ref, right_ref, low_ref, high_ref, low_out, high_out):
    depth, width = low_ref.shape
    rows = left_ref.shape[0]
    lane = lax.broadcasted_iota(jnp.int32, (depth, LANES), 1)
    pad = jnp.zeros((LANES - rows, LANES), f32)
    left = jnp.transpose(jnp.concatenate([left_ref[...].astype(f32), pad], axis=0))[0:depth]
    right = jnp.transpose(jnp.concatenate([right_ref[...].astype(f32), pad], axis=0))[0:depth]
    for row, body, out in ((0, low_ref, low_out), (rows - 1, high_ref, high_out)):
        after = pltpu.roll(right, (LANES - row) % LANES, 1)
        before = pltpu.roll(left, LANES - 1 - row, 1)
        out[:, 0:width] = body[...].astype(bf16)
        out[:, width : width + LANES] = jnp.where(lane == 0, after, before).astype(bf16)


def packed_rows(left, right, low, high):
    depth, width = low.shape
    return pl.pallas_call(
        rows_kernel,
        out_shape=[jax.ShapeDtypeStruct((depth, width + LANES), bf16)] * 2,
        compiler_params=plain_params(),
        name="rows",
    )(left, right, low, high)


def shifted(part, axis, back):
    count = lax.axis_size(axis)
    if back:
        return lax.ppermute(part, axis, [(i + 1, i) for i in range(count - 1)])
    return lax.ppermute(part, axis, [(i, i + 1) for i in range(count - 1)])


def squares_kernel(image_ref, cells_ref, sums, low_ref, high_ref):
    depth, rows, width = image_ref.shape
    tiles = width // LANES

    def one(t, carry):
        block, tile = t // tiles, t % tiles
        at = pl.multiple_of(tile * LANES, LANES)
        for pair in range(rows // 16):
            total = jnp.zeros((16, LANES), f32)
            for k in range(KNOT):
                values = image_ref[block * KNOT + k, 16 * pair : 16 * pair + 16, pl.ds(at, LANES)].astype(f32)
                total = total + values * values
            for half in range(2):
                row = block * (rows // KNOT) + 2 * pair + half
                sums[tile, pl.ds(row, 1), :] = jnp.sum(total[8 * half : 8 * half + 8], axis=0, keepdims=True)
        return carry

    lax.fori_loop(0, depth // KNOT * tiles, one, 0)

    def ends(block, carry):
        x = pl.multiple_of(block * KNOT, KNOT)
        low = [cells_ref[x + k, 0:16, :].astype(f32)[0:1] for k in range(KNOT)]
        high = [cells_ref[x + k, rows - 16 : rows, :].astype(f32)[15:16] for k in range(KNOT)]
        low_ref[pl.ds(x, KNOT), :] = jnp.concatenate(low, axis=0)
        high_ref[pl.ds(x, KNOT), :] = jnp.concatenate(high, axis=0)
        return carry

    lax.fori_loop(0, depth // KNOT, ends, 0)


def squares(image, cells):
    depth, rows, width = image.shape
    return pl.pallas_call(
        squares_kernel,
        out_shape=[
            jax.ShapeDtypeStruct((width // LANES, depth * rows // KNOT**2, LANES), f32),
            jax.ShapeDtypeStruct((depth, width), f32),
            jax.ShapeDtypeStruct((depth, width), f32),
        ],
        compiler_params=plain_params(),
        cost_estimate=pl.CostEstimate(flops=3 * image.size, bytes_accessed=2 * image.size, transcendentals=0),
        name="squares",
    )(image, cells)


def terms_kernel(sums, plane_ref, depth_ref, field_ref, diag_depth_ref, diag_plane_ref):
    tiles = sums.shape[0]
    for k in range(2):
        field = dot(plane_ref[k], depth_ref[k], ((1,), (0,)))
        for tile in range(tiles):
            field_ref[k, tile] = field[:, tile * LANES : (tile + 1) * LANES]
    squared = joined(sums)
    cells = jnp.full(squared.shape, float(KNOT * KNOT), f32)
    first, second = plane_ref[0], plane_ref[1]
    diag_depth_ref[0] = dot(first * first, squared, ((0,), (0,)))
    diag_depth_ref[1] = dot(second * second, cells, ((0,), (0,)))
    first, second = depth_ref[0], depth_ref[1]
    diag_plane_ref[0] = dot(squared, first * first, ((1,), (1,)))
    diag_plane_ref[1] = dot(cells, second * second, ((1,), (1,)))


def terms(sums, plane, depth_factors):
    nodes, width = plane.shape[1], depth_factors.shape[2]
    return pl.pallas_call(
        terms_kernel,
        out_shape=[
            jax.ShapeDtypeStruct((2, width // LANES, nodes, LANES), f32),
            jax.ShapeDtypeStruct((2, RANK, width), f32),
            jax.ShapeDtypeStruct((2, nodes, RANK), f32),
        ],
        compiler_params=plain_params(),
        cost_estimate=pl.CostEstimate(flops=40 * nodes * RANK * width, bytes_accessed=1 << 20, transcendentals=0),
        name="terms",
    )(sums, plane, depth_factors)


def warp_kernel(
    cells_ref, image_ref, shift_ref, left_ref, right_ref, low_ref, high_ref, field, plane_ref, depth_ref,
    diag_depth_ref, diag_plane_ref,
    residual_ref, depth_out, plane_out,
    ahead_ref, here_ref, behind_ref, columns, rims, blocks, energy, held,
):
    step = pl.program_id(0)
    last = pl.num_programs(0) - 1
    planes, rows, width = cells_ref.shape
    nodes = rows // KNOT
    tiles = width // LANES
    window = (ahead_ref, here_ref, behind_ref)
    pitch = rows + 2 * TOP
    plane_rows = tiles * pitch
    block_rows = planes * plane_rows

    def differences(wide):
        ahead = pltpu.roll(wide, wide.shape[1] - 1, 1) - wide
        return ahead, wide, pltpu.roll(ahead, 1, 1)

    @pl.when(step == 0)
    def _():
        columns[0] = left_ref[...].astype(f32)
        columns[1] = right_ref[...].astype(f32)
        energy[...] = jnp.zeros_like(energy)
        for c in range(3):
            window[c][3 * block_rows - plane_rows : 3 * block_rows, :] = jnp.zeros((plane_rows, LANES), f32)

    @pl.when(step < last)
    def _():
        lane = lax.broadcasted_iota(jnp.int32, (16, LANES), 1)
        slot = (step % 3) * block_rows
        for side, source in enumerate((low_ref, high_ref)):
            moved = differences(source[...].astype(f32))
            for c in range(3):
                for tile in range(tiles):
                    rims[(side * 3 + c) * tiles + tile] = moved[c][:, tile * LANES : (tile + 1) * LANES]

        for k in range(planes):
            x = step * planes + k
            first = pl.multiple_of(slot + k * plane_rows, 8)
            raw = cells_ref[k]
            right, left = columns[1], columns[0]
            for group in range(rows // 16):
                mine = slice(16 * group, 16 * group + 16)
                after = pltpu.roll(right[mine], (LANES - x) % LANES, 1)
                before = pltpu.roll(left[mine], LANES - 1 - x, 1)
                beyond = jnp.where(lane == 0, after, before)
                moved = differences(jnp.concatenate([raw[mine].astype(f32), beyond], axis=1))
                for c in range(3):
                    for tile in range(tiles):
                        window[c][pl.ds(first + tile * pitch + TOP + 16 * group, 16), :] = moved[c][
                            :, tile * LANES : (tile + 1) * LANES
                        ]
            for side, row in enumerate((0, TOP + rows)):
                for c in range(3):
                    for tile in range(tiles):
                        rim = rims[(side * 3 + c) * tiles + tile, pl.ds(k, 1), :]
                        window[c][pl.ds(first + tile * pitch + row, 8), :] = jnp.broadcast_to(rim, (8, LANES))
    @pl.when(step == last)
    def _():
        first = pl.multiple_of((step % 3) * block_rows, 8)
        for c in range(3):
            window[c][pl.ds(first, plane_rows), :] = jnp.zeros((plane_rows, LANES), f32)

    @pl.when(step > 0)
    def _():
        mid = (step + 2) % 3
        first_rows = (
            jnp.where(mid == 0, 3, mid) * block_rows - plane_rows,
            mid * block_rows,
            jnp.where(mid == 2, 0, mid + 1) * block_rows,
        )

        def one(t, total):
            tile = t % tiles
            pair = t // tiles
            at = pl.multiple_of(tile * LANES, LANES)
            top = pl.multiple_of(pair * 16, 16)
            origins = [first + tile * pitch + top + TOP for first in first_rows]
            for half in range(2):
                node = (step - 1) * nodes + pair * 2 + half
                mine = slice(8 * half, 8 * half + 8)

                def taps(x):
                    part = 0 if x == 0 else 2 if x == planes + 1 else 1
                    plus = (x - 1) * plane_rows + 8 * half if part == 1 else 8 * half
                    return [
                        [window[c][pl.ds(origins[part] + (plus + b), 8), :] for c in range(3)] for b in (-1, 0, 1)
                    ]

                contrast = jnp.broadcast_to(field[0, tile, pl.ds(node, 1), :], (8, LANES))
                brightness = jnp.broadcast_to(field[1, tile, pl.ds(node, 1), :], (8, LANES))
                by_image = jnp.zeros((8, LANES), f32)
                plain = jnp.zeros((8, LANES), f32)
                before, here = taps(0), taps(1)
                for k in range(planes):
                    after = taps(k + 2)
                    place = (k, pl.ds(top, 16), pl.ds(at, LANES))
                    sx, sy, sz = (shift_ref[(axis,) + place].astype(f32)[mine] for axis in range(3))
                    image = image_ref[place].astype(f32)[mine]
                    px, py, pz = sx > 0, sy > 0, sz > 0
                    ax, ay = jnp.abs(sx), jnp.abs(sy)

                    def sides(c):
                        far = [jnp.where(px, after[b][c], before[b][c]) for b in range(3)]
                        near = [here[b][c] for b in range(3)]
                        return [(v[1], jnp.where(py, v[2], v[0])) for v in (near, far)]

                    ahead, middle, behind = sides(0), sides(1), sides(2)
                    lines = []
                    for b in range(2):
                        near, far = (middle[v][b] + sz * jnp.where(pz, ahead[v][b], behind[v][b]) for v in range(2))
                        lines.append(near + ax * (far - near))
                    warped = lines[0] + ay * (lines[1] - lines[0])
                    misfit = warped - contrast * image - brightness
                    if half == 0:
                        held[k] = misfit
                    else:
                        residual_ref[place] = jnp.concatenate([held[k], misfit], axis=0).astype(bf16)
                    by_image = by_image + misfit * image
                    plain = plain + misfit
                    total = total + misfit * misfit
                    before, here = here, after
                for k, value in ((0, by_image), (1, plain)):
                    blocks[k, tile, pl.ds(node, 1), :] = jnp.sum(value, axis=0, keepdims=True)
            return total

        energy[...] = lax.fori_loop(0, (rows // 16) * tiles, one, energy[...])

    @pl.when(step == last)
    def _():
        parts = depth_out.shape[0]
        share = RANK // parts
        sums = [joined(blocks.at[k]) for k in range(2)]
        kinds = [split_dot(plane_ref[k], sums[k], 0) for k in range(2)]
        kinds = kinds + [diag_depth_ref[0], diag_depth_ref[1]]
        for p in range(parts):
            for k in range(4):
                depth_out[p, k * share : (k + 1) * share, :] = kinds[k][p * share : (p + 1) * share]
        local = jnp.sum(energy[...])
        kinds = [split_dot(sums[k], depth_ref[k], 1) for k in range(2)]
        kinds = kinds + [diag_plane_ref[0], diag_plane_ref[1]]
        for k in range(4):
            plane_out[:, k * RANK : (k + 1) * RANK] = kinds[k]
        count = plane_out.shape[0]
        plane_out[count // 2 :, 3 * RANK :] = jnp.full((count // 2, RANK), local, f32)


def warp(cells, image, shift, left, right, low, high, field, plane, depth_factors, diag_depth, diag_plane, parts):
    depth, rows, width = cells.shape
    nodes = plane.shape[1]
    tiles = width // LANES
    count = depth // KNOT
    behind = lambda i: (jnp.maximum(i - 1, 0), 0, 0)
    ahead = lambda i: (jnp.minimum(i, count - 1), 0, 0)
    flat = lambda i: (0, 0)
    whole = lambda i: (0, 0, 0)
    return pl.pallas_call(
        warp_kernel,
        grid=(count + 1,),
        in_specs=[
            pl.BlockSpec((KNOT, rows, width), ahead),
            pl.BlockSpec((KNOT, rows, width), behind),
            pl.BlockSpec((3, KNOT, rows, width), lambda i: (0, jnp.maximum(i - 1, 0), 0, 0)),
            pl.BlockSpec(left.shape, flat),
            pl.BlockSpec(right.shape, flat),
            pl.BlockSpec((KNOT, low.shape[1]), lambda i: (jnp.minimum(i, count - 1), 0)),
            pl.BlockSpec((KNOT, high.shape[1]), lambda i: (jnp.minimum(i, count - 1), 0)),
            pl.BlockSpec(field.shape, lambda i: (0, 0, 0, 0)),
            pl.BlockSpec(plane.shape, whole),
            pl.BlockSpec(depth_factors.shape, whole),
            pl.BlockSpec(diag_depth.shape, whole),
            pl.BlockSpec(diag_plane.shape, whole),
        ],
        out_specs=[
            pl.BlockSpec((KNOT, rows, width), behind),
            pl.BlockSpec((parts, 4 * RANK // parts, width), whole),
            pl.BlockSpec((nodes, 4 * RANK), flat),
        ],
        out_shape=[
            jax.ShapeDtypeStruct(cells.shape, bf16),
            jax.ShapeDtypeStruct((parts, 4 * RANK // parts, width), f32),
            jax.ShapeDtypeStruct((nodes, 4 * RANK), f32),
        ],
        scratch_shapes=[
            *[pltpu.VMEM((3 * KNOT * tiles * (rows + 2 * TOP), LANES), f32)] * 3,
            pltpu.VMEM((2, rows, LANES), f32),
            pltpu.VMEM((6 * tiles, KNOT, LANES), f32),
            pltpu.VMEM((2, tiles, nodes, LANES), f32),
            pltpu.VMEM((8, LANES), f32),
            pltpu.VMEM((KNOT, 8, LANES), f32),
        ],
        compiler_params=grid_params(),
        cost_estimate=pl.CostEstimate(flops=60 * cells.size, bytes_accessed=12 * cells.size, transcendentals=0),
        name="warp",
    )(cells, image, shift, left, right, low, high, field, plane, depth_factors, diag_depth, diag_plane)


def gather_kernel(depth_ref, *refs):
    depth_out, plane_out = refs[-2:]
    total = jnp.sum(depth_ref[...], axis=0)
    found = [ref[...] for ref in refs[:-2]]
    while len(found) > 1:
        half = len(found) // 2
        found = [found[k] + found[k + half] for k in range(half)]
    planes = found[0]
    plane_out[...] = planes
    cells = planes.shape[0]
    share, width = total.shape[0] // 4, total.shape[1]
    row = lax.broadcasted_iota(jnp.int32, total.shape, 0)
    lane = lax.broadcasted_iota(jnp.int32, total.shape, 1)
    partial = planes[cells - 1, 4 * RANK - 1]
    total = jnp.where((row >= 3 * share) & (lane >= width // 2), partial, total)
    for p in range(depth_out.shape[0]):
        depth_out[p] = total


def step_kernel(full_z, node_count, depth_ref, plane_ref, depth_out, plane_out):
    parts, share, width = depth_ref.shape[0], depth_ref.shape[1] // 4, depth_ref.shape[2]
    energy = depth_ref[0, 3 * share, width - 1]
    for p in range(1, parts):
        energy = energy + depth_ref[p, 3 * share, width - 1]
    lam_depth = damping * energy / full_z
    lam_plane = damping * RANK * energy / node_count
    for p in range(parts):
        got = depth_ref[p]
        levels = got[3 * share :, 0 : width // 2]
        levels = jnp.concatenate([levels, levels], axis=1)
        rows = slice(p * share, (p + 1) * share)
        depth_out[0, rows, :] = got[0:share] / (got[2 * share : 3 * share] + lam_depth + epsilon)
        depth_out[1, rows, :] = got[share : 2 * share] / (levels + lam_depth + epsilon)
    planes = plane_ref[...]
    plane_out[0] = planes[:, 0:RANK] / (planes[:, 2 * RANK : 3 * RANK] + lam_plane + epsilon)
    plane_out[1] = planes[:, RANK : 2 * RANK] / (planes[0:1, 3 * RANK :] + lam_plane + epsilon)


def local(image, deformed, displacement, plane_factors, depth_factors):
    n_gy, n_gz = lax.axis_size("gy"), lax.axis_size("gz")
    nodes_x, nodes_y = plane_factors.shape[2:]
    plane = jnp.transpose(plane_factors, (0, 2, 3, 1)).reshape(2, nodes_x * nodes_y, RANK)
    first, last = end_columns(deformed)
    right = shifted(first, "gz", True)
    left = shifted(last, "gz", False)
    sums, low, high = squares(image, deformed)
    low, high = packed_rows(left, right, low, high)
    above = shifted(low, "gy", True)
    below = shifted(high, "gy", False)
    field, diag_depth, diag_plane = terms(sums, plane, depth_factors)
    residual, depth_terms, plane_terms = warp(
        deformed, image, displacement, left, right, below, above, field, plane, depth_factors, diag_depth, diag_plane,
        n_gy,
    )
    others = [
        lax.ppermute(plane_terms, "gz", [(i, (i + hop) % n_gz) for i in range(n_gz)]) for hop in range(1, n_gz)
    ]
    depth_terms = lax.all_to_all(depth_terms, "gy", 0, 0)
    depth_terms, plane_terms = pl.pallas_call(
        gather_kernel,
        out_shape=[
            jax.ShapeDtypeStruct(depth_terms.shape, f32),
            jax.ShapeDtypeStruct(plane_terms.shape, f32),
        ],
        compiler_params=plain_params(),
        name="gather",
    )(depth_terms, plane_terms, *others)
    depth_terms = lax.all_to_all(depth_terms, "gy", 0, 0)
    width = depth_factors.shape[2]
    step_depth, step_plane = pl.pallas_call(
        functools.partial(step_kernel, width * n_gz, nodes_x * nodes_y * n_gy),
        out_shape=[
            jax.ShapeDtypeStruct(depth_factors.shape, f32),
            jax.ShapeDtypeStruct(plane.shape, f32),
        ],
        compiler_params=plain_params(),
        name="steps",
    )(depth_terms, plane_terms)
    step_plane = jnp.transpose(step_plane.reshape(2, nodes_x, nodes_y, RANK), (0, 3, 1, 2))
    return residual, step_plane, step_depth


def solution(mesh):
    placed = (
        P(None, "gy", "gz"),
        P(None, "gy", "gz"),
        P(None, None, "gy", "gz"),
        P(None, None, None, "gy"),
        P(None, None, "gz"),
    )
    return jax.shard_map(
        local,
        mesh=mesh,
        in_specs=placed,
        out_specs=(P(None, "gy", "gz"), P(None, None, None, "gy"), P(None, None, "gz")),
        check_vma=False,
    )
```

```python
import functools

import jax
import jax.numpy as jnp
from jax import lax
from jax.experimental import pallas as pl
from jax.experimental.pallas import tpu as pltpu
from jax.sharding import PartitionSpec as P

RANK = 32
KNOT = 8
LANES = 128
TOP = 8

epsilon = 1e-06
damping = 0.01
highest = lax.Precision.HIGHEST
f32 = jnp.float32
bf16 = jnp.bfloat16


def dot(left, right, dims):
    return lax.dot_general(left, right, ((dims[0], dims[1]), ((), ())), precision=highest, preferred_element_type=f32)


def split_dot(left, right, dim):
    left_high, right_high = left.astype(bf16), right.astype(bf16)
    left_low = (left - left_high.astype(f32)).astype(bf16)
    right_low = (right - right_high.astype(f32)).astype(bf16)
    left = jnp.concatenate([left_high, left_high, left_low], axis=dim)
    right = jnp.concatenate([right_high, right_low, right_high], axis=dim)
    return lax.dot_general(left, right, (((dim,), (dim,)), ((), ())), preferred_element_type=f32)


def joined(ref):
    return jnp.concatenate([ref[tile] for tile in range(ref.shape[0])], axis=1)


def grid_params():
    return pltpu.CompilerParams(dimension_semantics=("arbitrary",), vmem_limit_bytes=40000000)


def plain_params():
    return pltpu.CompilerParams(vmem_limit_bytes=32000000)


def columns_kernel(cells_ref, first_ref, last_ref):
    depth, rows, width = cells_ref.shape
    lane = lax.broadcasted_iota(jnp.int32, (rows, LANES), 1)
    first = jnp.zeros((rows, LANES), f32)
    last = jnp.zeros((rows, LANES), f32)
    for x in range(depth):
        near = cells_ref[x, :, 0:LANES].astype(f32)
        far = cells_ref[x, :, width - LANES : width].astype(f32)
        first = jnp.where(lane == x, pltpu.roll(near, x, 1), first)
        last = jnp.where(lane == x, pltpu.roll(far, (x + 1) % LANES, 1), last)
    first_ref[...] = first.astype(bf16)
    last_ref[...] = last.astype(bf16)


def end_columns(cells):
    rows = cells.shape[1]
    return pl.pallas_call(
        columns_kernel,
        out_shape=[jax.ShapeDtypeStruct((rows, LANES), bf16)] * 2,
        compiler_params=plain_params(),
        name="columns",
    )(cells)


def rows_kernel(left_ref, right_ref, low_ref, high_ref, low_out, high_out):
    depth, width = low_ref.shape
    rows = left_ref.shape[0]
    lane = lax.broadcasted_iota(jnp.int32, (depth, LANES), 1)
    pad = jnp.zeros((LANES - rows, LANES), f32)
    left = jnp.transpose(jnp.concatenate([left_ref[...].astype(f32), pad], axis=0))[0:depth]
    right = jnp.transpose(jnp.concatenate([right_ref[...].astype(f32), pad], axis=0))[0:depth]
    for row, body, out in ((0, low_ref, low_out), (rows - 1, high_ref, high_out)):
        after = pltpu.roll(right, (LANES - row) % LANES, 1)
        before = pltpu.roll(left, LANES - 1 - row, 1)
        out[:, 0:width] = body[...].astype(bf16)
        out[:, width : width + LANES] = jnp.where(lane == 0, after, before).astype(bf16)


def packed_rows(left, right, low, high):
    depth, width = low.shape
    return pl.pallas_call(
        rows_kernel,
        out_shape=[jax.ShapeDtypeStruct((depth, width + LANES), bf16)] * 2,
        compiler_params=plain_params(),
        name="rows",
    )(left, right, low, high)


def shifted(part, axis, back):
    count = lax.axis_size(axis)
    if back:
        return lax.ppermute(part, axis, [(i + 1, i) for i in range(count - 1)])
    return lax.ppermute(part, axis, [(i, i + 1) for i in range(count - 1)])


def squares_kernel(image_ref, cells_ref, sums, low_ref, high_ref):
    depth, rows, width = image_ref.shape
    tiles = width // LANES

    def one(t, carry):
        block, tile = t // tiles, t % tiles
        at = pl.multiple_of(tile * LANES, LANES)
        for pair in range(rows // 16):
            total = jnp.zeros((16, LANES), f32)
            for k in range(KNOT):
                values = image_ref[block * KNOT + k, 16 * pair : 16 * pair + 16, pl.ds(at, LANES)].astype(f32)
                total = total + values * values
            for half in range(2):
                row = block * (rows // KNOT) + 2 * pair + half
                sums[tile, pl.ds(row, 1), :] = jnp.sum(total[8 * half : 8 * half + 8], axis=0, keepdims=True)
        return carry

    lax.fori_loop(0, depth // KNOT * tiles, one, 0)

    def ends(block, carry):
        x = pl.multiple_of(block * KNOT, KNOT)
        low = [cells_ref[x + k, 0:16, :].astype(f32)[0:1] for k in range(KNOT)]
        high = [cells_ref[x + k, rows - 16 : rows, :].astype(f32)[15:16] for k in range(KNOT)]
        low_ref[pl.ds(x, KNOT), :] = jnp.concatenate(low, axis=0)
        high_ref[pl.ds(x, KNOT), :] = jnp.concatenate(high, axis=0)
        return carry

    lax.fori_loop(0, depth // KNOT, ends, 0)


def squares(image, cells):
    depth, rows, width = image.shape
    return pl.pallas_call(
        squares_kernel,
        out_shape=[
            jax.ShapeDtypeStruct((width // LANES, depth * rows // KNOT**2, LANES), f32),
            jax.ShapeDtypeStruct((depth, width), f32),
            jax.ShapeDtypeStruct((depth, width), f32),
        ],
        compiler_params=plain_params(),
        cost_estimate=pl.CostEstimate(flops=3 * image.size, bytes_accessed=2 * image.size, transcendentals=0),
        name="squares",
    )(image, cells)


def terms_kernel(
    sums, plane_ref, depth_ref, left_ref, right_ref, field_ref, diag_depth_ref, diag_plane_ref, beyond_ref
):
    tiles = sums.shape[0]
    left, right = left_ref[...].astype(f32), right_ref[...].astype(f32)
    lane = lax.broadcasted_iota(jnp.int32, left.shape, 1)
    for x in range(beyond_ref.shape[0]):
        after = pltpu.roll(right, (LANES - x) % LANES, 1)
        before = pltpu.roll(left, LANES - 1 - x, 1)
        beyond_ref[x] = jnp.where(lane == 0, after, before).astype(bf16)
    for k in range(2):
        field = dot(plane_ref[k], depth_ref[k], ((1,), (0,)))
        for tile in range(tiles):
            field_ref[k, tile] = field[:, tile * LANES : (tile + 1) * LANES]
    squared = joined(sums)
    cells = jnp.full(squared.shape, float(KNOT * KNOT), f32)
    first, second = plane_ref[0], plane_ref[1]
    diag_depth_ref[0] = dot(first * first, squared, ((0,), (0,)))
    diag_depth_ref[1] = dot(second * second, cells, ((0,), (0,)))
    first, second = depth_ref[0], depth_ref[1]
    diag_plane_ref[0] = dot(squared, first * first, ((1,), (1,)))
    diag_plane_ref[1] = dot(cells, second * second, ((1,), (1,)))


def terms(sums, plane, depth_factors, left, right, depth):
    nodes, width = plane.shape[1], depth_factors.shape[2]
    return pl.pallas_call(
        terms_kernel,
        out_shape=[
            jax.ShapeDtypeStruct((2, width // LANES, nodes, LANES), f32),
            jax.ShapeDtypeStruct((2, RANK, width), f32),
            jax.ShapeDtypeStruct((2, nodes, RANK), f32),
            jax.ShapeDtypeStruct((depth,) + left.shape, bf16),
        ],
        compiler_params=plain_params(),
        cost_estimate=pl.CostEstimate(flops=40 * nodes * RANK * width, bytes_accessed=1 << 20, transcendentals=0),
        name="terms",
    )(sums, plane, depth_factors, left, right)


def warp_kernel(
    cells_ref, image_ref, shift_ref, beyond_ref, low_ref, high_ref, field, plane_ref, depth_ref,
    diag_depth_ref, diag_plane_ref,
    residual_ref, depth_out, plane_out,
    ahead_ref, here_ref, behind_ref, wide, bands, rims, blocks, energy, held,
):
    step = pl.program_id(0)
    last = pl.num_programs(0) - 1
    planes, rows, width = cells_ref.shape
    nodes = rows // KNOT
    tiles = width // LANES
    window = (ahead_ref, here_ref, behind_ref)
    pitch = rows + 2 * TOP
    plane_rows = tiles * pitch
    block_rows = planes * plane_rows

    @pl.when(step == 0)
    def _():
        row = lax.broadcasted_iota(jnp.int32, bands.shape[1:], 0)
        column = lax.broadcasted_iota(jnp.int32, bands.shape[1:], 1)
        one, none = jnp.ones(bands.shape[1:], f32), jnp.zeros(bands.shape[1:], f32)
        up, down = jnp.where(row == column + 1, one, none), jnp.where(row == column, one, none)
        bands[0] = (up - down).astype(bf16)
        up = jnp.where(row == column + LANES, one, none)
        down = jnp.where(row == column + LANES - 1, one, none)
        bands[1] = (up - down).astype(bf16)
        energy[...] = jnp.zeros_like(energy)
        for c in range(3):
            window[c][3 * block_rows - plane_rows : 3 * block_rows, :] = jnp.zeros((plane_rows, LANES), f32)

    @pl.when(step < last)
    def _():
        slot = (step % 3) * block_rows
        span = planes * rows
        for k in range(planes):
            wide[k * rows : (k + 1) * rows, 0:width] = cells_ref[k]
            wide[k * rows : (k + 1) * rows, width:] = beyond_ref[k]
        wide[span:, :] = jnp.concatenate([low_ref[...].astype(f32), high_ref[...].astype(f32)], axis=0).astype(bf16)

        def put(c, tile, values):
            for k in range(planes):
                first = pl.multiple_of(slot + k * plane_rows + tile * pitch, 8)
                window[c][pl.ds(first + TOP, rows), :] = values[k * rows : (k + 1) * rows]
            for side, row in enumerate((0, TOP + rows)):
                rims[...] = values[span + side * planes : span + (side + 1) * planes]
                for k in range(planes):
                    first = pl.multiple_of(slot + k * plane_rows + tile * pitch, 8)
                    window[c][pl.ds(first + row, 8), :] = jnp.broadcast_to(rims[k : k + 1], (8, LANES))

        pieces = width // (2 * LANES)
        for piece in range(pieces):
            start = 2 * LANES * piece
            after = wide[:, start : start + 3 * LANES]
            if piece == 0:
                before = jnp.concatenate([wide[:, width:], wide[:, 0 : 2 * LANES]], axis=1)
            else:
                before = wide[:, start - LANES : start + 2 * LANES]
            ahead = jnp.dot(after, bands[0], preferred_element_type=f32)
            behind = jnp.dot(before, bands[1], preferred_element_type=f32)
            for half in range(2):
                mine = slice(half * LANES, (half + 1) * LANES)
                put(0, 2 * piece + half, ahead[:, mine])
                put(1, 2 * piece + half, wide[:, start + half * LANES : start + (half + 1) * LANES].astype(f32))
                put(2, 2 * piece + half, behind[:, mine])

    @pl.when(step == last)
    def _():
        first = pl.multiple_of((step % 3) * block_rows, 8)
        for c in range(3):
            window[c][pl.ds(first, plane_rows), :] = jnp.zeros((plane_rows, LANES), f32)

    @pl.when(step > 0)
    def _():
        mid = (step + 2) % 3
        first_rows = (
            jnp.where(mid == 0, 3, mid) * block_rows - plane_rows,
            mid * block_rows,
            jnp.where(mid == 2, 0, mid + 1) * block_rows,
        )

        def one(t, total):
            tile = t % tiles
            pair = t // tiles
            at = pl.multiple_of(tile * LANES, LANES)
            top = pl.multiple_of(pair * 16, 16)
            origins = [first + tile * pitch + top + TOP for first in first_rows]
            for half in range(2):
                node = (step - 1) * nodes + pair * 2 + half
                mine = slice(8 * half, 8 * half + 8)

                def taps(x):
                    part = 0 if x == 0 else 2 if x == planes + 1 else 1
                    plus = (x - 1) * plane_rows + 8 * half if part == 1 else 8 * half
                    return [
                        [window[c][pl.ds(origins[part] + (plus + b), 8), :] for c in range(3)] for b in (-1, 0, 1)
                    ]

                contrast = jnp.broadcast_to(field[0, tile, pl.ds(node, 1), :], (8, LANES))
                brightness = jnp.broadcast_to(field[1, tile, pl.ds(node, 1), :], (8, LANES))
                by_image = jnp.zeros((8, LANES), f32)
                plain = jnp.zeros((8, LANES), f32)
                before, here = taps(0), taps(1)
                for k in range(planes):
                    after = taps(k + 2)
                    place = (k, pl.ds(top, 16), pl.ds(at, LANES))
                    sx, sy, sz = (shift_ref[(axis,) + place].astype(f32)[mine] for axis in range(3))
                    image = image_ref[place].astype(f32)[mine]
                    px, py, pz = sx > 0, sy > 0, sz > 0
                    ax, ay = jnp.abs(sx), jnp.abs(sy)

                    def sides(c):
                        far = [jnp.where(px, after[b][c], before[b][c]) for b in range(3)]
                        near = [here[b][c] for b in range(3)]
                        return [(v[1], jnp.where(py, v[2], v[0])) for v in (near, far)]

                    ahead, middle, behind = sides(0), sides(1), sides(2)
                    lines = []
                    for b in range(2):
                        near, far = (middle[v][b] + sz * jnp.where(pz, ahead[v][b], behind[v][b]) for v in range(2))
                        lines.append(near + ax * (far - near))
                    warped = lines[0] + ay * (lines[1] - lines[0])
                    misfit = warped - contrast * image - brightness
                    if half == 0:
                        held[k] = misfit
                    else:
                        residual_ref[place] = jnp.concatenate([held[k], misfit], axis=0).astype(bf16)
                    by_image = by_image + misfit * image
                    plain = plain + misfit
                    total = total + misfit * misfit
                    before, here = here, after
                for k, value in ((0, by_image), (1, plain)):
                    blocks[k, tile, pl.ds(node, 1), :] = jnp.sum(value, axis=0, keepdims=True)
            return total

        energy[...] = lax.fori_loop(0, (rows // 16) * tiles, one, energy[...])

    @pl.when(step == last)
    def _():
        parts = depth_out.shape[0]
        share = RANK // parts
        sums = [joined(blocks.at[k]) for k in range(2)]
        kinds = [split_dot(plane_ref[k], sums[k], 0) for k in range(2)]
        kinds = kinds + [diag_depth_ref[0], diag_depth_ref[1]]
        for p in range(parts):
            for k in range(4):
                depth_out[p, k * share : (k + 1) * share, :] = kinds[k][p * share : (p + 1) * share]
        local = jnp.sum(energy[...])
        kinds = [split_dot(sums[k], depth_ref[k], 1) for k in range(2)]
        kinds = kinds + [diag_plane_ref[0], diag_plane_ref[1]]
        for k in range(4):
            plane_out[:, k * RANK : (k + 1) * RANK] = kinds[k]
        count = plane_out.shape[0]
        plane_out[count // 2 :, 3 * RANK :] = jnp.full((count // 2, RANK), local, f32)


def warp(cells, image, shift, beyond, low, high, field, plane, depth_factors, diag_depth, diag_plane, parts):
    depth, rows, width = cells.shape
    nodes = plane.shape[1]
    tiles = width // LANES
    count = depth // KNOT
    behind = lambda i: (jnp.maximum(i - 1, 0), 0, 0)
    ahead = lambda i: (jnp.minimum(i, count - 1), 0, 0)
    flat = lambda i: (0, 0)
    whole = lambda i: (0, 0, 0)
    return pl.pallas_call(
        warp_kernel,
        grid=(count + 1,),
        in_specs=[
            pl.BlockSpec((KNOT, rows, width), ahead),
            pl.BlockSpec((KNOT, rows, width), behind),
            pl.BlockSpec((3, KNOT, rows, width), lambda i: (0, jnp.maximum(i - 1, 0), 0, 0)),
            pl.BlockSpec((KNOT, rows, LANES), ahead),
            pl.BlockSpec((KNOT, low.shape[1]), lambda i: (jnp.minimum(i, count - 1), 0)),
            pl.BlockSpec((KNOT, high.shape[1]), lambda i: (jnp.minimum(i, count - 1), 0)),
            pl.BlockSpec(field.shape, lambda i: (0, 0, 0, 0)),
            pl.BlockSpec(plane.shape, whole),
            pl.BlockSpec(depth_factors.shape, whole),
            pl.BlockSpec(diag_depth.shape, whole),
            pl.BlockSpec(diag_plane.shape, whole),
        ],
        out_specs=[
            pl.BlockSpec((KNOT, rows, width), behind),
            pl.BlockSpec((parts, 4 * RANK // parts, width), whole),
            pl.BlockSpec((nodes, 4 * RANK), flat),
        ],
        out_shape=[
            jax.ShapeDtypeStruct(cells.shape, bf16),
            jax.ShapeDtypeStruct((parts, 4 * RANK // parts, width), f32),
            jax.ShapeDtypeStruct((nodes, 4 * RANK), f32),
        ],
        scratch_shapes=[
            *[pltpu.VMEM((3 * KNOT * tiles * (rows + 2 * TOP), LANES), f32)] * 3,
            pltpu.VMEM((KNOT * rows + 2 * KNOT, width + LANES), bf16),
            pltpu.VMEM((2, 3 * LANES, 2 * LANES), bf16),
            pltpu.VMEM((KNOT, LANES), f32),
            pltpu.VMEM((2, tiles, nodes, LANES), f32),
            pltpu.VMEM((8, LANES), f32),
            pltpu.VMEM((KNOT, 8, LANES), f32),
        ],
        compiler_params=grid_params(),
        cost_estimate=pl.CostEstimate(flops=60 * cells.size, bytes_accessed=12 * cells.size, transcendentals=0),
        name="warp",
    )(cells, image, shift, beyond, low, high, field, plane, depth_factors, diag_depth, diag_plane)


def gather_kernel(depth_ref, *refs):
    depth_out, plane_out = refs[-2:]
    total = jnp.sum(depth_ref[...], axis=0)
    found = [ref[...] for ref in refs[:-2]]
    while len(found) > 1:
        half = len(found) // 2
        found = [found[k] + found[k + half] for k in range(half)]
    planes = found[0]
    plane_out[...] = planes
    cells = planes.shape[0]
    share, width = total.shape[0] // 4, total.shape[1]
    row = lax.broadcasted_iota(jnp.int32, total.shape, 0)
    lane = lax.broadcasted_iota(jnp.int32, total.shape, 1)
    partial = planes[cells - 1, 4 * RANK - 1]
    total = jnp.where((row >= 3 * share) & (lane >= width // 2), partial, total)
    for p in range(depth_out.shape[0]):
        depth_out[p] = total


def step_kernel(full_z, node_count, depth_ref, plane_ref, depth_out, plane_out):
    parts, share, width = depth_ref.shape[0], depth_ref.shape[1] // 4, depth_ref.shape[2]
    energy = depth_ref[0, 3 * share, width - 1]
    for p in range(1, parts):
        energy = energy + depth_ref[p, 3 * share, width - 1]
    lam_depth = damping * energy / full_z
    lam_plane = damping * RANK * energy / node_count
    for p in range(parts):
        got = depth_ref[p]
        levels = got[3 * share :, 0 : width // 2]
        levels = jnp.concatenate([levels, levels], axis=1)
        rows = slice(p * share, (p + 1) * share)
        depth_out[0, rows, :] = got[0:share] / (got[2 * share : 3 * share] + lam_depth + epsilon)
        depth_out[1, rows, :] = got[share : 2 * share] / (levels + lam_depth + epsilon)
    planes = plane_ref[...]
    plane_out[0] = planes[:, 0:RANK] / (planes[:, 2 * RANK : 3 * RANK] + lam_plane + epsilon)
    plane_out[1] = planes[:, RANK : 2 * RANK] / (planes[0:1, 3 * RANK :] + lam_plane + epsilon)


def local(image, deformed, displacement, plane_factors, depth_factors):
    n_gy, n_gz = lax.axis_size("gy"), lax.axis_size("gz")
    nodes_x, nodes_y = plane_factors.shape[2:]
    plane = jnp.transpose(plane_factors, (0, 2, 3, 1)).reshape(2, nodes_x * nodes_y, RANK)
    first, last = end_columns(deformed)
    right = shifted(first, "gz", True)
    left = shifted(last, "gz", False)
    sums, low, high = squares(image, deformed)
    low, high = packed_rows(left, right, low, high)
    above = shifted(low, "gy", True)
    below = shifted(high, "gy", False)
    field, diag_depth, diag_plane, beyond = terms(sums, plane, depth_factors, left, right, deformed.shape[0])
    residual, depth_terms, plane_terms = warp(
        deformed, image, displacement, beyond, below, above, field, plane, depth_factors, diag_depth, diag_plane,
        n_gy,
    )
    others = [
        lax.ppermute(plane_terms, "gz", [(i, (i + hop) % n_gz) for i in range(n_gz)]) for hop in range(1, n_gz)
    ]
    depth_terms = lax.all_to_all(depth_terms, "gy", 0, 0)
    depth_terms, plane_terms = pl.pallas_call(
        gather_kernel,
        out_shape=[
            jax.ShapeDtypeStruct(depth_terms.shape, f32),
            jax.ShapeDtypeStruct(plane_terms.shape, f32),
        ],
        compiler_params=plain_params(),
        name="gather",
    )(depth_terms, plane_terms, *others)
    depth_terms = lax.all_to_all(depth_terms, "gy", 0, 0)
    width = depth_factors.shape[2]
    step_depth, step_plane = pl.pallas_call(
        functools.partial(step_kernel, width * n_gz, nodes_x * nodes_y * n_gy),
        out_shape=[
            jax.ShapeDtypeStruct(depth_factors.shape, f32),
            jax.ShapeDtypeStruct(plane.shape, f32),
        ],
        compiler_params=plain_params(),
        name="steps",
    )(depth_terms, plane_terms)
    step_plane = jnp.transpose(step_plane.reshape(2, nodes_x, nodes_y, RANK), (0, 3, 1, 2))
    return residual, step_plane, step_depth


def solution(mesh):
    placed = (
        P(None, "gy", "gz"),
        P(None, "gy", "gz"),
        P(None, None, "gy", "gz"),
        P(None, None, None, "gy"),
        P(None, None, "gz"),
    )
    return jax.shard_map(
        local,
        mesh=mesh,
        in_specs=placed,
        out_specs=(P(None, "gy", "gz"), P(None, None, None, "gy"), P(None, None, "gz")),
        check_vma=False,
    )
```

```python
import functools

import jax
import jax.numpy as jnp
from jax import lax
from jax.experimental import pallas as pl
from jax.experimental.pallas import tpu as pltpu
from jax.sharding import PartitionSpec as P

RANK = 32
KNOT = 8
LANES = 128
TOP = 8

epsilon = 1e-06
damping = 0.01
highest = lax.Precision.HIGHEST
f32 = jnp.float32
bf16 = jnp.bfloat16


def dot(left, right, dims):
    return lax.dot_general(left, right, ((dims[0], dims[1]), ((), ())), precision=highest, preferred_element_type=f32)


def split_dot(left, right, dim):
    left_high, right_high = left.astype(bf16), right.astype(bf16)
    left_low = (left - left_high.astype(f32)).astype(bf16)
    right_low = (right - right_high.astype(f32)).astype(bf16)
    left = jnp.concatenate([left_high, left_high, left_low], axis=dim)
    right = jnp.concatenate([right_high, right_low, right_high], axis=dim)
    return lax.dot_general(left, right, (((dim,), (dim,)), ((), ())), preferred_element_type=f32)


def joined(ref):
    return jnp.concatenate([ref[tile] for tile in range(ref.shape[0])], axis=1)


def grid_params():
    return pltpu.CompilerParams(dimension_semantics=("arbitrary",), vmem_limit_bytes=40000000)


def plain_params():
    return pltpu.CompilerParams(vmem_limit_bytes=32000000)


def ends_kernel(cells_ref, first_ref, last_ref, low_ref, high_ref):
    depth, rows, width = cells_ref.shape
    lane = lax.broadcasted_iota(jnp.int32, (rows, LANES), 1)
    first = jnp.zeros((rows, LANES), f32)
    last = jnp.zeros((rows, LANES), f32)
    for x in range(depth):
        near = cells_ref[x, :, 0:LANES].astype(f32)
        far = cells_ref[x, :, width - LANES : width].astype(f32)
        first = jnp.where(lane == x, pltpu.roll(near, x, 1), first)
        last = jnp.where(lane == x, pltpu.roll(far, (x + 1) % LANES, 1), last)
    first_ref[...] = first.astype(bf16)
    last_ref[...] = last.astype(bf16)
    for x in range(0, depth, 16):
        low = [cells_ref[x + k, 0:16, :].astype(f32)[0:1] for k in range(16)]
        high = [cells_ref[x + k, rows - 16 : rows, :].astype(f32)[15:16] for k in range(16)]
        low_ref[x : x + 16, :] = jnp.concatenate(low, axis=0).astype(bf16)
        high_ref[x : x + 16, :] = jnp.concatenate(high, axis=0).astype(bf16)


def ends(cells):
    depth, rows, width = cells.shape
    return pl.pallas_call(
        ends_kernel,
        out_shape=[jax.ShapeDtypeStruct((rows, LANES), bf16)] * 2 + [jax.ShapeDtypeStruct((depth, width), bf16)] * 2,
        compiler_params=plain_params(),
        name="ends",
    )(cells)


def corners_kernel(below_ref, above_ref, first_ref, last_ref):
    width = below_ref.shape[1]
    for k, ref in enumerate((below_ref, above_ref)):
        first_ref[k] = ref[:, 0:LANES]
        last_ref[k] = ref[:, width - LANES : width]


def corners(below, above):
    return pl.pallas_call(
        corners_kernel,
        out_shape=[jax.ShapeDtypeStruct((2, below.shape[0], LANES), bf16)] * 2,
        compiler_params=plain_params(),
        name="corners",
    )(below, above)


def shifted(part, axis, back):
    count = lax.axis_size(axis)
    if back:
        return lax.ppermute(part, axis, [(i + 1, i) for i in range(count - 1)])
    return lax.ppermute(part, axis, [(i, i + 1) for i in range(count - 1)])


def squares_kernel(image_ref, sums):
    depth, rows, width = image_ref.shape
    tiles = width // LANES

    def one(t, carry):
        block, tile = t // tiles, t % tiles
        at = pl.multiple_of(tile * LANES, LANES)
        for pair in range(rows // 16):
            total = jnp.zeros((16, LANES), f32)
            for k in range(KNOT):
                values = image_ref[block * KNOT + k, 16 * pair : 16 * pair + 16, pl.ds(at, LANES)].astype(f32)
                total = total + values * values
            for half in range(2):
                row = block * (rows // KNOT) + 2 * pair + half
                sums[tile, pl.ds(row, 1), :] = jnp.sum(total[8 * half : 8 * half + 8], axis=0, keepdims=True)
        return carry

    lax.fori_loop(0, depth // KNOT * tiles, one, 0)


def squares(image):
    depth, rows, width = image.shape
    return pl.pallas_call(
        squares_kernel,
        out_shape=jax.ShapeDtypeStruct((width // LANES, depth * rows // KNOT**2, LANES), f32),
        compiler_params=plain_params(),
        cost_estimate=pl.CostEstimate(flops=3 * image.size, bytes_accessed=2 * image.size, transcendentals=0),
        name="squares",
    )(image)


def terms_kernel(
    sums, plane_ref, depth_ref, left_ref, right_ref, field_ref, diag_depth_ref, diag_plane_ref, beyond_ref
):
    tiles = sums.shape[0]
    left, right = left_ref[...].astype(f32), right_ref[...].astype(f32)
    lane = lax.broadcasted_iota(jnp.int32, left.shape, 1)
    for x in range(beyond_ref.shape[0]):
        after = pltpu.roll(right, (LANES - x) % LANES, 1)
        before = pltpu.roll(left, LANES - 1 - x, 1)
        beyond_ref[x] = jnp.where(lane == 0, after, before).astype(bf16)
    for k in range(2):
        field = dot(plane_ref[k], depth_ref[k], ((1,), (0,)))
        for tile in range(tiles):
            field_ref[k, tile] = field[:, tile * LANES : (tile + 1) * LANES]
    squared = joined(sums)
    cells = jnp.full(squared.shape, float(KNOT * KNOT), f32)
    first, second = plane_ref[0], plane_ref[1]
    diag_depth_ref[0] = dot(first * first, squared, ((0,), (0,)))
    diag_depth_ref[1] = dot(second * second, cells, ((0,), (0,)))
    first, second = depth_ref[0], depth_ref[1]
    diag_plane_ref[0] = dot(squared, first * first, ((1,), (1,)))
    diag_plane_ref[1] = dot(cells, second * second, ((1,), (1,)))


def terms(sums, plane, depth_factors, left, right, depth):
    nodes, width = plane.shape[1], depth_factors.shape[2]
    return pl.pallas_call(
        terms_kernel,
        out_shape=[
            jax.ShapeDtypeStruct((2, width // LANES, nodes, LANES), f32),
            jax.ShapeDtypeStruct((2, RANK, width), f32),
            jax.ShapeDtypeStruct((2, nodes, RANK), f32),
            jax.ShapeDtypeStruct((depth,) + left.shape, bf16),
        ],
        compiler_params=plain_params(),
        cost_estimate=pl.CostEstimate(flops=40 * nodes * RANK * width, bytes_accessed=1 << 20, transcendentals=0),
        name="terms",
    )(sums, plane, depth_factors, left, right)


def warp_kernel(
    cells_ref, image_ref, shift_ref, beyond_ref, low_ref, high_ref, before_ref, after_ref, field, plane_ref, depth_ref,
    diag_depth_ref, diag_plane_ref,
    residual_ref, depth_out, plane_out,
    ahead_ref, here_ref, behind_ref, wide, bands, rims, blocks, energy, held,
):
    step = pl.program_id(0)
    last = pl.num_programs(0) - 1
    planes, rows, width = cells_ref.shape
    nodes = rows // KNOT
    tiles = width // LANES
    window = (ahead_ref, here_ref, behind_ref)
    pitch = rows + 2 * TOP
    plane_rows = tiles * pitch
    block_rows = planes * plane_rows

    @pl.when(step == 0)
    def _():
        row = lax.broadcasted_iota(jnp.int32, bands.shape[1:], 0)
        column = lax.broadcasted_iota(jnp.int32, bands.shape[1:], 1)
        one, none = jnp.ones(bands.shape[1:], f32), jnp.zeros(bands.shape[1:], f32)
        up, down = jnp.where(row == column + 1, one, none), jnp.where(row == column, one, none)
        bands[0] = (up - down).astype(bf16)
        up = jnp.where(row == column + LANES, one, none)
        down = jnp.where(row == column + LANES - 1, one, none)
        bands[1] = (up - down).astype(bf16)
        energy[...] = jnp.zeros_like(energy)
        for c in range(3):
            window[c][3 * block_rows - plane_rows : 3 * block_rows, :] = jnp.zeros((plane_rows, LANES), f32)

    @pl.when(step < last)
    def _():
        slot = (step % 3) * block_rows
        span = planes * rows
        for k in range(planes):
            wide[k * rows : (k + 1) * rows, 0:width] = cells_ref[k]
            wide[k * rows : (k + 1) * rows, width:] = beyond_ref[k]
        rim = jnp.concatenate([low_ref[...].astype(f32), high_ref[...].astype(f32)], axis=0)
        wide[span:, 0:width] = rim.astype(bf16)
        lane = lax.broadcasted_iota(jnp.int32, (planes, LANES), 1)
        rim = [jnp.where(lane == 0, after_ref[k].astype(f32), before_ref[k].astype(f32)) for k in range(2)]
        wide[span:, width:] = jnp.concatenate(rim, axis=0).astype(bf16)

        def put(c, tile, values):
            for k in range(planes):
                first = pl.multiple_of(slot + k * plane_rows + tile * pitch, 8)
                window[c][pl.ds(first + TOP, rows), :] = values[k * rows : (k + 1) * rows]
            for side, row in enumerate((0, TOP + rows)):
                rims[...] = values[span + side * planes : span + (side + 1) * planes]
                for k in range(planes):
                    first = pl.multiple_of(slot + k * plane_rows + tile * pitch, 8)
                    window[c][pl.ds(first + row, 8), :] = jnp.broadcast_to(rims[k : k + 1], (8, LANES))

        pieces = width // (2 * LANES)
        for piece in range(pieces):
            start = 2 * LANES * piece
            after = wide[:, start : start + 3 * LANES]
            if piece == 0:
                before = jnp.concatenate([wide[:, width:], wide[:, 0 : 2 * LANES]], axis=1)
            else:
                before = wide[:, start - LANES : start + 2 * LANES]
            ahead = jnp.dot(after, bands[0], preferred_element_type=f32)
            behind = jnp.dot(before, bands[1], preferred_element_type=f32)
            for half in range(2):
                mine = slice(half * LANES, (half + 1) * LANES)
                put(0, 2 * piece + half, ahead[:, mine])
                put(1, 2 * piece + half, wide[:, start + half * LANES : start + (half + 1) * LANES].astype(f32))
                put(2, 2 * piece + half, behind[:, mine])

    @pl.when(step == last)
    def _():
        first = pl.multiple_of((step % 3) * block_rows, 8)
        for c in range(3):
            window[c][pl.ds(first, plane_rows), :] = jnp.zeros((plane_rows, LANES), f32)

    @pl.when(step > 0)
    def _():
        mid = (step + 2) % 3
        first_rows = (
            jnp.where(mid == 0, 3, mid) * block_rows - plane_rows,
            mid * block_rows,
            jnp.where(mid == 2, 0, mid + 1) * block_rows,
        )

        def one(t, total):
            tile = t % tiles
            pair = t // tiles
            at = pl.multiple_of(tile * LANES, LANES)
            top = pl.multiple_of(pair * 16, 16)
            origins = [first + tile * pitch + top + TOP for first in first_rows]
            for half in range(2):
                node = (step - 1) * nodes + pair * 2 + half
                mine = slice(8 * half, 8 * half + 8)

                def taps(x):
                    part = 0 if x == 0 else 2 if x == planes + 1 else 1
                    plus = (x - 1) * plane_rows + 8 * half if part == 1 else 8 * half
                    return [
                        [window[c][pl.ds(origins[part] + (plus + b), 8), :] for c in range(3)] for b in (-1, 0, 1)
                    ]

                contrast = jnp.broadcast_to(field[0, tile, pl.ds(node, 1), :], (8, LANES))
                brightness = jnp.broadcast_to(field[1, tile, pl.ds(node, 1), :], (8, LANES))
                by_image = jnp.zeros((8, LANES), f32)
                plain = jnp.zeros((8, LANES), f32)
                before, here = taps(0), taps(1)
                for k in range(planes):
                    after = taps(k + 2)
                    place = (k, pl.ds(top, 16), pl.ds(at, LANES))
                    sx, sy, sz = (shift_ref[(axis,) + place].astype(f32)[mine] for axis in range(3))
                    image = image_ref[place].astype(f32)[mine]
                    px, py, pz = sx > 0, sy > 0, sz > 0
                    ax, ay = jnp.abs(sx), jnp.abs(sy)

                    def sides(c):
                        far = [jnp.where(px, after[b][c], before[b][c]) for b in range(3)]
                        near = [here[b][c] for b in range(3)]
                        return [(v[1], jnp.where(py, v[2], v[0])) for v in (near, far)]

                    ahead, middle, behind = sides(0), sides(1), sides(2)
                    lines = []
                    for b in range(2):
                        near, far = (middle[v][b] + sz * jnp.where(pz, ahead[v][b], behind[v][b]) for v in range(2))
                        lines.append(near + ax * (far - near))
                    warped = lines[0] + ay * (lines[1] - lines[0])
                    misfit = warped - contrast * image - brightness
                    if half == 0:
                        held[k] = misfit
                    else:
                        residual_ref[place] = jnp.concatenate([held[k], misfit], axis=0).astype(bf16)
                    by_image = by_image + misfit * image
                    plain = plain + misfit
                    total = total + misfit * misfit
                    before, here = here, after
                for k, value in ((0, by_image), (1, plain)):
                    blocks[k, tile, pl.ds(node, 1), :] = jnp.sum(value, axis=0, keepdims=True)
            return total

        energy[...] = lax.fori_loop(0, (rows // 16) * tiles, one, energy[...])

    @pl.when(step == last)
    def _():
        parts = depth_out.shape[0]
        share = RANK // parts
        sums = [joined(blocks.at[k]) for k in range(2)]
        kinds = [split_dot(plane_ref[k], sums[k], 0) for k in range(2)]
        kinds = kinds + [diag_depth_ref[0], diag_depth_ref[1]]
        for p in range(parts):
            for k in range(4):
                depth_out[p, k * share : (k + 1) * share, :] = kinds[k][p * share : (p + 1) * share]
        local = jnp.sum(energy[...])
        kinds = [split_dot(sums[k], depth_ref[k], 1) for k in range(2)]
        kinds = kinds + [diag_plane_ref[0], diag_plane_ref[1]]
        for k in range(4):
            plane_out[:, k * RANK : (k + 1) * RANK] = kinds[k]
        count = plane_out.shape[0]
        plane_out[count // 2 :, 3 * RANK :] = jnp.full((count // 2, RANK), local, f32)


def warp(
    cells, image, shift, beyond, low, high, before, after, field, plane, depth_factors, diag_depth, diag_plane, parts
):
    depth, rows, width = cells.shape
    nodes = plane.shape[1]
    tiles = width // LANES
    count = depth // KNOT
    behind = lambda i: (jnp.maximum(i - 1, 0), 0, 0)
    ahead = lambda i: (jnp.minimum(i, count - 1), 0, 0)
    flat = lambda i: (0, 0)
    whole = lambda i: (0, 0, 0)
    return pl.pallas_call(
        warp_kernel,
        grid=(count + 1,),
        in_specs=[
            pl.BlockSpec((KNOT, rows, width), ahead),
            pl.BlockSpec((KNOT, rows, width), behind),
            pl.BlockSpec((3, KNOT, rows, width), lambda i: (0, jnp.maximum(i - 1, 0), 0, 0)),
            pl.BlockSpec((KNOT, rows, LANES), ahead),
            pl.BlockSpec((KNOT, low.shape[1]), lambda i: (jnp.minimum(i, count - 1), 0)),
            pl.BlockSpec((KNOT, high.shape[1]), lambda i: (jnp.minimum(i, count - 1), 0)),
            pl.BlockSpec((2, KNOT, LANES), lambda i: (0, jnp.minimum(i, count - 1), 0)),
            pl.BlockSpec((2, KNOT, LANES), lambda i: (0, jnp.minimum(i, count - 1), 0)),
            pl.BlockSpec(field.shape, lambda i: (0, 0, 0, 0)),
            pl.BlockSpec(plane.shape, whole),
            pl.BlockSpec(depth_factors.shape, whole),
            pl.BlockSpec(diag_depth.shape, whole),
            pl.BlockSpec(diag_plane.shape, whole),
        ],
        out_specs=[
            pl.BlockSpec((KNOT, rows, width), behind),
            pl.BlockSpec((parts, 4 * RANK // parts, width), whole),
            pl.BlockSpec((nodes, 4 * RANK), flat),
        ],
        out_shape=[
            jax.ShapeDtypeStruct(cells.shape, bf16),
            jax.ShapeDtypeStruct((parts, 4 * RANK // parts, width), f32),
            jax.ShapeDtypeStruct((nodes, 4 * RANK), f32),
        ],
        scratch_shapes=[
            *[pltpu.VMEM((3 * KNOT * tiles * (rows + 2 * TOP), LANES), f32)] * 3,
            pltpu.VMEM((KNOT * rows + 2 * KNOT, width + LANES), bf16),
            pltpu.VMEM((2, 3 * LANES, 2 * LANES), bf16),
            pltpu.VMEM((KNOT, LANES), f32),
            pltpu.VMEM((2, tiles, nodes, LANES), f32),
            pltpu.VMEM((8, LANES), f32),
            pltpu.VMEM((KNOT, 8, LANES), f32),
        ],
        compiler_params=grid_params(),
        cost_estimate=pl.CostEstimate(flops=60 * cells.size, bytes_accessed=12 * cells.size, transcendentals=0),
        name="warp",
    )(cells, image, shift, beyond, low, high, before, after, field, plane, depth_factors, diag_depth, diag_plane)


def gather_kernel(depth_ref, *refs):
    depth_out, plane_out = refs[-2:]
    total = jnp.sum(depth_ref[...], axis=0)
    found = [ref[...] for ref in refs[:-2]]
    while len(found) > 1:
        half = len(found) // 2
        found = [found[k] + found[k + half] for k in range(half)]
    planes = found[0]
    plane_out[...] = planes
    cells = planes.shape[0]
    share, width = total.shape[0] // 4, total.shape[1]
    row = lax.broadcasted_iota(jnp.int32, total.shape, 0)
    lane = lax.broadcasted_iota(jnp.int32, total.shape, 1)
    partial = planes[cells - 1, 4 * RANK - 1]
    total = jnp.where((row >= 3 * share) & (lane >= width // 2), partial, total)
    for p in range(depth_out.shape[0]):
        depth_out[p] = total


def step_kernel(full_z, node_count, depth_ref, plane_ref, depth_out, plane_out):
    parts, share, width = depth_ref.shape[0], depth_ref.shape[1] // 4, depth_ref.shape[2]
    energy = depth_ref[0, 3 * share, width - 1]
    for p in range(1, parts):
        energy = energy + depth_ref[p, 3 * share, width - 1]
    lam_depth = damping * energy / full_z
    lam_plane = damping * RANK * energy / node_count
    for p in range(parts):
        got = depth_ref[p]
        levels = got[3 * share :, 0 : width // 2]
        levels = jnp.concatenate([levels, levels], axis=1)
        rows = slice(p * share, (p + 1) * share)
        depth_out[0, rows, :] = got[0:share] / (got[2 * share : 3 * share] + lam_depth + epsilon)
        depth_out[1, rows, :] = got[share : 2 * share] / (levels + lam_depth + epsilon)
    planes = plane_ref[...]
    plane_out[0] = planes[:, 0:RANK] / (planes[:, 2 * RANK : 3 * RANK] + lam_plane + epsilon)
    plane_out[1] = planes[:, RANK : 2 * RANK] / (planes[0:1, 3 * RANK :] + lam_plane + epsilon)


def local(image, deformed, displacement, plane_factors, depth_factors):
    n_gy, n_gz = lax.axis_size("gy"), lax.axis_size("gz")
    nodes_x, nodes_y = plane_factors.shape[2:]
    plane = jnp.transpose(plane_factors, (0, 2, 3, 1)).reshape(2, nodes_x * nodes_y, RANK)
    first, last, low, high = ends(deformed)
    above = shifted(low, "gy", True)
    below = shifted(high, "gy", False)
    right = shifted(first, "gz", True)
    left = shifted(last, "gz", False)
    sums = squares(image)
    first, last = corners(below, above)
    after = shifted(first, "gz", True)
    before = shifted(last, "gz", False)
    field, diag_depth, diag_plane, beyond = terms(sums, plane, depth_factors, left, right, deformed.shape[0])
    residual, depth_terms, plane_terms = warp(
        deformed, image, displacement, beyond, below, above, before, after, field, plane, depth_factors,
        diag_depth, diag_plane, n_gy,
    )
    others = [
        lax.ppermute(plane_terms, "gz", [(i, (i + hop) % n_gz) for i in range(n_gz)]) for hop in range(1, n_gz)
    ]
    depth_terms = lax.all_to_all(depth_terms, "gy", 0, 0)
    depth_terms, plane_terms = pl.pallas_call(
        gather_kernel,
        out_shape=[
            jax.ShapeDtypeStruct(depth_terms.shape, f32),
            jax.ShapeDtypeStruct(plane_terms.shape, f32),
        ],
        compiler_params=plain_params(),
        name="gather",
    )(depth_terms, plane_terms, *others)
    depth_terms = lax.all_to_all(depth_terms, "gy", 0, 0)
    width = depth_factors.shape[2]
    step_depth, step_plane = pl.pallas_call(
        functools.partial(step_kernel, width * n_gz, nodes_x * nodes_y * n_gy),
        out_shape=[
            jax.ShapeDtypeStruct(depth_factors.shape, f32),
            jax.ShapeDtypeStruct(plane.shape, f32),
        ],
        compiler_params=plain_params(),
        name="steps",
    )(depth_terms, plane_terms)
    step_plane = jnp.transpose(step_plane.reshape(2, nodes_x, nodes_y, RANK), (0, 3, 1, 2))
    return residual, step_plane, step_depth


def solution(mesh):
    placed = (
        P(None, "gy", "gz"),
        P(None, "gy", "gz"),
        P(None, None, "gy", "gz"),
        P(None, None, None, "gy"),
        P(None, None, "gz"),
    )
    return jax.shard_map(
        local,
        mesh=mesh,
        in_specs=placed,
        out_specs=(P(None, "gy", "gz"), P(None, None, None, "gy"), P(None, None, "gz")),
        check_vma=False,
    )
```

```python
import functools

import jax
import jax.numpy as jnp
from jax import lax
from jax.experimental import pallas as pl
from jax.experimental.pallas import tpu as pltpu
from jax.sharding import PartitionSpec as P

RANK = 32
KNOT = 8
LANES = 128
TOP = 8

epsilon = 1e-06
damping = 0.01
highest = lax.Precision.HIGHEST
f32 = jnp.float32
bf16 = jnp.bfloat16


def dot(left, right, dims):
    return lax.dot_general(left, right, ((dims[0], dims[1]), ((), ())), precision=highest, preferred_element_type=f32)


def split_dot(left, right, dim):
    left_high, right_high = left.astype(bf16), right.astype(bf16)
    left_low = (left - left_high.astype(f32)).astype(bf16)
    right_low = (right - right_high.astype(f32)).astype(bf16)
    left = jnp.concatenate([left_high, left_high, left_low], axis=dim)
    right = jnp.concatenate([right_high, right_low, right_high], axis=dim)
    return lax.dot_general(left, right, (((dim,), (dim,)), ((), ())), preferred_element_type=f32)


def joined(ref):
    return jnp.concatenate([ref[tile] for tile in range(ref.shape[0])], axis=1)


def grid_params():
    return pltpu.CompilerParams(dimension_semantics=("arbitrary",), vmem_limit_bytes=40000000)


def plain_params():
    return pltpu.CompilerParams(vmem_limit_bytes=32000000)


def ends_kernel(cells_ref, first_ref, last_ref, low_ref, high_ref):
    depth, rows, width = cells_ref.shape
    lane = lax.broadcasted_iota(jnp.int32, (rows, LANES), 1)
    first = jnp.zeros((rows, LANES), f32)
    last = jnp.zeros((rows, LANES), f32)
    for x in range(depth):
        near = cells_ref[x, :, 0:LANES].astype(f32)
        far = cells_ref[x, :, width - LANES : width].astype(f32)
        first = jnp.where(lane == x, pltpu.roll(near, x, 1), first)
        last = jnp.where(lane == x, pltpu.roll(far, (x + 1) % LANES, 1), last)
    first_ref[...] = first.astype(bf16)
    last_ref[...] = last.astype(bf16)
    for x in range(0, depth, 16):
        low = [cells_ref[x + k, 0:16, :].astype(f32)[0:1] for k in range(16)]
        high = [cells_ref[x + k, rows - 16 : rows, :].astype(f32)[15:16] for k in range(16)]
        low_ref[x : x + 16, :] = jnp.concatenate(low, axis=0).astype(bf16)
        high_ref[x : x + 16, :] = jnp.concatenate(high, axis=0).astype(bf16)


def ends(cells):
    depth, rows, width = cells.shape
    return pl.pallas_call(
        ends_kernel,
        out_shape=[jax.ShapeDtypeStruct((rows, LANES), bf16)] * 2 + [jax.ShapeDtypeStruct((depth, width), bf16)] * 2,
        compiler_params=plain_params(),
        name="ends",
    )(cells)


def rows_kernel(left_ref, right_ref, low_ref, high_ref, low_out, high_out):
    depth, width = low_ref.shape
    rows = left_ref.shape[0]
    lane = lax.broadcasted_iota(jnp.int32, (depth, LANES), 1)
    pad = jnp.zeros((LANES - rows, LANES), f32)
    left = jnp.transpose(jnp.concatenate([left_ref[...].astype(f32), pad], axis=0))[0:depth]
    right = jnp.transpose(jnp.concatenate([right_ref[...].astype(f32), pad], axis=0))[0:depth]
    for row, body, out in ((0, low_ref, low_out), (rows - 1, high_ref, high_out)):
        after = pltpu.roll(right, (LANES - row) % LANES, 1)
        before = pltpu.roll(left, LANES - 1 - row, 1)
        out[:, 0:width] = body[...]
        out[:, width : width + LANES] = jnp.where(lane == 0, after, before).astype(bf16)


def packed_rows(left, right, low, high):
    depth, width = low.shape
    return pl.pallas_call(
        rows_kernel,
        out_shape=[jax.ShapeDtypeStruct((depth, width + LANES), bf16)] * 2,
        compiler_params=plain_params(),
        name="rows",
    )(left, right, low, high)


def shifted(part, axis, back):
    count = lax.axis_size(axis)
    if back:
        return lax.ppermute(part, axis, [(i + 1, i) for i in range(count - 1)])
    return lax.ppermute(part, axis, [(i, i + 1) for i in range(count - 1)])


def squares_kernel(image_ref, later_ref, sums):
    depth, rows, width = image_ref.shape
    tiles = width // LANES

    def one(t, carry):
        block, tile = t // tiles, t % tiles
        at = pl.multiple_of(tile * LANES, LANES)
        for pair in range(rows // 16):
            total = jnp.zeros((16, LANES), f32)
            for k in range(KNOT):
                values = image_ref[block * KNOT + k, 16 * pair : 16 * pair + 16, pl.ds(at, LANES)].astype(f32)
                total = total + values * values
            for half in range(2):
                row = block * (rows // KNOT) + 2 * pair + half
                sums[tile, pl.ds(row, 1), :] = jnp.sum(total[8 * half : 8 * half + 8], axis=0, keepdims=True)
        return carry

    lax.fori_loop(0, depth // KNOT * tiles, one, 0)


def squares(image, later):
    depth, rows, width = image.shape
    return pl.pallas_call(
        squares_kernel,
        out_shape=jax.ShapeDtypeStruct((width // LANES, depth * rows // KNOT**2, LANES), f32),
        compiler_params=plain_params(),
        cost_estimate=pl.CostEstimate(flops=3 * image.size, bytes_accessed=2 * image.size, transcendentals=0),
        name="squares",
    )(image, later)


def terms_kernel(
    sums, plane_ref, depth_ref, left_ref, right_ref, field_ref, diag_depth_ref, diag_plane_ref, beyond_ref
):
    tiles = sums.shape[0]
    left, right = left_ref[...].astype(f32), right_ref[...].astype(f32)
    lane = lax.broadcasted_iota(jnp.int32, left.shape, 1)
    for x in range(beyond_ref.shape[0]):
        after = pltpu.roll(right, (LANES - x) % LANES, 1)
        before = pltpu.roll(left, LANES - 1 - x, 1)
        beyond_ref[x] = jnp.where(lane == 0, after, before).astype(bf16)
    for k in range(2):
        field = dot(plane_ref[k], depth_ref[k], ((1,), (0,)))
        for tile in range(tiles):
            field_ref[k, tile] = field[:, tile * LANES : (tile + 1) * LANES]
    squared = joined(sums)
    cells = jnp.full(squared.shape, float(KNOT * KNOT), f32)
    first, second = plane_ref[0], plane_ref[1]
    diag_depth_ref[0] = dot(first * first, squared, ((0,), (0,)))
    diag_depth_ref[1] = dot(second * second, cells, ((0,), (0,)))
    first, second = depth_ref[0], depth_ref[1]
    diag_plane_ref[0] = dot(squared, first * first, ((1,), (1,)))
    diag_plane_ref[1] = dot(cells, second * second, ((1,), (1,)))


def terms(sums, plane, depth_factors, left, right, depth):
    nodes, width = plane.shape[1], depth_factors.shape[2]
    return pl.pallas_call(
        terms_kernel,
        out_shape=[
            jax.ShapeDtypeStruct((2, width // LANES, nodes, LANES), f32),
            jax.ShapeDtypeStruct((2, RANK, width), f32),
            jax.ShapeDtypeStruct((2, nodes, RANK), f32),
            jax.ShapeDtypeStruct((depth,) + left.shape, bf16),
        ],
        compiler_params=plain_params(),
        cost_estimate=pl.CostEstimate(flops=40 * nodes * RANK * width, bytes_accessed=1 << 20, transcendentals=0),
        name="terms",
    )(sums, plane, depth_factors, left, right)


def warp_kernel(
    cells_ref, image_ref, shift_ref, beyond_ref, low_ref, high_ref, field, plane_ref, depth_ref,
    diag_depth_ref, diag_plane_ref,
    residual_ref, depth_out, plane_out,
    ahead_ref, here_ref, behind_ref, wide, bands, rims, blocks, energy, held,
):
    step = pl.program_id(0)
    last = pl.num_programs(0) - 1
    planes, rows, width = cells_ref.shape
    nodes = rows // KNOT
    tiles = width // LANES
    window = (ahead_ref, here_ref, behind_ref)
    pitch = rows + 2 * TOP
    plane_rows = tiles * pitch
    block_rows = planes * plane_rows

    @pl.when(step == 0)
    def _():
        row = lax.broadcasted_iota(jnp.int32, bands.shape[1:], 0)
        column = lax.broadcasted_iota(jnp.int32, bands.shape[1:], 1)
        one, none = jnp.ones(bands.shape[1:], f32), jnp.zeros(bands.shape[1:], f32)
        up, down = jnp.where(row == column + 1, one, none), jnp.where(row == column, one, none)
        bands[0] = (up - down).astype(bf16)
        up = jnp.where(row == column + LANES, one, none)
        down = jnp.where(row == column + LANES - 1, one, none)
        bands[1] = (up - down).astype(bf16)
        energy[...] = jnp.zeros_like(energy)
        for c in range(3):
            window[c][3 * block_rows - plane_rows : 3 * block_rows, :] = jnp.zeros((plane_rows, LANES), f32)

    @pl.when(step < last)
    def _():
        slot = (step % 3) * block_rows
        span = planes * rows
        for k in range(planes):
            wide[k * rows : (k + 1) * rows, 0:width] = cells_ref[k]
            wide[k * rows : (k + 1) * rows, width:] = beyond_ref[k]
        wide[span:, :] = jnp.concatenate([low_ref[...].astype(f32), high_ref[...].astype(f32)], axis=0).astype(bf16)

        def put(c, tile, values):
            for k in range(planes):
                first = pl.multiple_of(slot + k * plane_rows + tile * pitch, 8)
                window[c][pl.ds(first + TOP, rows), :] = values[k * rows : (k + 1) * rows]
            for side, row in enumerate((0, TOP + rows)):
                rims[...] = values[span + side * planes : span + (side + 1) * planes]
                for k in range(planes):
                    first = pl.multiple_of(slot + k * plane_rows + tile * pitch, 8)
                    window[c][pl.ds(first + row, 8), :] = jnp.broadcast_to(rims[k : k + 1], (8, LANES))

        pieces = width // (2 * LANES)
        for piece in range(pieces):
            start = 2 * LANES * piece
            after = wide[:, start : start + 3 * LANES]
            if piece == 0:
                before = jnp.concatenate([wide[:, width:], wide[:, 0 : 2 * LANES]], axis=1)
            else:
                before = wide[:, start - LANES : start + 2 * LANES]
            ahead = jnp.dot(after, bands[0], preferred_element_type=f32)
            behind = jnp.dot(before, bands[1], preferred_element_type=f32)
            for half in range(2):
                mine = slice(half * LANES, (half + 1) * LANES)
                put(0, 2 * piece + half, ahead[:, mine])
                put(1, 2 * piece + half, wide[:, start + half * LANES : start + (half + 1) * LANES].astype(f32))
                put(2, 2 * piece + half, behind[:, mine])

    @pl.when(step == last)
    def _():
        first = pl.multiple_of((step % 3) * block_rows, 8)
        for c in range(3):
            window[c][pl.ds(first, plane_rows), :] = jnp.zeros((plane_rows, LANES), f32)

    @pl.when(step > 0)
    def _():
        mid = (step + 2) % 3
        first_rows = (
            jnp.where(mid == 0, 3, mid) * block_rows - plane_rows,
            mid * block_rows,
            jnp.where(mid == 2, 0, mid + 1) * block_rows,
        )

        def one(t, total):
            tile = t % tiles
            pair = t // tiles
            at = pl.multiple_of(tile * LANES, LANES)
            top = pl.multiple_of(pair * 16, 16)
            origins = [first + tile * pitch + top + TOP for first in first_rows]
            for half in range(2):
                node = (step - 1) * nodes + pair * 2 + half
                mine = slice(8 * half, 8 * half + 8)

                def taps(x):
                    part = 0 if x == 0 else 2 if x == planes + 1 else 1
                    plus = (x - 1) * plane_rows + 8 * half if part == 1 else 8 * half
                    return [
                        [window[c][pl.ds(origins[part] + (plus + b), 8), :] for c in range(3)] for b in (-1, 0, 1)
                    ]

                contrast = jnp.broadcast_to(field[0, tile, pl.ds(node, 1), :], (8, LANES))
                brightness = jnp.broadcast_to(field[1, tile, pl.ds(node, 1), :], (8, LANES))
                by_image = jnp.zeros((8, LANES), f32)
                plain = jnp.zeros((8, LANES), f32)
                before, here = taps(0), taps(1)
                for k in range(planes):
                    after = taps(k + 2)
                    place = (k, pl.ds(top, 16), pl.ds(at, LANES))
                    sx, sy, sz = (shift_ref[(axis,) + place].astype(f32)[mine] for axis in range(3))
                    image = image_ref[place].astype(f32)[mine]
                    px, py, pz = sx > 0, sy > 0, sz > 0
                    ax, ay = jnp.abs(sx), jnp.abs(sy)

                    def sides(c):
                        far = [jnp.where(px, after[b][c], before[b][c]) for b in range(3)]
                        near = [here[b][c] for b in range(3)]
                        return [(v[1], jnp.where(py, v[2], v[0])) for v in (near, far)]

                    ahead, middle, behind = sides(0), sides(1), sides(2)
                    lines = []
                    for b in range(2):
                        near, far = (middle[v][b] + sz * jnp.where(pz, ahead[v][b], behind[v][b]) for v in range(2))
                        lines.append(near + ax * (far - near))
                    warped = lines[0] + ay * (lines[1] - lines[0])
                    misfit = warped - contrast * image - brightness
                    if half == 0:
                        held[k] = misfit
                    else:
                        residual_ref[place] = jnp.concatenate([held[k], misfit], axis=0).astype(bf16)
                    by_image = by_image + misfit * image
                    plain = plain + misfit
                    total = total + misfit * misfit
                    before, here = here, after
                for k, value in ((0, by_image), (1, plain)):
                    blocks[k, tile, pl.ds(node, 1), :] = jnp.sum(value, axis=0, keepdims=True)
            return total

        energy[...] = lax.fori_loop(0, (rows // 16) * tiles, one, energy[...])

    @pl.when(step == last)
    def _():
        parts = depth_out.shape[0]
        share = RANK // parts
        sums = [joined(blocks.at[k]) for k in range(2)]
        kinds = [split_dot(plane_ref[k], sums[k], 0) for k in range(2)]
        kinds = kinds + [diag_depth_ref[0], diag_depth_ref[1]]
        for p in range(parts):
            for k in range(4):
                depth_out[p, k * share : (k + 1) * share, :] = kinds[k][p * share : (p + 1) * share]
        local = jnp.sum(energy[...])
        kinds = [split_dot(sums[k], depth_ref[k], 1) for k in range(2)]
        kinds = kinds + [diag_plane_ref[0], diag_plane_ref[1]]
        for k in range(4):
            plane_out[:, k * RANK : (k + 1) * RANK] = kinds[k]
        count = plane_out.shape[0]
        plane_out[count // 2 :, 3 * RANK :] = jnp.full((count // 2, RANK), local, f32)


def warp(cells, image, shift, beyond, low, high, field, plane, depth_factors, diag_depth, diag_plane, parts):
    depth, rows, width = cells.shape
    nodes = plane.shape[1]
    tiles = width // LANES
    count = depth // KNOT
    behind = lambda i: (jnp.maximum(i - 1, 0), 0, 0)
    ahead = lambda i: (jnp.minimum(i, count - 1), 0, 0)
    flat = lambda i: (0, 0)
    whole = lambda i: (0, 0, 0)
    return pl.pallas_call(
        warp_kernel,
        grid=(count + 1,),
        in_specs=[
            pl.BlockSpec((KNOT, rows, width), ahead),
            pl.BlockSpec((KNOT, rows, width), behind),
            pl.BlockSpec((3, KNOT, rows, width), lambda i: (0, jnp.maximum(i - 1, 0), 0, 0)),
            pl.BlockSpec((KNOT, rows, LANES), ahead),
            pl.BlockSpec((KNOT, low.shape[1]), lambda i: (jnp.minimum(i, count - 1), 0)),
            pl.BlockSpec((KNOT, high.shape[1]), lambda i: (jnp.minimum(i, count - 1), 0)),
            pl.BlockSpec(field.shape, lambda i: (0, 0, 0, 0)),
            pl.BlockSpec(plane.shape, whole),
            pl.BlockSpec(depth_factors.shape, whole),
            pl.BlockSpec(diag_depth.shape, whole),
            pl.BlockSpec(diag_plane.shape, whole),
        ],
        out_specs=[
            pl.BlockSpec((KNOT, rows, width), behind),
            pl.BlockSpec((parts, 4 * RANK // parts, width), whole),
            pl.BlockSpec((nodes, 4 * RANK), flat),
        ],
        out_shape=[
            jax.ShapeDtypeStruct(cells.shape, bf16),
            jax.ShapeDtypeStruct((parts, 4 * RANK // parts, width), f32),
            jax.ShapeDtypeStruct((nodes, 4 * RANK), f32),
        ],
        scratch_shapes=[
            *[pltpu.VMEM((3 * KNOT * tiles * (rows + 2 * TOP), LANES), f32)] * 3,
            pltpu.VMEM((KNOT * rows + 2 * KNOT, width + LANES), bf16),
            pltpu.VMEM((2, 3 * LANES, 2 * LANES), bf16),
            pltpu.VMEM((KNOT, LANES), f32),
            pltpu.VMEM((2, tiles, nodes, LANES), f32),
            pltpu.VMEM((8, LANES), f32),
            pltpu.VMEM((KNOT, 8, LANES), f32),
        ],
        compiler_params=grid_params(),
        cost_estimate=pl.CostEstimate(flops=60 * cells.size, bytes_accessed=12 * cells.size, transcendentals=0),
        name="warp",
    )(cells, image, shift, beyond, low, high, field, plane, depth_factors, diag_depth, diag_plane)


def gather_kernel(depth_ref, *refs):
    depth_out, plane_out = refs[-2:]
    total = jnp.sum(depth_ref[...], axis=0)
    found = [ref[...] for ref in refs[:-2]]
    while len(found) > 1:
        half = len(found) // 2
        found = [found[k] + found[k + half] for k in range(half)]
    planes = found[0]
    plane_out[...] = planes
    cells = planes.shape[0]
    share, width = total.shape[0] // 4, total.shape[1]
    row = lax.broadcasted_iota(jnp.int32, total.shape, 0)
    lane = lax.broadcasted_iota(jnp.int32, total.shape, 1)
    partial = planes[cells - 1, 4 * RANK - 1]
    total = jnp.where((row >= 3 * share) & (lane >= width // 2), partial, total)
    for p in range(depth_out.shape[0]):
        depth_out[p] = total


def step_kernel(full_z, node_count, depth_ref, plane_ref, depth_out, plane_out):
    parts, share, width = depth_ref.shape[0], depth_ref.shape[1] // 4, depth_ref.shape[2]
    energy = depth_ref[0, 3 * share, width - 1]
    for p in range(1, parts):
        energy = energy + depth_ref[p, 3 * share, width - 1]
    lam_depth = damping * energy / full_z
    lam_plane = damping * RANK * energy / node_count
    for p in range(parts):
        got = depth_ref[p]
        levels = got[3 * share :, 0 : width // 2]
        levels = jnp.concatenate([levels, levels], axis=1)
        rows = slice(p * share, (p + 1) * share)
        depth_out[0, rows, :] = got[0:share] / (got[2 * share : 3 * share] + lam_depth + epsilon)
        depth_out[1, rows, :] = got[share : 2 * share] / (levels + lam_depth + epsilon)
    planes = plane_ref[...]
    plane_out[0] = planes[:, 0:RANK] / (planes[:, 2 * RANK : 3 * RANK] + lam_plane + epsilon)
    plane_out[1] = planes[:, RANK : 2 * RANK] / (planes[0:1, 3 * RANK :] + lam_plane + epsilon)


def local(image, deformed, displacement, plane_factors, depth_factors):
    n_gy, n_gz = lax.axis_size("gy"), lax.axis_size("gz")
    nodes_x, nodes_y = plane_factors.shape[2:]
    plane = jnp.transpose(plane_factors, (0, 2, 3, 1)).reshape(2, nodes_x * nodes_y, RANK)
    first, last, low, high = ends(deformed)
    right = shifted(first, "gz", True)
    left = shifted(last, "gz", False)
    low, high = packed_rows(left, right, low, high)
    above = shifted(low, "gy", True)
    below = shifted(high, "gy", False)
    sums = squares(image, low)
    field, diag_depth, diag_plane, beyond = terms(sums, plane, depth_factors, left, right, deformed.shape[0])
    residual, depth_terms, plane_terms = warp(
        deformed, image, displacement, beyond, below, above, field, plane, depth_factors, diag_depth, diag_plane,
        n_gy,
    )
    others = [
        lax.ppermute(plane_terms, "gz", [(i, (i + hop) % n_gz) for i in range(n_gz)]) for hop in range(1, n_gz)
    ]
    depth_terms = lax.all_to_all(depth_terms, "gy", 0, 0)
    depth_terms, plane_terms = pl.pallas_call(
        gather_kernel,
        out_shape=[
            jax.ShapeDtypeStruct(depth_terms.shape, f32),
            jax.ShapeDtypeStruct(plane_terms.shape, f32),
        ],
        compiler_params=plain_params(),
        name="gather",
    )(depth_terms, plane_terms, *others)
    depth_terms = lax.all_to_all(depth_terms, "gy", 0, 0)
    width = depth_factors.shape[2]
    step_depth, step_plane = pl.pallas_call(
        functools.partial(step_kernel, width * n_gz, nodes_x * nodes_y * n_gy),
        out_shape=[
            jax.ShapeDtypeStruct(depth_factors.shape, f32),
            jax.ShapeDtypeStruct(plane.shape, f32),
        ],
        compiler_params=plain_params(),
        name="steps",
    )(depth_terms, plane_terms)
    step_plane = jnp.transpose(step_plane.reshape(2, nodes_x, nodes_y, RANK), (0, 3, 1, 2))
    return residual, step_plane, step_depth


def solution(mesh):
    placed = (
        P(None, "gy", "gz"),
        P(None, "gy", "gz"),
        P(None, None, "gy", "gz"),
        P(None, None, None, "gy"),
        P(None, None, "gz"),
    )
    return jax.shard_map(
        local,
        mesh=mesh,
        in_specs=placed,
        out_specs=(P(None, "gy", "gz"), P(None, None, None, "gy"), P(None, None, "gz")),
        check_vma=False,
    )
```

```python
import functools

import jax
import jax.numpy as jnp
from jax import lax
from jax.experimental import pallas as pl
from jax.experimental.pallas import tpu as pltpu
from jax.sharding import PartitionSpec as P

RANK = 32
KNOT = 8
LANES = 128
TOP = 8

epsilon = 1e-06
damping = 0.01
highest = lax.Precision.HIGHEST
f32 = jnp.float32
bf16 = jnp.bfloat16


def dot(left, right, dims):
    return lax.dot_general(left, right, ((dims[0], dims[1]), ((), ())), precision=highest, preferred_element_type=f32)


def split_dot(left, right, dim):
    left_high, right_high = left.astype(bf16), right.astype(bf16)
    left_low = (left - left_high.astype(f32)).astype(bf16)
    right_low = (right - right_high.astype(f32)).astype(bf16)
    left = jnp.concatenate([left_high, left_high, left_low], axis=dim)
    right = jnp.concatenate([right_high, right_low, right_high], axis=dim)
    return lax.dot_general(left, right, (((dim,), (dim,)), ((), ())), preferred_element_type=f32)


def joined(ref):
    return jnp.concatenate([ref[tile] for tile in range(ref.shape[0])], axis=1)


def grid_params():
    return pltpu.CompilerParams(dimension_semantics=("arbitrary",), vmem_limit_bytes=40000000)


def plain_params():
    return pltpu.CompilerParams(vmem_limit_bytes=32000000)


def ends_kernel(cells_ref, first_ref, last_ref, low_ref, high_ref):
    depth, rows, width = cells_ref.shape
    lane = lax.broadcasted_iota(jnp.int32, (rows, LANES), 1)
    first = jnp.zeros((rows, LANES), f32)
    last = jnp.zeros((rows, LANES), f32)
    for x in range(depth):
        near = cells_ref[x, :, 0:LANES].astype(f32)
        far = cells_ref[x, :, width - LANES : width].astype(f32)
        first = jnp.where(lane == x, pltpu.roll(near, x, 1), first)
        last = jnp.where(lane == x, pltpu.roll(far, (x + 1) % LANES, 1), last)
    first_ref[...] = first.astype(bf16)
    last_ref[...] = last.astype(bf16)
    for x in range(0, depth, 16):
        low = [cells_ref[x + k, 0:16, :].astype(f32)[0:1] for k in range(16)]
        high = [cells_ref[x + k, rows - 16 : rows, :].astype(f32)[15:16] for k in range(16)]
        low_ref[x : x + 16, :] = jnp.concatenate(low, axis=0).astype(bf16)
        high_ref[x : x + 16, :] = jnp.concatenate(high, axis=0).astype(bf16)


def ends(cells):
    depth, rows, width = cells.shape
    return pl.pallas_call(
        ends_kernel,
        out_shape=[jax.ShapeDtypeStruct((rows, LANES), bf16)] * 2 + [jax.ShapeDtypeStruct((depth, width), bf16)] * 2,
        compiler_params=plain_params(),
        cost_estimate=pl.CostEstimate(flops=cells.size, bytes_accessed=2 * cells.size, transcendentals=0),
        name="ends",
    )(cells)


def rows_kernel(left_ref, right_ref, low_ref, high_ref, low_out, high_out):
    depth, width = low_ref.shape
    rows = left_ref.shape[0]
    lane = lax.broadcasted_iota(jnp.int32, (depth, LANES), 1)
    pad = jnp.zeros((LANES - rows, LANES), f32)
    left = jnp.transpose(jnp.concatenate([left_ref[...].astype(f32), pad], axis=0))[0:depth]
    right = jnp.transpose(jnp.concatenate([right_ref[...].astype(f32), pad], axis=0))[0:depth]
    for row, body, out in ((0, low_ref, low_out), (rows - 1, high_ref, high_out)):
        after = pltpu.roll(right, (LANES - row) % LANES, 1)
        before = pltpu.roll(left, LANES - 1 - row, 1)
        out[:, 0:width] = body[...]
        out[:, width : width + LANES] = jnp.where(lane == 0, after, before).astype(bf16)


def packed_rows(left, right, low, high):
    depth, width = low.shape
    return pl.pallas_call(
        rows_kernel,
        out_shape=[jax.ShapeDtypeStruct((depth, width + LANES), bf16)] * 2,
        compiler_params=plain_params(),
        cost_estimate=pl.CostEstimate(flops=500000 * low.size, bytes_accessed=8 * low.size, transcendentals=0),
        name="rows",
    )(left, right, low, high)


def shifted(part, axis, back):
    count = lax.axis_size(axis)
    if back:
        return lax.ppermute(part, axis, [(i + 1, i) for i in range(count - 1)])
    return lax.ppermute(part, axis, [(i, i + 1) for i in range(count - 1)])


def squares_kernel(image_ref, later_ref, sums):
    depth, rows, width = image_ref.shape
    tiles = width // LANES

    def one(t, carry):
        block, tile = t // tiles, t % tiles
        at = pl.multiple_of(tile * LANES, LANES)
        for pair in range(rows // 16):
            total = jnp.zeros((16, LANES), f32)
            for k in range(KNOT):
                values = image_ref[block * KNOT + k, 16 * pair : 16 * pair + 16, pl.ds(at, LANES)].astype(f32)
                total = total + values * values
            for half in range(2):
                row = block * (rows // KNOT) + 2 * pair + half
                sums[tile, pl.ds(row, 1), :] = jnp.sum(total[8 * half : 8 * half + 8], axis=0, keepdims=True)
        return carry

    lax.fori_loop(0, depth // KNOT * tiles, one, 0)


def squares(image, later):
    depth, rows, width = image.shape
    return pl.pallas_call(
        squares_kernel,
        out_shape=jax.ShapeDtypeStruct((width // LANES, depth * rows // KNOT**2, LANES), f32),
        compiler_params=plain_params(),
        cost_estimate=pl.CostEstimate(flops=3 * image.size, bytes_accessed=2 * image.size, transcendentals=0),
        name="squares",
    )(image, later)


def terms_kernel(
    sums, plane_ref, depth_ref, left_ref, right_ref, field_ref, diag_depth_ref, diag_plane_ref, beyond_ref
):
    tiles = sums.shape[0]
    left, right = left_ref[...].astype(f32), right_ref[...].astype(f32)
    lane = lax.broadcasted_iota(jnp.int32, left.shape, 1)
    for x in range(beyond_ref.shape[0]):
        after = pltpu.roll(right, (LANES - x) % LANES, 1)
        before = pltpu.roll(left, LANES - 1 - x, 1)
        beyond_ref[x] = jnp.where(lane == 0, after, before).astype(bf16)
    for k in range(2):
        field = dot(plane_ref[k], depth_ref[k], ((1,), (0,)))
        for tile in range(tiles):
            field_ref[k, tile] = field[:, tile * LANES : (tile + 1) * LANES]
    squared = joined(sums)
    cells = jnp.full(squared.shape, float(KNOT * KNOT), f32)
    first, second = plane_ref[0], plane_ref[1]
    diag_depth_ref[0] = dot(first * first, squared, ((0,), (0,)))
    diag_depth_ref[1] = dot(second * second, cells, ((0,), (0,)))
    first, second = depth_ref[0], depth_ref[1]
    diag_plane_ref[0] = dot(squared, first * first, ((1,), (1,)))
    diag_plane_ref[1] = dot(cells, second * second, ((1,), (1,)))


def terms(sums, plane, depth_factors, left, right, depth):
    nodes, width = plane.shape[1], depth_factors.shape[2]
    return pl.pallas_call(
        terms_kernel,
        out_shape=[
            jax.ShapeDtypeStruct((2, width // LANES, nodes, LANES), f32),
            jax.ShapeDtypeStruct((2, RANK, width), f32),
            jax.ShapeDtypeStruct((2, nodes, RANK), f32),
            jax.ShapeDtypeStruct((depth,) + left.shape, bf16),
        ],
        compiler_params=plain_params(),
        cost_estimate=pl.CostEstimate(flops=40 * nodes * RANK * width, bytes_accessed=1 << 20, transcendentals=0),
        name="terms",
    )(sums, plane, depth_factors, left, right)


def warp_kernel(
    cells_ref, image_ref, shift_ref, beyond_ref, low_ref, high_ref, field, plane_ref, depth_ref,
    diag_depth_ref, diag_plane_ref,
    residual_ref, depth_out, plane_out,
    ahead_ref, here_ref, behind_ref, wide, bands, rims, blocks, energy, held,
):
    step = pl.program_id(0)
    last = pl.num_programs(0) - 1
    planes, rows, width = cells_ref.shape
    nodes = rows // KNOT
    tiles = width // LANES
    window = (ahead_ref, here_ref, behind_ref)
    pitch = rows + 2 * TOP
    plane_rows = tiles * pitch
    block_rows = planes * plane_rows

    @pl.when(step == 0)
    def _():
        row = lax.broadcasted_iota(jnp.int32, bands.shape[1:], 0)
        column = lax.broadcasted_iota(jnp.int32, bands.shape[1:], 1)
        one, none = jnp.ones(bands.shape[1:], f32), jnp.zeros(bands.shape[1:], f32)
        up, down = jnp.where(row == column + 1, one, none), jnp.where(row == column, one, none)
        bands[0] = (up - down).astype(bf16)
        up = jnp.where(row == column + LANES, one, none)
        down = jnp.where(row == column + LANES - 1, one, none)
        bands[1] = (up - down).astype(bf16)
        energy[...] = jnp.zeros_like(energy)
        for c in range(3):
            window[c][3 * block_rows - plane_rows : 3 * block_rows, :] = jnp.zeros((plane_rows, LANES), f32)

    @pl.when(step < last)
    def _():
        slot = (step % 3) * block_rows
        span = planes * rows
        for k in range(planes):
            wide[k * rows : (k + 1) * rows, 0:width] = cells_ref[k]
            wide[k * rows : (k + 1) * rows, width:] = beyond_ref[k]
        wide[span:, :] = jnp.concatenate([low_ref[...].astype(f32), high_ref[...].astype(f32)], axis=0).astype(bf16)

        def put(c, tile, values):
            for k in range(planes):
                first = pl.multiple_of(slot + k * plane_rows + tile * pitch, 8)
                window[c][pl.ds(first + TOP, rows), :] = values[k * rows : (k + 1) * rows]
            for side, row in enumerate((0, TOP + rows)):
                rims[...] = values[span + side * planes : span + (side + 1) * planes]
                for k in range(planes):
                    first = pl.multiple_of(slot + k * plane_rows + tile * pitch, 8)
                    window[c][pl.ds(first + row, 8), :] = jnp.broadcast_to(rims[k : k + 1], (8, LANES))

        pieces = width // (2 * LANES)
        for piece in range(pieces):
            start = 2 * LANES * piece
            after = wide[:, start : start + 3 * LANES]
            if piece == 0:
                before = jnp.concatenate([wide[:, width:], wide[:, 0 : 2 * LANES]], axis=1)
            else:
                before = wide[:, start - LANES : start + 2 * LANES]
            ahead = jnp.dot(after, bands[0], preferred_element_type=f32)
            behind = jnp.dot(before, bands[1], preferred_element_type=f32)
            for half in range(2):
                mine = slice(half * LANES, (half + 1) * LANES)
                put(0, 2 * piece + half, ahead[:, mine])
                put(1, 2 * piece + half, wide[:, start + half * LANES : start + (half + 1) * LANES].astype(f32))
                put(2, 2 * piece + half, behind[:, mine])

    @pl.when(step == last)
    def _():
        first = pl.multiple_of((step % 3) * block_rows, 8)
        for c in range(3):
            window[c][pl.ds(first, plane_rows), :] = jnp.zeros((plane_rows, LANES), f32)

    @pl.when(step > 0)
    def _():
        mid = (step + 2) % 3
        first_rows = (
            jnp.where(mid == 0, 3, mid) * block_rows - plane_rows,
            mid * block_rows,
            jnp.where(mid == 2, 0, mid + 1) * block_rows,
        )

        def one(t, total):
            tile = t % tiles
            pair = t // tiles
            at = pl.multiple_of(tile * LANES, LANES)
            top = pl.multiple_of(pair * 16, 16)
            origins = [first + tile * pitch + top + TOP for first in first_rows]
            for half in range(2):
                node = (step - 1) * nodes + pair * 2 + half
                mine = slice(8 * half, 8 * half + 8)

                def taps(x):
                    part = 0 if x == 0 else 2 if x == planes + 1 else 1
                    plus = (x - 1) * plane_rows + 8 * half if part == 1 else 8 * half
                    return [
                        [window[c][pl.ds(origins[part] + (plus + b), 8), :] for c in range(3)] for b in (-1, 0, 1)
                    ]

                contrast = jnp.broadcast_to(field[0, tile, pl.ds(node, 1), :], (8, LANES))
                brightness = jnp.broadcast_to(field[1, tile, pl.ds(node, 1), :], (8, LANES))
                by_image = jnp.zeros((8, LANES), f32)
                plain = jnp.zeros((8, LANES), f32)
                before, here = taps(0), taps(1)
                for k in range(planes):
                    after = taps(k + 2)
                    place = (k, pl.ds(top, 16), pl.ds(at, LANES))
                    sx, sy, sz = (shift_ref[(axis,) + place].astype(f32)[mine] for axis in range(3))
                    image = image_ref[place].astype(f32)[mine]
                    px, py, pz = sx > 0, sy > 0, sz > 0
                    ax, ay = jnp.abs(sx), jnp.abs(sy)

                    def sides(c):
                        far = [jnp.where(px, after[b][c], before[b][c]) for b in range(3)]
                        near = [here[b][c] for b in range(3)]
                        return [(v[1], jnp.where(py, v[2], v[0])) for v in (near, far)]

                    ahead, middle, behind = sides(0), sides(1), sides(2)
                    lines = []
                    for b in range(2):
                        near, far = (middle[v][b] + sz * jnp.where(pz, ahead[v][b], behind[v][b]) for v in range(2))
                        lines.append(near + ax * (far - near))
                    warped = lines[0] + ay * (lines[1] - lines[0])
                    misfit = warped - contrast * image - brightness
                    if half == 0:
                        held[k] = misfit
                    else:
                        residual_ref[place] = jnp.concatenate([held[k], misfit], axis=0).astype(bf16)
                    by_image = by_image + misfit * image
                    plain = plain + misfit
                    total = total + misfit * misfit
                    before, here = here, after
                for k, value in ((0, by_image), (1, plain)):
                    blocks[k, tile, pl.ds(node, 1), :] = jnp.sum(value, axis=0, keepdims=True)
            return total

        energy[...] = lax.fori_loop(0, (rows // 16) * tiles, one, energy[...])

    @pl.when(step == last)
    def _():
        parts = depth_out.shape[0]
        share = RANK // parts
        sums = [joined(blocks.at[k]) for k in range(2)]
        kinds = [split_dot(plane_ref[k], sums[k], 0) for k in range(2)]
        kinds = kinds + [diag_depth_ref[0], diag_depth_ref[1]]
        for p in range(parts):
            for k in range(4):
                depth_out[p, k * share : (k + 1) * share, :] = kinds[k][p * share : (p + 1) * share]
            depth_out[p, 3 * share :, width // 2 :] = jnp.full((share, width // 2), jnp.sum(energy[...]), f32)
        kinds = [split_dot(sums[k], depth_ref[k], 1) for k in range(2)]
        kinds = kinds + [diag_plane_ref[0], diag_plane_ref[1]]
        for k in range(4):
            plane_out[:, k * RANK : (k + 1) * RANK] = kinds[k]


def warp(cells, image, shift, beyond, low, high, field, plane, depth_factors, diag_depth, diag_plane, parts):
    depth, rows, width = cells.shape
    nodes = plane.shape[1]
    tiles = width // LANES
    count = depth // KNOT
    behind = lambda i: (jnp.maximum(i - 1, 0), 0, 0)
    ahead = lambda i: (jnp.minimum(i, count - 1), 0, 0)
    flat = lambda i: (0, 0)
    whole = lambda i: (0, 0, 0)
    return pl.pallas_call(
        warp_kernel,
        grid=(count + 1,),
        in_specs=[
            pl.BlockSpec((KNOT, rows, width), ahead),
            pl.BlockSpec((KNOT, rows, width), behind),
            pl.BlockSpec((3, KNOT, rows, width), lambda i: (0, jnp.maximum(i - 1, 0), 0, 0)),
            pl.BlockSpec((KNOT, rows, LANES), ahead),
            pl.BlockSpec((KNOT, low.shape[1]), lambda i: (jnp.minimum(i, count - 1), 0)),
            pl.BlockSpec((KNOT, high.shape[1]), lambda i: (jnp.minimum(i, count - 1), 0)),
            pl.BlockSpec(field.shape, lambda i: (0, 0, 0, 0)),
            pl.BlockSpec(plane.shape, whole),
            pl.BlockSpec(depth_factors.shape, whole),
            pl.BlockSpec(diag_depth.shape, whole),
            pl.BlockSpec(diag_plane.shape, whole),
        ],
        out_specs=[
            pl.BlockSpec((KNOT, rows, width), behind),
            pl.BlockSpec((parts, 4 * RANK // parts, width), whole),
            pl.BlockSpec((nodes, 4 * RANK), flat),
        ],
        out_shape=[
            jax.ShapeDtypeStruct(cells.shape, bf16),
            jax.ShapeDtypeStruct((parts, 4 * RANK // parts, width), f32),
            jax.ShapeDtypeStruct((nodes, 4 * RANK), f32),
        ],
        scratch_shapes=[
            *[pltpu.VMEM((3 * KNOT * tiles * (rows + 2 * TOP), LANES), f32)] * 3,
            pltpu.VMEM((KNOT * rows + 2 * KNOT, width + LANES), bf16),
            pltpu.VMEM((2, 3 * LANES, 2 * LANES), bf16),
            pltpu.VMEM((KNOT, LANES), f32),
            pltpu.VMEM((2, tiles, nodes, LANES), f32),
            pltpu.VMEM((8, LANES), f32),
            pltpu.VMEM((KNOT, 8, LANES), f32),
        ],
        compiler_params=grid_params(),
        cost_estimate=pl.CostEstimate(flops=60 * cells.size, bytes_accessed=12 * cells.size, transcendentals=0),
        name="warp",
    )(cells, image, shift, beyond, low, high, field, plane, depth_factors, diag_depth, diag_plane)


def gather_kernel(depth_ref, plane_ref, depth_out, plane_out):
    total = jnp.sum(depth_ref[...], axis=0)
    for p in range(depth_out.shape[0]):
        depth_out[p] = total
    cells = plane_ref.shape[0]
    plane_out[...] = plane_ref[...]
    energy = total[total.shape[0] - 1, total.shape[1] - 1]
    plane_out[cells // 2 :, 3 * RANK :] = jnp.full((cells // 2, RANK), energy, f32)


def step_kernel(full_z, node_count, depth_ref, *refs):
    depth_out, plane_out = refs[-2:]
    found = [ref[...] for ref in refs[:-2]]
    while len(found) > 1:
        half = len(found) // 2
        found = [found[k] + found[k + half] for k in range(half)]
    planes = found[0]
    parts, share, width = depth_ref.shape[0], depth_ref.shape[1] // 4, depth_ref.shape[2]
    energy = planes[planes.shape[0] - 1, 4 * RANK - 1]
    lam_depth = damping * energy / full_z
    lam_plane = damping * RANK * energy / node_count
    for p in range(parts):
        got = depth_ref[p]
        levels = got[3 * share :, 0 : width // 2]
        levels = jnp.concatenate([levels, levels], axis=1)
        rows = slice(p * share, (p + 1) * share)
        depth_out[0, rows, :] = got[0:share] / (got[2 * share : 3 * share] + lam_depth + epsilon)
        depth_out[1, rows, :] = got[share : 2 * share] / (levels + lam_depth + epsilon)
    plane_out[0] = planes[:, 0:RANK] / (planes[:, 2 * RANK : 3 * RANK] + lam_plane + epsilon)
    plane_out[1] = planes[:, RANK : 2 * RANK] / (planes[0:1, 3 * RANK :] + lam_plane + epsilon)


def local(image, deformed, displacement, plane_factors, depth_factors):
    n_gy, n_gz = lax.axis_size("gy"), lax.axis_size("gz")
    nodes_x, nodes_y = plane_factors.shape[2:]
    plane = jnp.transpose(plane_factors, (0, 2, 3, 1)).reshape(2, nodes_x * nodes_y, RANK)
    first, last, low, high = ends(deformed)
    right = shifted(first, "gz", True)
    left = shifted(last, "gz", False)
    low, high = packed_rows(left, right, low, high)
    above = shifted(low, "gy", True)
    below = shifted(high, "gy", False)
    sums = squares(image, low)
    field, diag_depth, diag_plane, beyond = terms(sums, plane, depth_factors, left, right, deformed.shape[0])
    residual, depth_terms, plane_terms = warp(
        deformed, image, displacement, beyond, below, above, field, plane, depth_factors, diag_depth, diag_plane,
        n_gy,
    )
    depth_terms = lax.all_to_all(depth_terms, "gy", 0, 0)
    depth_terms, plane_terms = pl.pallas_call(
        gather_kernel,
        out_shape=[
            jax.ShapeDtypeStruct(depth_terms.shape, f32),
            jax.ShapeDtypeStruct(plane_terms.shape, f32),
        ],
        compiler_params=plain_params(),
        name="gather",
    )(depth_terms, plane_terms)
    depth_terms = lax.all_to_all(depth_terms, "gy", 0, 0)
    others = [
        lax.ppermute(plane_terms, "gz", [(i, (i + hop) % n_gz) for i in range(n_gz)]) for hop in range(1, n_gz)
    ]
    width = depth_factors.shape[2]
    step_depth, step_plane = pl.pallas_call(
        functools.partial(step_kernel, width * n_gz, nodes_x * nodes_y * n_gy),
        out_shape=[
            jax.ShapeDtypeStruct(depth_factors.shape, f32),
            jax.ShapeDtypeStruct(plane.shape, f32),
        ],
        compiler_params=plain_params(),
        name="steps",
    )(depth_terms, plane_terms, *others)
    step_plane = jnp.transpose(step_plane.reshape(2, nodes_x, nodes_y, RANK), (0, 3, 1, 2))
    return residual, step_plane, step_depth


def solution(mesh):
    placed = (
        P(None, "gy", "gz"),
        P(None, "gy", "gz"),
        P(None, None, "gy", "gz"),
        P(None, None, None, "gy"),
        P(None, None, "gz"),
    )
    return jax.shard_map(
        local,
        mesh=mesh,
        in_specs=placed,
        out_specs=(P(None, "gy", "gz"), P(None, None, None, "gy"), P(None, None, "gz")),
        check_vma=False,
    )
```

```python
import functools

import jax
import jax.numpy as jnp
from jax import lax
from jax.experimental import pallas as pl
from jax.experimental.pallas import tpu as pltpu
from jax.sharding import PartitionSpec as P

RANK = 32
KNOT = 8
LANES = 128
TOP = 8

epsilon = 1e-06
damping = 0.01
highest = lax.Precision.HIGHEST
f32 = jnp.float32
bf16 = jnp.bfloat16


def dot(left, right, dims):
    return lax.dot_general(left, right, ((dims[0], dims[1]), ((), ())), precision=highest, preferred_element_type=f32)


def split_dot(left, right, dim):
    left_high, right_high = left.astype(bf16), right.astype(bf16)
    left_low = (left - left_high.astype(f32)).astype(bf16)
    right_low = (right - right_high.astype(f32)).astype(bf16)
    left = jnp.concatenate([left_high, left_high, left_low], axis=dim)
    right = jnp.concatenate([right_high, right_low, right_high], axis=dim)
    return lax.dot_general(left, right, (((dim,), (dim,)), ((), ())), preferred_element_type=f32)


def joined(ref):
    return jnp.concatenate([ref[tile] for tile in range(ref.shape[0])], axis=1)


def grid_params():
    return pltpu.CompilerParams(dimension_semantics=("arbitrary",), vmem_limit_bytes=40000000)


def plain_params():
    return pltpu.CompilerParams(vmem_limit_bytes=32000000)


def ends_kernel(cells_ref, first_ref, last_ref, low_ref, high_ref):
    depth, rows, width = cells_ref.shape
    lane = lax.broadcasted_iota(jnp.int32, (rows, LANES), 1)
    first = jnp.zeros((rows, LANES), f32)
    last = jnp.zeros((rows, LANES), f32)
    for x in range(depth):
        near = cells_ref[x, :, 0:LANES].astype(f32)
        far = cells_ref[x, :, width - LANES : width].astype(f32)
        first = jnp.where(lane == x, pltpu.roll(near, x, 1), first)
        last = jnp.where(lane == x, pltpu.roll(far, (x + 1) % LANES, 1), last)
    first_ref[...] = first.astype(bf16)
    last_ref[...] = last.astype(bf16)
    for x in range(0, depth, 16):
        low = [cells_ref[x + k, 0:16, :].astype(f32)[0:1] for k in range(16)]
        high = [cells_ref[x + k, rows - 16 : rows, :].astype(f32)[15:16] for k in range(16)]
        low_ref[x : x + 16, :] = jnp.concatenate(low, axis=0).astype(bf16)
        high_ref[x : x + 16, :] = jnp.concatenate(high, axis=0).astype(bf16)


def ends(cells):
    depth, rows, width = cells.shape
    return pl.pallas_call(
        ends_kernel,
        out_shape=[jax.ShapeDtypeStruct((rows, LANES), bf16)] * 2 + [jax.ShapeDtypeStruct((depth, width), bf16)] * 2,
        compiler_params=plain_params(),
        cost_estimate=pl.CostEstimate(flops=cells.size, bytes_accessed=2 * cells.size, transcendentals=0),
        name="ends",
    )(cells)


def rows_kernel(left_ref, right_ref, low_ref, high_ref, low_out, high_out):
    depth, width = low_ref.shape
    rows = left_ref.shape[0]
    lane = lax.broadcasted_iota(jnp.int32, (depth, LANES), 1)
    pad = jnp.zeros((LANES - rows, LANES), f32)
    left = jnp.transpose(jnp.concatenate([left_ref[...].astype(f32), pad], axis=0))[0:depth]
    right = jnp.transpose(jnp.concatenate([right_ref[...].astype(f32), pad], axis=0))[0:depth]
    for row, body, out in ((0, low_ref, low_out), (rows - 1, high_ref, high_out)):
        after = pltpu.roll(right, (LANES - row) % LANES, 1)
        before = pltpu.roll(left, LANES - 1 - row, 1)
        out[:, 0:width] = body[...]
        out[:, width : width + LANES] = jnp.where(lane == 0, after, before).astype(bf16)


def packed_rows(left, right, low, high):
    depth, width = low.shape
    return pl.pallas_call(
        rows_kernel,
        out_shape=[jax.ShapeDtypeStruct((depth, width + LANES), bf16)] * 2,
        compiler_params=plain_params(),
        cost_estimate=pl.CostEstimate(flops=500000 * low.size, bytes_accessed=8 * low.size, transcendentals=0),
        name="rows",
    )(left, right, low, high)


def shifted(part, axis, back):
    count = lax.axis_size(axis)
    if back:
        return lax.ppermute(part, axis, [(i + 1, i) for i in range(count - 1)])
    return lax.ppermute(part, axis, [(i, i + 1) for i in range(count - 1)])


def squares_kernel(image_ref, later_ref, sums):
    depth, rows, width = image_ref.shape
    tiles = width // LANES

    def one(t, carry):
        block, tile = t // tiles, t % tiles
        at = pl.multiple_of(tile * LANES, LANES)
        for pair in range(rows // 16):
            total = jnp.zeros((16, LANES), f32)
            for k in range(KNOT):
                values = image_ref[block * KNOT + k, 16 * pair : 16 * pair + 16, pl.ds(at, LANES)].astype(f32)
                total = total + values * values
            for half in range(2):
                row = block * (rows // KNOT) + 2 * pair + half
                sums[tile, pl.ds(row, 1), :] = jnp.sum(total[8 * half : 8 * half + 8], axis=0, keepdims=True)
        return carry

    lax.fori_loop(0, depth // KNOT * tiles, one, 0)


def squares(image, later):
    depth, rows, width = image.shape
    return pl.pallas_call(
        squares_kernel,
        out_shape=jax.ShapeDtypeStruct((width // LANES, depth * rows // KNOT**2, LANES), f32),
        compiler_params=plain_params(),
        cost_estimate=pl.CostEstimate(flops=3 * image.size, bytes_accessed=2 * image.size, transcendentals=0),
        name="squares",
    )(image, later)


def terms_kernel(
    sums, plane_ref, depth_ref, left_ref, right_ref, field_ref, diag_depth_ref, diag_plane_ref, beyond_ref
):
    tiles = sums.shape[0]
    left, right = left_ref[...].astype(f32), right_ref[...].astype(f32)
    lane = lax.broadcasted_iota(jnp.int32, left.shape, 1)
    for x in range(beyond_ref.shape[0]):
        after = pltpu.roll(right, (LANES - x) % LANES, 1)
        before = pltpu.roll(left, LANES - 1 - x, 1)
        beyond_ref[x] = jnp.where(lane == 0, after, before).astype(bf16)
    for k in range(2):
        field = dot(plane_ref[k], depth_ref[k], ((1,), (0,)))
        for tile in range(tiles):
            field_ref[k, tile] = field[:, tile * LANES : (tile + 1) * LANES]
    squared = joined(sums)
    cells = jnp.full(squared.shape, float(KNOT * KNOT), f32)
    first, second = plane_ref[0], plane_ref[1]
    diag_depth_ref[0] = dot(first * first, squared, ((0,), (0,)))
    diag_depth_ref[1] = dot(second * second, cells, ((0,), (0,)))
    first, second = depth_ref[0], depth_ref[1]
    diag_plane_ref[0] = dot(squared, first * first, ((1,), (1,)))
    diag_plane_ref[1] = dot(cells, second * second, ((1,), (1,)))


def terms(sums, plane, depth_factors, left, right, depth):
    nodes, width = plane.shape[1], depth_factors.shape[2]
    return pl.pallas_call(
        terms_kernel,
        out_shape=[
            jax.ShapeDtypeStruct((2, width // LANES, nodes, LANES), f32),
            jax.ShapeDtypeStruct((2, RANK, width), f32),
            jax.ShapeDtypeStruct((2, nodes, RANK), f32),
            jax.ShapeDtypeStruct((depth,) + left.shape, bf16),
        ],
        compiler_params=plain_params(),
        cost_estimate=pl.CostEstimate(flops=40 * nodes * RANK * width, bytes_accessed=1 << 20, transcendentals=0),
        name="terms",
    )(sums, plane, depth_factors, left, right)


def warp_kernel(
    cells_ref, image_ref, shift_ref, beyond_ref, low_ref, high_ref, field, plane_ref, depth_ref,
    diag_depth_ref, diag_plane_ref,
    residual_ref, depth_out, plane_out,
    ahead_ref, here_ref, behind_ref, wide, bands, blocks, energy, held,
):
    step = pl.program_id(0)
    last = pl.num_programs(0) - 1
    planes, rows, width = cells_ref.shape
    nodes = rows // KNOT
    tiles = width // LANES
    window = (ahead_ref, here_ref, behind_ref)
    pitch = rows + 2 * TOP
    plane_rows = tiles * pitch
    block_rows = planes * plane_rows

    @pl.when(step == 0)
    def _():
        row = lax.broadcasted_iota(jnp.int32, bands.shape[1:], 0)
        column = lax.broadcasted_iota(jnp.int32, bands.shape[1:], 1)
        one, none = jnp.ones(bands.shape[1:], f32), jnp.zeros(bands.shape[1:], f32)
        up, down = jnp.where(row == column + 1, one, none), jnp.where(row == column, one, none)
        bands[0] = (up - down).astype(bf16)
        up = jnp.where(row == column + LANES, one, none)
        down = jnp.where(row == column + LANES - 1, one, none)
        bands[1] = (up - down).astype(bf16)
        energy[...] = jnp.zeros_like(energy)
        for c in range(3):
            window[c][4 * block_rows - plane_rows :, :] = jnp.zeros((plane_rows, LANES), f32)

    @pl.when(step < last - 1)
    def _():
        at = lax.broadcasted_iota(jnp.int32, (2 * TOP, width + LANES), 0)
        low, high = low_ref[...].astype(f32), high_ref[...].astype(f32)
        for k in range(planes):
            first = k * pitch
            wide[first : first + rows, 0:LANES] = beyond_ref[k]
            wide[first : first + rows, LANES : LANES + width] = cells_ref[k]
            wide[first : first + rows, LANES + width :] = beyond_ref[k]
            rim = jnp.where(at == TOP, high[k : k + 1], jnp.where(at == TOP - 1, low[k : k + 1], 0.0)).astype(bf16)
            wide[first + rows : first + pitch, 0:LANES] = rim[:, width:]
            wide[first + rows : first + pitch, LANES:] = rim

    @pl.when(step >= last - 1)
    def _():
        wide[...] = jnp.zeros_like(wide)

    slot = (step % 4) * block_rows
    pieces = width // (2 * LANES)

    def made(t):
        plane = pl.ds(pl.multiple_of((t // pieces) * pitch, 16), pitch)
        start = (t % pieces) * 2 * LANES
        before = wide[plane, pl.ds(pl.multiple_of(start, LANES), 3 * LANES)]
        after = wide[plane, pl.ds(pl.multiple_of(start + LANES, LANES), 3 * LANES)]
        ahead = jnp.dot(after, bands[0], preferred_element_type=f32)
        behind = jnp.dot(before, bands[1], preferred_element_type=f32)
        return ahead, after[:, 0 : 2 * LANES].astype(f32), behind

    def put(t, parts):
        first = slot + (t // pieces) * plane_rows + (t % pieces) * 2 * pitch
        for c in range(3):
            for half in range(2):
                start = pl.multiple_of(first + half * pitch, 8)
                values = parts[c][:, half * LANES : (half + 1) * LANES]
                window[c][pl.ds(start + TOP, rows), :] = values[0:rows]
                window[c][pl.ds(start, TOP), :] = values[rows : rows + TOP]
                window[c][pl.ds(start + TOP + rows, TOP), :] = values[rows + TOP :]

    turns = planes * pieces

    @pl.when(step < 2)
    def _():
        def one(t, carry):
            put(t, made(t))
            return carry

        lax.fori_loop(0, turns, one, 0)

    @pl.when(step > 1)
    def _():
        mid = (step + 2) % 4
        first_rows = (
            jnp.where(mid == 0, 4, mid) * block_rows - plane_rows,
            mid * block_rows,
            jnp.where(mid == 3, 0, mid + 1) * block_rows,
        )

        def one(t, total):
            tile = t % tiles
            pair = t // tiles
            at = pl.multiple_of(tile * LANES, LANES)
            top = pl.multiple_of(pair * 16, 16)
            origins = [first + tile * pitch + top + TOP for first in first_rows]
            parts = made(t)
            for half in range(2):
                node = (step - 2) * nodes + pair * 2 + half
                mine = slice(8 * half, 8 * half + 8)

                def taps(x):
                    part = 0 if x == 0 else 2 if x == planes + 1 else 1
                    plus = (x - 1) * plane_rows + 8 * half if part == 1 else 8 * half
                    return [
                        [window[c][pl.ds(origins[part] + (plus + b), 8), :] for c in range(3)] for b in (-1, 0, 1)
                    ]

                contrast = jnp.broadcast_to(field[0, tile, pl.ds(node, 1), :], (8, LANES))
                brightness = jnp.broadcast_to(field[1, tile, pl.ds(node, 1), :], (8, LANES))
                by_image = jnp.zeros((8, LANES), f32)
                plain = jnp.zeros((8, LANES), f32)
                before, here = taps(0), taps(1)
                for k in range(planes):
                    after = taps(k + 2)
                    place = (k, pl.ds(top, 16), pl.ds(at, LANES))
                    sx, sy, sz = (shift_ref[(axis,) + place].astype(f32)[mine] for axis in range(3))
                    image = image_ref[place].astype(f32)[mine]
                    px, py, pz = sx > 0, sy > 0, sz > 0
                    ax, ay = jnp.abs(sx), jnp.abs(sy)

                    def sides(c):
                        far = [jnp.where(px, after[b][c], before[b][c]) for b in range(3)]
                        near = [here[b][c] for b in range(3)]
                        return [(v[1], jnp.where(py, v[2], v[0])) for v in (near, far)]

                    ahead, middle, behind = sides(0), sides(1), sides(2)
                    lines = []
                    for b in range(2):
                        near, far = (middle[v][b] + sz * jnp.where(pz, ahead[v][b], behind[v][b]) for v in range(2))
                        lines.append(near + ax * (far - near))
                    warped = lines[0] + ay * (lines[1] - lines[0])
                    misfit = warped - contrast * image - brightness
                    if half == 0:
                        held[k] = misfit
                    else:
                        residual_ref[place] = jnp.concatenate([held[k], misfit], axis=0).astype(bf16)
                    by_image = by_image + misfit * image
                    plain = plain + misfit
                    total = total + misfit * misfit
                    before, here = here, after
                for k, value in ((0, by_image), (1, plain)):
                    blocks[k, tile, pl.ds(node, 1), :] = jnp.sum(value, axis=0, keepdims=True)
            put(t, parts)
            return total

        energy[...] = lax.fori_loop(0, turns, one, energy[...])

    @pl.when(step == last)
    def _():
        parts = depth_out.shape[0]
        share = RANK // parts
        sums = [joined(blocks.at[k]) for k in range(2)]
        kinds = [split_dot(plane_ref[k], sums[k], 0) for k in range(2)]
        kinds = kinds + [diag_depth_ref[0], diag_depth_ref[1]]
        for p in range(parts):
            for k in range(4):
                depth_out[p, k * share : (k + 1) * share, :] = kinds[k][p * share : (p + 1) * share]
            depth_out[p, 3 * share :, width // 2 :] = jnp.full((share, width // 2), jnp.sum(energy[...]), f32)
        kinds = [split_dot(sums[k], depth_ref[k], 1) for k in range(2)]
        kinds = kinds + [diag_plane_ref[0], diag_plane_ref[1]]
        for k in range(4):
            plane_out[:, k * RANK : (k + 1) * RANK] = kinds[k]


def warp(cells, image, shift, beyond, low, high, field, plane, depth_factors, diag_depth, diag_plane, parts):
    depth, rows, width = cells.shape
    nodes = plane.shape[1]
    tiles = width // LANES
    count = depth // KNOT
    behind = lambda i: (jnp.maximum(i - 2, 0), 0, 0)
    ahead = lambda i: (jnp.minimum(i, count - 1), 0, 0)
    flat = lambda i: (0, 0)
    whole = lambda i: (0, 0, 0)
    return pl.pallas_call(
        warp_kernel,
        grid=(count + 2,),
        in_specs=[
            pl.BlockSpec((KNOT, rows, width), ahead),
            pl.BlockSpec((KNOT, rows, width), behind),
            pl.BlockSpec((3, KNOT, rows, width), lambda i: (0, jnp.maximum(i - 2, 0), 0, 0)),
            pl.BlockSpec((KNOT, rows, LANES), ahead),
            pl.BlockSpec((KNOT, low.shape[1]), lambda i: (jnp.minimum(i, count - 1), 0)),
            pl.BlockSpec((KNOT, high.shape[1]), lambda i: (jnp.minimum(i, count - 1), 0)),
            pl.BlockSpec(field.shape, lambda i: (0, 0, 0, 0)),
            pl.BlockSpec(plane.shape, whole),
            pl.BlockSpec(depth_factors.shape, whole),
            pl.BlockSpec(diag_depth.shape, whole),
            pl.BlockSpec(diag_plane.shape, whole),
        ],
        out_specs=[
            pl.BlockSpec((KNOT, rows, width), behind),
            pl.BlockSpec((parts, 4 * RANK // parts, width), whole),
            pl.BlockSpec((nodes, 4 * RANK), flat),
        ],
        out_shape=[
            jax.ShapeDtypeStruct(cells.shape, bf16),
            jax.ShapeDtypeStruct((parts, 4 * RANK // parts, width), f32),
            jax.ShapeDtypeStruct((nodes, 4 * RANK), f32),
        ],
        scratch_shapes=[
            *[pltpu.VMEM((4 * KNOT * tiles * (rows + 2 * TOP), LANES), f32)] * 3,
            pltpu.VMEM((KNOT * (rows + 2 * TOP), width + 2 * LANES), bf16),
            pltpu.VMEM((2, 3 * LANES, 2 * LANES), bf16),
            pltpu.VMEM((2, tiles, nodes, LANES), f32),
            pltpu.VMEM((8, LANES), f32),
            pltpu.VMEM((KNOT, 8, LANES), f32),
        ],
        compiler_params=grid_params(),
        cost_estimate=pl.CostEstimate(flops=60 * cells.size, bytes_accessed=12 * cells.size, transcendentals=0),
        name="warp",
    )(cells, image, shift, beyond, low, high, field, plane, depth_factors, diag_depth, diag_plane)


def gather_kernel(depth_ref, plane_ref, depth_out, plane_out):
    total = jnp.sum(depth_ref[...], axis=0)
    for p in range(depth_out.shape[0]):
        depth_out[p] = total
    cells = plane_ref.shape[0]
    plane_out[...] = plane_ref[...]
    energy = total[total.shape[0] - 1, total.shape[1] - 1]
    plane_out[cells // 2 :, 3 * RANK :] = jnp.full((cells // 2, RANK), energy, f32)


def step_kernel(full_z, node_count, depth_ref, plane_ref, other_ref, depth_out, plane_out):
    planes = plane_ref[...] + other_ref[...]
    parts, share, width = depth_ref.shape[0], depth_ref.shape[1] // 4, depth_ref.shape[2]
    energy = planes[planes.shape[0] - 1, 4 * RANK - 1]
    lam_depth = damping * energy / full_z
    lam_plane = damping * RANK * energy / node_count
    for p in range(parts):
        got = depth_ref[p]
        levels = got[3 * share :, 0 : width // 2]
        levels = jnp.concatenate([levels, levels], axis=1)
        rows = slice(p * share, (p + 1) * share)
        depth_out[0, rows, :] = got[0:share] / (got[2 * share : 3 * share] + lam_depth + epsilon)
        depth_out[1, rows, :] = got[share : 2 * share] / (levels + lam_depth + epsilon)
    plane_out[0] = planes[:, 0:RANK] / (planes[:, 2 * RANK : 3 * RANK] + lam_plane + epsilon)
    plane_out[1] = planes[:, RANK : 2 * RANK] / (planes[0:1, 3 * RANK :] + lam_plane + epsilon)


def local(image, deformed, displacement, plane_factors, depth_factors):
    n_gy, n_gz = lax.axis_size("gy"), lax.axis_size("gz")
    nodes_x, nodes_y = plane_factors.shape[2:]
    plane = jnp.transpose(plane_factors, (0, 2, 3, 1)).reshape(2, nodes_x * nodes_y, RANK)
    first, last, low, high = ends(deformed)
    right = shifted(first, "gz", True)
    left = shifted(last, "gz", False)
    low, high = packed_rows(left, right, low, high)
    above = shifted(low, "gy", True)
    below = shifted(high, "gy", False)
    sums = squares(image, low)
    field, diag_depth, diag_plane, beyond = terms(sums, plane, depth_factors, left, right, deformed.shape[0])
    residual, depth_terms, plane_terms = warp(
        deformed, image, displacement, beyond, below, above, field, plane, depth_factors, diag_depth, diag_plane,
        n_gy,
    )
    depth_terms = lax.all_to_all(depth_terms, "gy", 0, 0)
    depth_terms, plane_terms = pl.pallas_call(
        gather_kernel,
        out_shape=[
            jax.ShapeDtypeStruct(depth_terms.shape, f32),
            jax.ShapeDtypeStruct(plane_terms.shape, f32),
        ],
        compiler_params=plain_params(),
        name="gather",
    )(depth_terms, plane_terms)
    depth_terms = lax.all_to_all(depth_terms, "gy", 0, 0)
    hop = 1
    while hop < n_gz:
        other = lax.ppermute(plane_terms, "gz", [(i, i ^ hop) for i in range(n_gz)])
        if 2 * hop < n_gz:
            plane_terms = plane_terms + other
        hop = 2 * hop
    width = depth_factors.shape[2]
    step_depth, step_plane = pl.pallas_call(
        functools.partial(step_kernel, width * n_gz, nodes_x * nodes_y * n_gy),
        out_shape=[
            jax.ShapeDtypeStruct(depth_factors.shape, f32),
            jax.ShapeDtypeStruct(plane.shape, f32),
        ],
        compiler_params=plain_params(),
        name="steps",
    )(depth_terms, plane_terms, other)
    step_plane = jnp.transpose(step_plane.reshape(2, nodes_x, nodes_y, RANK), (0, 3, 1, 2))
    return residual, step_plane, step_depth


def solution(mesh):
    placed = (
        P(None, "gy", "gz"),
        P(None, "gy", "gz"),
        P(None, None, "gy", "gz"),
        P(None, None, None, "gy"),
        P(None, None, "gz"),
    )
    return jax.shard_map(
        local,
        mesh=mesh,
        in_specs=placed,
        out_specs=(P(None, "gy", "gz"), P(None, None, None, "gy"), P(None, None, "gz")),
        check_vma=False,
    )
```

```python
import functools

import jax
import jax.numpy as jnp
from jax import lax
from jax.experimental import pallas as pl
from jax.experimental.pallas import tpu as pltpu
from jax.sharding import PartitionSpec as P

RANK = 32
KNOT = 8
LANES = 128
TOP = 8

epsilon = 1e-06
damping = 0.01
highest = lax.Precision.HIGHEST
f32 = jnp.float32
bf16 = jnp.bfloat16


def dot(left, right, dims):
    return lax.dot_general(left, right, ((dims[0], dims[1]), ((), ())), precision=highest, preferred_element_type=f32)


def split_dot(left, right, dim):
    left_high, right_high = left.astype(bf16), right.astype(bf16)
    left_low = (left - left_high.astype(f32)).astype(bf16)
    right_low = (right - right_high.astype(f32)).astype(bf16)
    left = jnp.concatenate([left_high, left_high, left_low], axis=dim)
    right = jnp.concatenate([right_high, right_low, right_high], axis=dim)
    return lax.dot_general(left, right, (((dim,), (dim,)), ((), ())), preferred_element_type=f32)


def joined(ref):
    return jnp.concatenate([ref[tile] for tile in range(ref.shape[0])], axis=1)


def grid_params():
    return pltpu.CompilerParams(dimension_semantics=("arbitrary",), vmem_limit_bytes=40000000)


def plain_params():
    return pltpu.CompilerParams(vmem_limit_bytes=32000000)


def ends_kernel(cells_ref, first_ref, last_ref, low_ref, high_ref):
    depth, rows, width = cells_ref.shape
    lane = lax.broadcasted_iota(jnp.int32, (rows, LANES), 1)
    first = jnp.zeros((rows, LANES), f32)
    last = jnp.zeros((rows, LANES), f32)
    for x in range(depth):
        near = cells_ref[x, :, 0:LANES].astype(f32)
        far = cells_ref[x, :, width - LANES : width].astype(f32)
        first = jnp.where(lane == x, pltpu.roll(near, x, 1), first)
        last = jnp.where(lane == x, pltpu.roll(far, (x + 1) % LANES, 1), last)
    first_ref[...] = first.astype(bf16)
    last_ref[...] = last.astype(bf16)
    for x in range(0, depth, 16):
        low = [cells_ref[x + k, 0:16, :].astype(f32)[0:1] for k in range(16)]
        high = [cells_ref[x + k, rows - 16 : rows, :].astype(f32)[15:16] for k in range(16)]
        low_ref[x : x + 16, :] = jnp.concatenate(low, axis=0).astype(bf16)
        high_ref[x : x + 16, :] = jnp.concatenate(high, axis=0).astype(bf16)


def ends(cells):
    depth, rows, width = cells.shape
    return pl.pallas_call(
        ends_kernel,
        out_shape=[jax.ShapeDtypeStruct((rows, LANES), bf16)] * 2 + [jax.ShapeDtypeStruct((depth, width), bf16)] * 2,
        compiler_params=plain_params(),
        cost_estimate=pl.CostEstimate(flops=cells.size, bytes_accessed=2 * cells.size, transcendentals=0),
        name="ends",
    )(cells)


def rows_kernel(left_ref, right_ref, low_ref, high_ref, low_out, high_out):
    depth, width = low_ref.shape
    rows = left_ref.shape[0]
    lane = lax.broadcasted_iota(jnp.int32, (depth, LANES), 1)
    pad = jnp.zeros((LANES - rows, LANES), f32)
    left = jnp.transpose(jnp.concatenate([left_ref[...].astype(f32), pad], axis=0))[0:depth]
    right = jnp.transpose(jnp.concatenate([right_ref[...].astype(f32), pad], axis=0))[0:depth]
    for row, body, out in ((0, low_ref, low_out), (rows - 1, high_ref, high_out)):
        after = pltpu.roll(right, (LANES - row) % LANES, 1)
        before = pltpu.roll(left, LANES - 1 - row, 1)
        out[:, 0:width] = body[...]
        out[:, width : width + LANES] = jnp.where(lane == 0, after, before).astype(bf16)


def packed_rows(left, right, low, high):
    depth, width = low.shape
    return pl.pallas_call(
        rows_kernel,
        out_shape=[jax.ShapeDtypeStruct((depth, width + LANES), bf16)] * 2,
        compiler_params=plain_params(),
        cost_estimate=pl.CostEstimate(flops=500000 * low.size, bytes_accessed=8 * low.size, transcendentals=0),
        name="rows",
    )(left, right, low, high)


def shifted(part, axis, back):
    count = lax.axis_size(axis)
    if back:
        return lax.ppermute(part, axis, [(i + 1, i) for i in range(count - 1)])
    return lax.ppermute(part, axis, [(i, i + 1) for i in range(count - 1)])


def squares_kernel(image_ref, later_ref, sums):
    depth, rows, width = image_ref.shape
    tiles = width // LANES

    def one(t, carry):
        block, tile = t // tiles, t % tiles
        at = pl.multiple_of(tile * LANES, LANES)
        for pair in range(rows // 16):
            total = jnp.zeros((16, LANES), f32)
            for k in range(KNOT):
                values = image_ref[block * KNOT + k, 16 * pair : 16 * pair + 16, pl.ds(at, LANES)].astype(f32)
                total = total + values * values
            for half in range(2):
                row = block * (rows // KNOT) + 2 * pair + half
                sums[tile, pl.ds(row, 1), :] = jnp.sum(total[8 * half : 8 * half + 8], axis=0, keepdims=True)
        return carry

    lax.fori_loop(0, depth // KNOT * tiles, one, 0)


def squares(image, later):
    depth, rows, width = image.shape
    return pl.pallas_call(
        squares_kernel,
        out_shape=jax.ShapeDtypeStruct((width // LANES, depth * rows // KNOT**2, LANES), f32),
        compiler_params=plain_params(),
        cost_estimate=pl.CostEstimate(flops=3 * image.size, bytes_accessed=2 * image.size, transcendentals=0),
        name="squares",
    )(image, later)


def terms_kernel(
    sums, plane_ref, depth_ref, left_ref, right_ref, field_ref, diag_depth_ref, diag_plane_ref, beyond_ref
):
    tiles = sums.shape[0]
    left, right = left_ref[...].astype(f32), right_ref[...].astype(f32)
    lane = lax.broadcasted_iota(jnp.int32, left.shape, 1)
    for x in range(beyond_ref.shape[0]):
        after = pltpu.roll(right, (LANES - x) % LANES, 1)
        before = pltpu.roll(left, LANES - 1 - x, 1)
        beyond_ref[x] = jnp.where(lane == 0, after, before).astype(bf16)
    for k in range(2):
        field = dot(plane_ref[k], depth_ref[k], ((1,), (0,)))
        for tile in range(tiles):
            field_ref[k, tile] = field[:, tile * LANES : (tile + 1) * LANES]
    squared = joined(sums)
    cells = jnp.full(squared.shape, float(KNOT * KNOT), f32)
    first, second = plane_ref[0], plane_ref[1]
    diag_depth_ref[0] = dot(first * first, squared, ((0,), (0,)))
    diag_depth_ref[1] = dot(second * second, cells, ((0,), (0,)))
    first, second = depth_ref[0], depth_ref[1]
    diag_plane_ref[0] = dot(squared, first * first, ((1,), (1,)))
    diag_plane_ref[1] = dot(cells, second * second, ((1,), (1,)))


def terms(sums, plane, depth_factors, left, right, depth):
    nodes, width = plane.shape[1], depth_factors.shape[2]
    return pl.pallas_call(
        terms_kernel,
        out_shape=[
            jax.ShapeDtypeStruct((2, width // LANES, nodes, LANES), f32),
            jax.ShapeDtypeStruct((2, RANK, width), f32),
            jax.ShapeDtypeStruct((2, nodes, RANK), f32),
            jax.ShapeDtypeStruct((depth,) + left.shape, bf16),
        ],
        compiler_params=plain_params(),
        cost_estimate=pl.CostEstimate(flops=40 * nodes * RANK * width, bytes_accessed=1 << 20, transcendentals=0),
        name="terms",
    )(sums, plane, depth_factors, left, right)


def warp_kernel(
    cells_ref, image_ref, shift_ref, beyond_ref, low_ref, high_ref, field, plane_ref, depth_ref,
    diag_depth_ref, diag_plane_ref,
    residual_ref, depth_out, plane_out,
    ahead_ref, here_ref, behind_ref, wide, bands, rims, blocks, energy, held,
):
    step = pl.program_id(0)
    last = pl.num_programs(0) - 1
    planes, rows, width = cells_ref.shape
    nodes = rows // KNOT
    tiles = width // LANES
    window = (ahead_ref, here_ref, behind_ref)
    pitch = rows + 2 * TOP
    plane_rows = tiles * pitch
    block_rows = planes * plane_rows

    @pl.when(step == 0)
    def _():
        row = lax.broadcasted_iota(jnp.int32, bands.shape[1:], 0)
        column = lax.broadcasted_iota(jnp.int32, bands.shape[1:], 1)
        one, none = jnp.ones(bands.shape[1:], f32), jnp.zeros(bands.shape[1:], f32)
        up, down = jnp.where(row == column + 1, one, none), jnp.where(row == column, one, none)
        bands[0] = (up - down).astype(bf16)
        up = jnp.where(row == column + LANES, one, none)
        down = jnp.where(row == column + LANES - 1, one, none)
        bands[1] = (up - down).astype(bf16)
        energy[...] = jnp.zeros_like(energy)
        for c in range(3):
            window[c][3 * block_rows - plane_rows : 3 * block_rows, :] = jnp.zeros((plane_rows, LANES), f32)

    @pl.when(step < last)
    def _():
        slot = (step % 3) * block_rows
        span = planes * rows
        for k in range(planes):
            wide[k * rows : (k + 1) * rows, 0:width] = cells_ref[k]
            wide[k * rows : (k + 1) * rows, width:] = beyond_ref[k]
        wide[span:, :] = jnp.concatenate([low_ref[...].astype(f32), high_ref[...].astype(f32)], axis=0).astype(bf16)

        def put(c, tile, values):
            for k in range(planes):
                first = pl.multiple_of(slot + k * plane_rows + tile * pitch, 8)
                window[c][pl.ds(first + TOP, rows), :] = values[k * rows : (k + 1) * rows]
            for side, row in enumerate((0, TOP + rows)):
                rims[...] = values[span + side * planes : span + (side + 1) * planes]
                for k in range(planes):
                    first = pl.multiple_of(slot + k * plane_rows + tile * pitch, 8)
                    window[c][pl.ds(first + row, 8), :] = jnp.broadcast_to(rims[k : k + 1], (8, LANES))

        pieces = width // (2 * LANES)
        for piece in range(pieces):
            start = 2 * LANES * piece
            after = wide[:, start : start + 3 * LANES]
            if piece == 0:
                before = jnp.concatenate([wide[:, width:], wide[:, 0 : 2 * LANES]], axis=1)
            else:
                before = wide[:, start - LANES : start + 2 * LANES]
            ahead = jnp.dot(after, bands[0], preferred_element_type=f32)
            behind = jnp.dot(before, bands[1], preferred_element_type=f32)
            for half in range(2):
                mine = slice(half * LANES, (half + 1) * LANES)
                put(0, 2 * piece + half, ahead[:, mine])
                put(1, 2 * piece + half, wide[:, start + half * LANES : start + (half + 1) * LANES].astype(f32))
                put(2, 2 * piece + half, behind[:, mine])

    @pl.when(step == last)
    def _():
        first = pl.multiple_of((step % 3) * block_rows, 8)
        for c in range(3):
            window[c][pl.ds(first, plane_rows), :] = jnp.zeros((plane_rows, LANES), f32)

    @pl.when(step > 0)
    def _():
        mid = (step + 2) % 3
        first_rows = (
            jnp.where(mid == 0, 3, mid) * block_rows - plane_rows,
            mid * block_rows,
            jnp.where(mid == 2, 0, mid + 1) * block_rows,
        )

        def one(t, total):
            tile = t % tiles
            pair = t // tiles
            at = pl.multiple_of(tile * LANES, LANES)
            top = pl.multiple_of(pair * 16, 16)
            origins = [first + tile * pitch + top + TOP for first in first_rows]
            for half in range(2):
                node = (step - 1) * nodes + pair * 2 + half
                mine = slice(8 * half, 8 * half + 8)

                def taps(x):
                    part = 0 if x == 0 else 2 if x == planes + 1 else 1
                    plus = (x - 1) * plane_rows + 8 * half if part == 1 else 8 * half
                    return [
                        [window[c][pl.ds(origins[part] + (plus + b), 8), :] for c in range(3)] for b in (-1, 0, 1)
                    ]

                contrast = jnp.broadcast_to(field[0, tile, pl.ds(node, 1), :], (8, LANES))
                brightness = jnp.broadcast_to(field[1, tile, pl.ds(node, 1), :], (8, LANES))
                by_image = jnp.zeros((8, LANES), f32)
                plain = jnp.zeros((8, LANES), f32)
                before, here = taps(0), taps(1)
                for k in range(planes):
                    after = taps(k + 2)
                    place = (k, pl.ds(top, 16), pl.ds(at, LANES))
                    sx, sy, sz = (shift_ref[(axis,) + place].astype(f32)[mine] for axis in range(3))
                    image = image_ref[place].astype(f32)[mine]
                    px, py, pz = sx > 0, sy > 0, sz > 0
                    ax, ay = jnp.abs(sx), jnp.abs(sy)

                    def sides(c):
                        far = [jnp.where(px, after[b][c], before[b][c]) for b in range(3)]
                        near = [here[b][c] for b in range(3)]
                        return [(v[1], jnp.where(py, v[2], v[0])) for v in (near, far)]

                    ahead, middle, behind = sides(0), sides(1), sides(2)
                    lines = []
                    for b in range(2):
                        near, far = (middle[v][b] + sz * jnp.where(pz, ahead[v][b], behind[v][b]) for v in range(2))
                        lines.append(near + ax * (far - near))
                    warped = lines[0] + ay * (lines[1] - lines[0])
                    misfit = warped - contrast * image - brightness
                    if half == 0:
                        held[k] = misfit
                    else:
                        residual_ref[place] = jnp.concatenate([held[k], misfit], axis=0).astype(bf16)
                    by_image = by_image + misfit * image
                    plain = plain + misfit
                    total = total + misfit * misfit
                    before, here = here, after
                for k, value in ((0, by_image), (1, plain)):
                    blocks[k, tile, pl.ds(node, 1), :] = jnp.sum(value, axis=0, keepdims=True)
            return total

        energy[...] = lax.fori_loop(0, (rows // 16) * tiles, one, energy[...], unroll=2)

    @pl.when(step == last)
    def _():
        parts = depth_out.shape[0]
        share = RANK // parts
        sums = [joined(blocks.at[k]) for k in range(2)]
        kinds = [split_dot(plane_ref[k], sums[k], 0) for k in range(2)]
        kinds = kinds + [diag_depth_ref[0], diag_depth_ref[1]]
        for p in range(parts):
            for k in range(4):
                depth_out[p, k * share : (k + 1) * share, :] = kinds[k][p * share : (p + 1) * share]
        local = jnp.sum(energy[...])
        kinds = [split_dot(sums[k], depth_ref[k], 1) for k in range(2)]
        kinds = kinds + [diag_plane_ref[0], diag_plane_ref[1]]
        for k in range(4):
            plane_out[:, k * RANK : (k + 1) * RANK] = kinds[k]
        count = plane_out.shape[0]
        plane_out[count // 2 :, 3 * RANK :] = jnp.full((count // 2, RANK), local, f32)


def warp(cells, image, shift, beyond, low, high, field, plane, depth_factors, diag_depth, diag_plane, parts):
    depth, rows, width = cells.shape
    nodes = plane.shape[1]
    tiles = width // LANES
    count = depth // KNOT
    behind = lambda i: (jnp.maximum(i - 1, 0), 0, 0)
    ahead = lambda i: (jnp.minimum(i, count - 1), 0, 0)
    flat = lambda i: (0, 0)
    whole = lambda i: (0, 0, 0)
    return pl.pallas_call(
        warp_kernel,
        grid=(count + 1,),
        in_specs=[
            pl.BlockSpec((KNOT, rows, width), ahead),
            pl.BlockSpec((KNOT, rows, width), behind),
            pl.BlockSpec((3, KNOT, rows, width), lambda i: (0, jnp.maximum(i - 1, 0), 0, 0)),
            pl.BlockSpec((KNOT, rows, LANES), ahead),
            pl.BlockSpec((KNOT, low.shape[1]), lambda i: (jnp.minimum(i, count - 1), 0)),
            pl.BlockSpec((KNOT, high.shape[1]), lambda i: (jnp.minimum(i, count - 1), 0)),
            pl.BlockSpec(field.shape, lambda i: (0, 0, 0, 0)),
            pl.BlockSpec(plane.shape, whole),
            pl.BlockSpec(depth_factors.shape, whole),
            pl.BlockSpec(diag_depth.shape, whole),
            pl.BlockSpec(diag_plane.shape, whole),
        ],
        out_specs=[
            pl.BlockSpec((KNOT, rows, width), behind),
            pl.BlockSpec((parts, 4 * RANK // parts, width), whole),
            pl.BlockSpec((nodes, 4 * RANK), flat),
        ],
        out_shape=[
            jax.ShapeDtypeStruct(cells.shape, bf16),
            jax.ShapeDtypeStruct((parts, 4 * RANK // parts, width), f32),
            jax.ShapeDtypeStruct((nodes, 4 * RANK), f32),
        ],
        scratch_shapes=[
            *[pltpu.VMEM((3 * KNOT * tiles * (rows + 2 * TOP), LANES), f32)] * 3,
            pltpu.VMEM((KNOT * rows + 2 * KNOT, width + LANES), bf16),
            pltpu.VMEM((2, 3 * LANES, 2 * LANES), bf16),
            pltpu.VMEM((KNOT, LANES), f32),
            pltpu.VMEM((2, tiles, nodes, LANES), f32),
            pltpu.VMEM((8, LANES), f32),
            pltpu.VMEM((KNOT, 8, LANES), f32),
        ],
        compiler_params=grid_params(),
        cost_estimate=pl.CostEstimate(flops=60 * cells.size, bytes_accessed=12 * cells.size, transcendentals=0),
        name="warp",
    )(cells, image, shift, beyond, low, high, field, plane, depth_factors, diag_depth, diag_plane)


def gather_kernel(depth_ref, plane_ref, other_ref, depth_out, plane_out):
    total = jnp.sum(depth_ref[...], axis=0)
    planes = plane_ref[...] + other_ref[...]
    plane_out[...] = planes
    cells = planes.shape[0]
    share, width = total.shape[0] // 4, total.shape[1]
    row = lax.broadcasted_iota(jnp.int32, total.shape, 0)
    lane = lax.broadcasted_iota(jnp.int32, total.shape, 1)
    partial = planes[cells - 1, 4 * RANK - 1]
    total = jnp.where((row >= 3 * share) & (lane >= width // 2), partial, total)
    for p in range(depth_out.shape[0]):
        depth_out[p] = total


def step_kernel(full_z, node_count, depth_ref, plane_ref, depth_out, plane_out):
    parts, share, width = depth_ref.shape[0], depth_ref.shape[1] // 4, depth_ref.shape[2]
    energy = depth_ref[0, 3 * share, width - 1]
    for p in range(1, parts):
        energy = energy + depth_ref[p, 3 * share, width - 1]
    lam_depth = damping * energy / full_z
    lam_plane = damping * RANK * energy / node_count
    for p in range(parts):
        got = depth_ref[p]
        levels = got[3 * share :, 0 : width // 2]
        levels = jnp.concatenate([levels, levels], axis=1)
        rows = slice(p * share, (p + 1) * share)
        depth_out[0, rows, :] = got[0:share] / (got[2 * share : 3 * share] + lam_depth + epsilon)
        depth_out[1, rows, :] = got[share : 2 * share] / (levels + lam_depth + epsilon)
    planes = plane_ref[...]
    plane_out[0] = planes[:, 0:RANK] / (planes[:, 2 * RANK : 3 * RANK] + lam_plane + epsilon)
    plane_out[1] = planes[:, RANK : 2 * RANK] / (planes[0:1, 3 * RANK :] + lam_plane + epsilon)


def local(image, deformed, displacement, plane_factors, depth_factors):
    n_gy, n_gz = lax.axis_size("gy"), lax.axis_size("gz")
    nodes_x, nodes_y = plane_factors.shape[2:]
    plane = jnp.transpose(plane_factors, (0, 2, 3, 1)).reshape(2, nodes_x * nodes_y, RANK)
    first, last, low, high = ends(deformed)
    right = shifted(first, "gz", True)
    left = shifted(last, "gz", False)
    low, high = packed_rows(left, right, low, high)
    above = shifted(low, "gy", True)
    below = shifted(high, "gy", False)
    sums = squares(image, low)
    field, diag_depth, diag_plane, beyond = terms(sums, plane, depth_factors, left, right, deformed.shape[0])
    residual, depth_terms, plane_terms = warp(
        deformed, image, displacement, beyond, below, above, field, plane, depth_factors, diag_depth, diag_plane,
        n_gy,
    )
    depth_terms = lax.all_to_all(depth_terms, "gy", 0, 0)
    hop = 1
    while hop < n_gz:
        other = lax.ppermute(plane_terms, "gz", [(i, i ^ hop) for i in range(n_gz)])
        if 2 * hop < n_gz:
            plane_terms = plane_terms + other
        hop = 2 * hop
    depth_terms, plane_terms = pl.pallas_call(
        gather_kernel,
        out_shape=[
            jax.ShapeDtypeStruct(depth_terms.shape, f32),
            jax.ShapeDtypeStruct(plane_terms.shape, f32),
        ],
        compiler_params=plain_params(),
        name="gather",
    )(depth_terms, plane_terms, other)
    depth_terms = lax.all_to_all(depth_terms, "gy", 0, 0)
    width = depth_factors.shape[2]
    step_depth, step_plane = pl.pallas_call(
        functools.partial(step_kernel, width * n_gz, nodes_x * nodes_y * n_gy),
        out_shape=[
            jax.ShapeDtypeStruct(depth_factors.shape, f32),
            jax.ShapeDtypeStruct(plane.shape, f32),
        ],
        compiler_params=plain_params(),
        name="steps",
    )(depth_terms, plane_terms)
    step_plane = jnp.transpose(step_plane.reshape(2, nodes_x, nodes_y, RANK), (0, 3, 1, 2))
    return residual, step_plane, step_depth


def solution(mesh):
    placed = (
        P(None, "gy", "gz"),
        P(None, "gy", "gz"),
        P(None, None, "gy", "gz"),
        P(None, None, None, "gy"),
        P(None, None, "gz"),
    )
    return jax.shard_map(
        local,
        mesh=mesh,
        in_specs=placed,
        out_specs=(P(None, "gy", "gz"), P(None, None, None, "gy"), P(None, None, "gz")),
        check_vma=False,
    )
```

```python
import functools

import jax
import jax.numpy as jnp
from jax import lax
from jax.experimental import pallas as pl
from jax.experimental.pallas import tpu as pltpu
from jax.sharding import PartitionSpec as P

RANK = 32
KNOT = 8
LANES = 128
TOP = 8

epsilon = 1e-06
damping = 0.01
highest = lax.Precision.HIGHEST
f32 = jnp.float32
bf16 = jnp.bfloat16


def dot(left, right, dims):
    return lax.dot_general(left, right, ((dims[0], dims[1]), ((), ())), precision=highest, preferred_element_type=f32)


def split_dot(left, right, dim):
    left_high, right_high = left.astype(bf16), right.astype(bf16)
    left_low = (left - left_high.astype(f32)).astype(bf16)
    right_low = (right - right_high.astype(f32)).astype(bf16)
    left = jnp.concatenate([left_high, left_high, left_low], axis=dim)
    right = jnp.concatenate([right_high, right_low, right_high], axis=dim)
    return lax.dot_general(left, right, (((dim,), (dim,)), ((), ())), preferred_element_type=f32)


def joined(ref):
    return jnp.concatenate([ref[tile] for tile in range(ref.shape[0])], axis=1)


def grid_params():
    return pltpu.CompilerParams(dimension_semantics=("arbitrary",), vmem_limit_bytes=40000000)


def plain_params():
    return pltpu.CompilerParams(vmem_limit_bytes=32000000)


def columns_kernel(*refs):
    first_ref, last_ref = refs[-2:]
    chunks = (len(refs) - 2) // 2
    rows = first_ref.shape[0]
    lane = lax.broadcasted_iota(jnp.int32, (rows, LANES), 1)
    first = jnp.zeros((rows, LANES), f32)
    last = jnp.zeros((rows, LANES), f32)
    for chunk in range(chunks):
        near, far = refs[chunk], refs[chunks + chunk]
        for k in range(near.shape[0]):
            x = chunk * near.shape[0] + k
            first = jnp.where(lane == x, pltpu.roll(near[k].astype(f32), x, 1), first)
            last = jnp.where(lane == x, pltpu.roll(far[k].astype(f32), (x + 1) % LANES, 1), last)
    first_ref[...] = first.astype(bf16)
    last_ref[...] = last.astype(bf16)


def end_columns(cells):
    depth, rows, width = cells.shape
    tiles = width // LANES
    chunks = 4
    block = (depth // chunks, rows, LANES)
    places = [(chunk, tile) for tile in (0, tiles - 1) for chunk in range(chunks)]
    return pl.pallas_call(
        columns_kernel,
        grid=(1,),
        in_specs=[pl.BlockSpec(block, functools.partial(lambda c, t, i: (c, 0, t), c, t)) for c, t in places],
        out_specs=[pl.BlockSpec((rows, LANES), lambda i: (0, 0))] * 2,
        out_shape=[jax.ShapeDtypeStruct((rows, LANES), bf16)] * 2,
        compiler_params=pltpu.CompilerParams(vmem_limit_bytes=60000000),
        name="columns",
    )(*[cells] * len(places))


def ends_kernel(cells_ref, low_ref, high_ref):
    depth, rows = cells_ref.shape[0:2]
    for x in range(0, depth, 16):
        low = [cells_ref[x + k, 0:16, :].astype(f32)[0:1] for k in range(16)]
        high = [cells_ref[x + k, rows - 16 : rows, :].astype(f32)[15:16] for k in range(16)]
        low_ref[x : x + 16, :] = jnp.concatenate(low, axis=0).astype(bf16)
        high_ref[x : x + 16, :] = jnp.concatenate(high, axis=0).astype(bf16)


def ends(cells):
    depth, rows, width = cells.shape
    return pl.pallas_call(
        ends_kernel,
        out_shape=[jax.ShapeDtypeStruct((depth, width), bf16)] * 2,
        compiler_params=plain_params(),
        cost_estimate=pl.CostEstimate(flops=cells.size, bytes_accessed=2 * cells.size, transcendentals=0),
        name="ends",
    )(cells)


def rows_kernel(left_ref, right_ref, low_ref, high_ref, across_out, inside_out):
    depth, width = low_ref.shape
    rows = left_ref.shape[0]
    odd = lax.axis_index("gy") % 2 == 1
    lane = lax.broadcasted_iota(jnp.int32, (depth, LANES), 1)
    pad = jnp.zeros((LANES - rows, LANES), f32)
    left = jnp.transpose(jnp.concatenate([left_ref[...].astype(f32), pad], axis=0))[0:depth]
    right = jnp.transpose(jnp.concatenate([right_ref[...].astype(f32), pad], axis=0))[0:depth]
    bodies, beyond = [], []
    for row, body in ((0, low_ref), (rows - 1, high_ref)):
        after = pltpu.roll(right, (LANES - row) % LANES, 1)
        before = pltpu.roll(left, LANES - 1 - row, 1)
        bodies.append(body[...].astype(f32))
        beyond.append(jnp.where(lane == 0, after, before))
    for out, first, second in ((across_out, 1, 0), (inside_out, 0, 1)):
        out[:, 0:width] = jnp.where(odd, bodies[first], bodies[second]).astype(bf16)
        out[:, width : width + LANES] = jnp.where(odd, beyond[first], beyond[second]).astype(bf16)


def packed_rows(left, right, low, high):
    depth, width = low.shape
    return pl.pallas_call(
        rows_kernel,
        out_shape=[jax.ShapeDtypeStruct((depth, width + LANES), bf16)] * 2,
        compiler_params=plain_params(),
        cost_estimate=pl.CostEstimate(flops=500000 * low.size, bytes_accessed=8 * low.size, transcendentals=0),
        name="rows",
    )(left, right, low, high)


def shifted(part, axis, back):
    count = lax.axis_size(axis)
    if back:
        return lax.ppermute(part, axis, [(i + 1, i) for i in range(count - 1)])
    return lax.ppermute(part, axis, [(i, i + 1) for i in range(count - 1)])


def swapped(part, axis, start):
    count = lax.axis_size(axis)
    pairs = [(i, i + 1) for i in range(start, count - 1, 2)]
    return lax.ppermute(part, axis, pairs + [(j, i) for i, j in pairs])


def squares_kernel(image_ref, later_ref, sums):
    depth, rows, width = image_ref.shape
    tiles = width // LANES

    def one(t, carry):
        block, tile = t // tiles, t % tiles
        at = pl.multiple_of(tile * LANES, LANES)
        for pair in range(rows // 16):
            total = jnp.zeros((16, LANES), f32)
            for k in range(KNOT):
                values = image_ref[block * KNOT + k, 16 * pair : 16 * pair + 16, pl.ds(at, LANES)].astype(f32)
                total = total + values * values
            for half in range(2):
                row = block * (rows // KNOT) + 2 * pair + half
                sums[tile, pl.ds(row, 1), :] = jnp.sum(total[8 * half : 8 * half + 8], axis=0, keepdims=True)
        return carry

    lax.fori_loop(0, depth // KNOT * tiles, one, 0)


def squares(image, later):
    depth, rows, width = image.shape
    return pl.pallas_call(
        squares_kernel,
        out_shape=jax.ShapeDtypeStruct((width // LANES, depth * rows // KNOT**2, LANES), f32),
        compiler_params=plain_params(),
        cost_estimate=pl.CostEstimate(flops=3 * image.size, bytes_accessed=2 * image.size, transcendentals=0),
        name="squares",
    )(image, later)


def terms_kernel(
    sums, plane_ref, depth_ref, left_ref, right_ref, field_ref, diag_depth_ref, diag_plane_ref, beyond_ref
):
    tiles = sums.shape[0]
    left, right = left_ref[...].astype(f32), right_ref[...].astype(f32)
    lane = lax.broadcasted_iota(jnp.int32, left.shape, 1)
    for x in range(beyond_ref.shape[0]):
        after = pltpu.roll(right, (LANES - x) % LANES, 1)
        before = pltpu.roll(left, LANES - 1 - x, 1)
        beyond_ref[x] = jnp.where(lane == 0, after, before).astype(bf16)
    for k in range(2):
        field = dot(plane_ref[k], depth_ref[k], ((1,), (0,)))
        for tile in range(tiles):
            field_ref[k, tile] = field[:, tile * LANES : (tile + 1) * LANES]
    squared = joined(sums)
    cells = jnp.full(squared.shape, float(KNOT * KNOT), f32)
    first, second = plane_ref[0], plane_ref[1]
    diag_depth_ref[0] = dot(first * first, squared, ((0,), (0,)))
    diag_depth_ref[1] = dot(second * second, cells, ((0,), (0,)))
    first, second = depth_ref[0], depth_ref[1]
    diag_plane_ref[0] = dot(squared, first * first, ((1,), (1,)))
    diag_plane_ref[1] = dot(cells, second * second, ((1,), (1,)))


def terms(sums, plane, depth_factors, left, right, depth):
    nodes, width = plane.shape[1], depth_factors.shape[2]
    return pl.pallas_call(
        terms_kernel,
        out_shape=[
            jax.ShapeDtypeStruct((2, width // LANES, nodes, LANES), f32),
            jax.ShapeDtypeStruct((2, RANK, width), f32),
            jax.ShapeDtypeStruct((2, nodes, RANK), f32),
            jax.ShapeDtypeStruct((depth,) + left.shape, bf16),
        ],
        compiler_params=plain_params(),
        cost_estimate=pl.CostEstimate(flops=40 * nodes * RANK * width, bytes_accessed=1 << 20, transcendentals=0),
        name="terms",
    )(sums, plane, depth_factors, left, right)


def warp_kernel(
    cells_ref, image_ref, shift_ref, beyond_ref, across_ref, inside_ref, field, plane_ref, depth_ref,
    diag_depth_ref, diag_plane_ref,
    residual_ref, depth_out, plane_out,
    ahead_ref, here_ref, behind_ref, wide, bands, rims, blocks, energy, held,
):
    step = pl.program_id(0)
    last = pl.num_programs(0) - 1
    planes, rows, width = cells_ref.shape
    nodes = rows // KNOT
    tiles = width // LANES
    window = (ahead_ref, here_ref, behind_ref)
    pitch = rows + 2 * TOP
    plane_rows = tiles * pitch
    block_rows = planes * plane_rows

    @pl.when(step == 0)
    def _():
        row = lax.broadcasted_iota(jnp.int32, bands.shape[1:], 0)
        column = lax.broadcasted_iota(jnp.int32, bands.shape[1:], 1)
        one, none = jnp.ones(bands.shape[1:], f32), jnp.zeros(bands.shape[1:], f32)
        up, down = jnp.where(row == column + 1, one, none), jnp.where(row == column, one, none)
        bands[0] = (up - down).astype(bf16)
        up = jnp.where(row == column + LANES, one, none)
        down = jnp.where(row == column + LANES - 1, one, none)
        bands[1] = (up - down).astype(bf16)
        energy[...] = jnp.zeros_like(energy)
        for c in range(3):
            window[c][3 * block_rows - plane_rows : 3 * block_rows, :] = jnp.zeros((plane_rows, LANES), f32)

    @pl.when(step < last)
    def _():
        slot = (step % 3) * block_rows
        span = planes * rows
        for k in range(planes):
            wide[k * rows : (k + 1) * rows, 0:width] = cells_ref[k]
            wide[k * rows : (k + 1) * rows, width:] = beyond_ref[k]
        odd = lax.axis_index("gy") % 2 == 1
        across, inside = across_ref[...].astype(f32), inside_ref[...].astype(f32)
        low, high = jnp.where(odd, inside, across), jnp.where(odd, across, inside)
        wide[span:, :] = jnp.concatenate([low, high], axis=0).astype(bf16)

        def put(c, tile, values):
            for k in range(planes):
                first = pl.multiple_of(slot + k * plane_rows + tile * pitch, 8)
                window[c][pl.ds(first + TOP, rows), :] = values[k * rows : (k + 1) * rows]
            for side, row in enumerate((0, TOP + rows)):
                rims[...] = values[span + side * planes : span + (side + 1) * planes]
                for k in range(planes):
                    first = pl.multiple_of(slot + k * plane_rows + tile * pitch, 8)
                    window[c][pl.ds(first + row, 8), :] = jnp.broadcast_to(rims[k : k + 1], (8, LANES))

        pieces = width // (2 * LANES)
        for piece in range(pieces):
            start = 2 * LANES * piece
            after = wide[:, start : start + 3 * LANES]
            if piece == 0:
                before = jnp.concatenate([wide[:, width:], wide[:, 0 : 2 * LANES]], axis=1)
            else:
                before = wide[:, start - LANES : start + 2 * LANES]
            ahead = jnp.dot(after, bands[0], preferred_element_type=f32)
            behind = jnp.dot(before, bands[1], preferred_element_type=f32)
            for half in range(2):
                mine = slice(half * LANES, (half + 1) * LANES)
                put(0, 2 * piece + half, ahead[:, mine])
                put(1, 2 * piece + half, wide[:, start + half * LANES : start + (half + 1) * LANES].astype(f32))
                put(2, 2 * piece + half, behind[:, mine])

    @pl.when(step == last)
    def _():
        first = pl.multiple_of((step % 3) * block_rows, 8)
        for c in range(3):
            window[c][pl.ds(first, plane_rows), :] = jnp.zeros((plane_rows, LANES), f32)

    @pl.when(step > 0)
    def _():
        mid = (step + 2) % 3
        first_rows = (
            jnp.where(mid == 0, 3, mid) * block_rows - plane_rows,
            mid * block_rows,
            jnp.where(mid == 2, 0, mid + 1) * block_rows,
        )

        def one(t, total):
            tile = t % tiles
            pair = t // tiles
            at = pl.multiple_of(tile * LANES, LANES)
            top = pl.multiple_of(pair * 16, 16)
            origins = [first + tile * pitch + top + TOP for first in first_rows]
            for half in range(2):
                node = (step - 1) * nodes + pair * 2 + half
                mine = slice(8 * half, 8 * half + 8)

                def taps(x):
                    part = 0 if x == 0 else 2 if x == planes + 1 else 1
                    plus = (x - 1) * plane_rows + 8 * half if part == 1 else 8 * half
                    return [
                        [window[c][pl.ds(origins[part] + (plus + b), 8), :] for c in range(3)] for b in (-1, 0, 1)
                    ]

                contrast = jnp.broadcast_to(field[0, tile, pl.ds(node, 1), :], (8, LANES))
                brightness = jnp.broadcast_to(field[1, tile, pl.ds(node, 1), :], (8, LANES))
                by_image = jnp.zeros((8, LANES), f32)
                plain = jnp.zeros((8, LANES), f32)
                before, here = taps(0), taps(1)
                for k in range(planes):
                    after = taps(k + 2)
                    place = (k, pl.ds(top, 16), pl.ds(at, LANES))
                    sx, sy, sz = (shift_ref[(axis,) + place].astype(f32)[mine] for axis in range(3))
                    image = image_ref[place].astype(f32)[mine]
                    px, py, pz = sx > 0, sy > 0, sz > 0
                    ax, ay = jnp.abs(sx), jnp.abs(sy)

                    def sides(c):
                        far = [jnp.where(px, after[b][c], before[b][c]) for b in range(3)]
                        near = [here[b][c] for b in range(3)]
                        return [(v[1], jnp.where(py, v[2], v[0])) for v in (near, far)]

                    ahead, middle, behind = sides(0), sides(1), sides(2)
                    lines = []
                    for b in range(2):
                        near, far = (middle[v][b] + sz * jnp.where(pz, ahead[v][b], behind[v][b]) for v in range(2))
                        lines.append(near + ax * (far - near))
                    warped = lines[0] + ay * (lines[1] - lines[0])
                    misfit = warped - contrast * image - brightness
                    if half == 0:
                        held[k] = misfit
                    else:
                        residual_ref[place] = jnp.concatenate([held[k], misfit], axis=0).astype(bf16)
                    by_image = by_image + misfit * image
                    plain = plain + misfit
                    total = total + misfit * misfit
                    before, here = here, after
                for k, value in ((0, by_image), (1, plain)):
                    blocks[k, tile, pl.ds(node, 1), :] = jnp.sum(value, axis=0, keepdims=True)
            return total

        energy[...] = lax.fori_loop(0, (rows // 16) * tiles, one, energy[...], unroll=2)

    @pl.when(step == last)
    def _():
        parts = depth_out.shape[0]
        share = RANK // parts
        sums = [joined(blocks.at[k]) for k in range(2)]
        kinds = [split_dot(plane_ref[k], sums[k], 0) for k in range(2)]
        kinds = kinds + [diag_depth_ref[0], diag_depth_ref[1]]
        for p in range(parts):
            for k in range(4):
                depth_out[p, k * share : (k + 1) * share, :] = kinds[k][p * share : (p + 1) * share]
        local = jnp.sum(energy[...])
        kinds = [split_dot(sums[k], depth_ref[k], 1) for k in range(2)]
        kinds = kinds + [diag_plane_ref[0], diag_plane_ref[1]]
        for k in range(4):
            plane_out[:, k * RANK : (k + 1) * RANK] = kinds[k]
        count = plane_out.shape[0]
        plane_out[count // 2 :, 3 * RANK :] = jnp.full((count // 2, RANK), local, f32)


def warp(cells, image, shift, beyond, across, inside, field, plane, depth_factors, diag_depth, diag_plane, parts):
    depth, rows, width = cells.shape
    nodes = plane.shape[1]
    tiles = width // LANES
    count = depth // KNOT
    behind = lambda i: (jnp.maximum(i - 1, 0), 0, 0)
    ahead = lambda i: (jnp.minimum(i, count - 1), 0, 0)
    flat = lambda i: (0, 0)
    whole = lambda i: (0, 0, 0)
    return pl.pallas_call(
        warp_kernel,
        grid=(count + 1,),
        in_specs=[
            pl.BlockSpec((KNOT, rows, width), ahead),
            pl.BlockSpec((KNOT, rows, width), behind),
            pl.BlockSpec((3, KNOT, rows, width), lambda i: (0, jnp.maximum(i - 1, 0), 0, 0)),
            pl.BlockSpec((KNOT, rows, LANES), ahead),
            pl.BlockSpec((KNOT, across.shape[1]), lambda i: (jnp.minimum(i, count - 1), 0)),
            pl.BlockSpec((KNOT, inside.shape[1]), lambda i: (jnp.minimum(i, count - 1), 0)),
            pl.BlockSpec(field.shape, lambda i: (0, 0, 0, 0)),
            pl.BlockSpec(plane.shape, whole),
            pl.BlockSpec(depth_factors.shape, whole),
            pl.BlockSpec(diag_depth.shape, whole),
            pl.BlockSpec(diag_plane.shape, whole),
        ],
        out_specs=[
            pl.BlockSpec((KNOT, rows, width), behind),
            pl.BlockSpec((parts, 4 * RANK // parts, width), whole),
            pl.BlockSpec((nodes, 4 * RANK), flat),
        ],
        out_shape=[
            jax.ShapeDtypeStruct(cells.shape, bf16),
            jax.ShapeDtypeStruct((parts, 4 * RANK // parts, width), f32),
            jax.ShapeDtypeStruct((nodes, 4 * RANK), f32),
        ],
        scratch_shapes=[
            *[pltpu.VMEM((3 * KNOT * tiles * (rows + 2 * TOP), LANES), f32)] * 3,
            pltpu.VMEM((KNOT * rows + 2 * KNOT, width + LANES), bf16),
            pltpu.VMEM((2, 3 * LANES, 2 * LANES), bf16),
            pltpu.VMEM((KNOT, LANES), f32),
            pltpu.VMEM((2, tiles, nodes, LANES), f32),
            pltpu.VMEM((8, LANES), f32),
            pltpu.VMEM((KNOT, 8, LANES), f32),
        ],
        compiler_params=grid_params(),
        cost_estimate=pl.CostEstimate(flops=60 * cells.size, bytes_accessed=12 * cells.size, transcendentals=0),
        name="warp",
    )(cells, image, shift, beyond, across, inside, field, plane, depth_factors, diag_depth, diag_plane)


def gather_kernel(depth_ref, plane_ref, other_ref, depth_out, plane_out):
    total = jnp.sum(depth_ref[...], axis=0)
    planes = plane_ref[...] + other_ref[...]
    plane_out[...] = planes
    cells = planes.shape[0]
    share, width = total.shape[0] // 4, total.shape[1]
    row = lax.broadcasted_iota(jnp.int32, total.shape, 0)
    lane = lax.broadcasted_iota(jnp.int32, total.shape, 1)
    partial = planes[cells - 1, 4 * RANK - 1]
    total = jnp.where((row >= 3 * share) & (lane >= width // 2), partial, total)
    for p in range(depth_out.shape[0]):
        depth_out[p] = total


def step_kernel(full_z, node_count, depth_ref, plane_ref, depth_out, plane_out):
    parts, share, width = depth_ref.shape[0], depth_ref.shape[1] // 4, depth_ref.shape[2]
    energy = depth_ref[0, 3 * share, width - 1]
    for p in range(1, parts):
        energy = energy + depth_ref[p, 3 * share, width - 1]
    lam_depth = damping * energy / full_z
    lam_plane = damping * RANK * energy / node_count
    for p in range(parts):
        got = depth_ref[p]
        levels = got[3 * share :, 0 : width // 2]
        levels = jnp.concatenate([levels, levels], axis=1)
        rows = slice(p * share, (p + 1) * share)
        depth_out[0, rows, :] = got[0:share] / (got[2 * share : 3 * share] + lam_depth + epsilon)
        depth_out[1, rows, :] = got[share : 2 * share] / (levels + lam_depth + epsilon)
    planes = plane_ref[...]
    plane_out[0] = planes[:, 0:RANK] / (planes[:, 2 * RANK : 3 * RANK] + lam_plane + epsilon)
    plane_out[1] = planes[:, RANK : 2 * RANK] / (planes[0:1, 3 * RANK :] + lam_plane + epsilon)


def local(image, deformed, displacement, plane_factors, depth_factors):
    n_gy, n_gz = lax.axis_size("gy"), lax.axis_size("gz")
    nodes_x, nodes_y = plane_factors.shape[2:]
    plane = jnp.transpose(plane_factors, (0, 2, 3, 1)).reshape(2, nodes_x * nodes_y, RANK)
    first, last = end_columns(deformed)
    right = shifted(first, "gz", True)
    left = shifted(last, "gz", False)
    low, high = ends(deformed)
    across, inside = packed_rows(left, right, low, high)
    later = across
    inside = swapped(inside, "gy", 0)
    across = swapped(across, "gy", 1)
    sums = squares(image, later)
    field, diag_depth, diag_plane, beyond = terms(sums, plane, depth_factors, left, right, deformed.shape[0])
    residual, depth_terms, plane_terms = warp(
        deformed, image, displacement, beyond, across, inside, field, plane, depth_factors, diag_depth, diag_plane,
        n_gy,
    )
    depth_terms = lax.all_to_all(depth_terms, "gy", 0, 0)
    hop = 1
    while hop < n_gz:
        other = lax.ppermute(plane_terms, "gz", [(i, i ^ hop) for i in range(n_gz)])
        if 2 * hop < n_gz:
            plane_terms = plane_terms + other
        hop = 2 * hop
    depth_terms, plane_terms = pl.pallas_call(
        gather_kernel,
        out_shape=[
            jax.ShapeDtypeStruct(depth_terms.shape, f32),
            jax.ShapeDtypeStruct(plane_terms.shape, f32),
        ],
        compiler_params=plain_params(),
        name="gather",
    )(depth_terms, plane_terms, other)
    depth_terms = lax.all_to_all(depth_terms, "gy", 0, 0)
    width = depth_factors.shape[2]
    step_depth, step_plane = pl.pallas_call(
        functools.partial(step_kernel, width * n_gz, nodes_x * nodes_y * n_gy),
        out_shape=[
            jax.ShapeDtypeStruct(depth_factors.shape, f32),
            jax.ShapeDtypeStruct(plane.shape, f32),
        ],
        compiler_params=plain_params(),
        name="steps",
    )(depth_terms, plane_terms)
    step_plane = jnp.transpose(step_plane.reshape(2, nodes_x, nodes_y, RANK), (0, 3, 1, 2))
    return residual, step_plane, step_depth


def solution(mesh):
    placed = (
        P(None, "gy", "gz"),
        P(None, "gy", "gz"),
        P(None, None, "gy", "gz"),
        P(None, None, None, "gy"),
        P(None, None, "gz"),
    )
    return jax.shard_map(
        local,
        mesh=mesh,
        in_specs=placed,
        out_specs=(P(None, "gy", "gz"), P(None, None, None, "gy"), P(None, None, "gz")),
        check_vma=False,
    )
```

```python
import functools

import jax
import jax.numpy as jnp
from jax import lax
from jax.experimental import pallas as pl
from jax.experimental.pallas import tpu as pltpu
from jax.sharding import PartitionSpec as P

RANK = 32
KNOT = 8
LANES = 128
TOP = 8

epsilon = 1e-06
damping = 0.01
highest = lax.Precision.HIGHEST
f32 = jnp.float32
bf16 = jnp.bfloat16


def dot(left, right, dims):
    return lax.dot_general(left, right, ((dims[0], dims[1]), ((), ())), precision=highest, preferred_element_type=f32)


def split_dot(left, right, dim):
    left_high, right_high = left.astype(bf16), right.astype(bf16)
    left_low = (left - left_high.astype(f32)).astype(bf16)
    right_low = (right - right_high.astype(f32)).astype(bf16)
    left = jnp.concatenate([left_high, left_high, left_low], axis=dim)
    right = jnp.concatenate([right_high, right_low, right_high], axis=dim)
    return lax.dot_general(left, right, (((dim,), (dim,)), ((), ())), preferred_element_type=f32)


def joined(ref):
    return jnp.concatenate([ref[tile] for tile in range(ref.shape[0])], axis=1)


def grid_params():
    return pltpu.CompilerParams(dimension_semantics=("arbitrary",), vmem_limit_bytes=40000000)


def plain_params():
    return pltpu.CompilerParams(vmem_limit_bytes=32000000)


def columns_kernel(*refs):
    inner_ref, outer_ref = refs[-2:]
    chunks = (len(refs) - 2) // 2
    rows = inner_ref.shape[0]
    lane = lax.broadcasted_iota(jnp.int32, (rows, LANES), 1)
    first = jnp.zeros((rows, LANES), f32)
    last = jnp.zeros((rows, LANES), f32)
    for chunk in range(chunks):
        near, far = refs[chunk], refs[chunks + chunk]
        for k in range(near.shape[0]):
            x = chunk * near.shape[0] + k
            first = jnp.where(lane == x, pltpu.roll(near[k].astype(f32), x, 1), first)
            last = jnp.where(lane == x, pltpu.roll(far[k].astype(f32), (x + 1) % LANES, 1), last)
    odd = lax.axis_index("gz") % 2 == 1
    inner_ref[...] = jnp.where(odd, first, last).astype(bf16)
    outer_ref[...] = jnp.where(odd, last, first).astype(bf16)


def end_columns(cells):
    depth, rows, width = cells.shape
    tiles = width // LANES
    chunks = 4
    block = (depth // chunks, rows, LANES)
    places = [(chunk, tile) for tile in (0, tiles - 1) for chunk in range(chunks)]
    return pl.pallas_call(
        columns_kernel,
        grid=(1,),
        in_specs=[pl.BlockSpec(block, functools.partial(lambda c, t, i: (c, 0, t), c, t)) for c, t in places],
        out_specs=[pl.BlockSpec((rows, LANES), lambda i: (0, 0))] * 2,
        out_shape=[jax.ShapeDtypeStruct((rows, LANES), bf16)] * 2,
        compiler_params=pltpu.CompilerParams(vmem_limit_bytes=60000000),
        name="columns",
    )(*[cells] * len(places))


def ends_kernel(cells_ref, low_ref, high_ref):
    depth, rows = cells_ref.shape[0:2]
    for x in range(0, depth, 16):
        low = [cells_ref[x + k, 0:16, :].astype(f32)[0:1] for k in range(16)]
        high = [cells_ref[x + k, rows - 16 : rows, :].astype(f32)[15:16] for k in range(16)]
        low_ref[x : x + 16, :] = jnp.concatenate(low, axis=0).astype(bf16)
        high_ref[x : x + 16, :] = jnp.concatenate(high, axis=0).astype(bf16)


def ends(cells):
    depth, rows, width = cells.shape
    return pl.pallas_call(
        ends_kernel,
        out_shape=[jax.ShapeDtypeStruct((depth, width), bf16)] * 2,
        compiler_params=plain_params(),
        cost_estimate=pl.CostEstimate(flops=cells.size, bytes_accessed=2 * cells.size, transcendentals=0),
        name="ends",
    )(cells)


def z_sides(inner_ref, outer_ref):
    odd = lax.axis_index("gz") % 2 == 1
    inner, outer = inner_ref[...].astype(f32), outer_ref[...].astype(f32)
    return jnp.where(odd, inner, outer), jnp.where(odd, outer, inner)


def rows_kernel(inner_ref, outer_ref, low_ref, high_ref, across_out, inside_out):
    depth, width = low_ref.shape
    rows = inner_ref.shape[0]
    odd = lax.axis_index("gy") % 2 == 1
    lane = lax.broadcasted_iota(jnp.int32, (depth, LANES), 1)
    pad = jnp.zeros((LANES - rows, LANES), f32)
    left, right = z_sides(inner_ref, outer_ref)
    left = jnp.transpose(jnp.concatenate([left, pad], axis=0))[0:depth]
    right = jnp.transpose(jnp.concatenate([right, pad], axis=0))[0:depth]
    bodies, beyond = [], []
    for row, body in ((0, low_ref), (rows - 1, high_ref)):
        after = pltpu.roll(right, (LANES - row) % LANES, 1)
        before = pltpu.roll(left, LANES - 1 - row, 1)
        bodies.append(body[...].astype(f32))
        beyond.append(jnp.where(lane == 0, after, before))
    for out, first, second in ((across_out, 1, 0), (inside_out, 0, 1)):
        out[:, 0:width] = jnp.where(odd, bodies[first], bodies[second]).astype(bf16)
        out[:, width : width + LANES] = jnp.where(odd, beyond[first], beyond[second]).astype(bf16)


def packed_rows(inner, outer, low, high):
    depth, width = low.shape
    return pl.pallas_call(
        rows_kernel,
        out_shape=[jax.ShapeDtypeStruct((depth, width + LANES), bf16)] * 2,
        compiler_params=plain_params(),
        cost_estimate=pl.CostEstimate(flops=500000 * low.size, bytes_accessed=8 * low.size, transcendentals=0),
        name="rows",
    )(inner, outer, low, high)


def swapped(part, axis, start):
    count = lax.axis_size(axis)
    pairs = [(i, i + 1) for i in range(start, count - 1, 2)]
    return lax.ppermute(part, axis, pairs + [(j, i) for i, j in pairs])


def squares_kernel(image_ref, later_ref, sums):
    depth, rows, width = image_ref.shape
    tiles = width // LANES

    def one(t, carry):
        block, tile = t // tiles, t % tiles
        at = pl.multiple_of(tile * LANES, LANES)
        for pair in range(rows // 16):
            total = jnp.zeros((16, LANES), f32)
            for k in range(KNOT):
                values = image_ref[block * KNOT + k, 16 * pair : 16 * pair + 16, pl.ds(at, LANES)].astype(f32)
                total = total + values * values
            for half in range(2):
                row = block * (rows // KNOT) + 2 * pair + half
                sums[tile, pl.ds(row, 1), :] = jnp.sum(total[8 * half : 8 * half + 8], axis=0, keepdims=True)
        return carry

    lax.fori_loop(0, depth // KNOT * tiles, one, 0)


def squares(image, later):
    depth, rows, width = image.shape
    return pl.pallas_call(
        squares_kernel,
        out_shape=jax.ShapeDtypeStruct((width // LANES, depth * rows // KNOT**2, LANES), f32),
        compiler_params=plain_params(),
        cost_estimate=pl.CostEstimate(flops=3 * image.size, bytes_accessed=2 * image.size, transcendentals=0),
        name="squares",
    )(image, later)


def terms_kernel(
    sums, plane_ref, depth_ref, inner_ref, outer_ref, field_ref, diag_depth_ref, diag_plane_ref, beyond_ref
):
    tiles = sums.shape[0]
    left, right = z_sides(inner_ref, outer_ref)
    lane = lax.broadcasted_iota(jnp.int32, left.shape, 1)
    for x in range(beyond_ref.shape[0]):
        after = pltpu.roll(right, (LANES - x) % LANES, 1)
        before = pltpu.roll(left, LANES - 1 - x, 1)
        beyond_ref[x] = jnp.where(lane == 0, after, before).astype(bf16)
    for k in range(2):
        field = dot(plane_ref[k], depth_ref[k], ((1,), (0,)))
        for tile in range(tiles):
            field_ref[k, tile] = field[:, tile * LANES : (tile + 1) * LANES]
    squared = joined(sums)
    cells = jnp.full(squared.shape, float(KNOT * KNOT), f32)
    first, second = plane_ref[0], plane_ref[1]
    diag_depth_ref[0] = dot(first * first, squared, ((0,), (0,)))
    diag_depth_ref[1] = dot(second * second, cells, ((0,), (0,)))
    first, second = depth_ref[0], depth_ref[1]
    diag_plane_ref[0] = dot(squared, first * first, ((1,), (1,)))
    diag_plane_ref[1] = dot(cells, second * second, ((1,), (1,)))


def terms(sums, plane, depth_factors, inner, outer, depth):
    nodes, width = plane.shape[1], depth_factors.shape[2]
    return pl.pallas_call(
        terms_kernel,
        out_shape=[
            jax.ShapeDtypeStruct((2, width // LANES, nodes, LANES), f32),
            jax.ShapeDtypeStruct((2, RANK, width), f32),
            jax.ShapeDtypeStruct((2, nodes, RANK), f32),
            jax.ShapeDtypeStruct((depth,) + inner.shape, bf16),
        ],
        compiler_params=plain_params(),
        cost_estimate=pl.CostEstimate(flops=40 * nodes * RANK * width, bytes_accessed=1 << 20, transcendentals=0),
        name="terms",
    )(sums, plane, depth_factors, inner, outer)


def warp_kernel(
    cells_ref, image_ref, shift_ref, beyond_ref, across_ref, inside_ref, field, plane_ref, depth_ref,
    diag_depth_ref, diag_plane_ref,
    residual_ref, depth_out, plane_out,
    ahead_ref, here_ref, behind_ref, wide, bands, rims, blocks, energy, held,
):
    step = pl.program_id(0)
    last = pl.num_programs(0) - 1
    planes, rows, width = cells_ref.shape
    nodes = rows // KNOT
    tiles = width // LANES
    window = (ahead_ref, here_ref, behind_ref)
    pitch = rows + 2 * TOP
    plane_rows = tiles * pitch
    block_rows = planes * plane_rows

    @pl.when(step == 0)
    def _():
        row = lax.broadcasted_iota(jnp.int32, bands.shape[1:], 0)
        column = lax.broadcasted_iota(jnp.int32, bands.shape[1:], 1)
        one, none = jnp.ones(bands.shape[1:], f32), jnp.zeros(bands.shape[1:], f32)
        up, down = jnp.where(row == column + 1, one, none), jnp.where(row == column, one, none)
        bands[0] = (up - down).astype(bf16)
        up = jnp.where(row == column + LANES, one, none)
        down = jnp.where(row == column + LANES - 1, one, none)
        bands[1] = (up - down).astype(bf16)
        energy[...] = jnp.zeros_like(energy)
        for c in range(3):
            window[c][3 * block_rows - plane_rows : 3 * block_rows, :] = jnp.zeros((plane_rows, LANES), f32)

    @pl.when(step < last)
    def _():
        slot = (step % 3) * block_rows
        span = planes * rows
        for k in range(planes):
            wide[k * rows : (k + 1) * rows, 0:width] = cells_ref[k]
            wide[k * rows : (k + 1) * rows, width:] = beyond_ref[k]
        odd = lax.axis_index("gy") % 2 == 1
        across, inside = across_ref[...].astype(f32), inside_ref[...].astype(f32)
        low, high = jnp.where(odd, inside, across), jnp.where(odd, across, inside)
        wide[span:, :] = jnp.concatenate([low, high], axis=0).astype(bf16)

        def put(c, tile, values):
            for k in range(planes):
                first = pl.multiple_of(slot + k * plane_rows + tile * pitch, 8)
                window[c][pl.ds(first + TOP, rows), :] = values[k * rows : (k + 1) * rows]
            for side, row in enumerate((0, TOP + rows)):
                rims[...] = values[span + side * planes : span + (side + 1) * planes]
                for k in range(planes):
                    first = pl.multiple_of(slot + k * plane_rows + tile * pitch, 8)
                    window[c][pl.ds(first + row, 8), :] = jnp.broadcast_to(rims[k : k + 1], (8, LANES))

        pieces = width // (2 * LANES)
        for piece in range(pieces):
            start = 2 * LANES * piece
            after = wide[:, start : start + 3 * LANES]
            if piece == 0:
                before = jnp.concatenate([wide[:, width:], wide[:, 0 : 2 * LANES]], axis=1)
            else:
                before = wide[:, start - LANES : start + 2 * LANES]
            ahead = jnp.dot(after, bands[0], preferred_element_type=f32)
            behind = jnp.dot(before, bands[1], preferred_element_type=f32)
            for half in range(2):
                mine = slice(half * LANES, (half + 1) * LANES)
                put(0, 2 * piece + half, ahead[:, mine])
                put(1, 2 * piece + half, wide[:, start + half * LANES : start + (half + 1) * LANES].astype(f32))
                put(2, 2 * piece + half, behind[:, mine])

    @pl.when(step == last)
    def _():
        first = pl.multiple_of((step % 3) * block_rows, 8)
        for c in range(3):
            window[c][pl.ds(first, plane_rows), :] = jnp.zeros((plane_rows, LANES), f32)

    @pl.when(step > 0)
    def _():
        mid = (step + 2) % 3
        first_rows = (
            jnp.where(mid == 0, 3, mid) * block_rows - plane_rows,
            mid * block_rows,
            jnp.where(mid == 2, 0, mid + 1) * block_rows,
        )

        def one(t, total):
            tile = t % tiles
            pair = t // tiles
            at = pl.multiple_of(tile * LANES, LANES)
            top = pl.multiple_of(pair * 16, 16)
            origins = [first + tile * pitch + top + TOP for first in first_rows]
            for half in range(2):
                node = (step - 1) * nodes + pair * 2 + half
                mine = slice(8 * half, 8 * half + 8)

                def taps(x):
                    part = 0 if x == 0 else 2 if x == planes + 1 else 1
                    plus = (x - 1) * plane_rows + 8 * half if part == 1 else 8 * half
                    return [
                        [window[c][pl.ds(origins[part] + (plus + b), 8), :] for c in range(3)] for b in (-1, 0, 1)
                    ]

                contrast = jnp.broadcast_to(field[0, tile, pl.ds(node, 1), :], (8, LANES))
                brightness = jnp.broadcast_to(field[1, tile, pl.ds(node, 1), :], (8, LANES))
                by_image = jnp.zeros((8, LANES), f32)
                plain = jnp.zeros((8, LANES), f32)
                before, here = taps(0), taps(1)
                for k in range(planes):
                    after = taps(k + 2)
                    place = (k, pl.ds(top, 16), pl.ds(at, LANES))
                    sx, sy, sz = (shift_ref[(axis,) + place].astype(f32)[mine] for axis in range(3))
                    image = image_ref[place].astype(f32)[mine]
                    px, py, pz = sx > 0, sy > 0, sz > 0
                    ax, ay = jnp.abs(sx), jnp.abs(sy)

                    def sides(c):
                        far = [jnp.where(px, after[b][c], before[b][c]) for b in range(3)]
                        near = [here[b][c] for b in range(3)]
                        return [(v[1], jnp.where(py, v[2], v[0])) for v in (near, far)]

                    ahead, middle, behind = sides(0), sides(1), sides(2)
                    lines = []
                    for b in range(2):
                        near, far = (middle[v][b] + sz * jnp.where(pz, ahead[v][b], behind[v][b]) for v in range(2))
                        lines.append(near + ax * (far - near))
                    warped = lines[0] + ay * (lines[1] - lines[0])
                    misfit = warped - contrast * image - brightness
                    if half == 0:
                        held[k] = misfit
                    else:
                        residual_ref[place] = jnp.concatenate([held[k], misfit], axis=0).astype(bf16)
                    by_image = by_image + misfit * image
                    plain = plain + misfit
                    total = total + misfit * misfit
                    before, here = here, after
                for k, value in ((0, by_image), (1, plain)):
                    blocks[k, tile, pl.ds(node, 1), :] = jnp.sum(value, axis=0, keepdims=True)
            return total

        energy[...] = lax.fori_loop(0, (rows // 16) * tiles, one, energy[...], unroll=2)

    @pl.when(step == last)
    def _():
        parts = depth_out.shape[0]
        share = RANK // parts
        sums = [joined(blocks.at[k]) for k in range(2)]
        kinds = [split_dot(plane_ref[k], sums[k], 0) for k in range(2)]
        kinds = kinds + [diag_depth_ref[0], diag_depth_ref[1]]
        for p in range(parts):
            for k in range(4):
                depth_out[p, k * share : (k + 1) * share, :] = kinds[k][p * share : (p + 1) * share]
        local = jnp.sum(energy[...])
        kinds = [split_dot(sums[k], depth_ref[k], 1) for k in range(2)]
        kinds = kinds + [diag_plane_ref[0], diag_plane_ref[1]]
        for k in range(4):
            plane_out[:, k * RANK : (k + 1) * RANK] = kinds[k]
        count = plane_out.shape[0]
        plane_out[count // 2 :, 3 * RANK :] = jnp.full((count // 2, RANK), local, f32)


def warp(cells, image, shift, beyond, across, inside, field, plane, depth_factors, diag_depth, diag_plane, parts):
    depth, rows, width = cells.shape
    nodes = plane.shape[1]
    tiles = width // LANES
    count = depth // KNOT
    behind = lambda i: (jnp.maximum(i - 1, 0), 0, 0)
    ahead = lambda i: (jnp.minimum(i, count - 1), 0, 0)
    flat = lambda i: (0, 0)
    whole = lambda i: (0, 0, 0)
    return pl.pallas_call(
        warp_kernel,
        grid=(count + 1,),
        in_specs=[
            pl.BlockSpec((KNOT, rows, width), ahead),
            pl.BlockSpec((KNOT, rows, width), behind),
            pl.BlockSpec((3, KNOT, rows, width), lambda i: (0, jnp.maximum(i - 1, 0), 0, 0)),
            pl.BlockSpec((KNOT, rows, LANES), ahead),
            pl.BlockSpec((KNOT, across.shape[1]), lambda i: (jnp.minimum(i, count - 1), 0)),
            pl.BlockSpec((KNOT, inside.shape[1]), lambda i: (jnp.minimum(i, count - 1), 0)),
            pl.BlockSpec(field.shape, lambda i: (0, 0, 0, 0)),
            pl.BlockSpec(plane.shape, whole),
            pl.BlockSpec(depth_factors.shape, whole),
            pl.BlockSpec(diag_depth.shape, whole),
            pl.BlockSpec(diag_plane.shape, whole),
        ],
        out_specs=[
            pl.BlockSpec((KNOT, rows, width), behind),
            pl.BlockSpec((parts, 4 * RANK // parts, width), whole),
            pl.BlockSpec((nodes, 4 * RANK), flat),
        ],
        out_shape=[
            jax.ShapeDtypeStruct(cells.shape, bf16),
            jax.ShapeDtypeStruct((parts, 4 * RANK // parts, width), f32),
            jax.ShapeDtypeStruct((nodes, 4 * RANK), f32),
        ],
        scratch_shapes=[
            *[pltpu.VMEM((3 * KNOT * tiles * (rows + 2 * TOP), LANES), f32)] * 3,
            pltpu.VMEM((KNOT * rows + 2 * KNOT, width + LANES), bf16),
            pltpu.VMEM((2, 3 * LANES, 2 * LANES), bf16),
            pltpu.VMEM((KNOT, LANES), f32),
            pltpu.VMEM((2, tiles, nodes, LANES), f32),
            pltpu.VMEM((8, LANES), f32),
            pltpu.VMEM((KNOT, 8, LANES), f32),
        ],
        compiler_params=grid_params(),
        cost_estimate=pl.CostEstimate(flops=60 * cells.size, bytes_accessed=12 * cells.size, transcendentals=0),
        name="warp",
    )(cells, image, shift, beyond, across, inside, field, plane, depth_factors, diag_depth, diag_plane)


def gather_kernel(depth_ref, plane_ref, other_ref, depth_out, plane_out):
    total = jnp.sum(depth_ref[...], axis=0)
    planes = plane_ref[...]
    plane_out[...] = planes
    cells = planes.shape[0]
    share, width = total.shape[0] // 4, total.shape[1]
    row = lax.broadcasted_iota(jnp.int32, total.shape, 0)
    lane = lax.broadcasted_iota(jnp.int32, total.shape, 1)
    partial = planes[cells - 1, 4 * RANK - 1] + other_ref[other_ref.shape[0] - 1, 4 * RANK - 1]
    total = jnp.where((row >= 3 * share) & (lane >= width // 2), partial, total)
    for p in range(depth_out.shape[0]):
        depth_out[p] = total


def step_kernel(full_z, node_count, depth_ref, plane_ref, other_ref, depth_out, plane_out):
    parts, share, width = depth_ref.shape[0], depth_ref.shape[1] // 4, depth_ref.shape[2]
    energy = depth_ref[0, 3 * share, width - 1]
    for p in range(1, parts):
        energy = energy + depth_ref[p, 3 * share, width - 1]
    lam_depth = damping * energy / full_z
    lam_plane = damping * RANK * energy / node_count
    for p in range(parts):
        got = depth_ref[p]
        levels = got[3 * share :, 0 : width // 2]
        levels = jnp.concatenate([levels, levels], axis=1)
        rows = slice(p * share, (p + 1) * share)
        depth_out[0, rows, :] = got[0:share] / (got[2 * share : 3 * share] + lam_depth + epsilon)
        depth_out[1, rows, :] = got[share : 2 * share] / (levels + lam_depth + epsilon)
    planes = plane_ref[...] + other_ref[...]
    plane_out[0] = planes[:, 0:RANK] / (planes[:, 2 * RANK : 3 * RANK] + lam_plane + epsilon)
    plane_out[1] = planes[:, RANK : 2 * RANK] / (planes[0:1, 3 * RANK :] + lam_plane + epsilon)


def local(image, deformed, displacement, plane_factors, depth_factors):
    n_gy, n_gz = lax.axis_size("gy"), lax.axis_size("gz")
    nodes_x, nodes_y = plane_factors.shape[2:]
    plane = jnp.transpose(plane_factors, (0, 2, 3, 1)).reshape(2, nodes_x * nodes_y, RANK)
    inner, outer = end_columns(deformed)
    inner = swapped(inner, "gz", 0)
    outer = swapped(outer, "gz", 1)
    low, high = ends(deformed)
    across, inside = packed_rows(inner, outer, low, high)
    later = across
    inside = swapped(inside, "gy", 0)
    across = swapped(across, "gy", 1)
    sums = squares(image, later)
    field, diag_depth, diag_plane, beyond = terms(sums, plane, depth_factors, inner, outer, deformed.shape[0])
    residual, depth_terms, plane_terms = warp(
        deformed, image, displacement, beyond, across, inside, field, plane, depth_factors, diag_depth, diag_plane,
        n_gy,
    )
    depth_terms = lax.all_to_all(depth_terms, "gy", 0, 0)
    hop = 1
    while 2 * hop < n_gz:
        plane_terms = plane_terms + lax.ppermute(plane_terms, "gz", [(i, i ^ hop) for i in range(n_gz)])
        hop = 2 * hop
    pairs = [(i, i ^ hop) for i in range(n_gz)]
    energy = lax.ppermute(plane_terms[-8:], "gz", pairs)
    depth_terms, plane_terms = pl.pallas_call(
        gather_kernel,
        out_shape=[
            jax.ShapeDtypeStruct(depth_terms.shape, f32),
            jax.ShapeDtypeStruct(plane_terms.shape, f32),
        ],
        compiler_params=plain_params(),
        name="gather",
    )(depth_terms, plane_terms, energy)
    depth_terms = lax.all_to_all(depth_terms, "gy", 0, 0)
    other = lax.ppermute(plane_terms, "gz", pairs)
    width = depth_factors.shape[2]
    step_depth, step_plane = pl.pallas_call(
        functools.partial(step_kernel, width * n_gz, nodes_x * nodes_y * n_gy),
        out_shape=[
            jax.ShapeDtypeStruct(depth_factors.shape, f32),
            jax.ShapeDtypeStruct(plane.shape, f32),
        ],
        compiler_params=plain_params(),
        name="steps",
    )(depth_terms, plane_terms, other)
    step_plane = jnp.transpose(step_plane.reshape(2, nodes_x, nodes_y, RANK), (0, 3, 1, 2))
    return residual, step_plane, step_depth


def solution(mesh):
    placed = (
        P(None, "gy", "gz"),
        P(None, "gy", "gz"),
        P(None, None, "gy", "gz"),
        P(None, None, None, "gy"),
        P(None, None, "gz"),
    )
    return jax.shard_map(
        local,
        mesh=mesh,
        in_specs=placed,
        out_specs=(P(None, "gy", "gz"), P(None, None, None, "gy"), P(None, None, "gz")),
        check_vma=False,
    )
```

```python
import functools

import jax
import jax.numpy as jnp
from jax import lax
from jax.experimental import pallas as pl
from jax.experimental.pallas import tpu as pltpu
from jax.sharding import PartitionSpec as P

RANK = 32
KNOT = 8
LANES = 128
TOP = 8

epsilon = 1e-06
damping = 0.01
highest = lax.Precision.HIGHEST
f32 = jnp.float32
bf16 = jnp.bfloat16


def dot(left, right, dims):
    return lax.dot_general(left, right, ((dims[0], dims[1]), ((), ())), precision=highest, preferred_element_type=f32)


def split_dot(left, right, dim):
    left_high, right_high = left.astype(bf16), right.astype(bf16)
    left_low = (left - left_high.astype(f32)).astype(bf16)
    right_low = (right - right_high.astype(f32)).astype(bf16)
    left = jnp.concatenate([left_high, left_high, left_low], axis=dim)
    right = jnp.concatenate([right_high, right_low, right_high], axis=dim)
    return lax.dot_general(left, right, (((dim,), (dim,)), ((), ())), preferred_element_type=f32)


def joined(ref):
    return jnp.concatenate([ref[tile] for tile in range(ref.shape[0])], axis=1)


def grid_params():
    return pltpu.CompilerParams(dimension_semantics=("arbitrary",), vmem_limit_bytes=40000000)


def plain_params():
    return pltpu.CompilerParams(vmem_limit_bytes=32000000)


def columns_kernel(*refs):
    inner_ref, outer_ref = refs[-2:]
    chunks = (len(refs) - 2) // 2
    rows = inner_ref.shape[0]
    lane = lax.broadcasted_iota(jnp.int32, (rows, LANES), 1)
    first = jnp.zeros((rows, LANES), f32)
    last = jnp.zeros((rows, LANES), f32)
    for chunk in range(chunks):
        near, far = refs[chunk], refs[chunks + chunk]
        for k in range(near.shape[0]):
            x = chunk * near.shape[0] + k
            first = jnp.where(lane == x, pltpu.roll(near[k].astype(f32), x, 1), first)
            last = jnp.where(lane == x, pltpu.roll(far[k].astype(f32), (x + 1) % LANES, 1), last)
    odd = lax.axis_index("gz") % 2 == 1
    inner_ref[...] = jnp.where(odd, first, last).astype(bf16)
    outer_ref[...] = jnp.where(odd, last, first).astype(bf16)


def end_columns(cells):
    depth, rows, width = cells.shape
    tiles = width // LANES
    chunks = 4
    block = (depth // chunks, rows, LANES)
    places = [(chunk, tile) for tile in (0, tiles - 1) for chunk in range(chunks)]
    return pl.pallas_call(
        columns_kernel,
        grid=(1,),
        in_specs=[pl.BlockSpec(block, functools.partial(lambda c, t, i: (c, 0, t), c, t)) for c, t in places],
        out_specs=[pl.BlockSpec((rows, LANES), lambda i: (0, 0))] * 2,
        out_shape=[jax.ShapeDtypeStruct((rows, LANES), bf16)] * 2,
        compiler_params=pltpu.CompilerParams(vmem_limit_bytes=60000000),
        name="columns",
    )(*[cells] * len(places))


def ends_kernel(*refs):
    low_ref, high_ref = refs[-2:]
    chunks = (len(refs) - 2) // 2
    for chunk in range(chunks):
        near, far = refs[chunk], refs[chunks + chunk]
        planes = near.shape[0]
        low = [near[k].astype(f32)[0:1] for k in range(planes)]
        high = [far[k].astype(f32)[15:16] for k in range(planes)]
        low_ref[chunk * planes : (chunk + 1) * planes, :] = jnp.concatenate(low, axis=0).astype(bf16)
        high_ref[chunk * planes : (chunk + 1) * planes, :] = jnp.concatenate(high, axis=0).astype(bf16)


def ends(cells):
    depth, rows, width = cells.shape
    chunks = 4
    block = (depth // chunks, 16, width)
    places = [(chunk, row) for row in (0, rows // 16 - 1) for chunk in range(chunks)]
    return pl.pallas_call(
        ends_kernel,
        grid=(1,),
        in_specs=[pl.BlockSpec(block, functools.partial(lambda c, r, i: (c, r, 0), c, r)) for c, r in places],
        out_specs=[pl.BlockSpec((depth, width), lambda i: (0, 0))] * 2,
        out_shape=[jax.ShapeDtypeStruct((depth, width), bf16)] * 2,
        compiler_params=pltpu.CompilerParams(vmem_limit_bytes=60000000),
        cost_estimate=pl.CostEstimate(flops=cells.size, bytes_accessed=2 * cells.size, transcendentals=0),
        name="ends",
    )(*[cells] * len(places))


def z_sides(inner_ref, outer_ref):
    odd = lax.axis_index("gz") % 2 == 1
    inner, outer = inner_ref[...].astype(f32), outer_ref[...].astype(f32)
    return jnp.where(odd, inner, outer), jnp.where(odd, outer, inner)


def rows_kernel(inner_ref, outer_ref, low_ref, high_ref, across_out, inside_out):
    depth, width = low_ref.shape
    rows = inner_ref.shape[0]
    odd = lax.axis_index("gy") % 2 == 1
    lane = lax.broadcasted_iota(jnp.int32, (depth, LANES), 1)
    pad = jnp.zeros((LANES - rows, LANES), f32)
    left, right = z_sides(inner_ref, outer_ref)
    left = jnp.transpose(jnp.concatenate([left, pad], axis=0))[0:depth]
    right = jnp.transpose(jnp.concatenate([right, pad], axis=0))[0:depth]
    bodies, beyond = [], []
    for row, body in ((0, low_ref), (rows - 1, high_ref)):
        after = pltpu.roll(right, (LANES - row) % LANES, 1)
        before = pltpu.roll(left, LANES - 1 - row, 1)
        bodies.append(body[...].astype(f32))
        beyond.append(jnp.where(lane == 0, after, before))
    for out, first, second in ((across_out, 1, 0), (inside_out, 0, 1)):
        out[:, 0:width] = jnp.where(odd, bodies[first], bodies[second]).astype(bf16)
        out[:, width : width + LANES] = jnp.where(odd, beyond[first], beyond[second]).astype(bf16)


def packed_rows(inner, outer, low, high):
    depth, width = low.shape
    return pl.pallas_call(
        rows_kernel,
        out_shape=[jax.ShapeDtypeStruct((depth, width + LANES), bf16)] * 2,
        compiler_params=plain_params(),
        cost_estimate=pl.CostEstimate(flops=500000 * low.size, bytes_accessed=8 * low.size, transcendentals=0),
        name="rows",
    )(inner, outer, low, high)


def swapped(part, axis, start):
    count = lax.axis_size(axis)
    pairs = [(i, i + 1) for i in range(start, count - 1, 2)]
    return lax.ppermute(part, axis, pairs + [(j, i) for i, j in pairs])


def squares_kernel(image_ref, later_ref, sums):
    depth, rows, width = image_ref.shape
    tiles = width // LANES

    def one(t, carry):
        block, tile = t // tiles, t % tiles
        at = pl.multiple_of(tile * LANES, LANES)
        for pair in range(rows // 16):
            total = jnp.zeros((16, LANES), f32)
            for k in range(KNOT):
                values = image_ref[block * KNOT + k, 16 * pair : 16 * pair + 16, pl.ds(at, LANES)].astype(f32)
                total = total + values * values
            for half in range(2):
                row = block * (rows // KNOT) + 2 * pair + half
                sums[tile, pl.ds(row, 1), :] = jnp.sum(total[8 * half : 8 * half + 8], axis=0, keepdims=True)
        return carry

    lax.fori_loop(0, depth // KNOT * tiles, one, 0)


def squares(image, later):
    depth, rows, width = image.shape
    return pl.pallas_call(
        squares_kernel,
        out_shape=jax.ShapeDtypeStruct((width // LANES, depth * rows // KNOT**2, LANES), f32),
        compiler_params=plain_params(),
        cost_estimate=pl.CostEstimate(flops=3 * image.size, bytes_accessed=2 * image.size, transcendentals=0),
        name="squares",
    )(image, later)


def terms_kernel(
    sums, plane_ref, depth_ref, inner_ref, outer_ref, field_ref, diag_depth_ref, diag_plane_ref, beyond_ref
):
    tiles = sums.shape[0]
    left, right = z_sides(inner_ref, outer_ref)
    lane = lax.broadcasted_iota(jnp.int32, left.shape, 1)
    for x in range(beyond_ref.shape[0]):
        after = pltpu.roll(right, (LANES - x) % LANES, 1)
        before = pltpu.roll(left, LANES - 1 - x, 1)
        beyond_ref[x] = jnp.where(lane == 0, after, before).astype(bf16)
    for k in range(2):
        field = dot(plane_ref[k], depth_ref[k], ((1,), (0,)))
        for tile in range(tiles):
            field_ref[k, tile] = field[:, tile * LANES : (tile + 1) * LANES]
    squared = joined(sums)
    cells = jnp.full(squared.shape, float(KNOT * KNOT), f32)
    first, second = plane_ref[0], plane_ref[1]
    diag_depth_ref[0] = dot(first * first, squared, ((0,), (0,)))
    diag_depth_ref[1] = dot(second * second, cells, ((0,), (0,)))
    first, second = depth_ref[0], depth_ref[1]
    diag_plane_ref[0] = dot(squared, first * first, ((1,), (1,)))
    diag_plane_ref[1] = dot(cells, second * second, ((1,), (1,)))


def terms(sums, plane, depth_factors, inner, outer, depth):
    nodes, width = plane.shape[1], depth_factors.shape[2]
    return pl.pallas_call(
        terms_kernel,
        out_shape=[
            jax.ShapeDtypeStruct((2, width // LANES, nodes, LANES), f32),
            jax.ShapeDtypeStruct((2, RANK, width), f32),
            jax.ShapeDtypeStruct((2, nodes, RANK), f32),
            jax.ShapeDtypeStruct((depth,) + inner.shape, bf16),
        ],
        compiler_params=plain_params(),
        cost_estimate=pl.CostEstimate(flops=40 * nodes * RANK * width, bytes_accessed=1 << 20, transcendentals=0),
        name="terms",
    )(sums, plane, depth_factors, inner, outer)


def warp_kernel(
    cells_ref, image_ref, shift_ref, beyond_ref, across_ref, inside_ref, field, plane_ref, depth_ref,
    diag_depth_ref, diag_plane_ref,
    residual_ref, depth_out, plane_out,
    ahead_ref, here_ref, behind_ref, wide, bands, rims, blocks, energy, held,
):
    step = pl.program_id(0)
    last = pl.num_programs(0) - 1
    planes, rows, width = cells_ref.shape
    nodes = rows // KNOT
    tiles = width // LANES
    window = (ahead_ref, here_ref, behind_ref)
    pitch = rows + 2 * TOP
    plane_rows = tiles * pitch
    block_rows = planes * plane_rows

    @pl.when(step == 0)
    def _():
        row = lax.broadcasted_iota(jnp.int32, bands.shape[1:], 0)
        column = lax.broadcasted_iota(jnp.int32, bands.shape[1:], 1)
        one, none = jnp.ones(bands.shape[1:], f32), jnp.zeros(bands.shape[1:], f32)
        up, down = jnp.where(row == column + 1, one, none), jnp.where(row == column, one, none)
        bands[0] = (up - down).astype(bf16)
        up = jnp.where(row == column + LANES, one, none)
        down = jnp.where(row == column + LANES - 1, one, none)
        bands[1] = (up - down).astype(bf16)
        energy[...] = jnp.zeros_like(energy)
        for c in range(3):
            window[c][3 * block_rows - plane_rows : 3 * block_rows, :] = jnp.zeros((plane_rows, LANES), f32)

    @pl.when(step < last)
    def _():
        slot = (step % 3) * block_rows
        span = planes * rows
        for k in range(planes):
            wide[k * rows : (k + 1) * rows, 0:width] = cells_ref[k]
            wide[k * rows : (k + 1) * rows, width:] = beyond_ref[k]
        odd = lax.axis_index("gy") % 2 == 1
        across, inside = across_ref[...].astype(f32), inside_ref[...].astype(f32)
        low, high = jnp.where(odd, inside, across), jnp.where(odd, across, inside)
        wide[span:, :] = jnp.concatenate([low, high], axis=0).astype(bf16)

        def put(c, tile, values):
            for k in range(planes):
                first = pl.multiple_of(slot + k * plane_rows + tile * pitch, 8)
                window[c][pl.ds(first + TOP, rows), :] = values[k * rows : (k + 1) * rows]
            for side, row in enumerate((0, TOP + rows)):
                rims[...] = values[span + side * planes : span + (side + 1) * planes]
                for k in range(planes):
                    first = pl.multiple_of(slot + k * plane_rows + tile * pitch, 8)
                    window[c][pl.ds(first + row, 8), :] = jnp.broadcast_to(rims[k : k + 1], (8, LANES))

        pieces = width // (2 * LANES)
        for piece in range(pieces):
            start = 2 * LANES * piece
            after = wide[:, start : start + 3 * LANES]
            if piece == 0:
                before = jnp.concatenate([wide[:, width:], wide[:, 0 : 2 * LANES]], axis=1)
            else:
                before = wide[:, start - LANES : start + 2 * LANES]
            ahead = jnp.dot(after, bands[0], preferred_element_type=f32)
            behind = jnp.dot(before, bands[1], preferred_element_type=f32)
            for half in range(2):
                mine = slice(half * LANES, (half + 1) * LANES)
                put(0, 2 * piece + half, ahead[:, mine])
                put(1, 2 * piece + half, wide[:, start + half * LANES : start + (half + 1) * LANES].astype(f32))
                put(2, 2 * piece + half, behind[:, mine])

    @pl.when(step == last)
    def _():
        first = pl.multiple_of((step % 3) * block_rows, 8)
        for c in range(3):
            window[c][pl.ds(first, plane_rows), :] = jnp.zeros((plane_rows, LANES), f32)

    @pl.when(step > 0)
    def _():
        mid = (step + 2) % 3
        first_rows = (
            jnp.where(mid == 0, 3, mid) * block_rows - plane_rows,
            mid * block_rows,
            jnp.where(mid == 2, 0, mid + 1) * block_rows,
        )

        def one(t, total):
            tile = t % tiles
            pair = t // tiles
            at = pl.multiple_of(tile * LANES, LANES)
            top = pl.multiple_of(pair * 16, 16)
            origins = [first + tile * pitch + top + TOP for first in first_rows]
            for half in range(2):
                node = (step - 1) * nodes + pair * 2 + half
                mine = slice(8 * half, 8 * half + 8)

                def taps(x):
                    part = 0 if x == 0 else 2 if x == planes + 1 else 1
                    plus = (x - 1) * plane_rows + 8 * half if part == 1 else 8 * half
                    return [
                        [window[c][pl.ds(origins[part] + (plus + b), 8), :] for c in range(3)] for b in (-1, 0, 1)
                    ]

                contrast = jnp.broadcast_to(field[0, tile, pl.ds(node, 1), :], (8, LANES))
                brightness = jnp.broadcast_to(field[1, tile, pl.ds(node, 1), :], (8, LANES))
                by_image = jnp.zeros((8, LANES), f32)
                plain = jnp.zeros((8, LANES), f32)
                before, here = taps(0), taps(1)
                for k in range(planes):
                    after = taps(k + 2)
                    place = (k, pl.ds(top, 16), pl.ds(at, LANES))
                    sx, sy, sz = (shift_ref[(axis,) + place].astype(f32)[mine] for axis in range(3))
                    image = image_ref[place].astype(f32)[mine]
                    px, py, pz = sx > 0, sy > 0, sz > 0
                    ax, ay = jnp.abs(sx), jnp.abs(sy)

                    def sides(c):
                        far = [jnp.where(px, after[b][c], before[b][c]) for b in range(3)]
                        near = [here[b][c] for b in range(3)]
                        return [(v[1], jnp.where(py, v[2], v[0])) for v in (near, far)]

                    ahead, middle, behind = sides(0), sides(1), sides(2)
                    lines = []
                    for b in range(2):
                        near, far = (middle[v][b] + sz * jnp.where(pz, ahead[v][b], behind[v][b]) for v in range(2))
                        lines.append(near + ax * (far - near))
                    warped = lines[0] + ay * (lines[1] - lines[0])
                    misfit = warped - contrast * image - brightness
                    if half == 0:
                        held[k] = misfit
                    else:
                        residual_ref[place] = jnp.concatenate([held[k], misfit], axis=0).astype(bf16)
                    by_image = by_image + misfit * image
                    plain = plain + misfit
                    total = total + misfit * misfit
                    before, here = here, after
                for k, value in ((0, by_image), (1, plain)):
                    blocks[k, tile, pl.ds(node, 1), :] = jnp.sum(value, axis=0, keepdims=True)
            return total

        energy[...] = lax.fori_loop(0, (rows // 16) * tiles, one, energy[...], unroll=2)

    @pl.when(step == last)
    def _():
        parts = depth_out.shape[0]
        share = RANK // parts
        sums = [joined(blocks.at[k]) for k in range(2)]
        kinds = [split_dot(plane_ref[k], sums[k], 0) for k in range(2)]
        kinds = kinds + [diag_depth_ref[0], diag_depth_ref[1]]
        for p in range(parts):
            for k in range(4):
                depth_out[p, k * share : (k + 1) * share, :] = kinds[k][p * share : (p + 1) * share]
        local = jnp.sum(energy[...])
        kinds = [split_dot(sums[k], depth_ref[k], 1) for k in range(2)]
        kinds = kinds + [diag_plane_ref[0], diag_plane_ref[1]]
        for k in range(4):
            plane_out[:, k * RANK : (k + 1) * RANK] = kinds[k]
        count = plane_out.shape[0]
        plane_out[count // 2 :, 3 * RANK :] = jnp.full((count // 2, RANK), local, f32)


def warp(cells, image, shift, beyond, across, inside, field, plane, depth_factors, diag_depth, diag_plane, parts):
    depth, rows, width = cells.shape
    nodes = plane.shape[1]
    tiles = width // LANES
    count = depth // KNOT
    behind = lambda i: (jnp.maximum(i - 1, 0), 0, 0)
    ahead = lambda i: (jnp.minimum(i, count - 1), 0, 0)
    flat = lambda i: (0, 0)
    whole = lambda i: (0, 0, 0)
    return pl.pallas_call(
        warp_kernel,
        grid=(count + 1,),
        in_specs=[
            pl.BlockSpec((KNOT, rows, width), ahead),
            pl.BlockSpec((KNOT, rows, width), behind),
            pl.BlockSpec((3, KNOT, rows, width), lambda i: (0, jnp.maximum(i - 1, 0), 0, 0)),
            pl.BlockSpec((KNOT, rows, LANES), ahead),
            pl.BlockSpec((KNOT, across.shape[1]), lambda i: (jnp.minimum(i, count - 1), 0)),
            pl.BlockSpec((KNOT, inside.shape[1]), lambda i: (jnp.minimum(i, count - 1), 0)),
            pl.BlockSpec(field.shape, lambda i: (0, 0, 0, 0)),
            pl.BlockSpec(plane.shape, whole),
            pl.BlockSpec(depth_factors.shape, whole),
            pl.BlockSpec(diag_depth.shape, whole),
            pl.BlockSpec(diag_plane.shape, whole),
        ],
        out_specs=[
            pl.BlockSpec((KNOT, rows, width), behind),
            pl.BlockSpec((parts, 4 * RANK // parts, width), whole),
            pl.BlockSpec((nodes, 4 * RANK), flat),
        ],
        out_shape=[
            jax.ShapeDtypeStruct(cells.shape, bf16),
            jax.ShapeDtypeStruct((parts, 4 * RANK // parts, width), f32),
            jax.ShapeDtypeStruct((nodes, 4 * RANK), f32),
        ],
        scratch_shapes=[
            *[pltpu.VMEM((3 * KNOT * tiles * (rows + 2 * TOP), LANES), f32)] * 3,
            pltpu.VMEM((KNOT * rows + 2 * KNOT, width + LANES), bf16),
            pltpu.VMEM((2, 3 * LANES, 2 * LANES), bf16),
            pltpu.VMEM((KNOT, LANES), f32),
            pltpu.VMEM((2, tiles, nodes, LANES), f32),
            pltpu.VMEM((8, LANES), f32),
            pltpu.VMEM((KNOT, 8, LANES), f32),
        ],
        compiler_params=grid_params(),
        cost_estimate=pl.CostEstimate(flops=60 * cells.size, bytes_accessed=12 * cells.size, transcendentals=0),
        name="warp",
    )(cells, image, shift, beyond, across, inside, field, plane, depth_factors, diag_depth, diag_plane)


def gather_kernel(depth_ref, *refs):
    depth_out, plane_out = refs[-2:]
    total = jnp.sum(depth_ref[...], axis=0)
    found = [ref[...] for ref in refs[:-2]]
    while len(found) > 1:
        half = len(found) // 2
        found = [found[k] + found[k + half] for k in range(half)]
    planes = found[0]
    plane_out[...] = planes
    cells = planes.shape[0]
    share, width = total.shape[0] // 4, total.shape[1]
    row = lax.broadcasted_iota(jnp.int32, total.shape, 0)
    lane = lax.broadcasted_iota(jnp.int32, total.shape, 1)
    partial = planes[cells - 1, 4 * RANK - 1]
    total = jnp.where((row >= 3 * share) & (lane >= width // 2), partial, total)
    for p in range(depth_out.shape[0]):
        depth_out[p] = total


def step_kernel(full_z, node_count, depth_ref, plane_ref, depth_out, plane_out):
    parts, share, width = depth_ref.shape[0], depth_ref.shape[1] // 4, depth_ref.shape[2]
    energy = depth_ref[0, 3 * share, width - 1]
    for p in range(1, parts):
        energy = energy + depth_ref[p, 3 * share, width - 1]
    lam_depth = damping * energy / full_z
    lam_plane = damping * RANK * energy / node_count
    for p in range(parts):
        got = depth_ref[p]
        levels = got[3 * share :, 0 : width // 2]
        levels = jnp.concatenate([levels, levels], axis=1)
        rows = slice(p * share, (p + 1) * share)
        depth_out[0, rows, :] = got[0:share] / (got[2 * share : 3 * share] + lam_depth + epsilon)
        depth_out[1, rows, :] = got[share : 2 * share] / (levels + lam_depth + epsilon)
    planes = plane_ref[...]
    plane_out[0] = planes[:, 0:RANK] / (planes[:, 2 * RANK : 3 * RANK] + lam_plane + epsilon)
    plane_out[1] = planes[:, RANK : 2 * RANK] / (planes[0:1, 3 * RANK :] + lam_plane + epsilon)


def local(image, deformed, displacement, plane_factors, depth_factors):
    n_gy, n_gz = lax.axis_size("gy"), lax.axis_size("gz")
    nodes_x, nodes_y = plane_factors.shape[2:]
    plane = jnp.transpose(plane_factors, (0, 2, 3, 1)).reshape(2, nodes_x * nodes_y, RANK)
    inner, outer = end_columns(deformed)
    inner = swapped(inner, "gz", 0)
    outer = swapped(outer, "gz", 1)
    low, high = ends(deformed)
    across, inside = packed_rows(inner, outer, low, high)
    later = across
    inside = swapped(inside, "gy", 0)
    across = swapped(across, "gy", 1)
    sums = squares(image, later)
    field, diag_depth, diag_plane, beyond = terms(sums, plane, depth_factors, inner, outer, deformed.shape[0])
    residual, depth_terms, plane_terms = warp(
        deformed, image, displacement, beyond, across, inside, field, plane, depth_factors, diag_depth, diag_plane,
        n_gy,
    )
    depth_terms = lax.all_to_all(depth_terms, "gy", 0, 0)
    others = [
        lax.ppermute(plane_terms, "gz", [(i, (i + hop) % n_gz) for i in range(n_gz)]) for hop in range(1, n_gz)
    ]
    depth_terms, plane_terms = pl.pallas_call(
        gather_kernel,
        out_shape=[
            jax.ShapeDtypeStruct(depth_terms.shape, f32),
            jax.ShapeDtypeStruct(plane_terms.shape, f32),
        ],
        compiler_params=plain_params(),
        name="gather",
    )(depth_terms, plane_terms, *others)
    depth_terms = lax.all_to_all(depth_terms, "gy", 0, 0)
    width = depth_factors.shape[2]
    step_depth, step_plane = pl.pallas_call(
        functools.partial(step_kernel, width * n_gz, nodes_x * nodes_y * n_gy),
        out_shape=[
            jax.ShapeDtypeStruct(depth_factors.shape, f32),
            jax.ShapeDtypeStruct(plane.shape, f32),
        ],
        compiler_params=plain_params(),
        name="steps",
    )(depth_terms, plane_terms)
    step_plane = jnp.transpose(step_plane.reshape(2, nodes_x, nodes_y, RANK), (0, 3, 1, 2))
    return residual, step_plane, step_depth


def solution(mesh):
    placed = (
        P(None, "gy", "gz"),
        P(None, "gy", "gz"),
        P(None, None, "gy", "gz"),
        P(None, None, None, "gy"),
        P(None, None, "gz"),
    )
    return jax.shard_map(
        local,
        mesh=mesh,
        in_specs=placed,
        out_specs=(P(None, "gy", "gz"), P(None, None, None, "gy"), P(None, None, "gz")),
        check_vma=False,
    )
```

```python
import functools

import jax
import jax.numpy as jnp
from jax import lax
from jax.experimental import pallas as pl
from jax.experimental.pallas import tpu as pltpu
from jax.sharding import PartitionSpec as P

RANK = 32
KNOT = 8
LANES = 128
TOP = 8

epsilon = 1e-06
damping = 0.01
highest = lax.Precision.HIGHEST
f32 = jnp.float32
bf16 = jnp.bfloat16


def dot(left, right, dims):
    return lax.dot_general(left, right, ((dims[0], dims[1]), ((), ())), precision=highest, preferred_element_type=f32)


def split_dot(left, right, dim):
    left_high, right_high = left.astype(bf16), right.astype(bf16)
    left_low = (left - left_high.astype(f32)).astype(bf16)
    right_low = (right - right_high.astype(f32)).astype(bf16)
    left = jnp.concatenate([left_high, left_high, left_low], axis=dim)
    right = jnp.concatenate([right_high, right_low, right_high], axis=dim)
    return lax.dot_general(left, right, (((dim,), (dim,)), ((), ())), preferred_element_type=f32)


def joined(ref):
    return jnp.concatenate([ref[tile] for tile in range(ref.shape[0])], axis=1)


def grid_params():
    return pltpu.CompilerParams(dimension_semantics=("arbitrary",), vmem_limit_bytes=40000000)


def plain_params():
    return pltpu.CompilerParams(vmem_limit_bytes=32000000)


def columns_kernel(*refs):
    inner_ref, outer_ref = refs[-2:]
    chunks = (len(refs) - 2) // 2
    rows = inner_ref.shape[0]
    lane = lax.broadcasted_iota(jnp.int32, (rows, LANES), 1)
    first = jnp.zeros((rows, LANES), f32)
    last = jnp.zeros((rows, LANES), f32)
    for chunk in range(chunks):
        near, far = refs[chunk], refs[chunks + chunk]
        for k in range(near.shape[0]):
            x = chunk * near.shape[0] + k
            first = jnp.where(lane == x, pltpu.roll(near[k].astype(f32), x, 1), first)
            last = jnp.where(lane == x, pltpu.roll(far[k].astype(f32), (x + 1) % LANES, 1), last)
    odd = lax.axis_index("gz") % 2 == 1
    inner_ref[...] = jnp.where(odd, first, last).astype(bf16)
    outer_ref[...] = jnp.where(odd, last, first).astype(bf16)


def end_columns(cells):
    depth, rows, width = cells.shape
    tiles = width // LANES
    chunks = 4
    block = (depth // chunks, rows, LANES)
    places = [(chunk, tile) for tile in (0, tiles - 1) for chunk in range(chunks)]
    return pl.pallas_call(
        columns_kernel,
        grid=(1,),
        in_specs=[pl.BlockSpec(block, functools.partial(lambda c, t, i: (c, 0, t), c, t)) for c, t in places],
        out_specs=[pl.BlockSpec((rows, LANES), lambda i: (0, 0))] * 2,
        out_shape=[jax.ShapeDtypeStruct((rows, LANES), bf16)] * 2,
        compiler_params=pltpu.CompilerParams(vmem_limit_bytes=60000000),
        name="columns",
    )(*[cells] * len(places))


def ends_kernel(cells_ref, low_ref, high_ref):
    depth, rows = cells_ref.shape[0:2]
    for x in range(0, depth, 16):
        low = [cells_ref[x + k, 0:16, :].astype(f32)[0:1] for k in range(16)]
        high = [cells_ref[x + k, rows - 16 : rows, :].astype(f32)[15:16] for k in range(16)]
        low_ref[x : x + 16, :] = jnp.concatenate(low, axis=0).astype(bf16)
        high_ref[x : x + 16, :] = jnp.concatenate(high, axis=0).astype(bf16)


def ends(cells):
    depth, rows, width = cells.shape
    return pl.pallas_call(
        ends_kernel,
        out_shape=[jax.ShapeDtypeStruct((depth, width), bf16)] * 2,
        compiler_params=plain_params(),
        cost_estimate=pl.CostEstimate(flops=cells.size, bytes_accessed=2 * cells.size, transcendentals=0),
        name="ends",
    )(cells)


def z_sides(inner_ref, outer_ref):
    odd = lax.axis_index("gz") % 2 == 1
    inner, outer = inner_ref[...].astype(f32), outer_ref[...].astype(f32)
    return jnp.where(odd, inner, outer), jnp.where(odd, outer, inner)


def rows_kernel(inner_ref, outer_ref, low_ref, high_ref, across_out, inside_out):
    depth, width = low_ref.shape
    rows = inner_ref.shape[0]
    odd = lax.axis_index("gy") % 2 == 1
    lane = lax.broadcasted_iota(jnp.int32, (depth, LANES), 1)
    pad = jnp.zeros((LANES - rows, LANES), f32)
    left, right = z_sides(inner_ref, outer_ref)
    left = jnp.transpose(jnp.concatenate([left, pad], axis=0))[0:depth]
    right = jnp.transpose(jnp.concatenate([right, pad], axis=0))[0:depth]
    bodies, beyond = [], []
    for row, body in ((0, low_ref), (rows - 1, high_ref)):
        after = pltpu.roll(right, (LANES - row) % LANES, 1)
        before = pltpu.roll(left, LANES - 1 - row, 1)
        bodies.append(body[...].astype(f32))
        beyond.append(jnp.where(lane == 0, after, before))
    for out, first, second in ((across_out, 1, 0), (inside_out, 0, 1)):
        out[:, 0:width] = jnp.where(odd, bodies[first], bodies[second]).astype(bf16)
        out[:, width : width + LANES] = jnp.where(odd, beyond[first], beyond[second]).astype(bf16)


def packed_rows(inner, outer, low, high):
    depth, width = low.shape
    return pl.pallas_call(
        rows_kernel,
        out_shape=[jax.ShapeDtypeStruct((depth, width + LANES), bf16)] * 2,
        compiler_params=plain_params(),
        cost_estimate=pl.CostEstimate(flops=500000 * low.size, bytes_accessed=8 * low.size, transcendentals=0),
        name="rows",
    )(inner, outer, low, high)


def swapped(part, axis, start):
    count = lax.axis_size(axis)
    pairs = [(i, i + 1) for i in range(start, count - 1, 2)]
    return lax.ppermute(part, axis, pairs + [(j, i) for i, j in pairs])


def squares_kernel(image_ref, later_ref, sums):
    depth, rows, width = image_ref.shape
    tiles = width // LANES

    def one(t, carry):
        block, tile = t // tiles, t % tiles
        at = pl.multiple_of(tile * LANES, LANES)
        for pair in range(rows // 16):
            total = jnp.zeros((16, LANES), f32)
            for k in range(KNOT):
                values = image_ref[block * KNOT + k, 16 * pair : 16 * pair + 16, pl.ds(at, LANES)].astype(f32)
                total = total + values * values
            for half in range(2):
                row = block * (rows // KNOT) + 2 * pair + half
                sums[tile, pl.ds(row, 1), :] = jnp.sum(total[8 * half : 8 * half + 8], axis=0, keepdims=True)
        return carry

    lax.fori_loop(0, depth // KNOT * tiles, one, 0)


def squares(image, later):
    depth, rows, width = image.shape
    return pl.pallas_call(
        squares_kernel,
        out_shape=jax.ShapeDtypeStruct((width // LANES, depth * rows // KNOT**2, LANES), f32),
        compiler_params=plain_params(),
        cost_estimate=pl.CostEstimate(flops=3 * image.size, bytes_accessed=2 * image.size, transcendentals=0),
        name="squares",
    )(image, later)


def terms_kernel(
    sums, plane_ref, depth_ref, inner_ref, outer_ref, field_ref, diag_depth_ref, diag_plane_ref, beyond_ref
):
    tiles = sums.shape[0]
    left, right = z_sides(inner_ref, outer_ref)
    lane = lax.broadcasted_iota(jnp.int32, left.shape, 1)
    for x in range(beyond_ref.shape[0]):
        after = pltpu.roll(right, (LANES - x) % LANES, 1)
        before = pltpu.roll(left, LANES - 1 - x, 1)
        beyond_ref[x] = jnp.where(lane == 0, after, before).astype(bf16)
    for k in range(2):
        field = dot(plane_ref[k], depth_ref[k], ((1,), (0,)))
        for tile in range(tiles):
            field_ref[k, tile] = field[:, tile * LANES : (tile + 1) * LANES]
    squared = joined(sums)
    cells = jnp.full(squared.shape, float(KNOT * KNOT), f32)
    first, second = plane_ref[0], plane_ref[1]
    diag_depth_ref[0] = dot(first * first, squared, ((0,), (0,)))
    diag_depth_ref[1] = dot(second * second, cells, ((0,), (0,)))
    first, second = depth_ref[0], depth_ref[1]
    diag_plane_ref[0] = dot(squared, first * first, ((1,), (1,)))
    diag_plane_ref[1] = dot(cells, second * second, ((1,), (1,)))


def terms(sums, plane, depth_factors, inner, outer, depth):
    nodes, width = plane.shape[1], depth_factors.shape[2]
    return pl.pallas_call(
        terms_kernel,
        out_shape=[
            jax.ShapeDtypeStruct((2, width // LANES, nodes, LANES), f32),
            jax.ShapeDtypeStruct((2, RANK, width), f32),
            jax.ShapeDtypeStruct((2, nodes, RANK), f32),
            jax.ShapeDtypeStruct((depth,) + inner.shape, bf16),
        ],
        compiler_params=plain_params(),
        cost_estimate=pl.CostEstimate(flops=40 * nodes * RANK * width, bytes_accessed=1 << 20, transcendentals=0),
        name="terms",
    )(sums, plane, depth_factors, inner, outer)


def warp_kernel(
    cells_ref, image_ref, shift_ref, beyond_ref, across_ref, inside_ref, field, plane_ref, depth_ref,
    diag_depth_ref, diag_plane_ref,
    residual_ref, depth_out, plane_out,
    ahead_ref, here_ref, behind_ref, wide, bands, blocks, energy, held,
):
    step = pl.program_id(0)
    last = pl.num_programs(0) - 1
    planes, rows, width = cells_ref.shape
    nodes = rows // KNOT
    tiles = width // LANES
    window = (ahead_ref, here_ref, behind_ref)
    pitch = rows + 2 * TOP
    plane_rows = tiles * pitch
    block_rows = planes * plane_rows

    @pl.when(step == 0)
    def _():
        row = lax.broadcasted_iota(jnp.int32, bands.shape[1:], 0)
        column = lax.broadcasted_iota(jnp.int32, bands.shape[1:], 1)
        one, none = jnp.ones(bands.shape[1:], f32), jnp.zeros(bands.shape[1:], f32)
        up, down = jnp.where(row == column + 1, one, none), jnp.where(row == column, one, none)
        bands[0] = (up - down).astype(bf16)
        up = jnp.where(row == column + LANES, one, none)
        down = jnp.where(row == column + LANES - 1, one, none)
        bands[1] = (up - down).astype(bf16)
        energy[...] = jnp.zeros_like(energy)
        for c in range(3):
            window[c][3 * block_rows - plane_rows : 3 * block_rows, :] = jnp.zeros((plane_rows, LANES), f32)

    @pl.when(step < last)
    def _():
        slot = (step % 3) * block_rows
        odd = lax.axis_index("gy") % 2 == 1
        across, inside = across_ref[...].astype(f32), inside_ref[...].astype(f32)
        low, high = jnp.where(odd, inside, across), jnp.where(odd, across, inside)
        at = lax.broadcasted_iota(jnp.int32, (2 * TOP, width + LANES), 0)
        for k in range(planes):
            first = k * pitch
            wide[first : first + rows, 0:width] = cells_ref[k]
            wide[first : first + rows, width:] = beyond_ref[k]
            rim = jnp.where(at == TOP, high[k : k + 1], jnp.where(at == TOP - 1, low[k : k + 1], 0.0))
            wide[first + rows : first + pitch, :] = rim.astype(bf16)

        def put(c, tile, values):
            for k in range(planes):
                first = pl.multiple_of(slot + k * plane_rows + tile * pitch, 8)
                mine = values[k * pitch : (k + 1) * pitch]
                window[c][pl.ds(first + TOP, rows), :] = mine[0:rows]
                window[c][pl.ds(first, TOP), :] = mine[rows : rows + TOP]
                window[c][pl.ds(first + TOP + rows, TOP), :] = mine[rows + TOP :]

        pieces = width // (2 * LANES)
        for piece in range(pieces):
            start = 2 * LANES * piece
            after = wide[:, start : start + 3 * LANES]
            if piece == 0:
                before = jnp.concatenate([wide[:, width:], wide[:, 0 : 2 * LANES]], axis=1)
            else:
                before = wide[:, start - LANES : start + 2 * LANES]
            ahead = jnp.dot(after, bands[0], preferred_element_type=f32)
            behind = jnp.dot(before, bands[1], preferred_element_type=f32)
            for half in range(2):
                mine = slice(half * LANES, (half + 1) * LANES)
                put(0, 2 * piece + half, ahead[:, mine])
                put(1, 2 * piece + half, wide[:, start + half * LANES : start + (half + 1) * LANES].astype(f32))
                put(2, 2 * piece + half, behind[:, mine])

    @pl.when(step == last)
    def _():
        first = pl.multiple_of((step % 3) * block_rows, 8)
        for c in range(3):
            window[c][pl.ds(first, plane_rows), :] = jnp.zeros((plane_rows, LANES), f32)

    @pl.when(step > 0)
    def _():
        mid = (step + 2) % 3
        first_rows = (
            jnp.where(mid == 0, 3, mid) * block_rows - plane_rows,
            mid * block_rows,
            jnp.where(mid == 2, 0, mid + 1) * block_rows,
        )

        def one(t, total):
            tile = t % tiles
            pair = t // tiles
            at = pl.multiple_of(tile * LANES, LANES)
            top = pl.multiple_of(pair * 16, 16)
            origins = [first + tile * pitch + top + TOP for first in first_rows]
            for half in range(2):
                node = (step - 1) * nodes + pair * 2 + half
                mine = slice(8 * half, 8 * half + 8)

                def taps(x):
                    part = 0 if x == 0 else 2 if x == planes + 1 else 1
                    plus = (x - 1) * plane_rows + 8 * half if part == 1 else 8 * half
                    return [
                        [window[c][pl.ds(origins[part] + (plus + b), 8), :] for c in range(3)] for b in (-1, 0, 1)
                    ]

                contrast = jnp.broadcast_to(field[0, tile, pl.ds(node, 1), :], (8, LANES))
                brightness = jnp.broadcast_to(field[1, tile, pl.ds(node, 1), :], (8, LANES))
                by_image = jnp.zeros((8, LANES), f32)
                plain = jnp.zeros((8, LANES), f32)
                before, here = taps(0), taps(1)
                for k in range(planes):
                    after = taps(k + 2)
                    place = (k, pl.ds(top, 16), pl.ds(at, LANES))
                    sx, sy, sz = (shift_ref[(axis,) + place].astype(f32)[mine] for axis in range(3))
                    image = image_ref[place].astype(f32)[mine]
                    px, py, pz = sx > 0, sy > 0, sz > 0
                    ax, ay = jnp.abs(sx), jnp.abs(sy)

                    def sides(c):
                        far = [jnp.where(px, after[b][c], before[b][c]) for b in range(3)]
                        near = [here[b][c] for b in range(3)]
                        return [(v[1], jnp.where(py, v[2], v[0])) for v in (near, far)]

                    ahead, middle, behind = sides(0), sides(1), sides(2)
                    lines = []
                    for b in range(2):
                        near, far = (middle[v][b] + sz * jnp.where(pz, ahead[v][b], behind[v][b]) for v in range(2))
                        lines.append(near + ax * (far - near))
                    warped = lines[0] + ay * (lines[1] - lines[0])
                    misfit = warped - contrast * image - brightness
                    if half == 0:
                        held[k] = misfit
                    else:
                        residual_ref[place] = jnp.concatenate([held[k], misfit], axis=0).astype(bf16)
                    by_image = by_image + misfit * image
                    plain = plain + misfit
                    total = total + misfit * misfit
                    before, here = here, after
                for k, value in ((0, by_image), (1, plain)):
                    blocks[k, tile, pl.ds(node, 1), :] = jnp.sum(value, axis=0, keepdims=True)
            return total

        energy[...] = lax.fori_loop(0, (rows // 16) * tiles, one, energy[...], unroll=2)

    @pl.when(step == last)
    def _():
        parts = depth_out.shape[0]
        share = RANK // parts
        sums = [joined(blocks.at[k]) for k in range(2)]
        kinds = [split_dot(plane_ref[k], sums[k], 0) for k in range(2)]
        kinds = kinds + [diag_depth_ref[0], diag_depth_ref[1]]
        for p in range(parts):
            for k in range(4):
                depth_out[p, k * share : (k + 1) * share, :] = kinds[k][p * share : (p + 1) * share]
        local = jnp.sum(energy[...])
        kinds = [split_dot(sums[k], depth_ref[k], 1) for k in range(2)]
        kinds = kinds + [diag_plane_ref[0], diag_plane_ref[1]]
        for k in range(4):
            plane_out[:, k * RANK : (k + 1) * RANK] = kinds[k]
        count = plane_out.shape[0]
        plane_out[count // 2 :, 3 * RANK :] = jnp.full((count // 2, RANK), local, f32)


def warp(cells, image, shift, beyond, across, inside, field, plane, depth_factors, diag_depth, diag_plane, parts):
    depth, rows, width = cells.shape
    nodes = plane.shape[1]
    tiles = width // LANES
    count = depth // KNOT
    behind = lambda i: (jnp.maximum(i - 1, 0), 0, 0)
    ahead = lambda i: (jnp.minimum(i, count - 1), 0, 0)
    flat = lambda i: (0, 0)
    whole = lambda i: (0, 0, 0)
    return pl.pallas_call(
        warp_kernel,
        grid=(count + 1,),
        in_specs=[
            pl.BlockSpec((KNOT, rows, width), ahead),
            pl.BlockSpec((KNOT, rows, width), behind),
            pl.BlockSpec((3, KNOT, rows, width), lambda i: (0, jnp.maximum(i - 1, 0), 0, 0)),
            pl.BlockSpec((KNOT, rows, LANES), ahead),
            pl.BlockSpec((KNOT, across.shape[1]), lambda i: (jnp.minimum(i, count - 1), 0)),
            pl.BlockSpec((KNOT, inside.shape[1]), lambda i: (jnp.minimum(i, count - 1), 0)),
            pl.BlockSpec(field.shape, lambda i: (0, 0, 0, 0)),
            pl.BlockSpec(plane.shape, whole),
            pl.BlockSpec(depth_factors.shape, whole),
            pl.BlockSpec(diag_depth.shape, whole),
            pl.BlockSpec(diag_plane.shape, whole),
        ],
        out_specs=[
            pl.BlockSpec((KNOT, rows, width), behind),
            pl.BlockSpec((parts, 4 * RANK // parts, width), whole),
            pl.BlockSpec((nodes, 4 * RANK), flat),
        ],
        out_shape=[
            jax.ShapeDtypeStruct(cells.shape, bf16),
            jax.ShapeDtypeStruct((parts, 4 * RANK // parts, width), f32),
            jax.ShapeDtypeStruct((nodes, 4 * RANK), f32),
        ],
        scratch_shapes=[
            *[pltpu.VMEM((3 * KNOT * tiles * (rows + 2 * TOP), LANES), f32)] * 3,
            pltpu.VMEM((KNOT * (rows + 2 * TOP), width + LANES), bf16),
            pltpu.VMEM((2, 3 * LANES, 2 * LANES), bf16),
            pltpu.VMEM((2, tiles, nodes, LANES), f32),
            pltpu.VMEM((8, LANES), f32),
            pltpu.VMEM((KNOT, 8, LANES), f32),
        ],
        compiler_params=grid_params(),
        cost_estimate=pl.CostEstimate(flops=60 * cells.size, bytes_accessed=12 * cells.size, transcendentals=0),
        name="warp",
    )(cells, image, shift, beyond, across, inside, field, plane, depth_factors, diag_depth, diag_plane)


def gather_kernel(depth_ref, *refs):
    depth_out, plane_out = refs[-2:]
    total = jnp.sum(depth_ref[...], axis=0)
    found = [ref[...] for ref in refs[:-2]]
    while len(found) > 1:
        half = len(found) // 2
        found = [found[k] + found[k + half] for k in range(half)]
    planes = found[0]
    plane_out[...] = planes
    cells = planes.shape[0]
    share, width = total.shape[0] // 4, total.shape[1]
    row = lax.broadcasted_iota(jnp.int32, total.shape, 0)
    lane = lax.broadcasted_iota(jnp.int32, total.shape, 1)
    partial = planes[cells - 1, 4 * RANK - 1]
    total = jnp.where((row >= 3 * share) & (lane >= width // 2), partial, total)
    for p in range(depth_out.shape[0]):
        depth_out[p] = total


def step_kernel(full_z, node_count, depth_ref, plane_ref, depth_out, plane_out):
    parts, share, width = depth_ref.shape[0], depth_ref.shape[1] // 4, depth_ref.shape[2]
    energy = depth_ref[0, 3 * share, width - 1]
    for p in range(1, parts):
        energy = energy + depth_ref[p, 3 * share, width - 1]
    lam_depth = damping * energy / full_z
    lam_plane = damping * RANK * energy / node_count
    for p in range(parts):
        got = depth_ref[p]
        levels = got[3 * share :, 0 : width // 2]
        levels = jnp.concatenate([levels, levels], axis=1)
        rows = slice(p * share, (p + 1) * share)
        depth_out[0, rows, :] = got[0:share] / (got[2 * share : 3 * share] + lam_depth + epsilon)
        depth_out[1, rows, :] = got[share : 2 * share] / (levels + lam_depth + epsilon)
    planes = plane_ref[...]
    plane_out[0] = planes[:, 0:RANK] / (planes[:, 2 * RANK : 3 * RANK] + lam_plane + epsilon)
    plane_out[1] = planes[:, RANK : 2 * RANK] / (planes[0:1, 3 * RANK :] + lam_plane + epsilon)


def local(image, deformed, displacement, plane_factors, depth_factors):
    n_gy, n_gz = lax.axis_size("gy"), lax.axis_size("gz")
    nodes_x, nodes_y = plane_factors.shape[2:]
    plane = jnp.transpose(plane_factors, (0, 2, 3, 1)).reshape(2, nodes_x * nodes_y, RANK)
    inner, outer = end_columns(deformed)
    inner = swapped(inner, "gz", 0)
    outer = swapped(outer, "gz", 1)
    low, high = ends(deformed)
    across, inside = packed_rows(inner, outer, low, high)
    later = across
    inside = swapped(inside, "gy", 0)
    across = swapped(across, "gy", 1)
    sums = squares(image, later)
    field, diag_depth, diag_plane, beyond = terms(sums, plane, depth_factors, inner, outer, deformed.shape[0])
    residual, depth_terms, plane_terms = warp(
        deformed, image, displacement, beyond, across, inside, field, plane, depth_factors, diag_depth, diag_plane,
        n_gy,
    )
    depth_terms = lax.all_to_all(depth_terms, "gy", 0, 0)
    others = [
        lax.ppermute(plane_terms, "gz", [(i, (i + hop) % n_gz) for i in range(n_gz)]) for hop in range(1, n_gz)
    ]
    depth_terms, plane_terms = pl.pallas_call(
        gather_kernel,
        out_shape=[
            jax.ShapeDtypeStruct(depth_terms.shape, f32),
            jax.ShapeDtypeStruct(plane_terms.shape, f32),
        ],
        compiler_params=plain_params(),
        name="gather",
    )(depth_terms, plane_terms, *others)
    depth_terms = lax.all_to_all(depth_terms, "gy", 0, 0)
    width = depth_factors.shape[2]
    step_depth, step_plane = pl.pallas_call(
        functools.partial(step_kernel, width * n_gz, nodes_x * nodes_y * n_gy),
        out_shape=[
            jax.ShapeDtypeStruct(depth_factors.shape, f32),
            jax.ShapeDtypeStruct(plane.shape, f32),
        ],
        compiler_params=plain_params(),
        name="steps",
    )(depth_terms, plane_terms)
    step_plane = jnp.transpose(step_plane.reshape(2, nodes_x, nodes_y, RANK), (0, 3, 1, 2))
    return residual, step_plane, step_depth


def solution(mesh):
    placed = (
        P(None, "gy", "gz"),
        P(None, "gy", "gz"),
        P(None, None, "gy", "gz"),
        P(None, None, None, "gy"),
        P(None, None, "gz"),
    )
    return jax.shard_map(
        local,
        mesh=mesh,
        in_specs=placed,
        out_specs=(P(None, "gy", "gz"), P(None, None, None, "gy"), P(None, None, "gz")),
        check_vma=False,
    )
```

```python
import functools

import jax
import jax.numpy as jnp
from jax import lax
from jax.experimental import pallas as pl
from jax.experimental.pallas import tpu as pltpu
from jax.sharding import PartitionSpec as P

RANK = 32
KNOT = 8
LANES = 128
TOP = 8

epsilon = 1e-06
damping = 0.01
highest = lax.Precision.HIGHEST
f32 = jnp.float32
bf16 = jnp.bfloat16


def dot(left, right, dims):
    return lax.dot_general(left, right, ((dims[0], dims[1]), ((), ())), precision=highest, preferred_element_type=f32)


def split_dot(left, right, dim):
    left_high, right_high = left.astype(bf16), right.astype(bf16)
    left_low = (left - left_high.astype(f32)).astype(bf16)
    right_low = (right - right_high.astype(f32)).astype(bf16)
    left = jnp.concatenate([left_high, left_high, left_low], axis=dim)
    right = jnp.concatenate([right_high, right_low, right_high], axis=dim)
    return lax.dot_general(left, right, (((dim,), (dim,)), ((), ())), preferred_element_type=f32)


def joined(ref):
    return jnp.concatenate([ref[tile] for tile in range(ref.shape[0])], axis=1)


def grid_params():
    return pltpu.CompilerParams(dimension_semantics=("arbitrary",), vmem_limit_bytes=40000000)


def plain_params():
    return pltpu.CompilerParams(vmem_limit_bytes=32000000)


def columns_kernel(*refs):
    inner_ref, outer_ref = refs[-2:]
    chunks = (len(refs) - 2) // 2
    rows = inner_ref.shape[0]
    lane = lax.broadcasted_iota(jnp.int32, (rows, LANES), 1)
    first = jnp.zeros((rows, LANES), f32)
    last = jnp.zeros((rows, LANES), f32)
    for chunk in range(chunks):
        near, far = refs[chunk], refs[chunks + chunk]
        for k in range(near.shape[0]):
            x = chunk * near.shape[0] + k
            first = jnp.where(lane == x, pltpu.roll(near[k].astype(f32), x, 1), first)
            last = jnp.where(lane == x, pltpu.roll(far[k].astype(f32), (x + 1) % LANES, 1), last)
    odd = lax.axis_index("gz") % 2 == 1
    inner_ref[...] = jnp.where(odd, first, last).astype(bf16)
    outer_ref[...] = jnp.where(odd, last, first).astype(bf16)


def end_columns(cells):
    depth, rows, width = cells.shape
    tiles = width // LANES
    chunks = 4
    block = (depth // chunks, rows, LANES)
    places = [(chunk, tile) for tile in (0, tiles - 1) for chunk in range(chunks)]
    return pl.pallas_call(
        columns_kernel,
        grid=(1,),
        in_specs=[pl.BlockSpec(block, functools.partial(lambda c, t, i: (c, 0, t), c, t)) for c, t in places],
        out_specs=[pl.BlockSpec((rows, LANES), lambda i: (0, 0))] * 2,
        out_shape=[jax.ShapeDtypeStruct((rows, LANES), bf16)] * 2,
        compiler_params=pltpu.CompilerParams(vmem_limit_bytes=60000000),
        name="columns",
    )(*[cells] * len(places))


def ends_kernel(cells_ref, low_ref, high_ref):
    depth, rows = cells_ref.shape[0:2]
    for x in range(0, depth, 16):
        low = [cells_ref[x + k, 0:16, :].astype(f32)[0:1] for k in range(16)]
        high = [cells_ref[x + k, rows - 16 : rows, :].astype(f32)[15:16] for k in range(16)]
        low_ref[x : x + 16, :] = jnp.concatenate(low, axis=0).astype(bf16)
        high_ref[x : x + 16, :] = jnp.concatenate(high, axis=0).astype(bf16)


def ends(cells):
    depth, rows, width = cells.shape
    return pl.pallas_call(
        ends_kernel,
        out_shape=[jax.ShapeDtypeStruct((depth, width), bf16)] * 2,
        compiler_params=plain_params(),
        cost_estimate=pl.CostEstimate(flops=cells.size, bytes_accessed=2 * cells.size, transcendentals=0),
        name="ends",
    )(cells)


def z_sides(inner_ref, outer_ref):
    odd = lax.axis_index("gz") % 2 == 1
    inner, outer = inner_ref[...].astype(f32), outer_ref[...].astype(f32)
    return jnp.where(odd, inner, outer), jnp.where(odd, outer, inner)


def rows_kernel(inner_ref, outer_ref, low_ref, high_ref, across_out, inside_out):
    depth, width = low_ref.shape
    rows = inner_ref.shape[0]
    odd = lax.axis_index("gy") % 2 == 1
    lane = lax.broadcasted_iota(jnp.int32, (depth, LANES), 1)
    pad = jnp.zeros((LANES - rows, LANES), f32)
    left, right = z_sides(inner_ref, outer_ref)
    left = jnp.transpose(jnp.concatenate([left, pad], axis=0))[0:depth]
    right = jnp.transpose(jnp.concatenate([right, pad], axis=0))[0:depth]
    bodies, beyond = [], []
    for row, body in ((0, low_ref), (rows - 1, high_ref)):
        after = pltpu.roll(right, (LANES - row) % LANES, 1)
        before = pltpu.roll(left, LANES - 1 - row, 1)
        bodies.append(body[...].astype(f32))
        beyond.append(jnp.where(lane == 0, after, before))
    for out, first, second in ((across_out, 1, 0), (inside_out, 0, 1)):
        out[:, 0:width] = jnp.where(odd, bodies[first], bodies[second]).astype(bf16)
        out[:, width : width + LANES] = jnp.where(odd, beyond[first], beyond[second]).astype(bf16)


def packed_rows(inner, outer, low, high):
    depth, width = low.shape
    return pl.pallas_call(
        rows_kernel,
        out_shape=[jax.ShapeDtypeStruct((depth, width + LANES), bf16)] * 2,
        compiler_params=plain_params(),
        cost_estimate=pl.CostEstimate(flops=500000 * low.size, bytes_accessed=8 * low.size, transcendentals=0),
        name="rows",
    )(inner, outer, low, high)


def swapped(part, axis, start):
    count = lax.axis_size(axis)
    pairs = [(i, i + 1) for i in range(start, count - 1, 2)]
    return lax.ppermute(part, axis, pairs + [(j, i) for i, j in pairs])


def squares_kernel(image_ref, later_ref, sums):
    depth, rows, width = image_ref.shape
    tiles = width // LANES

    def one(t, carry):
        block, tile = t // tiles, t % tiles
        at = pl.multiple_of(tile * LANES, LANES)
        for pair in range(rows // 16):
            total = jnp.zeros((16, LANES), f32)
            for k in range(KNOT):
                values = image_ref[block * KNOT + k, 16 * pair : 16 * pair + 16, pl.ds(at, LANES)].astype(f32)
                total = total + values * values
            for half in range(2):
                row = block * (rows // KNOT) + 2 * pair + half
                sums[tile, pl.ds(row, 1), :] = jnp.sum(total[8 * half : 8 * half + 8], axis=0, keepdims=True)
        return carry

    lax.fori_loop(0, depth // KNOT * tiles, one, 0)


def squares(image, later):
    depth, rows, width = image.shape
    return pl.pallas_call(
        squares_kernel,
        out_shape=jax.ShapeDtypeStruct((width // LANES, depth * rows // KNOT**2, LANES), f32),
        compiler_params=plain_params(),
        cost_estimate=pl.CostEstimate(flops=3 * image.size, bytes_accessed=2 * image.size, transcendentals=0),
        name="squares",
    )(image, later)


def terms_kernel(
    sums, plane_ref, depth_ref, inner_ref, outer_ref, field_ref, diag_depth_ref, diag_plane_ref, beyond_ref
):
    tiles = sums.shape[0]
    left, right = z_sides(inner_ref, outer_ref)
    lane = lax.broadcasted_iota(jnp.int32, left.shape, 1)
    for x in range(beyond_ref.shape[0]):
        after = pltpu.roll(right, (LANES - x) % LANES, 1)
        before = pltpu.roll(left, LANES - 1 - x, 1)
        beyond_ref[x] = jnp.where(lane == 0, after, before).astype(bf16)
    for k in range(2):
        field = dot(plane_ref[k], depth_ref[k], ((1,), (0,)))
        for tile in range(tiles):
            field_ref[k, tile] = field[:, tile * LANES : (tile + 1) * LANES]
    squared = joined(sums)
    cells = jnp.full(squared.shape, float(KNOT * KNOT), f32)
    first, second = plane_ref[0], plane_ref[1]
    diag_depth_ref[0] = dot(first * first, squared, ((0,), (0,)))
    diag_depth_ref[1] = dot(second * second, cells, ((0,), (0,)))
    first, second = depth_ref[0], depth_ref[1]
    diag_plane_ref[0] = dot(squared, first * first, ((1,), (1,)))
    diag_plane_ref[1] = dot(cells, second * second, ((1,), (1,)))


def terms(sums, plane, depth_factors, inner, outer, depth):
    nodes, width = plane.shape[1], depth_factors.shape[2]
    return pl.pallas_call(
        terms_kernel,
        out_shape=[
            jax.ShapeDtypeStruct((2, width // LANES, nodes, LANES), f32),
            jax.ShapeDtypeStruct((2, RANK, width), f32),
            jax.ShapeDtypeStruct((2, nodes, RANK), f32),
            jax.ShapeDtypeStruct((depth,) + inner.shape, bf16),
        ],
        compiler_params=plain_params(),
        cost_estimate=pl.CostEstimate(flops=40 * nodes * RANK * width, bytes_accessed=1 << 20, transcendentals=0),
        name="terms",
    )(sums, plane, depth_factors, inner, outer)


def warp_kernel(
    cells_ref, image_ref, shift_x_ref, shift_y_ref, shift_z_ref, beyond_ref, across_ref, inside_ref, field, plane_ref, depth_ref,
    diag_depth_ref, diag_plane_ref,
    residual_ref, depth_out, plane_out,
    ahead_ref, here_ref, behind_ref, wide, bands, blocks, energy, held,
):
    step = pl.program_id(0)
    last = pl.num_programs(0) - 1
    planes, rows, width = cells_ref.shape
    nodes = rows // KNOT
    tiles = width // LANES
    window = (ahead_ref, here_ref, behind_ref)
    shifts = (shift_x_ref, shift_y_ref, shift_z_ref)
    pitch = rows + 2 * TOP
    plane_rows = tiles * pitch
    block_rows = planes * plane_rows

    @pl.when(step == 0)
    def _():
        row = lax.broadcasted_iota(jnp.int32, bands.shape[1:], 0)
        column = lax.broadcasted_iota(jnp.int32, bands.shape[1:], 1)
        one, none = jnp.ones(bands.shape[1:], f32), jnp.zeros(bands.shape[1:], f32)
        up, down = jnp.where(row == column + 1, one, none), jnp.where(row == column, one, none)
        bands[0] = (up - down).astype(bf16)
        up = jnp.where(row == column + LANES, one, none)
        down = jnp.where(row == column + LANES - 1, one, none)
        bands[1] = (up - down).astype(bf16)
        energy[...] = jnp.zeros_like(energy)
        for c in range(3):
            window[c][3 * block_rows - plane_rows : 3 * block_rows, :] = jnp.zeros((plane_rows, LANES), f32)

    @pl.when(step < last)
    def _():
        slot = (step % 3) * block_rows
        odd = lax.axis_index("gy") % 2 == 1
        across, inside = across_ref[...].astype(f32), inside_ref[...].astype(f32)
        low, high = jnp.where(odd, inside, across), jnp.where(odd, across, inside)
        at = lax.broadcasted_iota(jnp.int32, (2 * TOP, width + LANES), 0)
        for k in range(planes):
            first = k * pitch
            wide[first : first + rows, 0:width] = cells_ref[k]
            wide[first : first + rows, width:] = beyond_ref[k]
            rim = jnp.where(at == TOP, high[k : k + 1], jnp.where(at == TOP - 1, low[k : k + 1], 0.0))
            wide[first + rows : first + pitch, :] = rim.astype(bf16)

        def put(c, tile, values):
            for k in range(planes):
                first = pl.multiple_of(slot + k * plane_rows + tile * pitch, 8)
                mine = values[k * pitch : (k + 1) * pitch]
                window[c][pl.ds(first + TOP, rows), :] = mine[0:rows]
                window[c][pl.ds(first, TOP), :] = mine[rows : rows + TOP]
                window[c][pl.ds(first + TOP + rows, TOP), :] = mine[rows + TOP :]

        pieces = width // (2 * LANES)
        for piece in range(pieces):
            start = 2 * LANES * piece
            after = wide[:, start : start + 3 * LANES]
            if piece == 0:
                before = jnp.concatenate([wide[:, width:], wide[:, 0 : 2 * LANES]], axis=1)
            else:
                before = wide[:, start - LANES : start + 2 * LANES]
            ahead = jnp.dot(after, bands[0], preferred_element_type=f32)
            behind = jnp.dot(before, bands[1], preferred_element_type=f32)
            for half in range(2):
                mine = slice(half * LANES, (half + 1) * LANES)
                put(0, 2 * piece + half, ahead[:, mine])
                put(1, 2 * piece + half, wide[:, start + half * LANES : start + (half + 1) * LANES].astype(f32))
                put(2, 2 * piece + half, behind[:, mine])

    @pl.when(step == last)
    def _():
        first = pl.multiple_of((step % 3) * block_rows, 8)
        for c in range(3):
            window[c][pl.ds(first, plane_rows), :] = jnp.zeros((plane_rows, LANES), f32)

    @pl.when(step > 0)
    def _():
        mid = (step + 2) % 3
        first_rows = (
            jnp.where(mid == 0, 3, mid) * block_rows - plane_rows,
            mid * block_rows,
            jnp.where(mid == 2, 0, mid + 1) * block_rows,
        )

        def one(t, total):
            tile = t % tiles
            pair = t // tiles
            at = pl.multiple_of(tile * LANES, LANES)
            top = pl.multiple_of(pair * 16, 16)
            origins = [first + tile * pitch + top + TOP for first in first_rows]
            for half in range(2):
                node = (step - 1) * nodes + pair * 2 + half
                mine = slice(8 * half, 8 * half + 8)

                def taps(x):
                    part = 0 if x == 0 else 2 if x == planes + 1 else 1
                    plus = (x - 1) * plane_rows + 8 * half if part == 1 else 8 * half
                    return [
                        [window[c][pl.ds(origins[part] + (plus + b), 8), :] for c in range(3)] for b in (-1, 0, 1)
                    ]

                contrast = jnp.broadcast_to(field[0, tile, pl.ds(node, 1), :], (8, LANES))
                brightness = jnp.broadcast_to(field[1, tile, pl.ds(node, 1), :], (8, LANES))
                by_image = jnp.zeros((8, LANES), f32)
                plain = jnp.zeros((8, LANES), f32)
                before, here = taps(0), taps(1)
                for k in range(planes):
                    after = taps(k + 2)
                    place = (k, pl.ds(top, 16), pl.ds(at, LANES))
                    sx, sy, sz = (ref[(0,) + place].astype(f32)[mine] for ref in shifts)
                    image = image_ref[place].astype(f32)[mine]
                    px, py, pz = sx > 0, sy > 0, sz > 0
                    ax, ay = jnp.abs(sx), jnp.abs(sy)

                    def sides(c):
                        far = [jnp.where(px, after[b][c], before[b][c]) for b in range(3)]
                        near = [here[b][c] for b in range(3)]
                        return [(v[1], jnp.where(py, v[2], v[0])) for v in (near, far)]

                    ahead, middle, behind = sides(0), sides(1), sides(2)
                    lines = []
                    for b in range(2):
                        near, far = (middle[v][b] + sz * jnp.where(pz, ahead[v][b], behind[v][b]) for v in range(2))
                        lines.append(near + ax * (far - near))
                    warped = lines[0] + ay * (lines[1] - lines[0])
                    misfit = warped - contrast * image - brightness
                    if half == 0:
                        held[k] = misfit
                    else:
                        residual_ref[place] = jnp.concatenate([held[k], misfit], axis=0).astype(bf16)
                    by_image = by_image + misfit * image
                    plain = plain + misfit
                    total = total + misfit * misfit
                    before, here = here, after
                for k, value in ((0, by_image), (1, plain)):
                    blocks[k, tile, pl.ds(node, 1), :] = jnp.sum(value, axis=0, keepdims=True)
            return total

        energy[...] = lax.fori_loop(0, (rows // 16) * tiles, one, energy[...], unroll=2)

    @pl.when(step == last)
    def _():
        parts = depth_out.shape[0]
        share = RANK // parts
        sums = [joined(blocks.at[k]) for k in range(2)]
        kinds = [split_dot(plane_ref[k], sums[k], 0) for k in range(2)]
        kinds = kinds + [diag_depth_ref[0], diag_depth_ref[1]]
        half = width // 2
        for p in range(parts):
            rows = slice(p * share, (p + 1) * share)
            for k in range(2):
                mine = slice(k * share, (k + 1) * share)
                depth_out[p, mine, 0:width] = kinds[k][rows]
                depth_out[p, mine, width : width + half] = kinds[2][rows, k * half : (k + 1) * half]
                depth_out[p, mine, width + half :] = kinds[3][rows, 0:LANES]
        local = jnp.sum(energy[...])
        kinds = [split_dot(sums[k], depth_ref[k], 1) for k in range(2)]
        kinds = kinds + [diag_plane_ref[0], diag_plane_ref[1]]
        for k in range(4):
            plane_out[:, k * RANK : (k + 1) * RANK] = kinds[k]
        count = plane_out.shape[0]
        plane_out[count // 2 :, 3 * RANK :] = jnp.full((count // 2, RANK), local, f32)


def warp(cells, image, shift, beyond, across, inside, field, plane, depth_factors, diag_depth, diag_plane, parts):
    depth, rows, width = cells.shape
    nodes = plane.shape[1]
    tiles = width // LANES
    count = depth // KNOT
    behind = lambda i: (jnp.maximum(i - 1, 0), 0, 0)
    ahead = lambda i: (jnp.minimum(i, count - 1), 0, 0)
    flat = lambda i: (0, 0)
    whole = lambda i: (0, 0, 0)
    return pl.pallas_call(
        warp_kernel,
        grid=(count + 1,),
        in_specs=[
            pl.BlockSpec((KNOT, rows, width), ahead),
            pl.BlockSpec((KNOT, rows, width), behind),
            pl.BlockSpec((1, KNOT, rows, width), lambda i: (0, jnp.maximum(i - 1, 0), 0, 0)),
            pl.BlockSpec((1, KNOT, rows, width), lambda i: (1, jnp.maximum(i - 1, 0), 0, 0)),
            pl.BlockSpec((1, KNOT, rows, width), lambda i: (2, jnp.maximum(i - 1, 0), 0, 0)),
            pl.BlockSpec((KNOT, rows, LANES), ahead),
            pl.BlockSpec((KNOT, across.shape[1]), lambda i: (jnp.minimum(i, count - 1), 0)),
            pl.BlockSpec((KNOT, inside.shape[1]), lambda i: (jnp.minimum(i, count - 1), 0)),
            pl.BlockSpec(field.shape, lambda i: (0, 0, 0, 0)),
            pl.BlockSpec(plane.shape, whole),
            pl.BlockSpec(depth_factors.shape, whole),
            pl.BlockSpec(diag_depth.shape, whole),
            pl.BlockSpec(diag_plane.shape, whole),
        ],
        out_specs=[
            pl.BlockSpec((KNOT, rows, width), behind),
            pl.BlockSpec((parts, 2 * RANK // parts, width + width // 2 + LANES), whole),
            pl.BlockSpec((nodes, 4 * RANK), flat),
        ],
        out_shape=[
            jax.ShapeDtypeStruct(cells.shape, bf16),
            jax.ShapeDtypeStruct((parts, 2 * RANK // parts, width + width // 2 + LANES), f32),
            jax.ShapeDtypeStruct((nodes, 4 * RANK), f32),
        ],
        scratch_shapes=[
            *[pltpu.VMEM((3 * KNOT * tiles * (rows + 2 * TOP), LANES), f32)] * 3,
            pltpu.VMEM((KNOT * (rows + 2 * TOP), width + LANES), bf16),
            pltpu.VMEM((2, 3 * LANES, 2 * LANES), bf16),
            pltpu.VMEM((2, tiles, nodes, LANES), f32),
            pltpu.VMEM((8, LANES), f32),
            pltpu.VMEM((KNOT, 8, LANES), f32),
        ],
        compiler_params=grid_params(),
        cost_estimate=pl.CostEstimate(flops=60 * cells.size, bytes_accessed=12 * cells.size, transcendentals=0),
        name="warp",
    )(cells, image, shift, shift, shift, beyond, across, inside, field, plane, depth_factors, diag_depth, diag_plane)


def gather_kernel(depth_ref, *refs):
    depth_out, plane_out = refs[-2:]
    total = jnp.sum(depth_ref[...], axis=0)
    found = [ref[...] for ref in refs[:-2]]
    while len(found) > 1:
        half = len(found) // 2
        found = [found[k] + found[k + half] for k in range(half)]
    planes = found[0]
    plane_out[...] = planes
    cells = planes.shape[0]
    share, width = total.shape[0] // 2, total.shape[1]
    row = lax.broadcasted_iota(jnp.int32, total.shape, 0)
    lane = lax.broadcasted_iota(jnp.int32, total.shape, 1)
    partial = planes[cells - 1, 4 * RANK - 1]
    total = jnp.where((row >= share) & (lane >= width - LANES), partial, total)
    for p in range(depth_out.shape[0]):
        depth_out[p] = total


def step_kernel(full_z, node_count, depth_ref, plane_ref, depth_out, plane_out):
    parts, share, width = depth_ref.shape[0], depth_ref.shape[1] // 2, depth_out.shape[2]
    half = width // 2
    energy = depth_ref[0, share, width + half]
    for p in range(1, parts):
        energy = energy + depth_ref[p, share, width + half]
    lam_depth = damping * energy / full_z
    lam_plane = damping * RANK * energy / node_count
    for p in range(parts):
        got = depth_ref[p]
        rows = slice(p * share, (p + 1) * share)
        first, second = got[0:share], got[share:]
        squared = jnp.concatenate([first[:, width : width + half], second[:, width : width + half]], axis=1)
        levels = jnp.concatenate([first[:, width + half :]] * (width // LANES), axis=1)
        depth_out[0, rows, :] = first[:, 0:width] / (squared + lam_depth + epsilon)
        depth_out[1, rows, :] = second[:, 0:width] / (levels + lam_depth + epsilon)
    planes = plane_ref[...]
    plane_out[0] = planes[:, 0:RANK] / (planes[:, 2 * RANK : 3 * RANK] + lam_plane + epsilon)
    plane_out[1] = planes[:, RANK : 2 * RANK] / (planes[0:1, 3 * RANK :] + lam_plane + epsilon)


def local(image, deformed, displacement, plane_factors, depth_factors):
    n_gy, n_gz = lax.axis_size("gy"), lax.axis_size("gz")
    nodes_x, nodes_y = plane_factors.shape[2:]
    plane = jnp.transpose(plane_factors, (0, 2, 3, 1)).reshape(2, nodes_x * nodes_y, RANK)
    inner, outer = end_columns(deformed)
    inner = swapped(inner, "gz", 0)
    outer = swapped(outer, "gz", 1)
    low, high = ends(deformed)
    across, inside = packed_rows(inner, outer, low, high)
    later = across
    inside = swapped(inside, "gy", 0)
    across = swapped(across, "gy", 1)
    sums = squares(image, later)
    field, diag_depth, diag_plane, beyond = terms(sums, plane, depth_factors, inner, outer, deformed.shape[0])
    residual, depth_terms, plane_terms = warp(
        deformed, image, displacement, beyond, across, inside, field, plane, depth_factors, diag_depth, diag_plane,
        n_gy,
    )
    depth_terms = lax.all_to_all(depth_terms, "gy", 0, 0)
    others = [
        lax.ppermute(plane_terms, "gz", [(i, (i + hop) % n_gz) for i in range(n_gz)]) for hop in range(1, n_gz)
    ]
    depth_terms, plane_terms = pl.pallas_call(
        gather_kernel,
        out_shape=[
            jax.ShapeDtypeStruct(depth_terms.shape, f32),
            jax.ShapeDtypeStruct(plane_terms.shape, f32),
        ],
        compiler_params=plain_params(),
        name="gather",
    )(depth_terms, plane_terms, *others)
    depth_terms = lax.all_to_all(depth_terms, "gy", 0, 0)
    width = depth_factors.shape[2]
    step_depth, step_plane = pl.pallas_call(
        functools.partial(step_kernel, width * n_gz, nodes_x * nodes_y * n_gy),
        out_shape=[
            jax.ShapeDtypeStruct(depth_factors.shape, f32),
            jax.ShapeDtypeStruct(plane.shape, f32),
        ],
        compiler_params=plain_params(),
        name="steps",
    )(depth_terms, plane_terms)
    step_plane = jnp.transpose(step_plane.reshape(2, nodes_x, nodes_y, RANK), (0, 3, 1, 2))
    return residual, step_plane, step_depth


def solution(mesh):
    placed = (
        P(None, "gy", "gz"),
        P(None, "gy", "gz"),
        P(None, None, "gy", "gz"),
        P(None, None, None, "gy"),
        P(None, None, "gz"),
    )
    return jax.shard_map(
        local,
        mesh=mesh,
        in_specs=placed,
        out_specs=(P(None, "gy", "gz"), P(None, None, None, "gy"), P(None, None, "gz")),
        check_vma=False,
    )
```

```python
import functools

import jax
import jax.numpy as jnp
from jax import lax
from jax.experimental import pallas as pl
from jax.experimental.pallas import tpu as pltpu
from jax.sharding import PartitionSpec as P

RANK = 32
KNOT = 8
LANES = 128
TOP = 8

epsilon = 1e-06
damping = 0.01
highest = lax.Precision.HIGHEST
f32 = jnp.float32
bf16 = jnp.bfloat16


def dot(left, right, dims):
    return lax.dot_general(left, right, ((dims[0], dims[1]), ((), ())), precision=highest, preferred_element_type=f32)


def split_dot(left, right, dim):
    left_high, right_high = left.astype(bf16), right.astype(bf16)
    left_low = (left - left_high.astype(f32)).astype(bf16)
    right_low = (right - right_high.astype(f32)).astype(bf16)
    left = jnp.concatenate([left_high, left_high, left_low], axis=dim)
    right = jnp.concatenate([right_high, right_low, right_high], axis=dim)
    return lax.dot_general(left, right, (((dim,), (dim,)), ((), ())), preferred_element_type=f32)


def joined(ref):
    return jnp.concatenate([ref[tile] for tile in range(ref.shape[0])], axis=1)


def grid_params():
    return pltpu.CompilerParams(dimension_semantics=("arbitrary",), vmem_limit_bytes=40000000)


def plain_params():
    return pltpu.CompilerParams(vmem_limit_bytes=32000000)


def columns_kernel(*refs):
    inner_ref, outer_ref = refs[-2:]
    chunks = (len(refs) - 2) // 2
    rows = inner_ref.shape[0]
    lane = lax.broadcasted_iota(jnp.int32, (rows, LANES), 1)
    first = jnp.zeros((rows, LANES), f32)
    last = jnp.zeros((rows, LANES), f32)
    for chunk in range(chunks):
        near, far = refs[chunk], refs[chunks + chunk]
        for k in range(near.shape[0]):
            x = chunk * near.shape[0] + k
            first = jnp.where(lane == x, pltpu.roll(near[k].astype(f32), x, 1), first)
            last = jnp.where(lane == x, pltpu.roll(far[k].astype(f32), (x + 1) % LANES, 1), last)
    odd = lax.axis_index("gz") % 2 == 1
    inner_ref[...] = jnp.where(odd, first, last).astype(bf16)
    outer_ref[...] = jnp.where(odd, last, first).astype(bf16)


def end_columns(cells):
    depth, rows, width = cells.shape
    tiles = width // LANES
    chunks = 4
    block = (depth // chunks, rows, LANES)
    places = [(chunk, tile) for tile in (0, tiles - 1) for chunk in range(chunks)]
    return pl.pallas_call(
        columns_kernel,
        grid=(1,),
        in_specs=[pl.BlockSpec(block, functools.partial(lambda c, t, i: (c, 0, t), c, t)) for c, t in places],
        out_specs=[pl.BlockSpec((rows, LANES), lambda i: (0, 0))] * 2,
        out_shape=[jax.ShapeDtypeStruct((rows, LANES), bf16)] * 2,
        compiler_params=pltpu.CompilerParams(vmem_limit_bytes=60000000),
        name="columns",
    )(*[cells] * len(places))


def ends_kernel(cells_ref, across_ref, inside_ref):
    depth, rows = cells_ref.shape[0:2]
    odd = lax.axis_index("gy") % 2 == 1
    for x in range(0, depth, 16):
        low = [cells_ref[x + k, 0:16, :].astype(f32)[0:1] for k in range(16)]
        high = [cells_ref[x + k, rows - 16 : rows, :].astype(f32)[15:16] for k in range(16)]
        low, high = jnp.concatenate(low, axis=0), jnp.concatenate(high, axis=0)
        across_ref[x : x + 16, :] = jnp.where(odd, high, low).astype(bf16)
        inside_ref[x : x + 16, :] = jnp.where(odd, low, high).astype(bf16)


def ends(cells):
    depth, rows, width = cells.shape
    return pl.pallas_call(
        ends_kernel,
        out_shape=[jax.ShapeDtypeStruct((depth, width), bf16)] * 2,
        compiler_params=plain_params(),
        cost_estimate=pl.CostEstimate(flops=cells.size, bytes_accessed=2 * cells.size, transcendentals=0),
        name="ends",
    )(cells)


def z_sides(inner_ref, outer_ref):
    odd = lax.axis_index("gz") % 2 == 1
    inner, outer = inner_ref[...].astype(f32), outer_ref[...].astype(f32)
    return jnp.where(odd, inner, outer), jnp.where(odd, outer, inner)


def corners_kernel(inner_ref, outer_ref, across_out, inside_out):
    rows, depth = inner_ref.shape[0], across_out.shape[0]
    odd = lax.axis_index("gy") % 2 == 1
    lane = lax.broadcasted_iota(jnp.int32, (depth, LANES), 1)
    pad = jnp.zeros((LANES - rows, LANES), f32)
    left, right = z_sides(inner_ref, outer_ref)
    left = jnp.transpose(jnp.concatenate([left, pad], axis=0))[0:depth]
    right = jnp.transpose(jnp.concatenate([right, pad], axis=0))[0:depth]
    low, high = (
        jnp.where(lane == 0, pltpu.roll(right, (LANES - row) % LANES, 1), pltpu.roll(left, LANES - 1 - row, 1))
        for row in (0, rows - 1)
    )
    across_out[...] = jnp.where(odd, high, low).astype(bf16)
    inside_out[...] = jnp.where(odd, low, high).astype(bf16)


def corners(inner, outer, depth):
    return pl.pallas_call(
        corners_kernel,
        out_shape=[jax.ShapeDtypeStruct((depth, LANES), bf16)] * 2,
        compiler_params=plain_params(),
        cost_estimate=pl.CostEstimate(flops=1 << 34, bytes_accessed=1 << 17, transcendentals=0),
        name="corners",
    )(inner, outer)


def swapped(part, axis, start):
    count = lax.axis_size(axis)
    pairs = [(i, i + 1) for i in range(start, count - 1, 2)]
    return lax.ppermute(part, axis, pairs + [(j, i) for i, j in pairs])


def squares_kernel(image_ref, later_ref, sums):
    depth, rows, width = image_ref.shape
    tiles = width // LANES

    def one(t, carry):
        block, tile = t // tiles, t % tiles
        at = pl.multiple_of(tile * LANES, LANES)
        for pair in range(rows // 16):
            total = jnp.zeros((16, LANES), f32)
            for k in range(KNOT):
                values = image_ref[block * KNOT + k, 16 * pair : 16 * pair + 16, pl.ds(at, LANES)].astype(f32)
                total = total + values * values
            for half in range(2):
                row = block * (rows // KNOT) + 2 * pair + half
                sums[tile, pl.ds(row, 1), :] = jnp.sum(total[8 * half : 8 * half + 8], axis=0, keepdims=True)
        return carry

    lax.fori_loop(0, depth // KNOT * tiles, one, 0)


def squares(image, later):
    depth, rows, width = image.shape
    return pl.pallas_call(
        squares_kernel,
        out_shape=jax.ShapeDtypeStruct((width // LANES, depth * rows // KNOT**2, LANES), f32),
        compiler_params=plain_params(),
        cost_estimate=pl.CostEstimate(flops=3 * image.size, bytes_accessed=2 * image.size, transcendentals=0),
        name="squares",
    )(image, later)


def terms_kernel(
    sums, plane_ref, depth_ref, inner_ref, outer_ref, field_ref, diag_depth_ref, diag_plane_ref, beyond_ref
):
    tiles = sums.shape[0]
    left, right = z_sides(inner_ref, outer_ref)
    lane = lax.broadcasted_iota(jnp.int32, left.shape, 1)
    for x in range(beyond_ref.shape[0]):
        after = pltpu.roll(right, (LANES - x) % LANES, 1)
        before = pltpu.roll(left, LANES - 1 - x, 1)
        beyond_ref[x] = jnp.where(lane == 0, after, before).astype(bf16)
    for k in range(2):
        field = dot(plane_ref[k], depth_ref[k], ((1,), (0,)))
        for tile in range(tiles):
            field_ref[k, tile] = field[:, tile * LANES : (tile + 1) * LANES]
    squared = joined(sums)
    cells = jnp.full(squared.shape, float(KNOT * KNOT), f32)
    first, second = plane_ref[0], plane_ref[1]
    diag_depth_ref[0] = dot(first * first, squared, ((0,), (0,)))
    diag_depth_ref[1] = dot(second * second, cells, ((0,), (0,)))
    first, second = depth_ref[0], depth_ref[1]
    diag_plane_ref[0] = dot(squared, first * first, ((1,), (1,)))
    diag_plane_ref[1] = dot(cells, second * second, ((1,), (1,)))


def terms(sums, plane, depth_factors, inner, outer, depth):
    nodes, width = plane.shape[1], depth_factors.shape[2]
    return pl.pallas_call(
        terms_kernel,
        out_shape=[
            jax.ShapeDtypeStruct((2, width // LANES, nodes, LANES), f32),
            jax.ShapeDtypeStruct((2, RANK, width), f32),
            jax.ShapeDtypeStruct((2, nodes, RANK), f32),
            jax.ShapeDtypeStruct((depth,) + inner.shape, bf16),
        ],
        compiler_params=plain_params(),
        cost_estimate=pl.CostEstimate(flops=40 * nodes * RANK * width, bytes_accessed=1 << 20, transcendentals=0),
        name="terms",
    )(sums, plane, depth_factors, inner, outer)


def warp_kernel(
    cells_ref, image_ref, shift_x_ref, shift_y_ref, shift_z_ref, beyond_ref, across_ref, inside_ref,
    across_tile_ref, inside_tile_ref, field, plane_ref, depth_ref,
    diag_depth_ref, diag_plane_ref,
    residual_ref, depth_out, plane_out,
    ahead_ref, here_ref, behind_ref, wide, bands, blocks, energy, held,
):
    step = pl.program_id(0)
    last = pl.num_programs(0) - 1
    planes, rows, width = cells_ref.shape
    nodes = rows // KNOT
    tiles = width // LANES
    window = (ahead_ref, here_ref, behind_ref)
    shifts = (shift_x_ref, shift_y_ref, shift_z_ref)
    pitch = rows + 2 * TOP
    plane_rows = tiles * pitch
    block_rows = planes * plane_rows

    @pl.when(step == 0)
    def _():
        row = lax.broadcasted_iota(jnp.int32, bands.shape[1:], 0)
        column = lax.broadcasted_iota(jnp.int32, bands.shape[1:], 1)
        one, none = jnp.ones(bands.shape[1:], f32), jnp.zeros(bands.shape[1:], f32)
        up, down = jnp.where(row == column + 1, one, none), jnp.where(row == column, one, none)
        bands[0] = (up - down).astype(bf16)
        up = jnp.where(row == column + LANES, one, none)
        down = jnp.where(row == column + LANES - 1, one, none)
        bands[1] = (up - down).astype(bf16)
        energy[...] = jnp.zeros_like(energy)
        for c in range(3):
            window[c][3 * block_rows - plane_rows : 3 * block_rows, :] = jnp.zeros((plane_rows, LANES), f32)

    @pl.when(step < last)
    def _():
        slot = (step % 3) * block_rows
        odd = lax.axis_index("gy") % 2 == 1
        across, inside = (
            jnp.concatenate([row[...].astype(f32), tile[...].astype(f32)], axis=1)
            for row, tile in ((across_ref, across_tile_ref), (inside_ref, inside_tile_ref))
        )
        low, high = jnp.where(odd, inside, across), jnp.where(odd, across, inside)
        at = lax.broadcasted_iota(jnp.int32, (2 * TOP, width + LANES), 0)
        for k in range(planes):
            first = k * pitch
            wide[first : first + rows, 0:width] = cells_ref[k]
            wide[first : first + rows, width:] = beyond_ref[k]
            rim = jnp.where(at == TOP, high[k : k + 1], jnp.where(at == TOP - 1, low[k : k + 1], 0.0))
            wide[first + rows : first + pitch, :] = rim.astype(bf16)

        def put(c, tile, values):
            for k in range(planes):
                first = pl.multiple_of(slot + k * plane_rows + tile * pitch, 8)
                mine = values[k * pitch : (k + 1) * pitch]
                window[c][pl.ds(first + TOP, rows), :] = mine[0:rows]
                window[c][pl.ds(first, TOP), :] = mine[rows : rows + TOP]
                window[c][pl.ds(first + TOP + rows, TOP), :] = mine[rows + TOP :]

        pieces = width // (2 * LANES)
        for piece in range(pieces):
            start = 2 * LANES * piece
            after = wide[:, start : start + 3 * LANES]
            if piece == 0:
                before = jnp.concatenate([wide[:, width:], wide[:, 0 : 2 * LANES]], axis=1)
            else:
                before = wide[:, start - LANES : start + 2 * LANES]
            ahead = jnp.dot(after, bands[0], preferred_element_type=f32)
            behind = jnp.dot(before, bands[1], preferred_element_type=f32)
            for half in range(2):
                mine = slice(half * LANES, (half + 1) * LANES)
                put(0, 2 * piece + half, ahead[:, mine])
                put(1, 2 * piece + half, wide[:, start + half * LANES : start + (half + 1) * LANES].astype(f32))
                put(2, 2 * piece + half, behind[:, mine])

    @pl.when(step == last)
    def _():
        first = pl.multiple_of((step % 3) * block_rows, 8)
        for c in range(3):
            window[c][pl.ds(first, plane_rows), :] = jnp.zeros((plane_rows, LANES), f32)

    @pl.when(step > 0)
    def _():
        mid = (step + 2) % 3
        first_rows = (
            jnp.where(mid == 0, 3, mid) * block_rows - plane_rows,
            mid * block_rows,
            jnp.where(mid == 2, 0, mid + 1) * block_rows,
        )

        def one(t, total):
            tile = t % tiles
            pair = t // tiles
            at = pl.multiple_of(tile * LANES, LANES)
            top = pl.multiple_of(pair * 16, 16)
            origins = [first + tile * pitch + top + TOP for first in first_rows]
            for half in range(2):
                node = (step - 1) * nodes + pair * 2 + half
                mine = slice(8 * half, 8 * half + 8)

                def taps(x):
                    part = 0 if x == 0 else 2 if x == planes + 1 else 1
                    plus = (x - 1) * plane_rows + 8 * half if part == 1 else 8 * half
                    return [
                        [window[c][pl.ds(origins[part] + (plus + b), 8), :] for c in range(3)] for b in (-1, 0, 1)
                    ]

                contrast = jnp.broadcast_to(field[0, tile, pl.ds(node, 1), :], (8, LANES))
                brightness = jnp.broadcast_to(field[1, tile, pl.ds(node, 1), :], (8, LANES))
                by_image = jnp.zeros((8, LANES), f32)
                plain = jnp.zeros((8, LANES), f32)
                before, here = taps(0), taps(1)
                for k in range(planes):
                    after = taps(k + 2)
                    place = (k, pl.ds(top, 16), pl.ds(at, LANES))
                    sx, sy, sz = (ref[(0,) + place].astype(f32)[mine] for ref in shifts)
                    image = image_ref[place].astype(f32)[mine]
                    px, py, pz = sx > 0, sy > 0, sz > 0
                    ax, ay = jnp.abs(sx), jnp.abs(sy)

                    def sides(c):
                        far = [jnp.where(px, after[b][c], before[b][c]) for b in range(3)]
                        near = [here[b][c] for b in range(3)]
                        return [(v[1], jnp.where(py, v[2], v[0])) for v in (near, far)]

                    ahead, middle, behind = sides(0), sides(1), sides(2)
                    lines = []
                    for b in range(2):
                        near, far = (middle[v][b] + sz * jnp.where(pz, ahead[v][b], behind[v][b]) for v in range(2))
                        lines.append(near + ax * (far - near))
                    warped = lines[0] + ay * (lines[1] - lines[0])
                    misfit = warped - contrast * image - brightness
                    if half == 0:
                        held[k] = misfit
                    else:
                        residual_ref[place] = jnp.concatenate([held[k], misfit], axis=0).astype(bf16)
                    by_image = by_image + misfit * image
                    plain = plain + misfit
                    total = total + misfit * misfit
                    before, here = here, after
                for k, value in ((0, by_image), (1, plain)):
                    blocks[k, tile, pl.ds(node, 1), :] = jnp.sum(value, axis=0, keepdims=True)
            return total

        energy[...] = lax.fori_loop(0, (rows // 16) * tiles, one, energy[...], unroll=2)

    @pl.when(step == last)
    def _():
        parts = depth_out.shape[0]
        share = RANK // parts
        sums = [joined(blocks.at[k]) for k in range(2)]
        kinds = [split_dot(plane_ref[k], sums[k], 0) for k in range(2)]
        kinds = kinds + [diag_depth_ref[0], diag_depth_ref[1]]
        half = width // 2
        for p in range(parts):
            rows = slice(p * share, (p + 1) * share)
            for k in range(2):
                mine = slice(k * share, (k + 1) * share)
                depth_out[p, mine, 0:width] = kinds[k][rows]
                depth_out[p, mine, width : width + half] = kinds[2][rows, k * half : (k + 1) * half]
                depth_out[p, mine, width + half :] = kinds[3][rows, 0:LANES]
        local = jnp.sum(energy[...])
        kinds = [split_dot(sums[k], depth_ref[k], 1) for k in range(2)]
        kinds = kinds + [diag_plane_ref[0], diag_plane_ref[1]]
        for k in range(4):
            plane_out[:, k * RANK : (k + 1) * RANK] = kinds[k]
        count = plane_out.shape[0]
        plane_out[count // 2 :, 3 * RANK :] = jnp.full((count // 2, RANK), local, f32)


def warp(
    cells, image, shift, beyond, across, inside, across_tile, inside_tile, field, plane, depth_factors, diag_depth,
    diag_plane, parts
):
    depth, rows, width = cells.shape
    nodes = plane.shape[1]
    tiles = width // LANES
    count = depth // KNOT
    behind = lambda i: (jnp.maximum(i - 1, 0), 0, 0)
    ahead = lambda i: (jnp.minimum(i, count - 1), 0, 0)
    flat = lambda i: (0, 0)
    whole = lambda i: (0, 0, 0)
    return pl.pallas_call(
        warp_kernel,
        grid=(count + 1,),
        in_specs=[
            pl.BlockSpec((KNOT, rows, width), ahead),
            pl.BlockSpec((KNOT, rows, width), behind),
            pl.BlockSpec((1, KNOT, rows, width), lambda i: (0, jnp.maximum(i - 1, 0), 0, 0)),
            pl.BlockSpec((1, KNOT, rows, width), lambda i: (1, jnp.maximum(i - 1, 0), 0, 0)),
            pl.BlockSpec((1, KNOT, rows, width), lambda i: (2, jnp.maximum(i - 1, 0), 0, 0)),
            pl.BlockSpec((KNOT, rows, LANES), ahead),
            pl.BlockSpec((KNOT, across.shape[1]), lambda i: (jnp.minimum(i, count - 1), 0)),
            pl.BlockSpec((KNOT, inside.shape[1]), lambda i: (jnp.minimum(i, count - 1), 0)),
            pl.BlockSpec((KNOT, LANES), lambda i: (jnp.minimum(i, count - 1), 0)),
            pl.BlockSpec((KNOT, LANES), lambda i: (jnp.minimum(i, count - 1), 0)),
            pl.BlockSpec(field.shape, lambda i: (0, 0, 0, 0)),
            pl.BlockSpec(plane.shape, whole),
            pl.BlockSpec(depth_factors.shape, whole),
            pl.BlockSpec(diag_depth.shape, whole),
            pl.BlockSpec(diag_plane.shape, whole),
        ],
        out_specs=[
            pl.BlockSpec((KNOT, rows, width), behind),
            pl.BlockSpec((parts, 2 * RANK // parts, width + width // 2 + LANES), whole),
            pl.BlockSpec((nodes, 4 * RANK), flat),
        ],
        out_shape=[
            jax.ShapeDtypeStruct(cells.shape, bf16),
            jax.ShapeDtypeStruct((parts, 2 * RANK // parts, width + width // 2 + LANES), f32),
            jax.ShapeDtypeStruct((nodes, 4 * RANK), f32),
        ],
        scratch_shapes=[
            *[pltpu.VMEM((3 * KNOT * tiles * (rows + 2 * TOP), LANES), f32)] * 3,
            pltpu.VMEM((KNOT * (rows + 2 * TOP), width + LANES), bf16),
            pltpu.VMEM((2, 3 * LANES, 2 * LANES), bf16),
            pltpu.VMEM((2, tiles, nodes, LANES), f32),
            pltpu.VMEM((8, LANES), f32),
            pltpu.VMEM((KNOT, 8, LANES), f32),
        ],
        compiler_params=grid_params(),
        cost_estimate=pl.CostEstimate(flops=60 * cells.size, bytes_accessed=12 * cells.size, transcendentals=0),
        name="warp",
    )(cells, image, shift, shift, shift, beyond, across, inside, across_tile, inside_tile, field, plane, depth_factors, diag_depth, diag_plane)


def gather_kernel(depth_ref, *refs):
    depth_out, plane_out = refs[-2:]
    total = jnp.sum(depth_ref[...], axis=0)
    found = [ref[...] for ref in refs[:-2]]
    while len(found) > 1:
        half = len(found) // 2
        found = [found[k] + found[k + half] for k in range(half)]
    planes = found[0]
    plane_out[...] = planes
    cells = planes.shape[0]
    share, width = total.shape[0] // 2, total.shape[1]
    row = lax.broadcasted_iota(jnp.int32, total.shape, 0)
    lane = lax.broadcasted_iota(jnp.int32, total.shape, 1)
    partial = planes[cells - 1, 4 * RANK - 1]
    total = jnp.where((row >= share) & (lane >= width - LANES), partial, total)
    for p in range(depth_out.shape[0]):
        depth_out[p] = total


def step_kernel(full_z, node_count, depth_ref, plane_ref, depth_out, plane_out):
    parts, share, width = depth_ref.shape[0], depth_ref.shape[1] // 2, depth_out.shape[2]
    half = width // 2
    energy = depth_ref[0, share, width + half]
    for p in range(1, parts):
        energy = energy + depth_ref[p, share, width + half]
    lam_depth = damping * energy / full_z
    lam_plane = damping * RANK * energy / node_count
    for p in range(parts):
        got = depth_ref[p]
        rows = slice(p * share, (p + 1) * share)
        first, second = got[0:share], got[share:]
        squared = jnp.concatenate([first[:, width : width + half], second[:, width : width + half]], axis=1)
        levels = jnp.concatenate([first[:, width + half :]] * (width // LANES), axis=1)
        depth_out[0, rows, :] = first[:, 0:width] / (squared + lam_depth + epsilon)
        depth_out[1, rows, :] = second[:, 0:width] / (levels + lam_depth + epsilon)
    planes = plane_ref[...]
    plane_out[0] = planes[:, 0:RANK] / (planes[:, 2 * RANK : 3 * RANK] + lam_plane + epsilon)
    plane_out[1] = planes[:, RANK : 2 * RANK] / (planes[0:1, 3 * RANK :] + lam_plane + epsilon)


def local(image, deformed, displacement, plane_factors, depth_factors):
    n_gy, n_gz = lax.axis_size("gy"), lax.axis_size("gz")
    nodes_x, nodes_y = plane_factors.shape[2:]
    plane = jnp.transpose(plane_factors, (0, 2, 3, 1)).reshape(2, nodes_x * nodes_y, RANK)
    inner, outer = end_columns(deformed)
    inner = swapped(inner, "gz", 0)
    outer = swapped(outer, "gz", 1)
    across, inside = ends(deformed)
    inside = swapped(inside, "gy", 0)
    across = swapped(across, "gy", 1)
    across_tile, inside_tile = corners(inner, outer, deformed.shape[0])
    sums = squares(image, across_tile)
    inside_tile = swapped(inside_tile, "gy", 0)
    across_tile = swapped(across_tile, "gy", 1)
    field, diag_depth, diag_plane, beyond = terms(sums, plane, depth_factors, inner, outer, deformed.shape[0])
    residual, depth_terms, plane_terms = warp(
        deformed, image, displacement, beyond, across, inside, across_tile, inside_tile, field, plane, depth_factors,
        diag_depth, diag_plane, n_gy,
    )
    depth_terms = lax.all_to_all(depth_terms, "gy", 0, 0)
    others = [
        lax.ppermute(plane_terms, "gz", [(i, (i + hop) % n_gz) for i in range(n_gz)]) for hop in range(1, n_gz)
    ]
    depth_terms, plane_terms = pl.pallas_call(
        gather_kernel,
        out_shape=[
            jax.ShapeDtypeStruct(depth_terms.shape, f32),
            jax.ShapeDtypeStruct(plane_terms.shape, f32),
        ],
        compiler_params=plain_params(),
        name="gather",
    )(depth_terms, plane_terms, *others)
    depth_terms = lax.all_to_all(depth_terms, "gy", 0, 0)
    width = depth_factors.shape[2]
    step_depth, step_plane = pl.pallas_call(
        functools.partial(step_kernel, width * n_gz, nodes_x * nodes_y * n_gy),
        out_shape=[
            jax.ShapeDtypeStruct(depth_factors.shape, f32),
            jax.ShapeDtypeStruct(plane.shape, f32),
        ],
        compiler_params=plain_params(),
        name="steps",
    )(depth_terms, plane_terms)
    step_plane = jnp.transpose(step_plane.reshape(2, nodes_x, nodes_y, RANK), (0, 3, 1, 2))
    return residual, step_plane, step_depth


def solution(mesh):
    placed = (
        P(None, "gy", "gz"),
        P(None, "gy", "gz"),
        P(None, None, "gy", "gz"),
        P(None, None, None, "gy"),
        P(None, None, "gz"),
    )
    return jax.shard_map(
        local,
        mesh=mesh,
        in_specs=placed,
        out_specs=(P(None, "gy", "gz"), P(None, None, None, "gy"), P(None, None, "gz")),
        check_vma=False,
    )
```

```python
import functools

import jax
import jax.numpy as jnp
from jax import lax
from jax.experimental import pallas as pl
from jax.experimental.pallas import tpu as pltpu
from jax.sharding import PartitionSpec as P

RANK = 32
KNOT = 8
LANES = 128
TOP = 8

epsilon = 1e-06
damping = 0.01
highest = lax.Precision.HIGHEST
f32 = jnp.float32
bf16 = jnp.bfloat16


def dot(left, right, dims):
    return lax.dot_general(left, right, ((dims[0], dims[1]), ((), ())), precision=highest, preferred_element_type=f32)


def split_dot(left, right, dim):
    left_high, right_high = left.astype(bf16), right.astype(bf16)
    left_low = (left - left_high.astype(f32)).astype(bf16)
    right_low = (right - right_high.astype(f32)).astype(bf16)
    left = jnp.concatenate([left_high, left_high, left_low], axis=dim)
    right = jnp.concatenate([right_high, right_low, right_high], axis=dim)
    return lax.dot_general(left, right, (((dim,), (dim,)), ((), ())), preferred_element_type=f32)


def joined(ref):
    return jnp.concatenate([ref[tile] for tile in range(ref.shape[0])], axis=1)


def grid_params():
    return pltpu.CompilerParams(dimension_semantics=("arbitrary",), vmem_limit_bytes=40000000)


def plain_params():
    return pltpu.CompilerParams(vmem_limit_bytes=32000000)


def columns_kernel(*refs):
    inner_ref, outer_ref = refs[-2:]
    chunks = (len(refs) - 2) // 2
    rows = inner_ref.shape[0]
    lane = lax.broadcasted_iota(jnp.int32, (rows, LANES), 1)
    first = jnp.zeros((rows, LANES), f32)
    last = jnp.zeros((rows, LANES), f32)
    for chunk in range(chunks):
        near, far = refs[chunk], refs[chunks + chunk]
        for k in range(near.shape[0]):
            x = chunk * near.shape[0] + k
            first = jnp.where(lane == x, pltpu.roll(near[k].astype(f32), x, 1), first)
            last = jnp.where(lane == x, pltpu.roll(far[k].astype(f32), (x + 1) % LANES, 1), last)
    odd = lax.axis_index("gz") % 2 == 1
    inner_ref[...] = jnp.where(odd, first, last).astype(bf16)
    outer_ref[...] = jnp.where(odd, last, first).astype(bf16)


def end_columns(cells):
    depth, rows, width = cells.shape
    tiles = width // LANES
    chunks = 4
    block = (depth // chunks, rows, LANES)
    places = [(chunk, tile) for tile in (0, tiles - 1) for chunk in range(chunks)]
    return pl.pallas_call(
        columns_kernel,
        grid=(1,),
        in_specs=[pl.BlockSpec(block, functools.partial(lambda c, t, i: (c, 0, t), c, t)) for c, t in places],
        out_specs=[pl.BlockSpec((rows, LANES), lambda i: (0, 0))] * 2,
        out_shape=[jax.ShapeDtypeStruct((rows, LANES), bf16)] * 2,
        compiler_params=pltpu.CompilerParams(vmem_limit_bytes=60000000),
        name="columns",
    )(*[cells] * len(places))


def ends_kernel(cells_ref, across_ref, inside_ref):
    depth, rows = cells_ref.shape[0:2]
    odd = lax.axis_index("gy") % 2 == 1
    for x in range(0, depth, 16):
        low = [cells_ref[x + k, 0:16, :].astype(f32)[0:1] for k in range(16)]
        high = [cells_ref[x + k, rows - 16 : rows, :].astype(f32)[15:16] for k in range(16)]
        low, high = jnp.concatenate(low, axis=0), jnp.concatenate(high, axis=0)
        across_ref[x : x + 16, :] = jnp.where(odd, high, low).astype(bf16)
        inside_ref[x : x + 16, :] = jnp.where(odd, low, high).astype(bf16)


def ends(cells):
    depth, rows, width = cells.shape
    return pl.pallas_call(
        ends_kernel,
        out_shape=[jax.ShapeDtypeStruct((depth, width), bf16)] * 2,
        compiler_params=plain_params(),
        cost_estimate=pl.CostEstimate(flops=cells.size, bytes_accessed=2 * cells.size, transcendentals=0),
        name="ends",
    )(cells)


def z_sides(inner_ref, outer_ref):
    odd = lax.axis_index("gz") % 2 == 1
    inner, outer = inner_ref[...].astype(f32), outer_ref[...].astype(f32)
    return jnp.where(odd, inner, outer), jnp.where(odd, outer, inner)


def corners_kernel(inner_ref, outer_ref, across_out, inside_out):
    rows, depth = inner_ref.shape[0], across_out.shape[0]
    odd = lax.axis_index("gy") % 2 == 1
    lane = lax.broadcasted_iota(jnp.int32, (depth, LANES), 1)
    pad = jnp.zeros((LANES - rows, LANES), f32)
    left, right = z_sides(inner_ref, outer_ref)
    left = jnp.transpose(jnp.concatenate([left, pad], axis=0))[0:depth]
    right = jnp.transpose(jnp.concatenate([right, pad], axis=0))[0:depth]
    low, high = (
        jnp.where(lane == 0, pltpu.roll(right, (LANES - row) % LANES, 1), pltpu.roll(left, LANES - 1 - row, 1))
        for row in (0, rows - 1)
    )
    across_out[...] = jnp.where(odd, high, low).astype(bf16)
    inside_out[...] = jnp.where(odd, low, high).astype(bf16)


def corners(inner, outer, depth):
    return pl.pallas_call(
        corners_kernel,
        out_shape=[jax.ShapeDtypeStruct((depth, LANES), bf16)] * 2,
        compiler_params=plain_params(),
        cost_estimate=pl.CostEstimate(flops=1 << 34, bytes_accessed=1 << 17, transcendentals=0),
        name="corners",
    )(inner, outer)


def swapped(part, axis, start):
    count = lax.axis_size(axis)
    pairs = [(i, i + 1) for i in range(start, count - 1, 2)]
    return lax.ppermute(part, axis, pairs + [(j, i) for i, j in pairs])


def squares_kernel(image_ref, later_ref, sums):
    depth, rows, width = image_ref.shape
    tiles = width // LANES

    def one(t, carry):
        block, tile = t // tiles, t % tiles
        at = pl.multiple_of(tile * LANES, LANES)
        for pair in range(rows // 16):
            total = jnp.zeros((16, LANES), f32)
            for k in range(KNOT):
                values = image_ref[block * KNOT + k, 16 * pair : 16 * pair + 16, pl.ds(at, LANES)].astype(f32)
                total = total + values * values
            for half in range(2):
                row = block * (rows // KNOT) + 2 * pair + half
                sums[tile, pl.ds(row, 1), :] = jnp.sum(total[8 * half : 8 * half + 8], axis=0, keepdims=True)
        return carry

    lax.fori_loop(0, depth // KNOT * tiles, one, 0)


def squares(image, later):
    depth, rows, width = image.shape
    return pl.pallas_call(
        squares_kernel,
        out_shape=jax.ShapeDtypeStruct((width // LANES, depth * rows // KNOT**2, LANES), f32),
        compiler_params=plain_params(),
        cost_estimate=pl.CostEstimate(flops=3 * image.size, bytes_accessed=2 * image.size, transcendentals=0),
        name="squares",
    )(image, later)


def terms_kernel(
    sums, plane_ref, depth_ref, inner_ref, outer_ref, field_ref, diag_depth_ref, diag_plane_ref, beyond_ref
):
    tiles = sums.shape[0]
    left, right = z_sides(inner_ref, outer_ref)
    lane = lax.broadcasted_iota(jnp.int32, left.shape, 1)
    for x in range(beyond_ref.shape[0]):
        after = pltpu.roll(right, (LANES - x) % LANES, 1)
        before = pltpu.roll(left, LANES - 1 - x, 1)
        beyond_ref[x] = jnp.where(lane == 0, after, before).astype(bf16)
    for k in range(2):
        field = dot(plane_ref[k], depth_ref[k], ((1,), (0,)))
        for tile in range(tiles):
            field_ref[k, tile] = field[:, tile * LANES : (tile + 1) * LANES]
    squared = joined(sums)
    cells = jnp.full(squared.shape, float(KNOT * KNOT), f32)
    first, second = plane_ref[0], plane_ref[1]
    diag_depth_ref[0] = dot(first * first, squared, ((0,), (0,)))
    diag_depth_ref[1] = dot(second * second, cells, ((0,), (0,)))
    first, second = depth_ref[0], depth_ref[1]
    diag_plane_ref[0] = dot(squared, first * first, ((1,), (1,)))
    diag_plane_ref[1] = dot(cells, second * second, ((1,), (1,)))


def terms(sums, plane, depth_factors, inner, outer, depth):
    nodes, width = plane.shape[1], depth_factors.shape[2]
    return pl.pallas_call(
        terms_kernel,
        out_shape=[
            jax.ShapeDtypeStruct((2, width // LANES, nodes, LANES), f32),
            jax.ShapeDtypeStruct((2, RANK, width), f32),
            jax.ShapeDtypeStruct((2, nodes, RANK), f32),
            jax.ShapeDtypeStruct((depth,) + inner.shape, bf16),
        ],
        compiler_params=plain_params(),
        cost_estimate=pl.CostEstimate(flops=40 * nodes * RANK * width, bytes_accessed=1 << 20, transcendentals=0),
        name="terms",
    )(sums, plane, depth_factors, inner, outer)


def warp_kernel(
    cells_ref, image_ref, shift_x_ref, shift_y_ref, shift_z_ref, beyond_ref, across_ref, inside_ref,
    across_tile_ref, inside_tile_ref, field, plane_ref, depth_ref,
    diag_depth_ref, diag_plane_ref,
    residual_ref, depth_out, plane_out,
    ahead_ref, here_ref, behind_ref, wide, bands, blocks, energy, held,
):
    step = pl.program_id(0)
    last = pl.num_programs(0) - 1
    planes, rows, width = cells_ref.shape
    nodes = rows // KNOT
    tiles = width // LANES
    window = (ahead_ref, here_ref, behind_ref)
    shifts = (shift_x_ref, shift_y_ref, shift_z_ref)
    pitch = rows + 2 * TOP
    plane_rows = tiles * pitch
    block_rows = planes * plane_rows

    @pl.when(step == 0)
    def _():
        row = lax.broadcasted_iota(jnp.int32, bands.shape[1:], 0)
        column = lax.broadcasted_iota(jnp.int32, bands.shape[1:], 1)
        one, none = jnp.ones(bands.shape[1:], f32), jnp.zeros(bands.shape[1:], f32)
        up, down = jnp.where(row == column + 1, one, none), jnp.where(row == column, one, none)
        bands[0] = (up - down).astype(bf16)
        up = jnp.where(row == column + LANES, one, none)
        down = jnp.where(row == column + LANES - 1, one, none)
        bands[1] = (up - down).astype(bf16)
        energy[...] = jnp.zeros_like(energy)
        for c in range(3):
            window[c][3 * block_rows - plane_rows : 3 * block_rows, :] = jnp.zeros((plane_rows, LANES), f32)

    @pl.when(step < last)
    def _():
        slot = (step % 3) * block_rows
        odd = lax.axis_index("gy") % 2 == 1
        across, inside = (
            jnp.concatenate([row[...].astype(f32), tile[...].astype(f32)], axis=1)
            for row, tile in ((across_ref, across_tile_ref), (inside_ref, inside_tile_ref))
        )
        low, high = jnp.where(odd, inside, across), jnp.where(odd, across, inside)
        at = lax.broadcasted_iota(jnp.int32, (2 * TOP, width + LANES), 0)
        for k in range(planes):
            first = k * pitch
            wide[first : first + rows, 0:width] = cells_ref[k]
            wide[first : first + rows, width:] = beyond_ref[k]
            rim = jnp.where(at == TOP, high[k : k + 1], jnp.where(at == TOP - 1, low[k : k + 1], 0.0))
            wide[first + rows : first + pitch, :] = rim.astype(bf16)

        def put(c, tile, values):
            for k in range(planes):
                first = pl.multiple_of(slot + k * plane_rows + tile * pitch, 8)
                mine = values[k * pitch : (k + 1) * pitch]
                window[c][pl.ds(first + TOP, rows), :] = mine[0:rows]
                window[c][pl.ds(first, TOP), :] = mine[rows : rows + TOP]
                window[c][pl.ds(first + TOP + rows, TOP), :] = mine[rows + TOP :]

        pieces = width // (2 * LANES)
        for piece in range(pieces):
            start = 2 * LANES * piece
            after = wide[:, start : start + 3 * LANES]
            if piece == 0:
                before = jnp.concatenate([wide[:, width:], wide[:, 0 : 2 * LANES]], axis=1)
            else:
                before = wide[:, start - LANES : start + 2 * LANES]
            ahead = jnp.dot(after, bands[0], preferred_element_type=f32)
            behind = jnp.dot(before, bands[1], preferred_element_type=f32)
            for half in range(2):
                mine = slice(half * LANES, (half + 1) * LANES)
                put(0, 2 * piece + half, ahead[:, mine])
                put(1, 2 * piece + half, wide[:, start + half * LANES : start + (half + 1) * LANES].astype(f32))
                put(2, 2 * piece + half, behind[:, mine])

    @pl.when(step == last)
    def _():
        first = pl.multiple_of((step % 3) * block_rows, 8)
        for c in range(3):
            window[c][pl.ds(first, plane_rows), :] = jnp.zeros((plane_rows, LANES), f32)

    @pl.when(step > 0)
    def _():
        mid = (step + 2) % 3
        first_rows = (
            jnp.where(mid == 0, 3, mid) * block_rows - plane_rows,
            mid * block_rows,
            jnp.where(mid == 2, 0, mid + 1) * block_rows,
        )

        def one(t, total):
            tile = t % tiles
            pair = t // tiles
            at = pl.multiple_of(tile * LANES, LANES)
            top = pl.multiple_of(pair * 16, 16)
            origins = [first + tile * pitch + top + TOP for first in first_rows]
            for half in range(2):
                node = (step - 1) * nodes + pair * 2 + half
                mine = slice(8 * half, 8 * half + 8)

                def taps(x):
                    part = 0 if x == 0 else 2 if x == planes + 1 else 1
                    plus = (x - 1) * plane_rows + 8 * half if part == 1 else 8 * half
                    return [
                        [window[c][pl.ds(origins[part] + (plus + b), 8), :] for c in range(3)] for b in (-1, 0, 1)
                    ]

                contrast = jnp.broadcast_to(field[0, tile, pl.ds(node, 1), :], (8, LANES))
                brightness = jnp.broadcast_to(field[1, tile, pl.ds(node, 1), :], (8, LANES))
                by_image = jnp.zeros((8, LANES), f32)
                plain = jnp.zeros((8, LANES), f32)
                before, here = taps(0), taps(1)
                for k in range(planes):
                    after = taps(k + 2)
                    place = (k, pl.ds(top, 16), pl.ds(at, LANES))
                    sx, sy, sz = (ref[(0,) + place].astype(f32)[mine] for ref in shifts)
                    image = image_ref[place].astype(f32)[mine]
                    px, py, pz = sx > 0, sy > 0, sz > 0
                    ax, ay = jnp.abs(sx), jnp.abs(sy)

                    def sides(c):
                        far = [jnp.where(px, after[b][c], before[b][c]) for b in range(3)]
                        near = [here[b][c] for b in range(3)]
                        return [(v[1], jnp.where(py, v[2], v[0])) for v in (near, far)]

                    ahead, middle, behind = sides(0), sides(1), sides(2)
                    lines = []
                    for b in range(2):
                        near, far = (middle[v][b] + sz * jnp.where(pz, ahead[v][b], behind[v][b]) for v in range(2))
                        lines.append(near + ax * (far - near))
                    warped = lines[0] + ay * (lines[1] - lines[0])
                    misfit = warped - contrast * image - brightness
                    if half == 0:
                        held[k] = misfit
                    else:
                        residual_ref[place] = jnp.concatenate([held[k], misfit], axis=0).astype(bf16)
                    by_image = by_image + misfit * image
                    plain = plain + misfit
                    total = total + misfit * misfit
                    before, here = here, after
                for k, value in ((0, by_image), (1, plain)):
                    blocks[k, tile, pl.ds(node, 1), :] = jnp.sum(value, axis=0, keepdims=True)
            return total

        energy[...] = lax.fori_loop(0, (rows // 16) * tiles, one, energy[...], unroll=2)

    @pl.when(step == last)
    def _():
        parts = depth_out.shape[0]
        share = RANK // parts
        sums = [joined(blocks.at[k]) for k in range(2)]
        kinds = [split_dot(plane_ref[k], sums[k], 0) for k in range(2)]
        kinds = kinds + [diag_depth_ref[0], diag_depth_ref[1]]
        half = width // 2
        for p in range(parts):
            rows = slice(p * share, (p + 1) * share)
            for k in range(2):
                mine = slice(k * share, (k + 1) * share)
                depth_out[p, mine, 0:width] = kinds[k][rows]
                depth_out[p, mine, width : width + half] = kinds[2][rows, k * half : (k + 1) * half]
                depth_out[p, mine, width + half :] = kinds[3][rows, 0:LANES]
        local = jnp.sum(energy[...])
        kinds = [split_dot(sums[k], depth_ref[k], 1) for k in range(2)]
        kinds = kinds + [diag_plane_ref[0], diag_plane_ref[1]]
        for k in range(4):
            plane_out[:, k * RANK : (k + 1) * RANK] = kinds[k]
        count = plane_out.shape[0]
        plane_out[count // 2 :, 3 * RANK :] = jnp.full((count // 2, RANK), local, f32)


def warp(
    cells, image, shift, beyond, across, inside, across_tile, inside_tile, field, plane, depth_factors, diag_depth,
    diag_plane, parts
):
    depth, rows, width = cells.shape
    nodes = plane.shape[1]
    tiles = width // LANES
    count = depth // KNOT
    behind = lambda i: (jnp.maximum(i - 1, 0), 0, 0)
    ahead = lambda i: (jnp.minimum(i, count - 1), 0, 0)
    flat = lambda i: (0, 0)
    whole = lambda i: (0, 0, 0)
    return pl.pallas_call(
        warp_kernel,
        grid=(count + 1,),
        in_specs=[
            pl.BlockSpec((KNOT, rows, width), ahead),
            pl.BlockSpec((KNOT, rows, width), behind),
            pl.BlockSpec((1, KNOT, rows, width), lambda i: (0, jnp.maximum(i - 1, 0), 0, 0)),
            pl.BlockSpec((1, KNOT, rows, width), lambda i: (1, jnp.maximum(i - 1, 0), 0, 0)),
            pl.BlockSpec((1, KNOT, rows, width), lambda i: (2, jnp.maximum(i - 1, 0), 0, 0)),
            pl.BlockSpec((KNOT, rows, LANES), ahead),
            pl.BlockSpec((KNOT, across.shape[1]), lambda i: (jnp.minimum(i, count - 1), 0)),
            pl.BlockSpec((KNOT, inside.shape[1]), lambda i: (jnp.minimum(i, count - 1), 0)),
            pl.BlockSpec((KNOT, LANES), lambda i: (jnp.minimum(i, count - 1), 0)),
            pl.BlockSpec((KNOT, LANES), lambda i: (jnp.minimum(i, count - 1), 0)),
            pl.BlockSpec(field.shape, lambda i: (0, 0, 0, 0)),
            pl.BlockSpec(plane.shape, whole),
            pl.BlockSpec(depth_factors.shape, whole),
            pl.BlockSpec(diag_depth.shape, whole),
            pl.BlockSpec(diag_plane.shape, whole),
        ],
        out_specs=[
            pl.BlockSpec((KNOT, rows, width), behind),
            pl.BlockSpec((parts, 2 * RANK // parts, width + width // 2 + LANES), whole),
            pl.BlockSpec((nodes, 4 * RANK), flat),
        ],
        out_shape=[
            jax.ShapeDtypeStruct(cells.shape, bf16),
            jax.ShapeDtypeStruct((parts, 2 * RANK // parts, width + width // 2 + LANES), f32),
            jax.ShapeDtypeStruct((nodes, 4 * RANK), f32),
        ],
        scratch_shapes=[
            *[pltpu.VMEM((3 * KNOT * tiles * (rows + 2 * TOP), LANES), f32)] * 3,
            pltpu.VMEM((KNOT * (rows + 2 * TOP), width + LANES), bf16),
            pltpu.VMEM((2, 3 * LANES, 2 * LANES), bf16),
            pltpu.VMEM((2, tiles, nodes, LANES), f32),
            pltpu.VMEM((8, LANES), f32),
            pltpu.VMEM((KNOT, 8, LANES), f32),
        ],
        compiler_params=grid_params(),
        cost_estimate=pl.CostEstimate(flops=60 * cells.size, bytes_accessed=12 * cells.size, transcendentals=0),
        name="warp",
    )(cells, image, shift, shift, shift, beyond, across, inside, across_tile, inside_tile, field, plane, depth_factors, diag_depth, diag_plane)


def gather_kernel(depth_ref, *refs):
    depth_out, plane_out = refs[-2:]
    total = jnp.sum(depth_ref[...], axis=0)
    found = [ref[...] for ref in refs[:-2]]
    while len(found) > 1:
        half = len(found) // 2
        found = [found[k] + found[k + half] for k in range(half)]
    planes = found[0]
    plane_out[...] = planes
    cells = planes.shape[0]
    share, width = total.shape[0] // 2, total.shape[1]
    row = lax.broadcasted_iota(jnp.int32, total.shape, 0)
    lane = lax.broadcasted_iota(jnp.int32, total.shape, 1)
    partial = planes[cells - 1, 4 * RANK - 1]
    total = jnp.where((row >= share) & (lane >= width - LANES), partial, total)
    for p in range(depth_out.shape[0]):
        depth_out[p] = total


def step_kernel(full_z, node_count, depth_ref, plane_ref, depth_out, plane_out):
    parts, share, width = depth_ref.shape[0], depth_ref.shape[1] // 2, depth_out.shape[2]
    half = width // 2
    energy = depth_ref[0, share, width + half]
    for p in range(1, parts):
        energy = energy + depth_ref[p, share, width + half]
    lam_depth = damping * energy / full_z
    lam_plane = damping * RANK * energy / node_count
    for p in range(parts):
        got = depth_ref[p]
        rows = slice(p * share, (p + 1) * share)
        first, second = got[0:share], got[share:]
        squared = jnp.concatenate([first[:, width : width + half], second[:, width : width + half]], axis=1)
        levels = jnp.concatenate([first[:, width + half :]] * (width // LANES), axis=1)
        depth_out[0, rows, :] = first[:, 0:width] / (squared + lam_depth + epsilon)
        depth_out[1, rows, :] = second[:, 0:width] / (levels + lam_depth + epsilon)
    planes = plane_ref[...]
    plane_out[0] = planes[:, 0:RANK] / (planes[:, 2 * RANK : 3 * RANK] + lam_plane + epsilon)
    plane_out[1] = planes[:, RANK : 2 * RANK] / (planes[0:1, 3 * RANK :] + lam_plane + epsilon)


def local(image, deformed, displacement, plane_factors, depth_factors):
    n_gy, n_gz = lax.axis_size("gy"), lax.axis_size("gz")
    nodes_x, nodes_y = plane_factors.shape[2:]
    plane = jnp.transpose(plane_factors, (0, 2, 3, 1)).reshape(2, nodes_x * nodes_y, RANK)
    inner, outer = end_columns(deformed)
    inner = swapped(inner, "gz", 0)
    outer = swapped(outer, "gz", 1)
    across, inside = ends(deformed)
    inside = swapped(inside, "gy", 0)
    across = swapped(across, "gy", 1)
    across_tile, inside_tile = corners(inner, outer, deformed.shape[0])
    sums = squares(image, across_tile)
    inside_tile = swapped(inside_tile, "gy", 0)
    across_tile = swapped(across_tile, "gy", 1)
    field, diag_depth, diag_plane, beyond = terms(sums, plane, depth_factors, inner, outer, deformed.shape[0])
    residual, depth_terms, plane_terms = warp(
        deformed, image, displacement, beyond, across, inside, across_tile, inside_tile, field, plane, depth_factors,
        diag_depth, diag_plane, n_gy,
    )
    depth_terms = lax.all_to_all(depth_terms, "gy", 0, 0)
    others = [
        lax.ppermute(plane_terms, "gz", [(i, i ^ hop) for i in range(n_gz)]) for hop in range(1, n_gz)
    ]
    depth_terms, plane_terms = pl.pallas_call(
        gather_kernel,
        out_shape=[
            jax.ShapeDtypeStruct(depth_terms.shape, f32),
            jax.ShapeDtypeStruct(plane_terms.shape, f32),
        ],
        compiler_params=plain_params(),
        name="gather",
    )(depth_terms, plane_terms, *others)
    depth_terms = lax.all_to_all(depth_terms, "gy", 0, 0)
    width = depth_factors.shape[2]
    step_depth, step_plane = pl.pallas_call(
        functools.partial(step_kernel, width * n_gz, nodes_x * nodes_y * n_gy),
        out_shape=[
            jax.ShapeDtypeStruct(depth_factors.shape, f32),
            jax.ShapeDtypeStruct(plane.shape, f32),
        ],
        compiler_params=plain_params(),
        name="steps",
    )(depth_terms, plane_terms)
    step_plane = jnp.transpose(step_plane.reshape(2, nodes_x, nodes_y, RANK), (0, 3, 1, 2))
    return residual, step_plane, step_depth


def solution(mesh):
    placed = (
        P(None, "gy", "gz"),
        P(None, "gy", "gz"),
        P(None, None, "gy", "gz"),
        P(None, None, None, "gy"),
        P(None, None, "gz"),
    )
    return jax.shard_map(
        local,
        mesh=mesh,
        in_specs=placed,
        out_specs=(P(None, "gy", "gz"), P(None, None, None, "gy"), P(None, None, "gz")),
        check_vma=False,
    )
```

```python
import functools

import jax
import jax.numpy as jnp
from jax import lax
from jax.experimental import pallas as pl
from jax.experimental.pallas import tpu as pltpu
from jax.sharding import PartitionSpec as P

RANK = 32
KNOT = 8
LANES = 128
TOP = 8

epsilon = 1e-06
damping = 0.01
highest = lax.Precision.HIGHEST
f32 = jnp.float32
bf16 = jnp.bfloat16


def dot(left, right, dims):
    return lax.dot_general(left, right, ((dims[0], dims[1]), ((), ())), precision=highest, preferred_element_type=f32)


def split_dot(left, right, dim):
    left_high, right_high = left.astype(bf16), right.astype(bf16)
    left_low = (left - left_high.astype(f32)).astype(bf16)
    right_low = (right - right_high.astype(f32)).astype(bf16)
    left = jnp.concatenate([left_high, left_high, left_low], axis=dim)
    right = jnp.concatenate([right_high, right_low, right_high], axis=dim)
    return lax.dot_general(left, right, (((dim,), (dim,)), ((), ())), preferred_element_type=f32)


def joined(ref):
    return jnp.concatenate([ref[tile] for tile in range(ref.shape[0])], axis=1)


def plain_params():
    return pltpu.CompilerParams(vmem_limit_bytes=32000000)


def columns_kernel(*refs):
    inner_ref, outer_ref = refs[-2:]
    chunks = (len(refs) - 2) // 2
    rows = inner_ref.shape[0]
    lane = lax.broadcasted_iota(jnp.int32, (rows, LANES), 1)
    first = jnp.zeros((rows, LANES), f32)
    last = jnp.zeros((rows, LANES), f32)
    for chunk in range(chunks):
        near, far = refs[chunk], refs[chunks + chunk]
        for k in range(near.shape[0]):
            x = chunk * near.shape[0] + k
            first = jnp.where(lane == x, pltpu.roll(near[k].astype(f32), x, 1), first)
            last = jnp.where(lane == x, pltpu.roll(far[k].astype(f32), (x + 1) % LANES, 1), last)
    odd = lax.axis_index("gz") % 2 == 1
    inner_ref[...] = jnp.where(odd, first, last).astype(bf16)
    outer_ref[...] = jnp.where(odd, last, first).astype(bf16)


def end_columns(cells):
    depth, rows, width = cells.shape
    tiles = width // LANES
    chunks = 4
    block = (depth // chunks, rows, LANES)
    places = [(chunk, tile) for tile in (0, tiles - 1) for chunk in range(chunks)]
    return pl.pallas_call(
        columns_kernel,
        grid=(1,),
        in_specs=[pl.BlockSpec(block, functools.partial(lambda c, t, i: (c, 0, t), c, t)) for c, t in places],
        out_specs=[pl.BlockSpec((rows, LANES), lambda i: (0, 0))] * 2,
        out_shape=[jax.ShapeDtypeStruct((rows, LANES), bf16)] * 2,
        compiler_params=pltpu.CompilerParams(vmem_limit_bytes=60000000),
        name="columns",
    )(*[cells] * len(places))


def ends_kernel(cells_ref, across_ref, inside_ref):
    depth, rows = cells_ref.shape[0:2]
    odd = lax.axis_index("gy") % 2 == 1
    for x in range(0, depth, 16):
        low = [cells_ref[x + k, 0:16, :].astype(f32)[0:1] for k in range(16)]
        high = [cells_ref[x + k, rows - 16 : rows, :].astype(f32)[15:16] for k in range(16)]
        low, high = jnp.concatenate(low, axis=0), jnp.concatenate(high, axis=0)
        across_ref[x : x + 16, :] = jnp.where(odd, high, low).astype(bf16)
        inside_ref[x : x + 16, :] = jnp.where(odd, low, high).astype(bf16)


def ends(cells):
    depth, rows, width = cells.shape
    return pl.pallas_call(
        ends_kernel,
        out_shape=[jax.ShapeDtypeStruct((depth, width), bf16)] * 2,
        compiler_params=plain_params(),
        cost_estimate=pl.CostEstimate(flops=cells.size, bytes_accessed=2 * cells.size, transcendentals=0),
        name="ends",
    )(cells)


def z_sides(inner_ref, outer_ref):
    odd = lax.axis_index("gz") % 2 == 1
    inner, outer = inner_ref[...].astype(f32), outer_ref[...].astype(f32)
    return jnp.where(odd, inner, outer), jnp.where(odd, outer, inner)


def corners_kernel(inner_ref, outer_ref, across_out, inside_out):
    rows, depth = inner_ref.shape[0], across_out.shape[0]
    odd = lax.axis_index("gy") % 2 == 1
    lane = lax.broadcasted_iota(jnp.int32, (depth, LANES), 1)
    pad = jnp.zeros((LANES - rows, LANES), f32)
    left, right = z_sides(inner_ref, outer_ref)
    left = jnp.transpose(jnp.concatenate([left, pad], axis=0))[0:depth]
    right = jnp.transpose(jnp.concatenate([right, pad], axis=0))[0:depth]
    low, high = (
        jnp.where(lane == 0, pltpu.roll(right, (LANES - row) % LANES, 1), pltpu.roll(left, LANES - 1 - row, 1))
        for row in (0, rows - 1)
    )
    across_out[...] = jnp.where(odd, high, low).astype(bf16)
    inside_out[...] = jnp.where(odd, low, high).astype(bf16)


def corners(inner, outer, depth):
    return pl.pallas_call(
        corners_kernel,
        out_shape=[jax.ShapeDtypeStruct((depth, LANES), bf16)] * 2,
        compiler_params=plain_params(),
        cost_estimate=pl.CostEstimate(flops=1 << 34, bytes_accessed=1 << 17, transcendentals=0),
        name="corners",
    )(inner, outer)


def swapped(part, axis, start):
    count = lax.axis_size(axis)
    pairs = [(i, i + 1) for i in range(start, count - 1, 2)]
    return lax.ppermute(part, axis, pairs + [(j, i) for i, j in pairs])


def squares_kernel(image_ref, later_ref, sums):
    depth, rows, width = image_ref.shape
    tiles = width // LANES

    def one(t, carry):
        block, tile = t // tiles, t % tiles
        at = pl.multiple_of(tile * LANES, LANES)
        for pair in range(rows // 16):
            total = jnp.zeros((16, LANES), f32)
            for k in range(KNOT):
                values = image_ref[block * KNOT + k, 16 * pair : 16 * pair + 16, pl.ds(at, LANES)].astype(f32)
                total = total + values * values
            for half in range(2):
                row = block * (rows // KNOT) + 2 * pair + half
                sums[tile, pl.ds(row, 1), :] = jnp.sum(total[8 * half : 8 * half + 8], axis=0, keepdims=True)
        return carry

    lax.fori_loop(0, depth // KNOT * tiles, one, 0)


def squares(image, later):
    depth, rows, width = image.shape
    return pl.pallas_call(
        squares_kernel,
        out_shape=jax.ShapeDtypeStruct((width // LANES, depth * rows // KNOT**2, LANES), f32),
        compiler_params=plain_params(),
        cost_estimate=pl.CostEstimate(flops=3 * image.size, bytes_accessed=2 * image.size, transcendentals=0),
        name="squares",
    )(image, later)


def terms_kernel(
    sums, plane_ref, depth_ref, inner_ref, outer_ref, field_ref, diag_depth_ref, diag_plane_ref, beyond_ref
):
    tiles = sums.shape[0]
    left, right = z_sides(inner_ref, outer_ref)
    lane = lax.broadcasted_iota(jnp.int32, left.shape, 1)
    for x in range(beyond_ref.shape[0]):
        after = pltpu.roll(right, (LANES - x) % LANES, 1)
        before = pltpu.roll(left, LANES - 1 - x, 1)
        beyond_ref[x] = jnp.where(lane == 0, after, before).astype(bf16)
    for k in range(2):
        field = dot(plane_ref[k], depth_ref[k], ((1,), (0,)))
        for tile in range(tiles):
            field_ref[k, tile] = field[:, tile * LANES : (tile + 1) * LANES]
    squared = joined(sums)
    cells = jnp.full(squared.shape, float(KNOT * KNOT), f32)
    first, second = plane_ref[0], plane_ref[1]
    diag_depth_ref[0] = dot(first * first, squared, ((0,), (0,)))
    diag_depth_ref[1] = dot(second * second, cells, ((0,), (0,)))
    first, second = depth_ref[0], depth_ref[1]
    diag_plane_ref[0] = dot(squared, first * first, ((1,), (1,)))
    diag_plane_ref[1] = dot(cells, second * second, ((1,), (1,)))


def terms(sums, plane, depth_factors, inner, outer, depth):
    nodes, width = plane.shape[1], depth_factors.shape[2]
    return pl.pallas_call(
        terms_kernel,
        out_shape=[
            jax.ShapeDtypeStruct((2, width // LANES, nodes, LANES), f32),
            jax.ShapeDtypeStruct((2, RANK, width), f32),
            jax.ShapeDtypeStruct((2, nodes, RANK), f32),
            jax.ShapeDtypeStruct((depth,) + inner.shape, bf16),
        ],
        compiler_params=plain_params(),
        cost_estimate=pl.CostEstimate(flops=40 * nodes * RANK * width, bytes_accessed=1 << 20, transcendentals=0),
        name="terms",
    )(sums, plane, depth_factors, inner, outer)


def warp_kernel(
    cells_ref, image_hbm, shift_hbm, beyond_ref, across_ref, inside_ref,
    across_tile_ref, inside_tile_ref, field, plane_ref, depth_ref,
    diag_depth_ref, diag_plane_ref,
    residual_hbm, depth_out, plane_out,
    ahead_ref, here_ref, behind_ref, wide, bands, blocks, energy, held,
    image_ref, shift_ref, residual_ref, got, sent,
):
    step = pl.program_id(0)
    last = pl.num_programs(0) - 1
    planes, rows, width = cells_ref.shape
    nodes = rows // KNOT
    tiles = width // LANES
    window = (ahead_ref, here_ref, behind_ref)
    pitch = rows + 2 * TOP
    plane_rows = tiles * pitch
    block_rows = planes * plane_rows

    @pl.when(step == 0)
    def _():
        row = lax.broadcasted_iota(jnp.int32, bands.shape[1:], 0)
        column = lax.broadcasted_iota(jnp.int32, bands.shape[1:], 1)
        one, none = jnp.ones(bands.shape[1:], f32), jnp.zeros(bands.shape[1:], f32)
        up, down = jnp.where(row == column + 1, one, none), jnp.where(row == column, one, none)
        bands[0] = (up - down).astype(bf16)
        up = jnp.where(row == column + LANES, one, none)
        down = jnp.where(row == column + LANES - 1, one, none)
        bands[1] = (up - down).astype(bf16)
        energy[...] = jnp.zeros_like(energy)
        for c in range(3):
            window[c][3 * block_rows - plane_rows : 3 * block_rows, :] = jnp.zeros((plane_rows, LANES), f32)

    def fetched(n):
        slot, part = n % 2, pl.ds(n * planes, planes)
        copies = [
            pltpu.make_async_copy(shift_hbm.at[axis, part], shift_ref.at[slot, axis], got.at[slot, axis])
            for axis in range(3)
        ]
        return copies + [pltpu.make_async_copy(image_hbm.at[part], image_ref.at[slot], got.at[slot, 3])]

    def leaving(n):
        slot, part = n % 2, pl.ds(n * planes, planes)
        return pltpu.make_async_copy(residual_ref.at[slot], residual_hbm.at[part], sent.at[slot])

    @pl.when(step < last)
    def _():
        for copy in fetched(step):
            copy.start()

    @pl.when(step < last)
    def _():
        slot = (step % 3) * block_rows
        odd = lax.axis_index("gy") % 2 == 1
        across, inside = (
            jnp.concatenate([row[...].astype(f32), tile[...].astype(f32)], axis=1)
            for row, tile in ((across_ref, across_tile_ref), (inside_ref, inside_tile_ref))
        )
        low, high = jnp.where(odd, inside, across), jnp.where(odd, across, inside)
        at = lax.broadcasted_iota(jnp.int32, (2 * TOP, width + LANES), 0)
        for k in range(planes):
            first = k * pitch
            wide[first : first + rows, 0:width] = cells_ref[k]
            wide[first : first + rows, width:] = beyond_ref[k]
            rim = jnp.where(at == TOP, high[k : k + 1], jnp.where(at == TOP - 1, low[k : k + 1], 0.0))
            wide[first + rows : first + pitch, :] = rim.astype(bf16)

        def put(c, tile, values):
            for k in range(planes):
                first = pl.multiple_of(slot + k * plane_rows + tile * pitch, 8)
                mine = values[k * pitch : (k + 1) * pitch]
                window[c][pl.ds(first + TOP, rows), :] = mine[0:rows]
                window[c][pl.ds(first, TOP), :] = mine[rows : rows + TOP]
                window[c][pl.ds(first + TOP + rows, TOP), :] = mine[rows + TOP :]

        pieces = width // (2 * LANES)
        for piece in range(pieces):
            start = 2 * LANES * piece
            after = wide[:, start : start + 3 * LANES]
            if piece == 0:
                before = jnp.concatenate([wide[:, width:], wide[:, 0 : 2 * LANES]], axis=1)
            else:
                before = wide[:, start - LANES : start + 2 * LANES]
            ahead = jnp.dot(after, bands[0], preferred_element_type=f32)
            behind = jnp.dot(before, bands[1], preferred_element_type=f32)
            for half in range(2):
                mine = slice(half * LANES, (half + 1) * LANES)
                put(0, 2 * piece + half, ahead[:, mine])
                put(1, 2 * piece + half, wide[:, start + half * LANES : start + (half + 1) * LANES].astype(f32))
                put(2, 2 * piece + half, behind[:, mine])

    @pl.when(step == last)
    def _():
        first = pl.multiple_of((step % 3) * block_rows, 8)
        for c in range(3):
            window[c][pl.ds(first, plane_rows), :] = jnp.zeros((plane_rows, LANES), f32)

    @pl.when(step > 0)
    def _():
        block = step - 1
        here_slot = block % 2
        for copy in fetched(block):
            copy.wait()

        @pl.when(block > 1)
        def _():
            leaving(block - 2).wait()

        mid = (step + 2) % 3
        first_rows = (
            jnp.where(mid == 0, 3, mid) * block_rows - plane_rows,
            mid * block_rows,
            jnp.where(mid == 2, 0, mid + 1) * block_rows,
        )

        def one(t, total):
            tile = t % tiles
            pair = t // tiles
            at = pl.multiple_of(tile * LANES, LANES)
            top = pl.multiple_of(pair * 16, 16)
            origins = [first + tile * pitch + top + TOP for first in first_rows]
            for half in range(2):
                node = (step - 1) * nodes + pair * 2 + half
                mine = slice(8 * half, 8 * half + 8)

                def taps(x):
                    part = 0 if x == 0 else 2 if x == planes + 1 else 1
                    plus = (x - 1) * plane_rows + 8 * half if part == 1 else 8 * half
                    return [
                        [window[c][pl.ds(origins[part] + (plus + b), 8), :] for c in range(3)] for b in (-1, 0, 1)
                    ]

                contrast = jnp.broadcast_to(field[0, tile, pl.ds(node, 1), :], (8, LANES))
                brightness = jnp.broadcast_to(field[1, tile, pl.ds(node, 1), :], (8, LANES))
                by_image = jnp.zeros((8, LANES), f32)
                plain = jnp.zeros((8, LANES), f32)
                before, here = taps(0), taps(1)
                for k in range(planes):
                    after = taps(k + 2)
                    place = (k, pl.ds(top, 16), pl.ds(at, LANES))
                    sx, sy, sz = (shift_ref[(here_slot, axis) + place].astype(f32)[mine] for axis in range(3))
                    image = image_ref[(here_slot,) + place].astype(f32)[mine]
                    px, py, pz = sx > 0, sy > 0, sz > 0
                    ax, ay = jnp.abs(sx), jnp.abs(sy)

                    def sides(c):
                        far = [jnp.where(px, after[b][c], before[b][c]) for b in range(3)]
                        near = [here[b][c] for b in range(3)]
                        return [(v[1], jnp.where(py, v[2], v[0])) for v in (near, far)]

                    ahead, middle, behind = sides(0), sides(1), sides(2)
                    lines = []
                    for b in range(2):
                        near, far = (middle[v][b] + sz * jnp.where(pz, ahead[v][b], behind[v][b]) for v in range(2))
                        lines.append(near + ax * (far - near))
                    warped = lines[0] + ay * (lines[1] - lines[0])
                    misfit = warped - contrast * image - brightness
                    if half == 0:
                        held[k] = misfit
                    else:
                        residual_ref[(here_slot,) + place] = jnp.concatenate([held[k], misfit], axis=0).astype(bf16)
                    by_image = by_image + misfit * image
                    plain = plain + misfit
                    total = total + misfit * misfit
                    before, here = here, after
                for k, value in ((0, by_image), (1, plain)):
                    blocks[k, tile, pl.ds(node, 1), :] = jnp.sum(value, axis=0, keepdims=True)
            return total

        energy[...] = lax.fori_loop(0, (rows // 16) * tiles, one, energy[...])
        leaving(block).start()

    @pl.when(step == last)
    def _():
        parts = depth_out.shape[0]
        share = RANK // parts
        sums = [joined(blocks.at[k]) for k in range(2)]
        kinds = [split_dot(plane_ref[k], sums[k], 0) for k in range(2)]
        kinds = kinds + [diag_depth_ref[0], diag_depth_ref[1]]
        half = width // 2
        for p in range(parts):
            rows = slice(p * share, (p + 1) * share)
            for k in range(2):
                mine = slice(k * share, (k + 1) * share)
                depth_out[p, mine, 0:width] = kinds[k][rows]
                depth_out[p, mine, width : width + half] = kinds[2][rows, k * half : (k + 1) * half]
                depth_out[p, mine, width + half :] = kinds[3][rows, 0:LANES]
        local = jnp.sum(energy[...])
        kinds = [split_dot(sums[k], depth_ref[k], 1) for k in range(2)]
        kinds = kinds + [diag_plane_ref[0], diag_plane_ref[1]]
        for k in range(4):
            plane_out[:, k * RANK : (k + 1) * RANK] = kinds[k]
        count = plane_out.shape[0]
        plane_out[count // 2 :, 3 * RANK :] = jnp.full((count // 2, RANK), local, f32)
        leaving(last - 2).wait()
        leaving(last - 1).wait()


def warp(
    cells, image, shift, beyond, across, inside, across_tile, inside_tile, field, plane, depth_factors, diag_depth,
    diag_plane, parts
):
    depth, rows, width = cells.shape
    nodes = plane.shape[1]
    tiles = width // LANES
    count = depth // KNOT
    ahead = lambda i: (jnp.minimum(i, count - 1), 0, 0)
    flat = lambda i: (0, 0)
    whole = lambda i: (0, 0, 0)
    return pl.pallas_call(
        warp_kernel,
        grid=(count + 1,),
        in_specs=[
            pl.BlockSpec((KNOT, rows, width), ahead),
            pl.BlockSpec(memory_space=pl.ANY),
            pl.BlockSpec(memory_space=pl.ANY),
            pl.BlockSpec((KNOT, rows, LANES), ahead),
            pl.BlockSpec((KNOT, across.shape[1]), lambda i: (jnp.minimum(i, count - 1), 0)),
            pl.BlockSpec((KNOT, inside.shape[1]), lambda i: (jnp.minimum(i, count - 1), 0)),
            pl.BlockSpec((KNOT, LANES), lambda i: (jnp.minimum(i, count - 1), 0)),
            pl.BlockSpec((KNOT, LANES), lambda i: (jnp.minimum(i, count - 1), 0)),
            pl.BlockSpec(field.shape, lambda i: (0, 0, 0, 0)),
            pl.BlockSpec(plane.shape, whole),
            pl.BlockSpec(depth_factors.shape, whole),
            pl.BlockSpec(diag_depth.shape, whole),
            pl.BlockSpec(diag_plane.shape, whole),
        ],
        out_specs=[
            pl.BlockSpec(memory_space=pl.ANY),
            pl.BlockSpec((parts, 2 * RANK // parts, width + width // 2 + LANES), whole),
            pl.BlockSpec((nodes, 4 * RANK), flat),
        ],
        out_shape=[
            jax.ShapeDtypeStruct(cells.shape, bf16),
            jax.ShapeDtypeStruct((parts, 2 * RANK // parts, width + width // 2 + LANES), f32),
            jax.ShapeDtypeStruct((nodes, 4 * RANK), f32),
        ],
        scratch_shapes=[
            *[pltpu.VMEM((3 * KNOT * tiles * (rows + 2 * TOP), LANES), f32)] * 3,
            pltpu.VMEM((KNOT * (rows + 2 * TOP), width + LANES), bf16),
            pltpu.VMEM((2, 3 * LANES, 2 * LANES), bf16),
            pltpu.VMEM((2, tiles, nodes, LANES), f32),
            pltpu.VMEM((8, LANES), f32),
            pltpu.VMEM((KNOT, 8, LANES), f32),
            pltpu.VMEM((2, KNOT, rows, width), bf16),
            pltpu.VMEM((2, 3, KNOT, rows, width), bf16),
            pltpu.VMEM((2, KNOT, rows, width), bf16),
            pltpu.SemaphoreType.DMA((2, 4)),
            pltpu.SemaphoreType.DMA((2,)),
        ],
        compiler_params=pltpu.CompilerParams(dimension_semantics=("arbitrary",), vmem_limit_bytes=53000000),
        cost_estimate=pl.CostEstimate(flops=60 * cells.size, bytes_accessed=12 * cells.size, transcendentals=0),
        name="warp",
    )(cells, image, shift, beyond, across, inside, across_tile, inside_tile, field, plane, depth_factors, diag_depth, diag_plane)


def gather_kernel(depth_ref, *refs):
    depth_out, plane_out = refs[-2:]
    total = jnp.sum(depth_ref[...], axis=0)
    found = [ref[...] for ref in refs[:-2]]
    while len(found) > 1:
        half = len(found) // 2
        found = [found[k] + found[k + half] for k in range(half)]
    planes = found[0]
    plane_out[...] = planes
    cells = planes.shape[0]
    share, width = total.shape[0] // 2, total.shape[1]
    row = lax.broadcasted_iota(jnp.int32, total.shape, 0)
    lane = lax.broadcasted_iota(jnp.int32, total.shape, 1)
    partial = planes[cells - 1, 4 * RANK - 1]
    total = jnp.where((row >= share) & (lane >= width - LANES), partial, total)
    for p in range(depth_out.shape[0]):
        depth_out[p] = total


def step_kernel(full_z, node_count, depth_ref, plane_ref, depth_out, plane_out):
    parts, share, width = depth_ref.shape[0], depth_ref.shape[1] // 2, depth_out.shape[2]
    half = width // 2
    energy = depth_ref[0, share, width + half]
    for p in range(1, parts):
        energy = energy + depth_ref[p, share, width + half]
    lam_depth = damping * energy / full_z
    lam_plane = damping * RANK * energy / node_count
    for p in range(parts):
        got = depth_ref[p]
        rows = slice(p * share, (p + 1) * share)
        first, second = got[0:share], got[share:]
        squared = jnp.concatenate([first[:, width : width + half], second[:, width : width + half]], axis=1)
        levels = jnp.concatenate([first[:, width + half :]] * (width // LANES), axis=1)
        depth_out[0, rows, :] = first[:, 0:width] / (squared + lam_depth + epsilon)
        depth_out[1, rows, :] = second[:, 0:width] / (levels + lam_depth + epsilon)
    planes = plane_ref[...]
    plane_out[0] = planes[:, 0:RANK] / (planes[:, 2 * RANK : 3 * RANK] + lam_plane + epsilon)
    plane_out[1] = planes[:, RANK : 2 * RANK] / (planes[0:1, 3 * RANK :] + lam_plane + epsilon)


def local(image, deformed, displacement, plane_factors, depth_factors):
    n_gy, n_gz = lax.axis_size("gy"), lax.axis_size("gz")
    nodes_x, nodes_y = plane_factors.shape[2:]
    plane = jnp.transpose(plane_factors, (0, 2, 3, 1)).reshape(2, nodes_x * nodes_y, RANK)
    inner, outer = end_columns(deformed)
    inner = swapped(inner, "gz", 0)
    outer = swapped(outer, "gz", 1)
    across, inside = ends(deformed)
    inside = swapped(inside, "gy", 0)
    across = swapped(across, "gy", 1)
    across_tile, inside_tile = corners(inner, outer, deformed.shape[0])
    sums = squares(image, across_tile)
    inside_tile = swapped(inside_tile, "gy", 0)
    across_tile = swapped(across_tile, "gy", 1)
    field, diag_depth, diag_plane, beyond = terms(sums, plane, depth_factors, inner, outer, deformed.shape[0])
    residual, depth_terms, plane_terms = warp(
        deformed, image, displacement, beyond, across, inside, across_tile, inside_tile, field, plane, depth_factors,
        diag_depth, diag_plane, n_gy,
    )
    depth_terms = lax.all_to_all(depth_terms, "gy", 0, 0)
    others = [
        lax.ppermute(plane_terms, "gz", [(i, i ^ hop) for i in range(n_gz)]) for hop in range(1, n_gz)
    ]
    depth_terms, plane_terms = pl.pallas_call(
        gather_kernel,
        out_shape=[
            jax.ShapeDtypeStruct(depth_terms.shape, f32),
            jax.ShapeDtypeStruct(plane_terms.shape, f32),
        ],
        compiler_params=plain_params(),
        name="gather",
    )(depth_terms, plane_terms, *others)
    depth_terms = lax.all_to_all(depth_terms, "gy", 0, 0)
    width = depth_factors.shape[2]
    step_depth, step_plane = pl.pallas_call(
        functools.partial(step_kernel, width * n_gz, nodes_x * nodes_y * n_gy),
        out_shape=[
            jax.ShapeDtypeStruct(depth_factors.shape, f32),
            jax.ShapeDtypeStruct(plane.shape, f32),
        ],
        compiler_params=plain_params(),
        name="steps",
    )(depth_terms, plane_terms)
    step_plane = jnp.transpose(step_plane.reshape(2, nodes_x, nodes_y, RANK), (0, 3, 1, 2))
    return residual, step_plane, step_depth


def solution(mesh):
    placed = (
        P(None, "gy", "gz"),
        P(None, "gy", "gz"),
        P(None, None, "gy", "gz"),
        P(None, None, None, "gy"),
        P(None, None, "gz"),
    )
    return jax.shard_map(
        local,
        mesh=mesh,
        in_specs=placed,
        out_specs=(P(None, "gy", "gz"), P(None, None, None, "gy"), P(None, None, "gz")),
        check_vma=False,
    )
```

```python
import functools

import jax
import jax.numpy as jnp
from jax import lax
from jax.experimental import pallas as pl
from jax.experimental.pallas import tpu as pltpu
from jax.sharding import PartitionSpec as P

RANK = 32
KNOT = 8
LANES = 128
TOP = 8

epsilon = 1e-06
damping = 0.01
highest = lax.Precision.HIGHEST
f32 = jnp.float32
bf16 = jnp.bfloat16


def dot(left, right, dims):
    return lax.dot_general(left, right, ((dims[0], dims[1]), ((), ())), precision=highest, preferred_element_type=f32)


def split_dot(left, right, dim):
    left_high, right_high = left.astype(bf16), right.astype(bf16)
    left_low = (left - left_high.astype(f32)).astype(bf16)
    right_low = (right - right_high.astype(f32)).astype(bf16)
    left = jnp.concatenate([left_high, left_high, left_low], axis=dim)
    right = jnp.concatenate([right_high, right_low, right_high], axis=dim)
    return lax.dot_general(left, right, (((dim,), (dim,)), ((), ())), preferred_element_type=f32)


def joined(ref):
    return jnp.concatenate([ref[tile] for tile in range(ref.shape[0])], axis=1)


def plain_params():
    return pltpu.CompilerParams(vmem_limit_bytes=32000000)


def ends_kernel(cells_hbm, inner_ref, outer_ref, across_ref, inside_ref, cells, got):
    depth, rows, width = cells.shape
    chunks = got.shape[0]
    planes = depth // chunks

    def fetched(n):
        part = pl.ds(n * planes, planes)
        return pltpu.make_async_copy(cells_hbm.at[part], cells.at[part], got.at[n])

    for n in range(chunks):
        fetched(n).start()
    odd_y, odd_z = lax.axis_index("gy") % 2 == 1, lax.axis_index("gz") % 2 == 1
    lane = lax.broadcasted_iota(jnp.int32, (rows, LANES), 1)
    first = jnp.zeros((rows, LANES), f32)
    last = jnp.zeros((rows, LANES), f32)
    for n in range(chunks):
        fetched(n).wait()
        for x in range(n * planes, (n + 1) * planes):
            near = cells[x, :, 0:LANES].astype(f32)
            far = cells[x, :, width - LANES : width].astype(f32)
            first = jnp.where(lane == x, pltpu.roll(near, x, 1), first)
            last = jnp.where(lane == x, pltpu.roll(far, (x + 1) % LANES, 1), last)
        if (n + 1) * planes % 16 == 0:
            x = (n + 1) * planes - 16
            low = [cells[x + k, 0:16, :].astype(f32)[0:1] for k in range(16)]
            high = [cells[x + k, rows - 16 : rows, :].astype(f32)[15:16] for k in range(16)]
            low, high = jnp.concatenate(low, axis=0), jnp.concatenate(high, axis=0)
            across_ref[x : x + 16, :] = jnp.where(odd_y, high, low).astype(bf16)
            inside_ref[x : x + 16, :] = jnp.where(odd_y, low, high).astype(bf16)
    inner_ref[...] = jnp.where(odd_z, first, last).astype(bf16)
    outer_ref[...] = jnp.where(odd_z, last, first).astype(bf16)


def ends(cells):
    depth, rows, width = cells.shape
    return pl.pallas_call(
        ends_kernel,
        in_specs=[pl.BlockSpec(memory_space=pl.ANY)],
        out_shape=[jax.ShapeDtypeStruct((rows, LANES), bf16)] * 2 + [jax.ShapeDtypeStruct((depth, width), bf16)] * 2,
        scratch_shapes=[pltpu.VMEM(cells.shape, bf16), pltpu.SemaphoreType.DMA((depth // KNOT,))],
        compiler_params=pltpu.CompilerParams(vmem_limit_bytes=61000000),
        cost_estimate=pl.CostEstimate(flops=cells.size, bytes_accessed=2 * cells.size, transcendentals=0),
        name="ends",
    )(cells)


def z_sides(inner_ref, outer_ref):
    odd = lax.axis_index("gz") % 2 == 1
    inner, outer = inner_ref[...].astype(f32), outer_ref[...].astype(f32)
    return jnp.where(odd, inner, outer), jnp.where(odd, outer, inner)


def corners_kernel(inner_ref, outer_ref, across_out, inside_out):
    rows, depth = inner_ref.shape[0], across_out.shape[0]
    odd = lax.axis_index("gy") % 2 == 1
    lane = lax.broadcasted_iota(jnp.int32, (depth, LANES), 1)
    pad = jnp.zeros((LANES - rows, LANES), f32)
    left, right = z_sides(inner_ref, outer_ref)
    left = jnp.transpose(jnp.concatenate([left, pad], axis=0))[0:depth]
    right = jnp.transpose(jnp.concatenate([right, pad], axis=0))[0:depth]
    low, high = (
        jnp.where(lane == 0, pltpu.roll(right, (LANES - row) % LANES, 1), pltpu.roll(left, LANES - 1 - row, 1))
        for row in (0, rows - 1)
    )
    across_out[...] = jnp.where(odd, high, low).astype(bf16)
    inside_out[...] = jnp.where(odd, low, high).astype(bf16)


def corners(inner, outer, depth):
    return pl.pallas_call(
        corners_kernel,
        out_shape=[jax.ShapeDtypeStruct((depth, LANES), bf16)] * 2,
        compiler_params=plain_params(),
        cost_estimate=pl.CostEstimate(flops=1 << 34, bytes_accessed=1 << 17, transcendentals=0),
        name="corners",
    )(inner, outer)


def swapped(part, axis, start):
    count = lax.axis_size(axis)
    pairs = [(i, i + 1) for i in range(start, count - 1, 2)]
    return lax.ppermute(part, axis, pairs + [(j, i) for i, j in pairs])


def squares_kernel(image_ref, later_ref, sums):
    depth, rows, width = image_ref.shape
    tiles = width // LANES

    def one(t, carry):
        block, tile = t // tiles, t % tiles
        at = pl.multiple_of(tile * LANES, LANES)
        for pair in range(rows // 16):
            total = jnp.zeros((16, LANES), f32)
            for k in range(KNOT):
                values = image_ref[block * KNOT + k, 16 * pair : 16 * pair + 16, pl.ds(at, LANES)].astype(f32)
                total = total + values * values
            for half in range(2):
                row = block * (rows // KNOT) + 2 * pair + half
                sums[tile, pl.ds(row, 1), :] = jnp.sum(total[8 * half : 8 * half + 8], axis=0, keepdims=True)
        return carry

    lax.fori_loop(0, depth // KNOT * tiles, one, 0)


def squares(image, later):
    depth, rows, width = image.shape
    return pl.pallas_call(
        squares_kernel,
        out_shape=jax.ShapeDtypeStruct((width // LANES, depth * rows // KNOT**2, LANES), f32),
        compiler_params=plain_params(),
        cost_estimate=pl.CostEstimate(flops=3 * image.size, bytes_accessed=2 * image.size, transcendentals=0),
        name="squares",
    )(image, later)


def terms_kernel(
    sums, plane_ref, depth_ref, inner_ref, outer_ref, field_ref, diag_depth_ref, diag_plane_ref, beyond_ref
):
    tiles = sums.shape[0]
    left, right = z_sides(inner_ref, outer_ref)
    lane = lax.broadcasted_iota(jnp.int32, left.shape, 1)
    for x in range(beyond_ref.shape[0]):
        after = pltpu.roll(right, (LANES - x) % LANES, 1)
        before = pltpu.roll(left, LANES - 1 - x, 1)
        beyond_ref[x] = jnp.where(lane == 0, after, before).astype(bf16)
    for k in range(2):
        field = dot(plane_ref[k], depth_ref[k], ((1,), (0,)))
        for tile in range(tiles):
            field_ref[k, tile] = field[:, tile * LANES : (tile + 1) * LANES]
    squared = joined(sums)
    cells = jnp.full(squared.shape, float(KNOT * KNOT), f32)
    first, second = plane_ref[0], plane_ref[1]
    diag_depth_ref[0] = dot(first * first, squared, ((0,), (0,)))
    diag_depth_ref[1] = dot(second * second, cells, ((0,), (0,)))
    first, second = depth_ref[0], depth_ref[1]
    diag_plane_ref[0] = dot(squared, first * first, ((1,), (1,)))
    diag_plane_ref[1] = dot(cells, second * second, ((1,), (1,)))


def terms(sums, plane, depth_factors, inner, outer, depth):
    nodes, width = plane.shape[1], depth_factors.shape[2]
    return pl.pallas_call(
        terms_kernel,
        out_shape=[
            jax.ShapeDtypeStruct((2, width // LANES, nodes, LANES), f32),
            jax.ShapeDtypeStruct((2, RANK, width), f32),
            jax.ShapeDtypeStruct((2, nodes, RANK), f32),
            jax.ShapeDtypeStruct((depth,) + inner.shape, bf16),
        ],
        compiler_params=plain_params(),
        cost_estimate=pl.CostEstimate(flops=40 * nodes * RANK * width, bytes_accessed=1 << 20, transcendentals=0),
        name="terms",
    )(sums, plane, depth_factors, inner, outer)


def warp_kernel(
    cells_ref, image_hbm, shift_hbm, beyond_ref, across_ref, inside_ref,
    across_tile_ref, inside_tile_ref, field, plane_ref, depth_ref,
    diag_depth_ref, diag_plane_ref,
    residual_hbm, depth_out, plane_out,
    ahead_ref, here_ref, behind_ref, wide, bands, blocks, energy, held,
    image_ref, shift_ref, residual_ref, got, sent,
):
    step = pl.program_id(0)
    last = pl.num_programs(0) - 1
    planes, rows, width = cells_ref.shape
    nodes = rows // KNOT
    tiles = width // LANES
    window = (ahead_ref, here_ref, behind_ref)
    pitch = rows + 2 * TOP
    plane_rows = tiles * pitch
    block_rows = planes * plane_rows

    @pl.when(step == 0)
    def _():
        row = lax.broadcasted_iota(jnp.int32, bands.shape[1:], 0)
        column = lax.broadcasted_iota(jnp.int32, bands.shape[1:], 1)
        one, none = jnp.ones(bands.shape[1:], f32), jnp.zeros(bands.shape[1:], f32)
        up, down = jnp.where(row == column + 1, one, none), jnp.where(row == column, one, none)
        bands[0] = (up - down).astype(bf16)
        up = jnp.where(row == column + LANES, one, none)
        down = jnp.where(row == column + LANES - 1, one, none)
        bands[1] = (up - down).astype(bf16)
        energy[...] = jnp.zeros_like(energy)
        for c in range(3):
            window[c][3 * block_rows - plane_rows : 3 * block_rows, :] = jnp.zeros((plane_rows, LANES), f32)

    def fetched(n):
        slot, part = n % 2, pl.ds(n * planes, planes)
        copies = [
            pltpu.make_async_copy(shift_hbm.at[axis, part], shift_ref.at[slot, axis], got.at[slot, axis])
            for axis in range(3)
        ]
        return copies + [pltpu.make_async_copy(image_hbm.at[part], image_ref.at[slot], got.at[slot, 3])]

    def leaving(n):
        slot, part = n % 2, pl.ds(n * planes, planes)
        return pltpu.make_async_copy(residual_ref.at[slot], residual_hbm.at[part], sent.at[slot])

    @pl.when(step < last)
    def _():
        for copy in fetched(step):
            copy.start()

    @pl.when(step < last)
    def _():
        slot = (step % 3) * block_rows
        odd = lax.axis_index("gy") % 2 == 1
        across, inside = (
            jnp.concatenate([row[...].astype(f32), tile[...].astype(f32)], axis=1)
            for row, tile in ((across_ref, across_tile_ref), (inside_ref, inside_tile_ref))
        )
        low, high = jnp.where(odd, inside, across), jnp.where(odd, across, inside)
        at = lax.broadcasted_iota(jnp.int32, (2 * TOP, width + LANES), 0)
        for k in range(planes):
            first = k * pitch
            wide[first : first + rows, 0:width] = cells_ref[k]
            wide[first : first + rows, width:] = beyond_ref[k]
            rim = jnp.where(at == TOP, high[k : k + 1], jnp.where(at == TOP - 1, low[k : k + 1], 0.0))
            wide[first + rows : first + pitch, :] = rim.astype(bf16)

        def put(c, tile, values):
            for k in range(planes):
                first = pl.multiple_of(slot + k * plane_rows + tile * pitch, 8)
                mine = values[k * pitch : (k + 1) * pitch]
                window[c][pl.ds(first + TOP, rows), :] = mine[0:rows]
                window[c][pl.ds(first, TOP), :] = mine[rows : rows + TOP]
                window[c][pl.ds(first + TOP + rows, TOP), :] = mine[rows + TOP :]

        pieces = width // (2 * LANES)
        for piece in range(pieces):
            start = 2 * LANES * piece
            after = wide[:, start : start + 3 * LANES]
            if piece == 0:
                before = jnp.concatenate([wide[:, width:], wide[:, 0 : 2 * LANES]], axis=1)
            else:
                before = wide[:, start - LANES : start + 2 * LANES]
            ahead = jnp.dot(after, bands[0], preferred_element_type=f32)
            behind = jnp.dot(before, bands[1], preferred_element_type=f32)
            for half in range(2):
                mine = slice(half * LANES, (half + 1) * LANES)
                put(0, 2 * piece + half, ahead[:, mine])
                put(1, 2 * piece + half, wide[:, start + half * LANES : start + (half + 1) * LANES].astype(f32))
                put(2, 2 * piece + half, behind[:, mine])

    @pl.when(step == last)
    def _():
        first = pl.multiple_of((step % 3) * block_rows, 8)
        for c in range(3):
            window[c][pl.ds(first, plane_rows), :] = jnp.zeros((plane_rows, LANES), f32)

    @pl.when(step > 0)
    def _():
        block = step - 1
        here_slot = block % 2
        for copy in fetched(block):
            copy.wait()

        @pl.when(block > 1)
        def _():
            leaving(block - 2).wait()

        mid = (step + 2) % 3
        first_rows = (
            jnp.where(mid == 0, 3, mid) * block_rows - plane_rows,
            mid * block_rows,
            jnp.where(mid == 2, 0, mid + 1) * block_rows,
        )

        def one(t, total):
            tile = t % tiles
            pair = t // tiles
            at = pl.multiple_of(tile * LANES, LANES)
            top = pl.multiple_of(pair * 16, 16)
            origins = [first + tile * pitch + top + TOP for first in first_rows]
            for half in range(2):
                node = (step - 1) * nodes + pair * 2 + half
                mine = slice(8 * half, 8 * half + 8)

                def taps(x):
                    part = 0 if x == 0 else 2 if x == planes + 1 else 1
                    plus = (x - 1) * plane_rows + 8 * half if part == 1 else 8 * half
                    return [
                        [window[c][pl.ds(origins[part] + (plus + b), 8), :] for c in range(3)] for b in (-1, 0, 1)
                    ]

                contrast = jnp.broadcast_to(field[0, tile, pl.ds(node, 1), :], (8, LANES))
                brightness = jnp.broadcast_to(field[1, tile, pl.ds(node, 1), :], (8, LANES))
                by_image = jnp.zeros((8, LANES), f32)
                plain = jnp.zeros((8, LANES), f32)
                before, here = taps(0), taps(1)
                for k in range(planes):
                    after = taps(k + 2)
                    place = (k, pl.ds(top, 16), pl.ds(at, LANES))
                    sx, sy, sz = (shift_ref[(here_slot, axis) + place].astype(f32)[mine] for axis in range(3))
                    image = image_ref[(here_slot,) + place].astype(f32)[mine]
                    px, py, pz = sx > 0, sy > 0, sz > 0
                    ax, ay = jnp.abs(sx), jnp.abs(sy)

                    def sides(c):
                        far = [jnp.where(px, after[b][c], before[b][c]) for b in range(3)]
                        near = [here[b][c] for b in range(3)]
                        return [(v[1], jnp.where(py, v[2], v[0])) for v in (near, far)]

                    ahead, middle, behind = sides(0), sides(1), sides(2)
                    lines = []
                    for b in range(2):
                        near, far = (middle[v][b] + sz * jnp.where(pz, ahead[v][b], behind[v][b]) for v in range(2))
                        lines.append(near + ax * (far - near))
                    warped = lines[0] + ay * (lines[1] - lines[0])
                    misfit = warped - contrast * image - brightness
                    if half == 0:
                        held[k] = misfit
                    else:
                        residual_ref[(here_slot,) + place] = jnp.concatenate([held[k], misfit], axis=0).astype(bf16)
                    by_image = by_image + misfit * image
                    plain = plain + misfit
                    total = total + misfit * misfit
                    before, here = here, after
                for k, value in ((0, by_image), (1, plain)):
                    blocks[k, tile, pl.ds(node, 1), :] = jnp.sum(value, axis=0, keepdims=True)
            return total

        energy[...] = lax.fori_loop(0, (rows // 16) * tiles, one, energy[...])
        leaving(block).start()

    @pl.when(step == last)
    def _():
        parts = depth_out.shape[0]
        share = RANK // parts
        sums = [joined(blocks.at[k]) for k in range(2)]
        kinds = [split_dot(plane_ref[k], sums[k], 0) for k in range(2)]
        kinds = kinds + [diag_depth_ref[0], diag_depth_ref[1]]
        half = width // 2
        for p in range(parts):
            rows = slice(p * share, (p + 1) * share)
            for k in range(2):
                mine = slice(k * share, (k + 1) * share)
                depth_out[p, mine, 0:width] = kinds[k][rows]
                depth_out[p, mine, width : width + half] = kinds[2][rows, k * half : (k + 1) * half]
                depth_out[p, mine, width + half :] = kinds[3][rows, 0:LANES]
        local = jnp.sum(energy[...])
        kinds = [split_dot(sums[k], depth_ref[k], 1) for k in range(2)]
        kinds = kinds + [diag_plane_ref[0], diag_plane_ref[1]]
        for k in range(4):
            plane_out[:, k * RANK : (k + 1) * RANK] = kinds[k]
        count = plane_out.shape[0]
        plane_out[count // 2 :, 3 * RANK :] = jnp.full((count // 2, RANK), local, f32)
        leaving(last - 2).wait()
        leaving(last - 1).wait()


def warp(
    cells, image, shift, beyond, across, inside, across_tile, inside_tile, field, plane, depth_factors, diag_depth,
    diag_plane, parts
):
    depth, rows, width = cells.shape
    nodes = plane.shape[1]
    tiles = width // LANES
    count = depth // KNOT
    ahead = lambda i: (jnp.minimum(i, count - 1), 0, 0)
    flat = lambda i: (0, 0)
    whole = lambda i: (0, 0, 0)
    return pl.pallas_call(
        warp_kernel,
        grid=(count + 1,),
        in_specs=[
            pl.BlockSpec((KNOT, rows, width), ahead),
            pl.BlockSpec(memory_space=pl.ANY),
            pl.BlockSpec(memory_space=pl.ANY),
            pl.BlockSpec((KNOT, rows, LANES), ahead),
            pl.BlockSpec((KNOT, across.shape[1]), lambda i: (jnp.minimum(i, count - 1), 0)),
            pl.BlockSpec((KNOT, inside.shape[1]), lambda i: (jnp.minimum(i, count - 1), 0)),
            pl.BlockSpec((KNOT, LANES), lambda i: (jnp.minimum(i, count - 1), 0)),
            pl.BlockSpec((KNOT, LANES), lambda i: (jnp.minimum(i, count - 1), 0)),
            pl.BlockSpec(field.shape, lambda i: (0, 0, 0, 0)),
            pl.BlockSpec(plane.shape, whole),
            pl.BlockSpec(depth_factors.shape, whole),
            pl.BlockSpec(diag_depth.shape, whole),
            pl.BlockSpec(diag_plane.shape, whole),
        ],
        out_specs=[
            pl.BlockSpec(memory_space=pl.ANY),
            pl.BlockSpec((parts, 2 * RANK // parts, width + width // 2 + LANES), whole),
            pl.BlockSpec((nodes, 4 * RANK), flat),
        ],
        out_shape=[
            jax.ShapeDtypeStruct(cells.shape, bf16),
            jax.ShapeDtypeStruct((parts, 2 * RANK // parts, width + width // 2 + LANES), f32),
            jax.ShapeDtypeStruct((nodes, 4 * RANK), f32),
        ],
        scratch_shapes=[
            *[pltpu.VMEM((3 * KNOT * tiles * (rows + 2 * TOP), LANES), f32)] * 3,
            pltpu.VMEM((KNOT * (rows + 2 * TOP), width + LANES), bf16),
            pltpu.VMEM((2, 3 * LANES, 2 * LANES), bf16),
            pltpu.VMEM((2, tiles, nodes, LANES), f32),
            pltpu.VMEM((8, LANES), f32),
            pltpu.VMEM((KNOT, 8, LANES), f32),
            pltpu.VMEM((2, KNOT, rows, width), bf16),
            pltpu.VMEM((2, 3, KNOT, rows, width), bf16),
            pltpu.VMEM((2, KNOT, rows, width), bf16),
            pltpu.SemaphoreType.DMA((2, 4)),
            pltpu.SemaphoreType.DMA((2,)),
        ],
        compiler_params=pltpu.CompilerParams(dimension_semantics=("arbitrary",), vmem_limit_bytes=53000000),
        cost_estimate=pl.CostEstimate(flops=60 * cells.size, bytes_accessed=12 * cells.size, transcendentals=0),
        name="warp",
    )(cells, image, shift, beyond, across, inside, across_tile, inside_tile, field, plane, depth_factors, diag_depth, diag_plane)


def gather_kernel(depth_ref, *refs):
    depth_out, plane_out = refs[-2:]
    total = jnp.sum(depth_ref[...], axis=0)
    found = [ref[...] for ref in refs[:-2]]
    while len(found) > 1:
        half = len(found) // 2
        found = [found[k] + found[k + half] for k in range(half)]
    planes = found[0]
    plane_out[...] = planes
    cells = planes.shape[0]
    share, width = total.shape[0] // 2, total.shape[1]
    row = lax.broadcasted_iota(jnp.int32, total.shape, 0)
    lane = lax.broadcasted_iota(jnp.int32, total.shape, 1)
    partial = planes[cells - 1, 4 * RANK - 1]
    total = jnp.where((row >= share) & (lane >= width - LANES), partial, total)
    for p in range(depth_out.shape[0]):
        depth_out[p] = total


def step_kernel(full_z, node_count, depth_ref, plane_ref, depth_out, plane_out):
    parts, share, width = depth_ref.shape[0], depth_ref.shape[1] // 2, depth_out.shape[2]
    half = width // 2
    energy = depth_ref[0, share, width + half]
    for p in range(1, parts):
        energy = energy + depth_ref[p, share, width + half]
    lam_depth = damping * energy / full_z
    lam_plane = damping * RANK * energy / node_count
    for p in range(parts):
        got = depth_ref[p]
        rows = slice(p * share, (p + 1) * share)
        first, second = got[0:share], got[share:]
        squared = jnp.concatenate([first[:, width : width + half], second[:, width : width + half]], axis=1)
        levels = jnp.concatenate([first[:, width + half :]] * (width // LANES), axis=1)
        depth_out[0, rows, :] = first[:, 0:width] / (squared + lam_depth + epsilon)
        depth_out[1, rows, :] = second[:, 0:width] / (levels + lam_depth + epsilon)
    planes = plane_ref[...]
    plane_out[0] = planes[:, 0:RANK] / (planes[:, 2 * RANK : 3 * RANK] + lam_plane + epsilon)
    plane_out[1] = planes[:, RANK : 2 * RANK] / (planes[0:1, 3 * RANK :] + lam_plane + epsilon)


def local(image, deformed, displacement, plane_factors, depth_factors):
    n_gy, n_gz = lax.axis_size("gy"), lax.axis_size("gz")
    nodes_x, nodes_y = plane_factors.shape[2:]
    plane = jnp.transpose(plane_factors, (0, 2, 3, 1)).reshape(2, nodes_x * nodes_y, RANK)
    inner, outer, across, inside = ends(deformed)
    inner = swapped(inner, "gz", 0)
    outer = swapped(outer, "gz", 1)
    inside = swapped(inside, "gy", 0)
    across = swapped(across, "gy", 1)
    across_tile, inside_tile = corners(inner, outer, deformed.shape[0])
    sums = squares(image, across_tile)
    inside_tile = swapped(inside_tile, "gy", 0)
    across_tile = swapped(across_tile, "gy", 1)
    field, diag_depth, diag_plane, beyond = terms(sums, plane, depth_factors, inner, outer, deformed.shape[0])
    residual, depth_terms, plane_terms = warp(
        deformed, image, displacement, beyond, across, inside, across_tile, inside_tile, field, plane, depth_factors,
        diag_depth, diag_plane, n_gy,
    )
    depth_terms = lax.all_to_all(depth_terms, "gy", 0, 0)
    others = [
        lax.ppermute(plane_terms, "gz", [(i, i ^ hop) for i in range(n_gz)]) for hop in range(1, n_gz)
    ]
    depth_terms, plane_terms = pl.pallas_call(
        gather_kernel,
        out_shape=[
            jax.ShapeDtypeStruct(depth_terms.shape, f32),
            jax.ShapeDtypeStruct(plane_terms.shape, f32),
        ],
        compiler_params=plain_params(),
        name="gather",
    )(depth_terms, plane_terms, *others)
    depth_terms = lax.all_to_all(depth_terms, "gy", 0, 0)
    width = depth_factors.shape[2]
    step_depth, step_plane = pl.pallas_call(
        functools.partial(step_kernel, width * n_gz, nodes_x * nodes_y * n_gy),
        out_shape=[
            jax.ShapeDtypeStruct(depth_factors.shape, f32),
            jax.ShapeDtypeStruct(plane.shape, f32),
        ],
        compiler_params=plain_params(),
        name="steps",
    )(depth_terms, plane_terms)
    step_plane = jnp.transpose(step_plane.reshape(2, nodes_x, nodes_y, RANK), (0, 3, 1, 2))
    return residual, step_plane, step_depth


def solution(mesh):
    placed = (
        P(None, "gy", "gz"),
        P(None, "gy", "gz"),
        P(None, None, "gy", "gz"),
        P(None, None, None, "gy"),
        P(None, None, "gz"),
    )
    return jax.shard_map(
        local,
        mesh=mesh,
        in_specs=placed,
        out_specs=(P(None, "gy", "gz"), P(None, None, None, "gy"), P(None, None, "gz")),
        check_vma=False,
    )
```

```python
import functools

import jax
import jax.numpy as jnp
from jax import lax
from jax.experimental import pallas as pl
from jax.experimental.pallas import tpu as pltpu
from jax.sharding import PartitionSpec as P

RANK = 32
KNOT = 8
LANES = 128
TOP = 8

epsilon = 1e-06
damping = 0.01
highest = lax.Precision.HIGHEST
f32 = jnp.float32
bf16 = jnp.bfloat16


def dot(left, right, dims):
    return lax.dot_general(left, right, ((dims[0], dims[1]), ((), ())), precision=highest, preferred_element_type=f32)


def split_dot(left, right, dim):
    left_high, right_high = left.astype(bf16), right.astype(bf16)
    left_low = (left - left_high.astype(f32)).astype(bf16)
    right_low = (right - right_high.astype(f32)).astype(bf16)
    left = jnp.concatenate([left_high, left_high, left_low], axis=dim)
    right = jnp.concatenate([right_high, right_low, right_high], axis=dim)
    return lax.dot_general(left, right, (((dim,), (dim,)), ((), ())), preferred_element_type=f32)


def joined(ref):
    return jnp.concatenate([ref[tile] for tile in range(ref.shape[0])], axis=1)


def plain_params():
    return pltpu.CompilerParams(vmem_limit_bytes=32000000)


def ends_kernel(cells_hbm, inner_ref, outer_ref, across_ref, inside_ref, cells, got):
    depth, rows, width = cells.shape
    chunks = got.shape[0]
    planes = depth // chunks

    def fetched(n):
        part = pl.ds(n * planes, planes)
        return pltpu.make_async_copy(cells_hbm.at[part], cells.at[part], got.at[n])

    for n in range(chunks):
        fetched(n).start()
    odd_y, odd_z = lax.axis_index("gy") % 2 == 1, lax.axis_index("gz") % 2 == 1
    lane = lax.broadcasted_iota(jnp.int32, (rows, LANES), 1)
    first = jnp.zeros((rows, LANES), f32)
    last = jnp.zeros((rows, LANES), f32)
    for n in range(chunks):
        fetched(n).wait()
        for x in range(n * planes, (n + 1) * planes):
            near = cells[x, :, 0:LANES].astype(f32)
            far = cells[x, :, width - LANES : width].astype(f32)
            first = jnp.where(lane == x, pltpu.roll(near, x, 1), first)
            last = jnp.where(lane == x, pltpu.roll(far, (x + 1) % LANES, 1), last)
        if (n + 1) * planes % 16 == 0:
            x = (n + 1) * planes - 16
            low = [cells[x + k, 0:16, :].astype(f32)[0:1] for k in range(16)]
            high = [cells[x + k, rows - 16 : rows, :].astype(f32)[15:16] for k in range(16)]
            low, high = jnp.concatenate(low, axis=0), jnp.concatenate(high, axis=0)
            across_ref[x : x + 16, :] = jnp.where(odd_y, high, low).astype(bf16)
            inside_ref[x : x + 16, :] = jnp.where(odd_y, low, high).astype(bf16)
    inner_ref[...] = jnp.where(odd_z, first, last).astype(bf16)
    outer_ref[...] = jnp.where(odd_z, last, first).astype(bf16)


def ends(cells):
    depth, rows, width = cells.shape
    return pl.pallas_call(
        ends_kernel,
        in_specs=[pl.BlockSpec(memory_space=pl.ANY)],
        out_shape=[jax.ShapeDtypeStruct((rows, LANES), bf16)] * 2 + [jax.ShapeDtypeStruct((depth, width), bf16)] * 2,
        scratch_shapes=[pltpu.VMEM(cells.shape, bf16), pltpu.SemaphoreType.DMA((depth // KNOT,))],
        compiler_params=pltpu.CompilerParams(vmem_limit_bytes=61000000),
        cost_estimate=pl.CostEstimate(flops=cells.size, bytes_accessed=2 * cells.size, transcendentals=0),
        name="ends",
    )(cells)


def z_sides(inner_ref, outer_ref):
    odd = lax.axis_index("gz") % 2 == 1
    inner, outer = inner_ref[...].astype(f32), outer_ref[...].astype(f32)
    return jnp.where(odd, inner, outer), jnp.where(odd, outer, inner)


def corners_kernel(inner_ref, outer_ref, across_out, inside_out):
    rows, depth = inner_ref.shape[0], across_out.shape[0]
    odd = lax.axis_index("gy") % 2 == 1
    lane = lax.broadcasted_iota(jnp.int32, (depth, LANES), 1)
    pad = jnp.zeros((LANES - rows, LANES), f32)
    left, right = z_sides(inner_ref, outer_ref)
    left = jnp.transpose(jnp.concatenate([left, pad], axis=0))[0:depth]
    right = jnp.transpose(jnp.concatenate([right, pad], axis=0))[0:depth]
    low, high = (
        jnp.where(lane == 0, pltpu.roll(right, (LANES - row) % LANES, 1), pltpu.roll(left, LANES - 1 - row, 1))
        for row in (0, rows - 1)
    )
    across_out[...] = jnp.where(odd, high, low).astype(bf16)
    inside_out[...] = jnp.where(odd, low, high).astype(bf16)


def corners(inner, outer, depth):
    return pl.pallas_call(
        corners_kernel,
        out_shape=[jax.ShapeDtypeStruct((depth, LANES), bf16)] * 2,
        compiler_params=plain_params(),
        cost_estimate=pl.CostEstimate(flops=1 << 34, bytes_accessed=1 << 17, transcendentals=0),
        name="corners",
    )(inner, outer)


def swapped(part, axis, start):
    count = lax.axis_size(axis)
    pairs = [(i, i + 1) for i in range(start, count - 1, 2)]
    return lax.ppermute(part, axis, pairs + [(j, i) for i, j in pairs])


def squares_kernel(image_ref, later_ref, sums):
    depth, rows, width = image_ref.shape
    tiles = width // LANES

    def one(t, carry):
        block, tile = t // tiles, t % tiles
        at = pl.multiple_of(tile * LANES, LANES)
        for pair in range(rows // 16):
            total = jnp.zeros((16, LANES), f32)
            for k in range(KNOT):
                values = image_ref[block * KNOT + k, 16 * pair : 16 * pair + 16, pl.ds(at, LANES)].astype(f32)
                total = total + values * values
            for half in range(2):
                row = block * (rows // KNOT) + 2 * pair + half
                sums[tile, pl.ds(row, 1), :] = jnp.sum(total[8 * half : 8 * half + 8], axis=0, keepdims=True)
        return carry

    lax.fori_loop(0, depth // KNOT * tiles, one, 0)


def squares(image, later):
    depth, rows, width = image.shape
    return pl.pallas_call(
        squares_kernel,
        out_shape=jax.ShapeDtypeStruct((width // LANES, depth * rows // KNOT**2, LANES), f32),
        compiler_params=plain_params(),
        cost_estimate=pl.CostEstimate(flops=3 * image.size, bytes_accessed=2 * image.size, transcendentals=0),
        name="squares",
    )(image, later)


def terms_kernel(
    sums, plane_ref, depth_ref, inner_ref, outer_ref, field_ref, diag_depth_ref, diag_plane_ref, beyond_ref
):
    tiles = sums.shape[0]
    left, right = z_sides(inner_ref, outer_ref)
    lane = lax.broadcasted_iota(jnp.int32, left.shape, 1)
    for x in range(beyond_ref.shape[0]):
        after = pltpu.roll(right, (LANES - x) % LANES, 1)
        before = pltpu.roll(left, LANES - 1 - x, 1)
        beyond_ref[x] = jnp.where(lane == 0, after, before).astype(bf16)
    for k in range(2):
        field = dot(plane_ref[k], depth_ref[k], ((1,), (0,)))
        for tile in range(tiles):
            field_ref[k, tile] = field[:, tile * LANES : (tile + 1) * LANES]
    squared = joined(sums)
    cells = jnp.full(squared.shape, float(KNOT * KNOT), f32)
    first, second = plane_ref[0], plane_ref[1]
    diag_depth_ref[0] = dot(first * first, squared, ((0,), (0,)))
    diag_depth_ref[1] = dot(second * second, cells, ((0,), (0,)))
    first, second = depth_ref[0], depth_ref[1]
    diag_plane_ref[0] = dot(squared, first * first, ((1,), (1,)))
    diag_plane_ref[1] = dot(cells, second * second, ((1,), (1,)))


def terms(sums, plane, depth_factors, inner, outer, depth):
    nodes, width = plane.shape[1], depth_factors.shape[2]
    return pl.pallas_call(
        terms_kernel,
        out_shape=[
            jax.ShapeDtypeStruct((2, width // LANES, nodes, LANES), f32),
            jax.ShapeDtypeStruct((2, RANK, width), f32),
            jax.ShapeDtypeStruct((2, nodes, RANK), f32),
            jax.ShapeDtypeStruct((depth,) + inner.shape, bf16),
        ],
        compiler_params=plain_params(),
        cost_estimate=pl.CostEstimate(flops=40 * nodes * RANK * width, bytes_accessed=1 << 20, transcendentals=0),
        name="terms",
    )(sums, plane, depth_factors, inner, outer)


def warp_kernel(
    cells_ref, image_hbm, shift_hbm, beyond_ref, across_ref, inside_ref,
    across_tile_ref, inside_tile_ref, field, plane_ref, depth_ref,
    diag_depth_ref, diag_plane_ref,
    residual_hbm, depth_out, plane_out,
    ahead_ref, here_ref, behind_ref, wide, bands, blocks, energy, held,
    image_ref, shift_ref, residual_ref, got, sent,
):
    step = pl.program_id(0)
    last = pl.num_programs(0) - 1
    planes, rows, width = cells_ref.shape
    nodes = rows // KNOT
    tiles = width // LANES
    window = (ahead_ref, here_ref, behind_ref)
    pitch = rows + 2 * TOP
    plane_rows = tiles * pitch
    block_rows = planes * plane_rows

    @pl.when(step == 0)
    def _():
        row = lax.broadcasted_iota(jnp.int32, bands.shape[1:], 0)
        column = lax.broadcasted_iota(jnp.int32, bands.shape[1:], 1)
        one, none = jnp.ones(bands.shape[1:], f32), jnp.zeros(bands.shape[1:], f32)
        up, down = jnp.where(row == column + 1, one, none), jnp.where(row == column, one, none)
        bands[0] = (up - down).astype(bf16)
        up = jnp.where(row == column + LANES, one, none)
        down = jnp.where(row == column + LANES - 1, one, none)
        bands[1] = (up - down).astype(bf16)
        energy[...] = jnp.zeros_like(energy)
        for c in range(3):
            window[c][3 * block_rows - plane_rows : 3 * block_rows, :] = jnp.zeros((plane_rows, LANES), f32)

    def fetched(n):
        slot, part = n % 2, pl.ds(n * planes, planes)
        copies = [
            pltpu.make_async_copy(shift_hbm.at[axis, part], shift_ref.at[slot, axis], got.at[slot, axis])
            for axis in range(3)
        ]
        return copies + [pltpu.make_async_copy(image_hbm.at[part], image_ref.at[slot], got.at[slot, 3])]

    def leaving(n):
        slot, part = n % 2, pl.ds(n * planes, planes)
        return pltpu.make_async_copy(residual_ref.at[slot], residual_hbm.at[part], sent.at[slot])

    @pl.when(step < last)
    def _():
        for copy in fetched(step):
            copy.start()

    @pl.when(step < last)
    def _():
        slot = (step % 3) * block_rows
        odd = lax.axis_index("gy") % 2 == 1
        across, inside = (
            jnp.concatenate([row[...].astype(f32), tile[...].astype(f32)], axis=1)
            for row, tile in ((across_ref, across_tile_ref), (inside_ref, inside_tile_ref))
        )
        low, high = jnp.where(odd, inside, across), jnp.where(odd, across, inside)
        at = lax.broadcasted_iota(jnp.int32, (2 * TOP, width + LANES), 0)
        for k in range(planes):
            first = k * pitch
            wide[first : first + rows, 0:width] = cells_ref[k]
            wide[first : first + rows, width:] = beyond_ref[k]
            rim = jnp.where(at == TOP, high[k : k + 1], jnp.where(at == TOP - 1, low[k : k + 1], 0.0))
            wide[first + rows : first + pitch, :] = rim.astype(bf16)

        def put(c, tile, values):
            for k in range(planes):
                first = pl.multiple_of(slot + k * plane_rows + tile * pitch, 8)
                mine = values[k * pitch : (k + 1) * pitch]
                window[c][pl.ds(first + TOP, rows), :] = mine[0:rows]
                window[c][pl.ds(first, TOP), :] = mine[rows : rows + TOP]
                window[c][pl.ds(first + TOP + rows, TOP), :] = mine[rows + TOP :]

        pieces = width // (2 * LANES)
        for piece in range(pieces):
            start = 2 * LANES * piece
            after = wide[:, start : start + 3 * LANES]
            if piece == 0:
                before = jnp.concatenate([wide[:, width:], wide[:, 0 : 2 * LANES]], axis=1)
            else:
                before = wide[:, start - LANES : start + 2 * LANES]
            ahead = jnp.dot(after, bands[0], preferred_element_type=f32)
            behind = jnp.dot(before, bands[1], preferred_element_type=f32)
            for half in range(2):
                mine = slice(half * LANES, (half + 1) * LANES)
                put(0, 2 * piece + half, ahead[:, mine])
                put(1, 2 * piece + half, wide[:, start + half * LANES : start + (half + 1) * LANES].astype(f32))
                put(2, 2 * piece + half, behind[:, mine])

    @pl.when(step == last)
    def _():
        first = pl.multiple_of((step % 3) * block_rows, 8)
        for c in range(3):
            window[c][pl.ds(first, plane_rows), :] = jnp.zeros((plane_rows, LANES), f32)

    @pl.when(step > 0)
    def _():
        block = step - 1
        here_slot = block % 2
        for copy in fetched(block):
            copy.wait()

        @pl.when(block > 1)
        def _():
            leaving(block - 2).wait()

        mid = (step + 2) % 3
        first_rows = (
            jnp.where(mid == 0, 3, mid) * block_rows - plane_rows,
            mid * block_rows,
            jnp.where(mid == 2, 0, mid + 1) * block_rows,
        )

        def one(t, total):
            tile = t % tiles
            pair = t // tiles
            at = pl.multiple_of(tile * LANES, LANES)
            top = pl.multiple_of(pair * 16, 16)
            origins = [first + tile * pitch + top + TOP for first in first_rows]
            for half in range(2):
                node = (step - 1) * nodes + pair * 2 + half
                mine = slice(8 * half, 8 * half + 8)

                def taps(x):
                    part = 0 if x == 0 else 2 if x == planes + 1 else 1
                    plus = (x - 1) * plane_rows + 8 * half if part == 1 else 8 * half
                    return [
                        [window[c][pl.ds(origins[part] + (plus + b), 8), :] for c in range(3)] for b in (-1, 0, 1)
                    ]

                contrast = jnp.broadcast_to(field[0, tile, pl.ds(node, 1), :], (8, LANES))
                brightness = jnp.broadcast_to(field[1, tile, pl.ds(node, 1), :], (8, LANES))
                by_image = jnp.zeros((8, LANES), f32)
                plain = jnp.zeros((8, LANES), f32)
                here = taps(1)
                for k in range(planes):
                    before, after = taps(k), taps(k + 2)
                    place = (k, pl.ds(top, 16), pl.ds(at, LANES))
                    sx, sy, sz = (shift_ref[(here_slot, axis) + place].astype(f32)[mine] for axis in range(3))
                    image = image_ref[(here_slot,) + place].astype(f32)[mine]
                    px, py, pz = sx > 0, sy > 0, sz > 0
                    ax, ay = jnp.abs(sx), jnp.abs(sy)

                    def sides(c):
                        far = [jnp.where(px, after[b][c], before[b][c]) for b in range(3)]
                        near = [here[b][c] for b in range(3)]
                        return [(v[1], jnp.where(py, v[2], v[0])) for v in (near, far)]

                    ahead, middle, behind = sides(0), sides(1), sides(2)
                    lines = []
                    for b in range(2):
                        near, far = (middle[v][b] + sz * jnp.where(pz, ahead[v][b], behind[v][b]) for v in range(2))
                        lines.append(near + ax * (far - near))
                    warped = lines[0] + ay * (lines[1] - lines[0])
                    misfit = warped - contrast * image - brightness
                    if half == 0:
                        held[k] = misfit
                    else:
                        residual_ref[(here_slot,) + place] = jnp.concatenate([held[k], misfit], axis=0).astype(bf16)
                    by_image = by_image + misfit * image
                    plain = plain + misfit
                    total = total + misfit * misfit
                    here = after
                for k, value in ((0, by_image), (1, plain)):
                    blocks[k, tile, pl.ds(node, 1), :] = jnp.sum(value, axis=0, keepdims=True)
            return total

        energy[...] = lax.fori_loop(0, (rows // 16) * tiles, one, energy[...])
        leaving(block).start()

    @pl.when(step == last)
    def _():
        parts = depth_out.shape[0]
        share = RANK // parts
        sums = [joined(blocks.at[k]) for k in range(2)]
        kinds = [split_dot(plane_ref[k], sums[k], 0) for k in range(2)]
        kinds = kinds + [diag_depth_ref[0], diag_depth_ref[1]]
        half = width // 2
        for p in range(parts):
            rows = slice(p * share, (p + 1) * share)
            for k in range(2):
                mine = slice(k * share, (k + 1) * share)
                depth_out[p, mine, 0:width] = kinds[k][rows]
                depth_out[p, mine, width : width + half] = kinds[2][rows, k * half : (k + 1) * half]
                depth_out[p, mine, width + half :] = kinds[3][rows, 0:LANES]
        local = jnp.sum(energy[...])
        kinds = [split_dot(sums[k], depth_ref[k], 1) for k in range(2)]
        kinds = kinds + [diag_plane_ref[0], diag_plane_ref[1]]
        for k in range(4):
            plane_out[:, k * RANK : (k + 1) * RANK] = kinds[k]
        count = plane_out.shape[0]
        plane_out[count // 2 :, 3 * RANK :] = jnp.full((count // 2, RANK), local, f32)
        leaving(last - 2).wait()
        leaving(last - 1).wait()


def warp(
    cells, image, shift, beyond, across, inside, across_tile, inside_tile, field, plane, depth_factors, diag_depth,
    diag_plane, parts
):
    depth, rows, width = cells.shape
    nodes = plane.shape[1]
    tiles = width // LANES
    count = depth // KNOT
    ahead = lambda i: (jnp.minimum(i, count - 1), 0, 0)
    flat = lambda i: (0, 0)
    whole = lambda i: (0, 0, 0)
    return pl.pallas_call(
        warp_kernel,
        grid=(count + 1,),
        in_specs=[
            pl.BlockSpec((KNOT, rows, width), ahead),
            pl.BlockSpec(memory_space=pl.ANY),
            pl.BlockSpec(memory_space=pl.ANY),
            pl.BlockSpec((KNOT, rows, LANES), ahead),
            pl.BlockSpec((KNOT, across.shape[1]), lambda i: (jnp.minimum(i, count - 1), 0)),
            pl.BlockSpec((KNOT, inside.shape[1]), lambda i: (jnp.minimum(i, count - 1), 0)),
            pl.BlockSpec((KNOT, LANES), lambda i: (jnp.minimum(i, count - 1), 0)),
            pl.BlockSpec((KNOT, LANES), lambda i: (jnp.minimum(i, count - 1), 0)),
            pl.BlockSpec(field.shape, lambda i: (0, 0, 0, 0)),
            pl.BlockSpec(plane.shape, whole),
            pl.BlockSpec(depth_factors.shape, whole),
            pl.BlockSpec(diag_depth.shape, whole),
            pl.BlockSpec(diag_plane.shape, whole),
        ],
        out_specs=[
            pl.BlockSpec(memory_space=pl.ANY),
            pl.BlockSpec((parts, 2 * RANK // parts, width + width // 2 + LANES), whole),
            pl.BlockSpec((nodes, 4 * RANK), flat),
        ],
        out_shape=[
            jax.ShapeDtypeStruct(cells.shape, bf16),
            jax.ShapeDtypeStruct((parts, 2 * RANK // parts, width + width // 2 + LANES), f32),
            jax.ShapeDtypeStruct((nodes, 4 * RANK), f32),
        ],
        scratch_shapes=[
            *[pltpu.VMEM((3 * KNOT * tiles * (rows + 2 * TOP), LANES), f32)] * 3,
            pltpu.VMEM((KNOT * (rows + 2 * TOP), width + LANES), bf16),
            pltpu.VMEM((2, 3 * LANES, 2 * LANES), bf16),
            pltpu.VMEM((2, tiles, nodes, LANES), f32),
            pltpu.VMEM((8, LANES), f32),
            pltpu.VMEM((KNOT, 8, LANES), f32),
            pltpu.VMEM((2, KNOT, rows, width), bf16),
            pltpu.VMEM((2, 3, KNOT, rows, width), bf16),
            pltpu.VMEM((2, KNOT, rows, width), bf16),
            pltpu.SemaphoreType.DMA((2, 4)),
            pltpu.SemaphoreType.DMA((2,)),
        ],
        compiler_params=pltpu.CompilerParams(dimension_semantics=("arbitrary",), vmem_limit_bytes=53000000),
        cost_estimate=pl.CostEstimate(flops=60 * cells.size, bytes_accessed=12 * cells.size, transcendentals=0),
        name="warp",
    )(cells, image, shift, beyond, across, inside, across_tile, inside_tile, field, plane, depth_factors, diag_depth, diag_plane)


def gather_kernel(depth_ref, *refs):
    depth_out, plane_out = refs[-2:]
    total = jnp.sum(depth_ref[...], axis=0)
    found = [ref[...] for ref in refs[:-2]]
    while len(found) > 1:
        half = len(found) // 2
        found = [found[k] + found[k + half] for k in range(half)]
    planes = found[0]
    plane_out[...] = planes
    cells = planes.shape[0]
    share, width = total.shape[0] // 2, total.shape[1]
    row = lax.broadcasted_iota(jnp.int32, total.shape, 0)
    lane = lax.broadcasted_iota(jnp.int32, total.shape, 1)
    partial = planes[cells - 1, 4 * RANK - 1]
    total = jnp.where((row >= share) & (lane >= width - LANES), partial, total)
    for p in range(depth_out.shape[0]):
        depth_out[p] = total


def step_kernel(full_z, node_count, depth_ref, plane_ref, depth_out, plane_out):
    parts, share, width = depth_ref.shape[0], depth_ref.shape[1] // 2, depth_out.shape[2]
    half = width // 2
    energy = depth_ref[0, share, width + half]
    for p in range(1, parts):
        energy = energy + depth_ref[p, share, width + half]
    lam_depth = damping * energy / full_z
    lam_plane = damping * RANK * energy / node_count
    for p in range(parts):
        got = depth_ref[p]
        rows = slice(p * share, (p + 1) * share)
        first, second = got[0:share], got[share:]
        squared = jnp.concatenate([first[:, width : width + half], second[:, width : width + half]], axis=1)
        levels = jnp.concatenate([first[:, width + half :]] * (width // LANES), axis=1)
        depth_out[0, rows, :] = first[:, 0:width] / (squared + lam_depth + epsilon)
        depth_out[1, rows, :] = second[:, 0:width] / (levels + lam_depth + epsilon)
    planes = plane_ref[...]
    plane_out[0] = planes[:, 0:RANK] / (planes[:, 2 * RANK : 3 * RANK] + lam_plane + epsilon)
    plane_out[1] = planes[:, RANK : 2 * RANK] / (planes[0:1, 3 * RANK :] + lam_plane + epsilon)


def local(image, deformed, displacement, plane_factors, depth_factors):
    n_gy, n_gz = lax.axis_size("gy"), lax.axis_size("gz")
    nodes_x, nodes_y = plane_factors.shape[2:]
    plane = jnp.transpose(plane_factors, (0, 2, 3, 1)).reshape(2, nodes_x * nodes_y, RANK)
    inner, outer, across, inside = ends(deformed)
    inner = swapped(inner, "gz", 0)
    outer = swapped(outer, "gz", 1)
    inside = swapped(inside, "gy", 0)
    across = swapped(across, "gy", 1)
    across_tile, inside_tile = corners(inner, outer, deformed.shape[0])
    sums = squares(image, across_tile)
    inside_tile = swapped(inside_tile, "gy", 0)
    across_tile = swapped(across_tile, "gy", 1)
    field, diag_depth, diag_plane, beyond = terms(sums, plane, depth_factors, inner, outer, deformed.shape[0])
    residual, depth_terms, plane_terms = warp(
        deformed, image, displacement, beyond, across, inside, across_tile, inside_tile, field, plane, depth_factors,
        diag_depth, diag_plane, n_gy,
    )
    depth_terms = lax.all_to_all(depth_terms, "gy", 0, 0)
    others = [
        lax.ppermute(plane_terms, "gz", [(i, i ^ hop) for i in range(n_gz)]) for hop in range(1, n_gz)
    ]
    depth_terms, plane_terms = pl.pallas_call(
        gather_kernel,
        out_shape=[
            jax.ShapeDtypeStruct(depth_terms.shape, f32),
            jax.ShapeDtypeStruct(plane_terms.shape, f32),
        ],
        compiler_params=plain_params(),
        name="gather",
    )(depth_terms, plane_terms, *others)
    depth_terms = lax.all_to_all(depth_terms, "gy", 0, 0)
    width = depth_factors.shape[2]
    step_depth, step_plane = pl.pallas_call(
        functools.partial(step_kernel, width * n_gz, nodes_x * nodes_y * n_gy),
        out_shape=[
            jax.ShapeDtypeStruct(depth_factors.shape, f32),
            jax.ShapeDtypeStruct(plane.shape, f32),
        ],
        compiler_params=plain_params(),
        name="steps",
    )(depth_terms, plane_terms)
    step_plane = jnp.transpose(step_plane.reshape(2, nodes_x, nodes_y, RANK), (0, 3, 1, 2))
    return residual, step_plane, step_depth


def solution(mesh):
    placed = (
        P(None, "gy", "gz"),
        P(None, "gy", "gz"),
        P(None, None, "gy", "gz"),
        P(None, None, None, "gy"),
        P(None, None, "gz"),
    )
    return jax.shard_map(
        local,
        mesh=mesh,
        in_specs=placed,
        out_specs=(P(None, "gy", "gz"), P(None, None, None, "gy"), P(None, None, "gz")),
        check_vma=False,
    )
```

```python
import functools

import jax
import jax.numpy as jnp
from jax import lax
from jax.experimental import pallas as pl
from jax.experimental.pallas import tpu as pltpu
from jax.sharding import PartitionSpec as P

RANK = 32
KNOT = 8
LANES = 128
TOP = 8

epsilon = 1e-06
damping = 0.01
highest = lax.Precision.HIGHEST
f32 = jnp.float32
bf16 = jnp.bfloat16


def dot(left, right, dims):
    return lax.dot_general(left, right, ((dims[0], dims[1]), ((), ())), precision=highest, preferred_element_type=f32)


def split_dot(left, right, dim):
    left_high, right_high = left.astype(bf16), right.astype(bf16)
    left_low = (left - left_high.astype(f32)).astype(bf16)
    right_low = (right - right_high.astype(f32)).astype(bf16)
    left = jnp.concatenate([left_high, left_high, left_low], axis=dim)
    right = jnp.concatenate([right_high, right_low, right_high], axis=dim)
    return lax.dot_general(left, right, (((dim,), (dim,)), ((), ())), preferred_element_type=f32)


def joined(ref):
    return jnp.concatenate([ref[tile] for tile in range(ref.shape[0])], axis=1)


def plain_params():
    return pltpu.CompilerParams(vmem_limit_bytes=32000000)


def ends_kernel(cells_hbm, inner_ref, outer_ref, across_ref, inside_ref, cells, got):
    depth, rows, width = cells.shape
    chunks = got.shape[0]
    planes = depth // chunks

    def fetched(n):
        part = pl.ds(n * planes, planes)
        return pltpu.make_async_copy(cells_hbm.at[part], cells.at[part], got.at[n])

    for n in range(chunks):
        fetched(n).start()
    odd_y, odd_z = lax.axis_index("gy") % 2 == 1, lax.axis_index("gz") % 2 == 1
    lane = lax.broadcasted_iota(jnp.int32, (rows, LANES), 1)
    first = jnp.zeros((rows, LANES), f32)
    last = jnp.zeros((rows, LANES), f32)
    for n in range(chunks):
        fetched(n).wait()
        for x in range(n * planes, (n + 1) * planes):
            near = cells[x, :, 0:LANES].astype(f32)
            far = cells[x, :, width - LANES : width].astype(f32)
            first = jnp.where(lane == x, pltpu.roll(near, x, 1), first)
            last = jnp.where(lane == x, pltpu.roll(far, (x + 1) % LANES, 1), last)
        if (n + 1) * planes % 16 == 0:
            x = (n + 1) * planes - 16
            low = [cells[x + k, 0:16, :].astype(f32)[0:1] for k in range(16)]
            high = [cells[x + k, rows - 16 : rows, :].astype(f32)[15:16] for k in range(16)]
            low, high = jnp.concatenate(low, axis=0), jnp.concatenate(high, axis=0)
            across_ref[x : x + 16, :] = jnp.where(odd_y, high, low).astype(bf16)
            inside_ref[x : x + 16, :] = jnp.where(odd_y, low, high).astype(bf16)
    inner_ref[...] = jnp.where(odd_z, first, last).astype(bf16)
    outer_ref[...] = jnp.where(odd_z, last, first).astype(bf16)


def ends(cells):
    depth, rows, width = cells.shape
    return pl.pallas_call(
        ends_kernel,
        in_specs=[pl.BlockSpec(memory_space=pl.ANY)],
        out_shape=[jax.ShapeDtypeStruct((rows, LANES), bf16)] * 2 + [jax.ShapeDtypeStruct((depth, width), bf16)] * 2,
        scratch_shapes=[pltpu.VMEM(cells.shape, bf16), pltpu.SemaphoreType.DMA((depth // KNOT,))],
        compiler_params=pltpu.CompilerParams(vmem_limit_bytes=61000000),
        cost_estimate=pl.CostEstimate(flops=cells.size, bytes_accessed=2 * cells.size, transcendentals=0),
        name="ends",
    )(cells)


def z_sides(inner_ref, outer_ref):
    odd = lax.axis_index("gz") % 2 == 1
    inner, outer = inner_ref[...].astype(f32), outer_ref[...].astype(f32)
    return jnp.where(odd, inner, outer), jnp.where(odd, outer, inner)


def corners_kernel(inner_ref, outer_ref, across_out, inside_out):
    rows, depth = inner_ref.shape[0], across_out.shape[0]
    odd = lax.axis_index("gy") % 2 == 1
    lane = lax.broadcasted_iota(jnp.int32, (depth, LANES), 1)
    pad = jnp.zeros((LANES - rows, LANES), f32)
    left, right = z_sides(inner_ref, outer_ref)
    left = jnp.transpose(jnp.concatenate([left, pad], axis=0))[0:depth]
    right = jnp.transpose(jnp.concatenate([right, pad], axis=0))[0:depth]
    low, high = (
        jnp.where(lane == 0, pltpu.roll(right, (LANES - row) % LANES, 1), pltpu.roll(left, LANES - 1 - row, 1))
        for row in (0, rows - 1)
    )
    across_out[...] = jnp.where(odd, high, low).astype(bf16)
    inside_out[...] = jnp.where(odd, low, high).astype(bf16)


def corners(inner, outer, depth):
    return pl.pallas_call(
        corners_kernel,
        out_shape=[jax.ShapeDtypeStruct((depth, LANES), bf16)] * 2,
        compiler_params=plain_params(),
        cost_estimate=pl.CostEstimate(flops=1 << 34, bytes_accessed=1 << 17, transcendentals=0),
        name="corners",
    )(inner, outer)


def swapped(part, axis, start):
    count = lax.axis_size(axis)
    pairs = [(i, i + 1) for i in range(start, count - 1, 2)]
    return lax.ppermute(part, axis, pairs + [(j, i) for i, j in pairs])


def squares_kernel(image_ref, later_ref, sums):
    depth, rows, width = image_ref.shape
    tiles = width // LANES

    def one(t, carry):
        block, tile = t // tiles, t % tiles
        at = pl.multiple_of(tile * LANES, LANES)
        for pair in range(rows // 16):
            total = jnp.zeros((16, LANES), f32)
            for k in range(KNOT):
                values = image_ref[block * KNOT + k, 16 * pair : 16 * pair + 16, pl.ds(at, LANES)].astype(f32)
                total = total + values * values
            for half in range(2):
                row = block * (rows // KNOT) + 2 * pair + half
                sums[tile, pl.ds(row, 1), :] = jnp.sum(total[8 * half : 8 * half + 8], axis=0, keepdims=True)
        return carry

    lax.fori_loop(0, depth // KNOT * tiles, one, 0)


def squares(image, later):
    depth, rows, width = image.shape
    return pl.pallas_call(
        squares_kernel,
        out_shape=jax.ShapeDtypeStruct((width // LANES, depth * rows // KNOT**2, LANES), f32),
        compiler_params=plain_params(),
        cost_estimate=pl.CostEstimate(flops=3 * image.size, bytes_accessed=2 * image.size, transcendentals=0),
        name="squares",
    )(image, later)


def terms_kernel(
    sums, plane_ref, depth_ref, inner_ref, outer_ref, field_ref, diag_depth_ref, diag_plane_ref, beyond_ref
):
    tiles = sums.shape[0]
    left, right = z_sides(inner_ref, outer_ref)
    lane = lax.broadcasted_iota(jnp.int32, left.shape, 1)
    for x in range(beyond_ref.shape[0]):
        after = pltpu.roll(right, (LANES - x) % LANES, 1)
        before = pltpu.roll(left, LANES - 1 - x, 1)
        beyond_ref[x] = jnp.where(lane == 0, after, before).astype(bf16)
    for k in range(2):
        field = dot(plane_ref[k], depth_ref[k], ((1,), (0,)))
        for tile in range(tiles):
            field_ref[k, tile] = field[:, tile * LANES : (tile + 1) * LANES]
    squared = joined(sums)
    cells = jnp.full(squared.shape, float(KNOT * KNOT), f32)
    first, second = plane_ref[0], plane_ref[1]
    diag_depth_ref[0] = dot(first * first, squared, ((0,), (0,)))
    diag_depth_ref[1] = dot(second * second, cells, ((0,), (0,)))
    first, second = depth_ref[0], depth_ref[1]
    diag_plane_ref[0] = dot(squared, first * first, ((1,), (1,)))
    diag_plane_ref[1] = dot(cells, second * second, ((1,), (1,)))


def terms(sums, plane, depth_factors, inner, outer, depth):
    nodes, width = plane.shape[1], depth_factors.shape[2]
    return pl.pallas_call(
        terms_kernel,
        out_shape=[
            jax.ShapeDtypeStruct((2, width // LANES, nodes, LANES), f32),
            jax.ShapeDtypeStruct((2, RANK, width), f32),
            jax.ShapeDtypeStruct((2, nodes, RANK), f32),
            jax.ShapeDtypeStruct((depth,) + inner.shape, bf16),
        ],
        compiler_params=plain_params(),
        cost_estimate=pl.CostEstimate(flops=40 * nodes * RANK * width, bytes_accessed=1 << 20, transcendentals=0),
        name="terms",
    )(sums, plane, depth_factors, inner, outer)


def warp_kernel(
    cells_ref, image_hbm, shift_hbm, beyond_ref, across_ref, inside_ref,
    across_tile_ref, inside_tile_ref, field, plane_ref, depth_ref,
    diag_depth_ref, diag_plane_ref,
    residual_hbm, depth_out, plane_out,
    ahead_ref, here_ref, behind_ref, wide, bands, blocks, energy, held,
    image_ref, shift_ref, residual_ref, got, sent,
):
    step = pl.program_id(0)
    last = pl.num_programs(0) - 1
    planes, rows, width = cells_ref.shape
    nodes = rows // KNOT
    tiles = width // LANES
    window = (ahead_ref, here_ref, behind_ref)
    pitch = rows + 2 * TOP
    plane_rows = tiles * pitch
    block_rows = planes * plane_rows

    @pl.when(step == 0)
    def _():
        row = lax.broadcasted_iota(jnp.int32, bands.shape[1:], 0)
        column = lax.broadcasted_iota(jnp.int32, bands.shape[1:], 1)
        one, none = jnp.ones(bands.shape[1:], f32), jnp.zeros(bands.shape[1:], f32)
        up, down = jnp.where(row == column + 1, one, none), jnp.where(row == column, one, none)
        bands[0] = (up - down).astype(bf16)
        up = jnp.where(row == column + LANES, one, none)
        down = jnp.where(row == column + LANES - 1, one, none)
        bands[1] = (up - down).astype(bf16)
        energy[...] = jnp.zeros_like(energy)
        for c in range(3):
            window[c][3 * block_rows - plane_rows : 3 * block_rows, :] = jnp.zeros((plane_rows, LANES), f32)

    def fetched(n):
        slot, part = n % 2, pl.ds(n * planes, planes)
        copies = [
            pltpu.make_async_copy(shift_hbm.at[axis, part], shift_ref.at[slot, axis], got.at[slot, axis])
            for axis in range(3)
        ]
        return copies + [pltpu.make_async_copy(image_hbm.at[part], image_ref.at[slot], got.at[slot, 3])]

    def leaving(n):
        slot, part = n % 2, pl.ds(n * planes, planes)
        return pltpu.make_async_copy(residual_ref.at[slot], residual_hbm.at[part], sent.at[slot])

    @pl.when(step < last)
    def _():
        for copy in fetched(step):
            copy.start()

    @pl.when(step < last)
    def _():
        slot = (step % 3) * block_rows
        odd = lax.axis_index("gy") % 2 == 1

        def rim_rows(row, tile):
            both = jnp.concatenate([row[...].astype(f32), tile[...].astype(f32)], axis=1)
            return jnp.where(step % 2 == 0, both[0:planes], both[planes:])

        across, inside = rim_rows(across_ref, across_tile_ref), rim_rows(inside_ref, inside_tile_ref)
        low, high = jnp.where(odd, inside, across), jnp.where(odd, across, inside)
        at = lax.broadcasted_iota(jnp.int32, (2 * TOP, width + LANES), 0)
        for k in range(planes):
            first = k * pitch
            wide[first : first + rows, 0:width] = cells_ref[k]
            wide[first : first + rows, width:] = beyond_ref[k]
            rim = jnp.where(at == TOP, high[k : k + 1], jnp.where(at == TOP - 1, low[k : k + 1], 0.0))
            wide[first + rows : first + pitch, :] = rim.astype(bf16)

        def put(c, tile, values):
            for k in range(planes):
                first = pl.multiple_of(slot + k * plane_rows + tile * pitch, 8)
                mine = values[k * pitch : (k + 1) * pitch]
                window[c][pl.ds(first + TOP, rows), :] = mine[0:rows]
                window[c][pl.ds(first, TOP), :] = mine[rows : rows + TOP]
                window[c][pl.ds(first + TOP + rows, TOP), :] = mine[rows + TOP :]

        pieces = width // (2 * LANES)
        for piece in range(pieces):
            start = 2 * LANES * piece
            after = wide[:, start : start + 3 * LANES]
            if piece == 0:
                before = jnp.concatenate([wide[:, width:], wide[:, 0 : 2 * LANES]], axis=1)
            else:
                before = wide[:, start - LANES : start + 2 * LANES]
            ahead = jnp.dot(after, bands[0], preferred_element_type=f32)
            behind = jnp.dot(before, bands[1], preferred_element_type=f32)
            for half in range(2):
                mine = slice(half * LANES, (half + 1) * LANES)
                put(0, 2 * piece + half, ahead[:, mine])
                put(1, 2 * piece + half, wide[:, start + half * LANES : start + (half + 1) * LANES].astype(f32))
                put(2, 2 * piece + half, behind[:, mine])

    @pl.when(step == last)
    def _():
        first = pl.multiple_of((step % 3) * block_rows, 8)
        for c in range(3):
            window[c][pl.ds(first, plane_rows), :] = jnp.zeros((plane_rows, LANES), f32)

    @pl.when(step > 0)
    def _():
        block = step - 1
        here_slot = block % 2
        for copy in fetched(block):
            copy.wait()

        @pl.when(block > 1)
        def _():
            leaving(block - 2).wait()

        mid = (step + 2) % 3
        first_rows = (
            jnp.where(mid == 0, 3, mid) * block_rows - plane_rows,
            mid * block_rows,
            jnp.where(mid == 2, 0, mid + 1) * block_rows,
        )

        def one(t, total):
            tile = t % tiles
            pair = t // tiles
            at = pl.multiple_of(tile * LANES, LANES)
            top = pl.multiple_of(pair * 16, 16)
            origins = [first + tile * pitch + top + TOP for first in first_rows]
            for half in range(2):
                node = (step - 1) * nodes + pair * 2 + half
                mine = slice(8 * half, 8 * half + 8)

                def taps(x):
                    part = 0 if x == 0 else 2 if x == planes + 1 else 1
                    plus = (x - 1) * plane_rows + 8 * half if part == 1 else 8 * half
                    return [
                        [window[c][pl.ds(origins[part] + (plus + b), 8), :] for c in range(3)] for b in (-1, 0, 1)
                    ]

                contrast = jnp.broadcast_to(field[0, tile, pl.ds(node, 1), :], (8, LANES))
                brightness = jnp.broadcast_to(field[1, tile, pl.ds(node, 1), :], (8, LANES))
                by_image = jnp.zeros((8, LANES), f32)
                plain = jnp.zeros((8, LANES), f32)
                here = taps(1)
                for k in range(planes):
                    before, after = taps(k), taps(k + 2)
                    place = (k, pl.ds(top, 16), pl.ds(at, LANES))
                    sx, sy, sz = (shift_ref[(here_slot, axis) + place].astype(f32)[mine] for axis in range(3))
                    image = image_ref[(here_slot,) + place].astype(f32)[mine]
                    px, py, pz = sx > 0, sy > 0, sz > 0
                    ax, ay = jnp.abs(sx), jnp.abs(sy)

                    def sides(c):
                        far = [jnp.where(px, after[b][c], before[b][c]) for b in range(3)]
                        near = [here[b][c] for b in range(3)]
                        return [(v[1], jnp.where(py, v[2], v[0])) for v in (near, far)]

                    ahead, middle, behind = sides(0), sides(1), sides(2)
                    lines = []
                    for b in range(2):
                        near, far = (middle[v][b] + sz * jnp.where(pz, ahead[v][b], behind[v][b]) for v in range(2))
                        lines.append(near + ax * (far - near))
                    warped = lines[0] + ay * (lines[1] - lines[0])
                    misfit = warped - contrast * image - brightness
                    if half == 0:
                        held[k] = misfit
                    else:
                        residual_ref[(here_slot,) + place] = jnp.concatenate([held[k], misfit], axis=0).astype(bf16)
                    by_image = by_image + misfit * image
                    plain = plain + misfit
                    total = total + misfit * misfit
                    here = after
                for k, value in ((0, by_image), (1, plain)):
                    blocks[k, tile, pl.ds(node, 1), :] = jnp.sum(value, axis=0, keepdims=True)
            return total

        energy[...] = lax.fori_loop(0, (rows // 16) * tiles, one, energy[...])
        leaving(block).start()

    @pl.when(step == last)
    def _():
        parts = depth_out.shape[0]
        share = RANK // parts
        sums = [joined(blocks.at[k]) for k in range(2)]
        kinds = [split_dot(plane_ref[k], sums[k], 0) for k in range(2)]
        kinds = kinds + [diag_depth_ref[0], diag_depth_ref[1]]
        half = width // 2
        for p in range(parts):
            rows = slice(p * share, (p + 1) * share)
            for k in range(2):
                mine = slice(k * share, (k + 1) * share)
                depth_out[p, mine, 0:width] = kinds[k][rows]
                depth_out[p, mine, width : width + half] = kinds[2][rows, k * half : (k + 1) * half]
                depth_out[p, mine, width + half :] = kinds[3][rows, 0:LANES]
        local = jnp.sum(energy[...])
        kinds = [split_dot(sums[k], depth_ref[k], 1) for k in range(2)]
        kinds = kinds + [diag_plane_ref[0], diag_plane_ref[1]]
        for k in range(4):
            plane_out[:, k * RANK : (k + 1) * RANK] = kinds[k]
        count = plane_out.shape[0]
        plane_out[count // 2 :, 3 * RANK :] = jnp.full((count // 2, RANK), local, f32)
        leaving(last - 2).wait()
        leaving(last - 1).wait()


def warp(
    cells, image, shift, beyond, across, inside, across_tile, inside_tile, field, plane, depth_factors, diag_depth,
    diag_plane, parts
):
    depth, rows, width = cells.shape
    nodes = plane.shape[1]
    tiles = width // LANES
    count = depth // KNOT
    ahead = lambda i: (jnp.minimum(i, count - 1), 0, 0)
    flat = lambda i: (0, 0)
    whole = lambda i: (0, 0, 0)
    return pl.pallas_call(
        warp_kernel,
        grid=(count + 1,),
        in_specs=[
            pl.BlockSpec((KNOT, rows, width), ahead),
            pl.BlockSpec(memory_space=pl.ANY),
            pl.BlockSpec(memory_space=pl.ANY),
            pl.BlockSpec((KNOT, rows, LANES), ahead),
            pl.BlockSpec((2 * KNOT, across.shape[1]), lambda i: (jnp.minimum(i, count - 1) // 2, 0)),
            pl.BlockSpec((2 * KNOT, inside.shape[1]), lambda i: (jnp.minimum(i, count - 1) // 2, 0)),
            pl.BlockSpec((2 * KNOT, LANES), lambda i: (jnp.minimum(i, count - 1) // 2, 0)),
            pl.BlockSpec((2 * KNOT, LANES), lambda i: (jnp.minimum(i, count - 1) // 2, 0)),
            pl.BlockSpec(field.shape, lambda i: (0, 0, 0, 0)),
            pl.BlockSpec(plane.shape, whole),
            pl.BlockSpec(depth_factors.shape, whole),
            pl.BlockSpec(diag_depth.shape, whole),
            pl.BlockSpec(diag_plane.shape, whole),
        ],
        out_specs=[
            pl.BlockSpec(memory_space=pl.ANY),
            pl.BlockSpec((parts, 2 * RANK // parts, width + width // 2 + LANES), whole),
            pl.BlockSpec((nodes, 4 * RANK), flat),
        ],
        out_shape=[
            jax.ShapeDtypeStruct(cells.shape, bf16),
            jax.ShapeDtypeStruct((parts, 2 * RANK // parts, width + width // 2 + LANES), f32),
            jax.ShapeDtypeStruct((nodes, 4 * RANK), f32),
        ],
        scratch_shapes=[
            *[pltpu.VMEM((3 * KNOT * tiles * (rows + 2 * TOP), LANES), f32)] * 3,
            pltpu.VMEM((KNOT * (rows + 2 * TOP), width + LANES), bf16),
            pltpu.VMEM((2, 3 * LANES, 2 * LANES), bf16),
            pltpu.VMEM((2, tiles, nodes, LANES), f32),
            pltpu.VMEM((8, LANES), f32),
            pltpu.VMEM((KNOT, 8, LANES), f32),
            pltpu.VMEM((2, KNOT, rows, width), bf16),
            pltpu.VMEM((2, 3, KNOT, rows, width), bf16),
            pltpu.VMEM((2, KNOT, rows, width), bf16),
            pltpu.SemaphoreType.DMA((2, 4)),
            pltpu.SemaphoreType.DMA((2,)),
        ],
        compiler_params=pltpu.CompilerParams(dimension_semantics=("arbitrary",), vmem_limit_bytes=53000000),
        cost_estimate=pl.CostEstimate(flops=60 * cells.size, bytes_accessed=12 * cells.size, transcendentals=0),
        name="warp",
    )(cells, image, shift, beyond, across, inside, across_tile, inside_tile, field, plane, depth_factors, diag_depth, diag_plane)


def gather_kernel(depth_ref, *refs):
    depth_out, plane_out = refs[-2:]
    total = jnp.sum(depth_ref[...], axis=0)
    found = [ref[...] for ref in refs[:-2]]
    while len(found) > 1:
        half = len(found) // 2
        found = [found[k] + found[k + half] for k in range(half)]
    planes = found[0]
    plane_out[...] = planes
    cells = planes.shape[0]
    share, width = total.shape[0] // 2, total.shape[1]
    row = lax.broadcasted_iota(jnp.int32, total.shape, 0)
    lane = lax.broadcasted_iota(jnp.int32, total.shape, 1)
    partial = planes[cells - 1, 4 * RANK - 1]
    total = jnp.where((row >= share) & (lane >= width - LANES), partial, total)
    for p in range(depth_out.shape[0]):
        depth_out[p] = total


def step_kernel(full_z, node_count, depth_ref, plane_ref, depth_out, plane_out):
    parts, share, width = depth_ref.shape[0], depth_ref.shape[1] // 2, depth_out.shape[2]
    half = width // 2
    energy = depth_ref[0, share, width + half]
    for p in range(1, parts):
        energy = energy + depth_ref[p, share, width + half]
    lam_depth = damping * energy / full_z
    lam_plane = damping * RANK * energy / node_count
    for p in range(parts):
        got = depth_ref[p]
        rows = slice(p * share, (p + 1) * share)
        first, second = got[0:share], got[share:]
        squared = jnp.concatenate([first[:, width : width + half], second[:, width : width + half]], axis=1)
        levels = jnp.concatenate([first[:, width + half :]] * (width // LANES), axis=1)
        depth_out[0, rows, :] = first[:, 0:width] / (squared + lam_depth + epsilon)
        depth_out[1, rows, :] = second[:, 0:width] / (levels + lam_depth + epsilon)
    planes = plane_ref[...]
    plane_out[0] = planes[:, 0:RANK] / (planes[:, 2 * RANK : 3 * RANK] + lam_plane + epsilon)
    plane_out[1] = planes[:, RANK : 2 * RANK] / (planes[0:1, 3 * RANK :] + lam_plane + epsilon)


def local(image, deformed, displacement, plane_factors, depth_factors):
    n_gy, n_gz = lax.axis_size("gy"), lax.axis_size("gz")
    nodes_x, nodes_y = plane_factors.shape[2:]
    plane = jnp.transpose(plane_factors, (0, 2, 3, 1)).reshape(2, nodes_x * nodes_y, RANK)
    inner, outer, across, inside = ends(deformed)
    inner = swapped(inner, "gz", 0)
    outer = swapped(outer, "gz", 1)
    inside = swapped(inside, "gy", 0)
    across = swapped(across, "gy", 1)
    across_tile, inside_tile = corners(inner, outer, deformed.shape[0])
    sums = squares(image, across_tile)
    inside_tile = swapped(inside_tile, "gy", 0)
    across_tile = swapped(across_tile, "gy", 1)
    field, diag_depth, diag_plane, beyond = terms(sums, plane, depth_factors, inner, outer, deformed.shape[0])
    residual, depth_terms, plane_terms = warp(
        deformed, image, displacement, beyond, across, inside, across_tile, inside_tile, field, plane, depth_factors,
        diag_depth, diag_plane, n_gy,
    )
    depth_terms = lax.all_to_all(depth_terms, "gy", 0, 0)
    others = [
        lax.ppermute(plane_terms, "gz", [(i, i ^ hop) for i in range(n_gz)]) for hop in range(1, n_gz)
    ]
    depth_terms, plane_terms = pl.pallas_call(
        gather_kernel,
        out_shape=[
            jax.ShapeDtypeStruct(depth_terms.shape, f32),
            jax.ShapeDtypeStruct(plane_terms.shape, f32),
        ],
        compiler_params=plain_params(),
        name="gather",
    )(depth_terms, plane_terms, *others)
    depth_terms = lax.all_to_all(depth_terms, "gy", 0, 0)
    width = depth_factors.shape[2]
    step_depth, step_plane = pl.pallas_call(
        functools.partial(step_kernel, width * n_gz, nodes_x * nodes_y * n_gy),
        out_shape=[
            jax.ShapeDtypeStruct(depth_factors.shape, f32),
            jax.ShapeDtypeStruct(plane.shape, f32),
        ],
        compiler_params=plain_params(),
        name="steps",
    )(depth_terms, plane_terms)
    step_plane = jnp.transpose(step_plane.reshape(2, nodes_x, nodes_y, RANK), (0, 3, 1, 2))
    return residual, step_plane, step_depth


def solution(mesh):
    placed = (
        P(None, "gy", "gz"),
        P(None, "gy", "gz"),
        P(None, None, "gy", "gz"),
        P(None, None, None, "gy"),
        P(None, None, "gz"),
    )
    return jax.shard_map(
        local,
        mesh=mesh,
        in_specs=placed,
        out_specs=(P(None, "gy", "gz"), P(None, None, None, "gy"), P(None, None, "gz")),
        check_vma=False,
    )
```

```python
import functools

import jax
import jax.numpy as jnp
from jax import lax
from jax.experimental import pallas as pl
from jax.experimental.pallas import tpu as pltpu
from jax.sharding import PartitionSpec as P

RANK = 32
KNOT = 8
LANES = 128
TOP = 8

epsilon = 1e-06
damping = 0.01
highest = lax.Precision.HIGHEST
f32 = jnp.float32
bf16 = jnp.bfloat16


def dot(left, right, dims):
    return lax.dot_general(left, right, ((dims[0], dims[1]), ((), ())), precision=highest, preferred_element_type=f32)


def split_dot(left, right, dim):
    left_high, right_high = left.astype(bf16), right.astype(bf16)
    left_low = (left - left_high.astype(f32)).astype(bf16)
    right_low = (right - right_high.astype(f32)).astype(bf16)
    left = jnp.concatenate([left_high, left_high, left_low], axis=dim)
    right = jnp.concatenate([right_high, right_low, right_high], axis=dim)
    return lax.dot_general(left, right, (((dim,), (dim,)), ((), ())), preferred_element_type=f32)


def joined(ref):
    return jnp.concatenate([ref[tile] for tile in range(ref.shape[0])], axis=1)


def plain_params():
    return pltpu.CompilerParams(vmem_limit_bytes=32000000)


def ends_kernel(cells_hbm, inner_ref, outer_ref, across_ref, inside_ref, cells, got):
    depth, rows, width = cells.shape
    chunks = got.shape[0]
    planes = depth // chunks

    def fetched(n):
        part = pl.ds(n * planes, planes)
        return pltpu.make_async_copy(cells_hbm.at[part], cells.at[part], got.at[n])

    for n in range(chunks):
        fetched(n).start()
    odd_y, odd_z = lax.axis_index("gy") % 2 == 1, lax.axis_index("gz") % 2 == 1
    lane = lax.broadcasted_iota(jnp.int32, (rows, LANES), 1)
    first = jnp.zeros((rows, LANES), f32)
    last = jnp.zeros((rows, LANES), f32)
    for n in range(chunks):
        fetched(n).wait()
        for x in range(n * planes, (n + 1) * planes):
            near = cells[x, :, 0:LANES].astype(f32)
            far = cells[x, :, width - LANES : width].astype(f32)
            first = jnp.where(lane == x, pltpu.roll(near, x, 1), first)
            last = jnp.where(lane == x, pltpu.roll(far, (x + 1) % LANES, 1), last)
        if (n + 1) * planes % 16 == 0:
            x = (n + 1) * planes - 16
            low = [cells[x + k, 0:16, :].astype(f32)[0:1] for k in range(16)]
            high = [cells[x + k, rows - 16 : rows, :].astype(f32)[15:16] for k in range(16)]
            low, high = jnp.concatenate(low, axis=0), jnp.concatenate(high, axis=0)
            across_ref[x : x + 16, :] = jnp.where(odd_y, high, low).astype(bf16)
            inside_ref[x : x + 16, :] = jnp.where(odd_y, low, high).astype(bf16)
    inner_ref[...] = jnp.where(odd_z, first, last).astype(bf16)
    outer_ref[...] = jnp.where(odd_z, last, first).astype(bf16)


def ends(cells):
    depth, rows, width = cells.shape
    return pl.pallas_call(
        ends_kernel,
        in_specs=[pl.BlockSpec(memory_space=pl.ANY)],
        out_shape=[jax.ShapeDtypeStruct((rows, LANES), bf16)] * 2 + [jax.ShapeDtypeStruct((depth, width), bf16)] * 2,
        scratch_shapes=[pltpu.VMEM(cells.shape, bf16), pltpu.SemaphoreType.DMA((depth // KNOT,))],
        compiler_params=pltpu.CompilerParams(vmem_limit_bytes=61000000),
        cost_estimate=pl.CostEstimate(flops=cells.size, bytes_accessed=2 * cells.size, transcendentals=0),
        name="ends",
    )(cells)


def z_sides(inner_ref, outer_ref):
    odd = lax.axis_index("gz") % 2 == 1
    inner, outer = inner_ref[...].astype(f32), outer_ref[...].astype(f32)
    return jnp.where(odd, inner, outer), jnp.where(odd, outer, inner)


def corners_kernel(inner_ref, outer_ref, across_out, inside_out):
    rows, depth = inner_ref.shape[0], across_out.shape[0]
    odd = lax.axis_index("gy") % 2 == 1
    lane = lax.broadcasted_iota(jnp.int32, (depth, LANES), 1)
    pad = jnp.zeros((LANES - rows, LANES), f32)
    left, right = z_sides(inner_ref, outer_ref)
    left = jnp.transpose(jnp.concatenate([left, pad], axis=0))[0:depth]
    right = jnp.transpose(jnp.concatenate([right, pad], axis=0))[0:depth]
    low, high = (
        jnp.where(lane == 0, pltpu.roll(right, (LANES - row) % LANES, 1), pltpu.roll(left, LANES - 1 - row, 1))
        for row in (0, rows - 1)
    )
    across_out[...] = jnp.where(odd, high, low).astype(bf16)
    inside_out[...] = jnp.where(odd, low, high).astype(bf16)


def corners(inner, outer, depth):
    return pl.pallas_call(
        corners_kernel,
        out_shape=[jax.ShapeDtypeStruct((depth, LANES), bf16)] * 2,
        compiler_params=plain_params(),
        cost_estimate=pl.CostEstimate(flops=1 << 34, bytes_accessed=1 << 17, transcendentals=0),
        name="corners",
    )(inner, outer)


def swapped(part, axis, start):
    count = lax.axis_size(axis)
    pairs = [(i, i + 1) for i in range(start, count - 1, 2)]
    return lax.ppermute(part, axis, pairs + [(j, i) for i, j in pairs])


def squares_kernel(image_ref, later_ref, sums):
    depth, rows, width = image_ref.shape
    tiles = width // LANES

    def one(t, carry):
        block, tile = t // tiles, t % tiles
        at = pl.multiple_of(tile * LANES, LANES)
        for pair in range(rows // 16):
            total = jnp.zeros((16, LANES), f32)
            for k in range(KNOT):
                values = image_ref[block * KNOT + k, 16 * pair : 16 * pair + 16, pl.ds(at, LANES)].astype(f32)
                total = total + values * values
            for half in range(2):
                row = block * (rows // KNOT) + 2 * pair + half
                sums[tile, pl.ds(row, 1), :] = jnp.sum(total[8 * half : 8 * half + 8], axis=0, keepdims=True)
        return carry

    lax.fori_loop(0, depth // KNOT * tiles, one, 0)


def squares(image, later):
    depth, rows, width = image.shape
    return pl.pallas_call(
        squares_kernel,
        out_shape=jax.ShapeDtypeStruct((width // LANES, depth * rows // KNOT**2, LANES), f32),
        compiler_params=plain_params(),
        cost_estimate=pl.CostEstimate(flops=3 * image.size, bytes_accessed=2 * image.size, transcendentals=0),
        name="squares",
    )(image, later)


def terms_kernel(
    sums, plane_ref, depth_ref, inner_ref, outer_ref, field_ref, diag_depth_ref, diag_plane_ref, beyond_ref
):
    tiles = sums.shape[0]
    left, right = z_sides(inner_ref, outer_ref)
    lane = lax.broadcasted_iota(jnp.int32, left.shape, 1)
    for x in range(beyond_ref.shape[0]):
        after = pltpu.roll(right, (LANES - x) % LANES, 1)
        before = pltpu.roll(left, LANES - 1 - x, 1)
        beyond_ref[x] = jnp.where(lane == 0, after, before).astype(bf16)
    for k in range(2):
        field = dot(plane_ref[k], depth_ref[k], ((1,), (0,)))
        for tile in range(tiles):
            field_ref[k, tile] = field[:, tile * LANES : (tile + 1) * LANES]
    squared = joined(sums)
    cells = jnp.full(squared.shape, float(KNOT * KNOT), f32)
    first, second = plane_ref[0], plane_ref[1]
    diag_depth_ref[0] = dot(first * first, squared, ((0,), (0,)))
    diag_depth_ref[1] = dot(second * second, cells, ((0,), (0,)))
    first, second = depth_ref[0], depth_ref[1]
    diag_plane_ref[0] = dot(squared, first * first, ((1,), (1,)))
    diag_plane_ref[1] = dot(cells, second * second, ((1,), (1,)))


def terms(sums, plane, depth_factors, inner, outer, depth):
    nodes, width = plane.shape[1], depth_factors.shape[2]
    return pl.pallas_call(
        terms_kernel,
        out_shape=[
            jax.ShapeDtypeStruct((2, width // LANES, nodes, LANES), f32),
            jax.ShapeDtypeStruct((2, RANK, width), f32),
            jax.ShapeDtypeStruct((2, nodes, RANK), f32),
            jax.ShapeDtypeStruct((depth,) + inner.shape, bf16),
        ],
        compiler_params=plain_params(),
        cost_estimate=pl.CostEstimate(flops=40 * nodes * RANK * width, bytes_accessed=1 << 20, transcendentals=0),
        name="terms",
    )(sums, plane, depth_factors, inner, outer)


def warp_kernel(
    cells_ref, image_hbm, shift_hbm, beyond_ref, across_ref, inside_ref,
    across_tile_ref, inside_tile_ref, field, plane_ref, depth_ref,
    diag_depth_ref, diag_plane_ref,
    residual_hbm, depth_out, plane_out,
    ahead_ref, here_ref, behind_ref, wide, bands, blocks, energy,
    image_ref, shift_ref, residual_ref, got, sent,
):
    step = pl.program_id(0)
    last = pl.num_programs(0) - 1
    planes, rows, width = cells_ref.shape
    nodes = rows // KNOT
    tiles = width // LANES
    window = (ahead_ref, here_ref, behind_ref)
    pitch = rows + 2 * TOP
    plane_rows = tiles * pitch
    block_rows = planes * plane_rows

    @pl.when(step == 0)
    def _():
        row = lax.broadcasted_iota(jnp.int32, bands.shape[1:], 0)
        column = lax.broadcasted_iota(jnp.int32, bands.shape[1:], 1)
        one, none = jnp.ones(bands.shape[1:], f32), jnp.zeros(bands.shape[1:], f32)
        up, down = jnp.where(row == column + 1, one, none), jnp.where(row == column, one, none)
        bands[0] = (up - down).astype(bf16)
        up = jnp.where(row == column + LANES, one, none)
        down = jnp.where(row == column + LANES - 1, one, none)
        bands[1] = (up - down).astype(bf16)
        energy[...] = jnp.zeros_like(energy)
        for c in range(3):
            window[c][3 * block_rows - plane_rows : 3 * block_rows, :] = jnp.zeros((plane_rows, LANES), f32)

    def fetched(n):
        slot, part = n % 2, pl.ds(n * planes, planes)
        copies = [
            pltpu.make_async_copy(shift_hbm.at[axis, part], shift_ref.at[slot, axis], got.at[slot, axis])
            for axis in range(3)
        ]
        return copies + [pltpu.make_async_copy(image_hbm.at[part], image_ref.at[slot], got.at[slot, 3])]

    def leaving(n):
        slot, part = n % 2, pl.ds(n * planes, planes)
        return pltpu.make_async_copy(residual_ref.at[slot], residual_hbm.at[part], sent.at[slot])

    @pl.when(step < last)
    def _():
        for copy in fetched(step):
            copy.start()

    @pl.when(step < last)
    def _():
        slot = (step % 3) * block_rows
        odd = lax.axis_index("gy") % 2 == 1

        def rim_rows(row, tile):
            both = jnp.concatenate([row[...].astype(f32), tile[...].astype(f32)], axis=1)
            return jnp.where(step % 2 == 0, both[0:planes], both[planes:])

        across, inside = rim_rows(across_ref, across_tile_ref), rim_rows(inside_ref, inside_tile_ref)
        low, high = jnp.where(odd, inside, across), jnp.where(odd, across, inside)
        at = lax.broadcasted_iota(jnp.int32, (2 * TOP, width + LANES), 0)
        for k in range(planes):
            first = k * pitch
            wide[first : first + rows, 0:width] = cells_ref[k]
            wide[first : first + rows, width:] = beyond_ref[k]
            rim = jnp.where(at == TOP, high[k : k + 1], jnp.where(at == TOP - 1, low[k : k + 1], 0.0))
            wide[first + rows : first + pitch, :] = rim.astype(bf16)

        def put(c, tile, values):
            for k in range(planes):
                first = pl.multiple_of(slot + k * plane_rows + tile * pitch, 8)
                mine = values[k * pitch : (k + 1) * pitch]
                window[c][pl.ds(first + TOP, rows), :] = mine[0:rows]
                window[c][pl.ds(first, TOP), :] = mine[rows : rows + TOP]
                window[c][pl.ds(first + TOP + rows, TOP), :] = mine[rows + TOP :]

        pieces = width // (2 * LANES)
        for piece in range(pieces):
            start = 2 * LANES * piece
            after = wide[:, start : start + 3 * LANES]
            if piece == 0:
                before = jnp.concatenate([wide[:, width:], wide[:, 0 : 2 * LANES]], axis=1)
            else:
                before = wide[:, start - LANES : start + 2 * LANES]
            ahead = jnp.dot(after, bands[0], preferred_element_type=f32)
            behind = jnp.dot(before, bands[1], preferred_element_type=f32)
            for half in range(2):
                mine = slice(half * LANES, (half + 1) * LANES)
                put(0, 2 * piece + half, ahead[:, mine])
                put(1, 2 * piece + half, wide[:, start + half * LANES : start + (half + 1) * LANES].astype(f32))
                put(2, 2 * piece + half, behind[:, mine])

    @pl.when(step == last)
    def _():
        first = pl.multiple_of((step % 3) * block_rows, 8)
        for c in range(3):
            window[c][pl.ds(first, plane_rows), :] = jnp.zeros((plane_rows, LANES), f32)

    @pl.when(step > 0)
    def _():
        block = step - 1
        here_slot = block % 2
        for copy in fetched(block):
            copy.wait()

        @pl.when(block > 1)
        def _():
            leaving(block - 2).wait()

        mid = (step + 2) % 3
        first_rows = (
            jnp.where(mid == 0, 3, mid) * block_rows - plane_rows,
            mid * block_rows,
            jnp.where(mid == 2, 0, mid + 1) * block_rows,
        )

        def one(t, total):
            tile = t % tiles
            pair = t // tiles
            at = pl.multiple_of(tile * LANES, LANES)
            top = pl.multiple_of(pair * 16, 16)
            origins = [first + tile * pitch + top + TOP for first in first_rows]
            first_node = (step - 1) * nodes + pair * 2

            def taps(x, half):
                part = 0 if x == 0 else 2 if x == planes + 1 else 1
                plus = (x - 1) * plane_rows + 8 * half if part == 1 else 8 * half
                return [[window[c][pl.ds(origins[part] + (plus + b), 8), :] for c in range(3)] for b in (-1, 0, 1)]

            def node_rows(k, half):
                return jnp.broadcast_to(field[k, tile, pl.ds(first_node + half, 1), :], (8, LANES))

            by_image = [jnp.zeros((8, LANES), f32) for _ in range(2)]
            plain = [jnp.zeros((8, LANES), f32) for _ in range(2)]
            here = [taps(1, half) for half in range(2)]
            for k in range(planes):
                place = (k, pl.ds(top, 16), pl.ds(at, LANES))
                inputs = [shift_ref[(here_slot, axis) + place].astype(f32) for axis in range(3)]
                inputs.append(image_ref[(here_slot,) + place].astype(f32))
                results = []
                for half in range(2):
                    before, after = taps(k, half), taps(k + 2, half)
                    sx, sy, sz, image = (v[8 * half : 8 * half + 8] for v in inputs)
                    px, py, pz = sx > 0, sy > 0, sz > 0
                    ax, ay = jnp.abs(sx), jnp.abs(sy)

                    def sides(c):
                        far = [jnp.where(px, after[b][c], before[b][c]) for b in range(3)]
                        near = [here[half][b][c] for b in range(3)]
                        return [(v[1], jnp.where(py, v[2], v[0])) for v in (near, far)]

                    ahead, middle, behind = sides(0), sides(1), sides(2)
                    lines = []
                    for b in range(2):
                        near, far = (middle[v][b] + sz * jnp.where(pz, ahead[v][b], behind[v][b]) for v in range(2))
                        lines.append(near + ax * (far - near))
                    warped = lines[0] + ay * (lines[1] - lines[0])
                    misfit = warped - node_rows(0, half) * image - node_rows(1, half)
                    results.append(misfit)
                    by_image[half] = by_image[half] + misfit * image
                    plain[half] = plain[half] + misfit
                    total = total + misfit * misfit
                    here[half] = after
                residual_ref[(here_slot,) + place] = jnp.concatenate(results, axis=0).astype(bf16)
            for half in range(2):
                for k, value in ((0, by_image[half]), (1, plain[half])):
                    blocks[k, tile, pl.ds(first_node + half, 1), :] = jnp.sum(value, axis=0, keepdims=True)
            return total

        energy[...] = lax.fori_loop(0, (rows // 16) * tiles, one, energy[...])
        leaving(block).start()

    @pl.when(step == last)
    def _():
        parts = depth_out.shape[0]
        share = RANK // parts
        sums = [joined(blocks.at[k]) for k in range(2)]
        kinds = [split_dot(plane_ref[k], sums[k], 0) for k in range(2)]
        kinds = kinds + [diag_depth_ref[0], diag_depth_ref[1]]
        half = width // 2
        for p in range(parts):
            rows = slice(p * share, (p + 1) * share)
            for k in range(2):
                mine = slice(k * share, (k + 1) * share)
                depth_out[p, mine, 0:width] = kinds[k][rows]
                depth_out[p, mine, width : width + half] = kinds[2][rows, k * half : (k + 1) * half]
                depth_out[p, mine, width + half :] = kinds[3][rows, 0:LANES]
        local = jnp.sum(energy[...])
        kinds = [split_dot(sums[k], depth_ref[k], 1) for k in range(2)]
        kinds = kinds + [diag_plane_ref[0], diag_plane_ref[1]]
        for k in range(4):
            plane_out[:, k * RANK : (k + 1) * RANK] = kinds[k]
        count = plane_out.shape[0]
        plane_out[count // 2 :, 3 * RANK :] = jnp.full((count // 2, RANK), local, f32)
        leaving(last - 2).wait()
        leaving(last - 1).wait()


def warp(
    cells, image, shift, beyond, across, inside, across_tile, inside_tile, field, plane, depth_factors, diag_depth,
    diag_plane, parts
):
    depth, rows, width = cells.shape
    nodes = plane.shape[1]
    tiles = width // LANES
    count = depth // KNOT
    ahead = lambda i: (jnp.minimum(i, count - 1), 0, 0)
    flat = lambda i: (0, 0)
    whole = lambda i: (0, 0, 0)
    return pl.pallas_call(
        warp_kernel,
        grid=(count + 1,),
        in_specs=[
            pl.BlockSpec((KNOT, rows, width), ahead),
            pl.BlockSpec(memory_space=pl.ANY),
            pl.BlockSpec(memory_space=pl.ANY),
            pl.BlockSpec((KNOT, rows, LANES), ahead),
            pl.BlockSpec((2 * KNOT, across.shape[1]), lambda i: (jnp.minimum(i, count - 1) // 2, 0)),
            pl.BlockSpec((2 * KNOT, inside.shape[1]), lambda i: (jnp.minimum(i, count - 1) // 2, 0)),
            pl.BlockSpec((2 * KNOT, LANES), lambda i: (jnp.minimum(i, count - 1) // 2, 0)),
            pl.BlockSpec((2 * KNOT, LANES), lambda i: (jnp.minimum(i, count - 1) // 2, 0)),
            pl.BlockSpec(field.shape, lambda i: (0, 0, 0, 0)),
            pl.BlockSpec(plane.shape, whole),
            pl.BlockSpec(depth_factors.shape, whole),
            pl.BlockSpec(diag_depth.shape, whole),
            pl.BlockSpec(diag_plane.shape, whole),
        ],
        out_specs=[
            pl.BlockSpec(memory_space=pl.ANY),
            pl.BlockSpec((parts, 2 * RANK // parts, width + width // 2 + LANES), whole),
            pl.BlockSpec((nodes, 4 * RANK), flat),
        ],
        out_shape=[
            jax.ShapeDtypeStruct(cells.shape, bf16),
            jax.ShapeDtypeStruct((parts, 2 * RANK // parts, width + width // 2 + LANES), f32),
            jax.ShapeDtypeStruct((nodes, 4 * RANK), f32),
        ],
        scratch_shapes=[
            *[pltpu.VMEM((3 * KNOT * tiles * (rows + 2 * TOP), LANES), f32)] * 3,
            pltpu.VMEM((KNOT * (rows + 2 * TOP), width + LANES), bf16),
            pltpu.VMEM((2, 3 * LANES, 2 * LANES), bf16),
            pltpu.VMEM((2, tiles, nodes, LANES), f32),
            pltpu.VMEM((8, LANES), f32),
            pltpu.VMEM((2, KNOT, rows, width), bf16),
            pltpu.VMEM((2, 3, KNOT, rows, width), bf16),
            pltpu.VMEM((2, KNOT, rows, width), bf16),
            pltpu.SemaphoreType.DMA((2, 4)),
            pltpu.SemaphoreType.DMA((2,)),
        ],
        compiler_params=pltpu.CompilerParams(dimension_semantics=("arbitrary",), vmem_limit_bytes=53000000),
        cost_estimate=pl.CostEstimate(flops=60 * cells.size, bytes_accessed=12 * cells.size, transcendentals=0),
        name="warp",
    )(cells, image, shift, beyond, across, inside, across_tile, inside_tile, field, plane, depth_factors, diag_depth, diag_plane)


def gather_kernel(depth_ref, *refs):
    depth_out, plane_out = refs[-2:]
    total = jnp.sum(depth_ref[...], axis=0)
    found = [ref[...] for ref in refs[:-2]]
    while len(found) > 1:
        half = len(found) // 2
        found = [found[k] + found[k + half] for k in range(half)]
    planes = found[0]
    plane_out[...] = planes
    cells = planes.shape[0]
    share, width = total.shape[0] // 2, total.shape[1]
    row = lax.broadcasted_iota(jnp.int32, total.shape, 0)
    lane = lax.broadcasted_iota(jnp.int32, total.shape, 1)
    partial = planes[cells - 1, 4 * RANK - 1]
    total = jnp.where((row >= share) & (lane >= width - LANES), partial, total)
    for p in range(depth_out.shape[0]):
        depth_out[p] = total


def step_kernel(full_z, node_count, depth_ref, plane_ref, depth_out, plane_out):
    parts, share, width = depth_ref.shape[0], depth_ref.shape[1] // 2, depth_out.shape[2]
    half = width // 2
    energy = depth_ref[0, share, width + half]
    for p in range(1, parts):
        energy = energy + depth_ref[p, share, width + half]
    lam_depth = damping * energy / full_z
    lam_plane = damping * RANK * energy / node_count
    for p in range(parts):
        got = depth_ref[p]
        rows = slice(p * share, (p + 1) * share)
        first, second = got[0:share], got[share:]
        squared = jnp.concatenate([first[:, width : width + half], second[:, width : width + half]], axis=1)
        levels = jnp.concatenate([first[:, width + half :]] * (width // LANES), axis=1)
        depth_out[0, rows, :] = first[:, 0:width] / (squared + lam_depth + epsilon)
        depth_out[1, rows, :] = second[:, 0:width] / (levels + lam_depth + epsilon)
    planes = plane_ref[...]
    plane_out[0] = planes[:, 0:RANK] / (planes[:, 2 * RANK : 3 * RANK] + lam_plane + epsilon)
    plane_out[1] = planes[:, RANK : 2 * RANK] / (planes[0:1, 3 * RANK :] + lam_plane + epsilon)


def local(image, deformed, displacement, plane_factors, depth_factors):
    n_gy, n_gz = lax.axis_size("gy"), lax.axis_size("gz")
    nodes_x, nodes_y = plane_factors.shape[2:]
    plane = jnp.transpose(plane_factors, (0, 2, 3, 1)).reshape(2, nodes_x * nodes_y, RANK)
    inner, outer, across, inside = ends(deformed)
    inner = swapped(inner, "gz", 0)
    outer = swapped(outer, "gz", 1)
    inside = swapped(inside, "gy", 0)
    across = swapped(across, "gy", 1)
    across_tile, inside_tile = corners(inner, outer, deformed.shape[0])
    sums = squares(image, across_tile)
    inside_tile = swapped(inside_tile, "gy", 0)
    across_tile = swapped(across_tile, "gy", 1)
    field, diag_depth, diag_plane, beyond = terms(sums, plane, depth_factors, inner, outer, deformed.shape[0])
    residual, depth_terms, plane_terms = warp(
        deformed, image, displacement, beyond, across, inside, across_tile, inside_tile, field, plane, depth_factors,
        diag_depth, diag_plane, n_gy,
    )
    depth_terms = lax.all_to_all(depth_terms, "gy", 0, 0)
    others = [
        lax.ppermute(plane_terms, "gz", [(i, i ^ hop) for i in range(n_gz)]) for hop in range(1, n_gz)
    ]
    depth_terms, plane_terms = pl.pallas_call(
        gather_kernel,
        out_shape=[
            jax.ShapeDtypeStruct(depth_terms.shape, f32),
            jax.ShapeDtypeStruct(plane_terms.shape, f32),
        ],
        compiler_params=plain_params(),
        name="gather",
    )(depth_terms, plane_terms, *others)
    depth_terms = lax.all_to_all(depth_terms, "gy", 0, 0)
    width = depth_factors.shape[2]
    step_depth, step_plane = pl.pallas_call(
        functools.partial(step_kernel, width * n_gz, nodes_x * nodes_y * n_gy),
        out_shape=[
            jax.ShapeDtypeStruct(depth_factors.shape, f32),
            jax.ShapeDtypeStruct(plane.shape, f32),
        ],
        compiler_params=plain_params(),
        name="steps",
    )(depth_terms, plane_terms)
    step_plane = jnp.transpose(step_plane.reshape(2, nodes_x, nodes_y, RANK), (0, 3, 1, 2))
    return residual, step_plane, step_depth


def solution(mesh):
    placed = (
        P(None, "gy", "gz"),
        P(None, "gy", "gz"),
        P(None, None, "gy", "gz"),
        P(None, None, None, "gy"),
        P(None, None, "gz"),
    )
    return jax.shard_map(
        local,
        mesh=mesh,
        in_specs=placed,
        out_specs=(P(None, "gy", "gz"), P(None, None, None, "gy"), P(None, None, "gz")),
        check_vma=False,
    )
```
